128 devices in a mesh: shard: 32 (over z_lo, x, y), rep: 4 (over z_hi, core).
Axes of the slice: x: 4, y: 4, z: 4 (z_hi: 2, z_lo: 2; z = z_hi * 2 + z_lo), core: 2. Of those that a mesh axis runs over, the one named last changes fastest.
Arguments:
- layer_input: bfloat16 [4, 4096, 1536], P('rep', 'shard'), may hold values from -6 to 6
- segments: int32 [4, 4096], P('rep', 'shard'), may hold values from 0 to 4, as said below
- choices: int32 [4, 4096, 8], P('rep', 'shard'), may hold values from 0 to 9, all different within a row; in each aligned block of 128 rows (0 to 127, 128 to 255, ..., all dimensions but the last counted through in order) at most 112 rows name the same one
- first_gain: bfloat16 [1536], P('shard'), may hold values from 0.25 to 1.75
- query_weight: bfloat16 [1536, 1536], P('shard'), may hold values from -0.625 to 0.625
- key_value_matrix: bfloat16 [1536, 1024], P('shard'), may hold values from -0.625 to 0.625
- output_weight: bfloat16 [1536, 1536], P('shard'), may hold values from -1 to 1
- second_gain: bfloat16 [1536], P('shard'), may hold values from 0.25 to 1.75
- router_weight: bfloat16 [1536, 10], P('shard'), may hold values from -0.078125 to 0.078125
- gate_up_weight: bfloat16 [1536, 10, 1024], P('shard'), may hold values from -0.15625 to 0.15625
- down_weight: bfloat16 [1536, 10, 512], P('shard'), may hold values from -6 to 6
- cotangent: bfloat16 [4, 4096, 1536], P('rep', 'shard'), may hold values from -6 to 6
Outputs:
- layer_output: bfloat16 [4, 4096, 1536], P('rep', 'shard')
- input_grad: float32 [4, 4096, 1536], P('rep', 'shard')
- first_gain_grad: float32 [1536], P('shard')
- query_weight_grad: float32 [1536, 1536], P('shard')
- key_value_weight_grad: float32 [1536, 1024], P('shard')
- output_weight_grad: float32 [1536, 1536], P('shard')
- second_gain_grad: float32 [1536], P('shard')
- router_weight_grad: float32 [1536, 10], P('shard')
- gate_up_weight_grad: float32 [1536, 10, 1024], P('shard')
- down_weight_grad: float32 [1536, 10, 512], P('shard')
The draws below stay inside these ranges and needn't reach their ends.
Inputs may be any that keep to these rules, and one draw needn't show every extreme that they name: `segments`: segment numbers start at 0 in each sequence, never fall along it, and rise by one at each document start; each sequence packs exactly five documents. `choices`: each token names 8 different experts. Among the 128 tokens of one device no expert is named more than 112 times.
All inputs are finite; a program needn't handle non-finite values.
Results may differ from the reference program's by a relative error of at most 0.033.
Values may be sent and summed in bfloat16 or wider, within the bound.
A program may use at most 320 MiB of HBM per device.

```python
import math
import jax
import jax.numpy as jnp
import numpy as np
from jax import lax

MODEL_DIM = 1536
QUERY_HEADS = 24
KEY_VALUE_HEADS = 8
HEAD_DIM = 64
FF = 512
TOP = 8
EXPERTS = 10
TOK_DEV = 128
SEQ = 4096
SEQS = 4
CAP = 112


def draw_segments(key, part):
    key = jax.random.fold_in(key, 11)
    seq_keys = jax.random.split(key, SEQS)
    shortest = max(1, SEQ // 20)
    longest = SEQ // 10

    def one_sequence(subkey):
        first_key, second_key, third_key, fourth_key = jax.random.split(subkey, 4)
        front_one = jax.random.randint(first_key, (), shortest, longest + 1)
        front_two = jax.random.randint(second_key, (), shortest, longest + 1)
        back_one = jax.random.randint(third_key, (), shortest, longest + 1)
        back_two = jax.random.randint(fourth_key, (), shortest, longest + 1)
        border_one = front_one
        border_two = front_one + front_two
        border_three = SEQ - back_one - back_two
        border_four = SEQ - back_two
        position = jnp.arange(SEQ, dtype=jnp.int32)
        return (position >= border_one).astype(jnp.int32) + (position >= border_two).astype(jnp.int32) + (position >= border_three).astype(jnp.int32) + (position >= border_four).astype(jnp.int32)
    return jax.vmap(one_sequence)(seq_keys)


def block_scale(stream_key, extent, shards, low, largest):
    def one(dim, shards_of):
        draws = jax.random.uniform(jax.random.fold_in(jax.random.fold_in(stream_key, 6), dim), (shards_of,), jnp.float32, low / len(shards), largest / len(shards))
        return jnp.repeat(jnp.exp(draws), extent[dim] // shards_of).reshape((-1,) + (1,) * (len(extent) - dim - 1))

    level = one(*shards[0])
    for cut in shards[1:]:
        level = level * one(*cut)
    return level


def deal_out(key, own, number, rows, number_of, top, limit, slope):
    order = jax.random.permutation(key, number_of)
    packed, common = portions_of(number_of, rows * top, limit, slope, True), portions_of(number_of, rows * top, limit, slope, False)
    places = jnp.arange(number_of)

    def named(lengths, rotation):
        used = int((lengths > 0).sum())
        fixed = max(1, used // 4)
        passed = fixed + (places - fixed + rotation * (used - fixed)) % max(1, number_of - fixed)
        return jnp.zeros((number_of,), jnp.int32).at[order[jnp.where(places < fixed, places, passed)]].set(jnp.asarray(lengths, jnp.int32))

    lengths = jnp.where(number % 4 == 0, named(packed, number // 4), named(common, number - number // 4 - 1))
    mixed = jax.random.permutation(jax.random.fold_in(own, 3), number_of)
    source_of, sink = mixed[0:number_of // 2 * 2:2], mixed[1:number_of // 2 * 2:2]
    margin = jnp.minimum(lengths[source_of] - 1, limit - lengths[sink]) // 2
    margin = jnp.where((source_of == order[0]) | (sink == order[0]) | (lengths[sink] == 0), 0, jnp.maximum(margin, 0))
    passed = jax.random.randint(jax.random.fold_in(own, 4), (number_of // 2,), 0, 1 << 20) % (margin + 1)
    lengths = lengths.at[source_of].add(-passed).at[sink].add(passed)
    labels = jnp.searchsorted(jnp.cumsum(lengths), jnp.arange(rows * top), side="right").astype(jnp.int32)
    table = labels.reshape(top, rows).T
    table = table[jax.random.permutation(jax.random.fold_in(own, 1), rows)]
    rotation = jax.random.randint(jax.random.fold_in(own, 2), (rows, 1), 0, top)
    return jnp.take_along_axis(table, (jnp.arange(top)[None, :] + rotation) % top, axis=1)


def portions_of(number_of, total, most, lean, full):
    portions = [(1 << 20) // math.isqrt(standing ** lean) + 1 for standing in range(1, number_of + 1)]
    largest = most if full else min(most, max(-(-total // number_of), total * portions[0] // sum(portions)))
    least = 1 if total - largest >= number_of - 1 else 0
    counts, surplus = [largest] + [least] * (number_of - 1), total - largest - least * (number_of - 1)
    while surplus > 0:
        candidates = [i for i in range(1, number_of) if counts[i] < largest] or [i for i in range(1, number_of) if counts[i] < most]
        pool, left = sum([portions[i] for i in candidates]), surplus
        for i in candidates:
            extra = min(most - counts[i], max(1, left * portions[i] // pool), surplus)
            counts[i] = counts[i] + extra
            surplus = surplus - extra
    return np.array(counts)


def centred(stream_key, shape, width, limit, cuts=(), held_as=jnp.bfloat16):
    factor_of = block_scale(stream_key, shape, cuts, -0.22, 0.18) if cuts else 1.0
    drawn = jax.random.normal(stream_key, shape, jnp.float32) * width * factor_of
    return jnp.minimum(jnp.maximum(drawn, -limit), limit).astype(held_as)


def setup_inputs(seed: int = 0) -> dict:
    key_list = jax.random.split(jax.random.key(seed), 13)
    layer_input = centred(key_list[0], (SEQS, SEQ, MODEL_DIM), 1.0, 6.0, ((0, 4), (1, 32)))
    segments = draw_segments(jax.random.fold_in(key_list[12], 71), 0)
    choices_keys = jax.random.split(jax.random.fold_in(key_list[2], 1), SEQS * SEQ // TOK_DEV)
    choices_turns = jax.random.permutation(jax.random.fold_in(key_list[2], 3), SEQS * SEQ // TOK_DEV)
    choices = jax.vmap(lambda own, number: deal_out(jax.random.fold_in(key_list[2], 2), own, number, TOK_DEV, EXPERTS, TOP, CAP, 0))(choices_keys, choices_turns).reshape((SEQS, SEQ, TOP))
    first_gain = jnp.clip(1.0 + 0.15 * jax.random.normal(key_list[3], (MODEL_DIM,), jnp.float32), 0.25, 1.75).astype(jnp.bfloat16)
    query_weight = centred(key_list[4], (MODEL_DIM, QUERY_HEADS * HEAD_DIM), (MODEL_DIM // 16) ** -0.5, 0.625, ((0, 32),))
    key_value_matrix = centred(key_list[5], (MODEL_DIM, 2 * KEY_VALUE_HEADS * HEAD_DIM), (MODEL_DIM // 16) ** -0.5, 0.625, ((0, 32),))
    output_weight = centred(key_list[6], (QUERY_HEADS * HEAD_DIM, MODEL_DIM), (QUERY_HEADS * HEAD_DIM // 48) ** -0.5, 1.0, ((0, 32),))
    second_gain = jnp.clip(1.0 + 0.15 * jax.random.normal(key_list[7], (MODEL_DIM,), jnp.float32), 0.25, 1.75).astype(jnp.bfloat16)
    router_weight = centred(key_list[8], (MODEL_DIM, EXPERTS), (4 * MODEL_DIM) ** -0.5, 0.078125, ((0, 32),))
    gate_up_weight = centred(key_list[9], (MODEL_DIM, EXPERTS, 2 * FF), MODEL_DIM ** -0.5, 0.15625, ((0, 32),))
    down_weight = centred(key_list[10], (MODEL_DIM, EXPERTS, FF), 1 ** -0.5, 6.0, ((0, 32),))
    cotangent = centred(key_list[11], (SEQS, SEQ, MODEL_DIM), 1.0, 6.0, ((0, 4), (1, 32)))
    return dict(layer_input=layer_input, segments=segments, choices=choices, first_gain=first_gain, query_weight=query_weight, key_value_matrix=key_value_matrix, output_weight=output_weight, second_gain=second_gain, router_weight=router_weight, gate_up_weight=gate_up_weight, down_weight=down_weight, cotangent=cotangent)


@jax.custom_vjp
def reduced_precision(v):
    return lax.optimization_barrier(v.astype(jnp.bfloat16)).astype(jnp.float32)

@jax.custom_vjp
def low_back(v):
    return v

def low_keep(v):
    return (reduced_precision(v), None)

def low_pass(kept, grad):
    return (grad,)

def back_keep(v):
    return (v, None)

def back_low(kept, grad):
    return (reduced_precision(grad),)
reduced_precision.defvjp(low_keep, low_pass)
low_back.defvjp(back_keep, back_low)
NORM_EPS = 1e-06
RESIDUAL_SCALE = 0.22
SCORE_SCALE = 0.015625
ROPE_BASE = 10000.0
MASK_FILL = -1e+30
PRECISE = lax.Precision.HIGHEST

def rms_scale(values):
    return lax.rsqrt(lax.optimization_barrier(jnp.mean(values * values, -1, keepdims=True)) + NORM_EPS)

def apply_rotary(values, rotary_angles):
    half_size = values.shape[-1] // 2
    cosine = jnp.cos(rotary_angles)[:, None, :]
    sine_part = jnp.sin(rotary_angles)[:, None, :]
    front = values[..., :half_size]
    behind = values[..., half_size:]
    return jnp.concatenate([front * cosine - behind * sine_part, behind * cosine + front * sine_part], -1)

def swiglu(joined):
    gate_part = joined[..., :FF]
    up_part = joined[..., FF:]
    return gate_part / (1.0 + jnp.exp(-gate_part)) * up_part

def sequence_layer(tokens, segment, chosen_ids, weights):
    gain_one, query_full, keyval_full, output_full, gain_two, router_full, gate_up_full, down_full = weights
    token_length = tokens.shape[0]
    query_group_size = QUERY_HEADS // KEY_VALUE_HEADS
    frequency = ROPE_BASE ** (-jnp.arange(0, HEAD_DIM, 2, dtype=jnp.float32) / HEAD_DIM)
    rotary_angles = jnp.arange(token_length, dtype=jnp.float32)[:, None] * frequency[None, :]
    normed = reduced_precision(tokens * rms_scale(tokens) * gain_one)
    query_linear = low_back(jnp.dot(normed, query_full, precision=PRECISE))
    key_value_linear = low_back(jnp.dot(normed, keyval_full, precision=PRECISE))
    split_position = KEY_VALUE_HEADS * HEAD_DIM
    query_rotated = reduced_precision(apply_rotary(query_linear.reshape(token_length, QUERY_HEADS, HEAD_DIM), rotary_angles)).reshape(token_length, KEY_VALUE_HEADS, query_group_size, HEAD_DIM)
    key_rotated = reduced_precision(apply_rotary(key_value_linear[:, :split_position].reshape(token_length, KEY_VALUE_HEADS, HEAD_DIM), rotary_angles))
    value_reduced = reduced_precision(key_value_linear[:, split_position:].reshape(token_length, KEY_VALUE_HEADS, HEAD_DIM))
    block_rows = min(512, token_length)
    key_place = jnp.arange(token_length, dtype=jnp.int32)

    def attend(row_start):
        query_block = lax.dynamic_slice_in_dim(query_rotated, row_start, block_rows, 0)
        segment_block = lax.dynamic_slice_in_dim(segment, row_start, block_rows, 0)
        scores = low_back(SCORE_SCALE * jnp.einsum('tgrd,kgd->grtk', query_block, key_rotated, precision=PRECISE))
        query_place = row_start + jnp.arange(block_rows, dtype=jnp.int32)
        visible = (key_place[None, :] <= query_place[:, None]) & (segment[None, :] == segment_block[:, None])
        scores = jnp.where(visible[None, None], scores, MASK_FILL)
        exponent = jnp.exp(scores - lax.optimization_barrier(jnp.max(scores, -1, keepdims=True)))
        probs_low = reduced_precision(exponent / lax.optimization_barrier(jnp.sum(exponent, -1, keepdims=True)))
        return jnp.einsum('grtk,kgd->tgrd', probs_low, value_reduced, precision=PRECISE)
    row_starts = jnp.arange(0, token_length, block_rows, dtype=jnp.int32)
    attended = lax.map(jax.checkpoint(attend), row_starts).reshape(token_length, QUERY_HEADS * HEAD_DIM)
    attention_low = reduced_precision(low_back(attended))
    attention_lin = low_back(jnp.dot(attention_low, output_full, precision=PRECISE))
    residual = tokens + RESIDUAL_SCALE * attention_lin
    normed_two = reduced_precision(residual * rms_scale(residual) * gain_two)
    logits = jnp.dot(normed_two, router_full, precision=PRECISE)
    chosen = jnp.take_along_axis(logits, chosen_ids, 1)
    exponent = jnp.exp(chosen - lax.optimization_barrier(jnp.max(chosen, -1, keepdims=True)))
    gate_values = exponent / lax.optimization_barrier(jnp.sum(exponent, -1, keepdims=True))
    matches = chosen_ids[:, :, None] == jnp.arange(EXPERTS, dtype=jnp.int32)[None, None, :]
    shares = lax.optimization_barrier(jnp.sum(jnp.where(matches, gate_values[:, :, None], 0.0), 1))

    def expert_term(running, inputs):
        gate_up, down_rows, gate_share = inputs
        joined = low_back(jnp.dot(normed_two, gate_up, precision=PRECISE))
        hidden = reduced_precision(swiglu(joined))
        produced = low_back(jnp.dot(hidden, down_rows.T, precision=PRECISE))
        return (running + gate_share[:, None] * produced, None)
    mixture, unused = lax.scan(jax.checkpoint(expert_term), jnp.zeros_like(residual), (jnp.moveaxis(gate_up_full, 1, 0), jnp.moveaxis(down_full, 1, 0), shares.T))
    return residual + RESIDUAL_SCALE * mixture

def reference(layer_input, segments, choices, first_gain, query_weight, key_value_matrix, output_weight, second_gain, router_weight, gate_up_weight, down_weight, cotangent):
    floats = (layer_input.astype(jnp.float32), first_gain.astype(jnp.float32), query_weight.astype(jnp.float32), key_value_matrix.astype(jnp.float32), output_weight.astype(jnp.float32), second_gain.astype(jnp.float32), router_weight.astype(jnp.float32), gate_up_weight.astype(jnp.float32), down_weight.astype(jnp.float32))

    def forward(tokens_all, *weights):

        def one_sequence(members):
            return sequence_layer(members[0], members[1], members[2], weights)
        return lax.map(jax.checkpoint(one_sequence), (tokens_all, segments, choices))
    outputs, pullback = jax.vjp(forward, *floats)
    gradients = pullback(cotangent.astype(jnp.float32))
    return (outputs.astype(jnp.bfloat16), gradients[0], gradients[1], gradients[2], gradients[3], gradients[4], gradients[5], gradients[6], gradients[7], gradients[8])
```

```python
import functools

import jax
import jax.numpy as jnp
from jax import lax
from jax.experimental import pallas as pl
from jax.experimental.pallas import tpu as pltpu
from jax.sharding import PartitionSpec as P

D = 1536
HEADS = 8
GROUP = 3
HEAD_DIM = 64
HALF = HEAD_DIM // 2
FF = 512
EXPERTS = 10
TOK = 128
SEQ = 4096
PLANE = 16
RUN = 512
QROWS = GROUP * HEAD_DIM
PACK = 384
ROUTER_AT = 320
GAIN_ONE_AT = 330
GAIN_TWO_AT = 331

NORM_EPS = 1e-06
RESIDUAL_SCALE = 0.22
SCORE_SCALE = 0.015625
ROPE_BASE = 10000.0
MASK_FILL = -1e30
PRECISE = lax.Precision.HIGHEST
BF16 = jnp.bfloat16
F32 = jnp.float32
VMEM_LIMIT = 56 * 1024 * 1024


def my_place():
    return lax.axis_index("shard"), lax.axis_index("rep")


def parts_of(shard):
    place = lax.rem(shard, PLANE)
    return shard // PLANE, place, place // 4, lax.rem(place, 4)


def same(one, other):
    return jnp.logical_and(one[0] == other[0], one[1] == other[1])


class Route:
    def __init__(self, n, to, source, pieces, index=None, may_be_self=False):
        self.n, self.to, self.source, self.pieces = n, to, source, pieces
        self.index = index or (lambda i: i)
        self.may_be_self = may_be_self


def each(n, body):
    if n <= 8:
        for i in range(n):
            body(i)
    else:

        def step(i, carry):
            body(i)
            return carry

        lax.fori_loop(0, n, step, 0)


def exchange(inputs, out_shapes, collective_id, plan):
    n_in, n_out = len(inputs), len(out_shapes)

    def kernel(*refs):
        ins, outs = refs[:n_in], refs[n_in : n_in + n_out]
        sems = refs[n_in + n_out :]
        me = my_place()
        routes, own = plan(me)
        barrier = pltpu.get_barrier_semaphore()
        awaited = 0
        for route in routes:

            def greet(i, route=route):
                source = route.source(i)

                def signal():
                    pl.semaphore_signal(
                        barrier, inc=1, device_id={"shard": source[0], "rep": source[1]}
                    )

                if route.may_be_self:
                    pl.when(jnp.logical_not(same(source, me)))(signal)
                else:
                    signal()

            each(route.n, greet)
            awaited = awaited + route.n
            if route.may_be_self:
                for i in range(route.n):
                    awaited = awaited - same(route.to(i), me).astype(jnp.int32)
        pl.semaphore_wait(barrier, awaited)

        def remote(route, send_sem, recv_sem, i, k, piece):
            source_in, cut, target_out, slot, unused = piece
            place = route.to(i)
            return pltpu.make_async_remote_copy(
                src_ref=ins[source_in].at[cut(i)],
                dst_ref=outs[target_out].at[slot(i)],
                send_sem=send_sem.at[i * len(route.pieces) + k],
                recv_sem=recv_sem.at[route.index(i) * len(route.pieces) + k],
                device_id={"shard": place[0], "rep": place[1]},
            )

        def within(route, own_sem, i, k, piece):
            source_in, cut, target_out, slot, unused = piece
            return pltpu.make_async_copy(
                ins[source_in].at[cut(i)], outs[target_out].at[slot(i)], own_sem.at[k]
            )

        for number, route in enumerate(routes):
            send_sem, recv_sem, own_sem = sems[3 * number : 3 * number + 3]

            def start(i, route=route, send_sem=send_sem, recv_sem=recv_sem, own_sem=own_sem):
                for k, piece in enumerate(route.pieces):
                    copy = remote(route, send_sem, recv_sem, i, k, piece)
                    if route.may_be_self:
                        here = same(route.to(i), me)
                        pl.when(jnp.logical_not(here))(copy.start)
                        pl.when(here)(within(route, own_sem, i, k, piece).start)
                    else:
                        copy.start()

            each(route.n, start)
        local_sem = sems[3 * len(routes)]
        local = [
            pltpu.make_async_copy(ins[a].at[cut], outs[b].at[slot], local_sem.at[k])
            for k, (a, cut, b, slot) in enumerate(own)
        ]
        for copy in local:
            copy.start()
        for copy in local:
            copy.wait()
        for number, route in enumerate(routes):
            send_sem, recv_sem, own_sem = sems[3 * number : 3 * number + 3]

            def arrive(i, route=route, recv_sem=recv_sem):
                for k, piece in enumerate(route.pieces):
                    source_in, cut, target_out, unused, slot = piece
                    region = outs[target_out].at[slot(i)]
                    place = route.source(i)
                    copy = pltpu.make_async_remote_copy(
                        src_ref=region,
                        dst_ref=region,
                        send_sem=recv_sem.at[i * len(route.pieces) + k],
                        recv_sem=recv_sem.at[i * len(route.pieces) + k],
                        device_id={"shard": place[0], "rep": place[1]},
                    )
                    if route.may_be_self:
                        pl.when(jnp.logical_not(same(place, me)))(copy.wait_recv)
                    else:
                        copy.wait_recv()

            each(route.n, arrive)

            def leave(i, route=route, send_sem=send_sem, recv_sem=recv_sem, own_sem=own_sem):
                for k, piece in enumerate(route.pieces):
                    copy = remote(route, send_sem, recv_sem, i, k, piece)
                    if route.may_be_self:
                        here = same(route.to(i), me)
                        pl.when(jnp.logical_not(here))(copy.wait_send)
                        pl.when(here)(within(route, own_sem, i, k, piece).wait)
                    else:
                        copy.wait_send()

            each(route.n, leave)

    routes, own = plan((0, 0))
    scratch = []
    for route in routes:
        count = route.n * len(route.pieces)
        scratch += [
            pltpu.SemaphoreType.DMA((count,)),
            pltpu.SemaphoreType.DMA((count,)),
            pltpu.SemaphoreType.DMA((len(route.pieces),)),
        ]
    scratch.append(pltpu.SemaphoreType.DMA((max(1, len(own)),)))
    return pl.pallas_call(
        kernel,
        out_shape=[jax.ShapeDtypeStruct(s, t) for s, t in out_shapes],
        in_specs=[pl.BlockSpec(memory_space=pl.ANY)] * n_in,
        out_specs=[pl.BlockSpec(memory_space=pl.ANY)] * n_out,
        scratch_shapes=scratch,
        compiler_params=pltpu.CompilerParams(collective_id=collective_id, has_side_effects=True),
    )(*inputs)


def column_route(me, pieces):
    z, place, unused, unused2 = parts_of(me[0])
    mine = z * 4 + me[1]

    def where(member):
        return (member // 4) * PLANE + place, lax.rem(member, 4)

    def after(i):
        return lax.rem(mine + 1 + i, 8)

    def before(i):
        return lax.rem(mine + 7 - i, 8)

    return Route(
        7,
        lambda i: where(after(i)),
        lambda i: where(before(i)),
        [
            (
                a,
                lambda i, cut=cut: cut(after(i)),
                b,
                lambda i, slot=slot: slot(mine),
                lambda i, slot=slot: slot(before(i)),
            )
            for a, cut, b, slot in pieces
        ],
    )


def plane_route(me, pieces):
    z, place, unused, unused2 = parts_of(me[0])

    def after(i):
        return lax.rem(place + 1 + i, PLANE)

    def before(i):
        return lax.rem(place + 15 - i, PLANE)

    return Route(
        15,
        lambda i: (z * PLANE + after(i), me[1]),
        lambda i: (z * PLANE + before(i), me[1]),
        [
            (
                a,
                lambda i, cut=cut: cut(after(i)),
                b,
                lambda i, slot=slot: slot(place),
                lambda i, slot=slot: slot(before(i)),
            )
            for a, cut, b, slot in pieces
        ],
    )


def shard_route(me, pieces):
    def after(i):
        return lax.rem(me[0] + 1 + i, 32)

    def before(i):
        return lax.rem(me[0] + 31 - i, 32)

    return Route(
        31,
        lambda i: (after(i), me[1]),
        lambda i: (before(i), me[1]),
        [
            (
                a,
                lambda i, cut=cut: cut(after(i)),
                b,
                lambda i, slot=slot: slot(me[0]),
                lambda i, slot=slot: slot(before(i)),
            )
            for a, cut, b, slot in pieces
        ],
    )


def rows_of(number, size):
    return pl.ds(pl.multiple_of(number * size, size), size)


def gather_start(x, dy, ints, gate_up, down, attn):
    def plan(me):
        z, place, unused, unused2 = parts_of(me[0])
        mine = z * 4 + me[1]
        one = lambda member: (0,)
        routes = [
            column_route(me, [(0, lambda m: slice(None), 0, lambda m: m), (2, lambda m: slice(None), 2, lambda m: m)]),
            shard_route(me, [(5, lambda s: s // PLANE, 5, lambda s: rows_of(s, 48))]),
            column_route(me, [(1, lambda m: slice(None), 1, lambda m: m)]),
            shard_route(
                me,
                [
                    (3, lambda s: s // PLANE, 3, lambda s: rows_of(s, 48)),
                    (4, lambda s: s // PLANE, 4, lambda s: rows_of(s, 48)),
                ],
            ),
        ]
        own = [
            (0, slice(None), 0, mine),
            (1, slice(None), 1, mine),
            (2, slice(None), 2, mine),
            (3, z, 3, rows_of(me[0], 48)),
            (4, z, 4, rows_of(me[0], 48)),
            (5, z, 5, rows_of(me[0], 48)),
        ]
        return routes, own

    return exchange(
        [x, dy, ints, gate_up, down, attn],
        [
            ((8, TOK, D), BF16),
            ((8, TOK, D), BF16),
            ((8, 16, TOK), jnp.int32),
            ((D, 1280), BF16),
            ((D, 640), BF16),
            ((D, PACK), BF16),
        ],
        0,
        plan,
    )


def mirrored(z, x):
    return x + z * (3 - 2 * x)


def query_routes(me, q_in, q_out):
    z_me, place, x, y = parts_of(me[0])
    base = z_me * PLANE

    def plain(i):
        return lax.rem(y + 1 + i, 4)

    def plain_before(i):
        return lax.rem(y + 3 - i, 4)

    def other(i):
        return lax.rem(y + i, 4)

    def other_before(i):
        return lax.rem(y + 4 - i, 4)

    first = Route(
        3,
        lambda i: (base + 4 * x + plain(i), me[1]),
        lambda i: (base + 4 * x + plain_before(i), me[1]),
        [(q_in, lambda i: (0, plain(i)), q_out, lambda i: (0, y), lambda i: (0, plain_before(i)))],
    )
    second = Route(
        4,
        lambda i: (base + 4 * (3 - x) + other(i), me[1]),
        lambda i: (base + 4 * (3 - x) + other_before(i), me[1]),
        [(q_in, lambda i: (1, other(i)), q_out, lambda i: (1, y), lambda i: (1, other_before(i)))],
    )
    return [first, second], [(q_in, (0, y), q_out, (0, y))]


def to_attention(q, kv, ints):
    def plan(me):
        z_me, place, x, y = parts_of(me[0])
        routes, own = query_routes(me, 0, 0)
        routes = [
            plane_route(
                me,
                [
                    (1, lambda p: (0, lax.rem(p, 4)), 1, lambda p: (0, p)),
                    (1, lambda p: (1, lax.rem(p, 4)), 1, lambda p: (1, p)),
                    (2, lambda p: lax.rem(p, 4), 2, lambda p: p),
                ],
            )
        ] + routes
        own = own + [
            (1, (0, y), 1, (0, place)),
            (1, (1, y), 1, (1, place)),
            (2, y, 2, place),
        ]
        return routes, own

    return exchange(
        [q, kv, ints],
        [((2, 4, QROWS, TOK), BF16), ((2, PLANE, TOK, TOK), BF16), ((PLANE, 8, TOK), jnp.int32)],
        1,
        plan,
    )


def from_attention(q, kv):
    def plan(me):
        z_me, place, x, y = parts_of(me[0])
        routes, own = query_routes(me, 0, 0)
        routes = [plane_route(me, [(1, lambda p: (slice(None), p), 1, lambda p: p)])] + routes
        own = own + [(1, (slice(None), place), 1, place)]
        return routes, own

    return exchange(
        [q, kv],
        [((2, 4, QROWS, TOK), BF16), ((PLANE, 2, TOK, TOK), BF16)],
        6,
        plan,
    )


def head_places(me):
    z, place, x, y = parts_of(me[0])
    quarter = mirrored(z, x)

    def place_of(m):
        return (m // 4) * PLANE + 4 * quarter + me[1], lax.rem(m, 4)

    return place_of, (z, y)


def owner_places(me):
    z, place, x, y = parts_of(me[0])

    def place_of(i):
        run, other = i // 4, lax.rem(i, 4)
        return run * PLANE + 4 * mirrored(run, x) + other, y

    return place_of, z * 4 + me[1]


def to_owners(o):
    def plan(me):
        owner, mine = owner_places(me)
        head, slot = head_places(me)
        route = Route(
            8,
            owner,
            head,
            [(0, lambda i: (i // 4, i % 4), 0, lambda i: mine, lambda i: i)],
            index=lambda i: mine,
            may_be_self=True,
        )
        return [route], []

    return exchange([o], [((HEADS, QROWS, TOK), BF16)], 2, plan)[0]


def to_heads(do):
    def plan(me):
        owner, mine = owner_places(me)
        head, slot = head_places(me)
        route = Route(
            8,
            head,
            owner,
            [(0, lambda i: i, 0, lambda i: slot, lambda i: (i // 4, i % 4))],
            index=lambda i: slot[0] * 4 + slot[1],
            may_be_self=True,
        )
        return [route], []

    return exchange([do], [((2, 4, QROWS, TOK), BF16)], 5, plan)[0]


def column_gather(values, collective_id):
    def plan(me):
        z, place, unused, unused2 = parts_of(me[0])
        route = column_route(me, [(0, lambda m: slice(None), 0, lambda m: m)])
        return [route], [(0, slice(None), 0, z * 4 + me[1])]

    return exchange([values], [((8,) + values.shape, values.dtype)], collective_id, plan)[0]


def column_swap(arrays, collective_id):
    def plan(me):
        z, place, unused, unused2 = parts_of(me[0])
        mine = z * 4 + me[1]
        route = column_route(me, [(k, lambda m: m, k, lambda m: m) for k in range(len(arrays))])
        return [route], [(k, mine, k, mine) for k in range(len(arrays))]

    return exchange(arrays, [(a.shape, a.dtype) for a in arrays], collective_id, plan)


def plane_sums(attn, gate_up, down, out_rows, dq, dkv):
    def plan(me):
        z, place, unused, unused2 = parts_of(me[0])
        mine = z * 4 + me[1]
        both = lambda p: (slice(None), p)
        routes = [
            column_route(me, [(4, lambda m: m, 4, lambda m: m), (5, lambda m: m, 5, lambda m: m)]),
            plane_route(
                me,
                [(0, both, 0, lambda p: p), (3, lambda p: p, 3, lambda p: p)]
                + [(1, both, 1, lambda p: p), (2, both, 2, lambda p: p)],
            ),
        ]
        own = [
            (0, (slice(None), place), 0, place),
            (1, (slice(None), place), 1, place),
            (2, (slice(None), place), 2, place),
            (3, place, 3, place),
            (4, mine, 4, mine),
            (5, mine, 5, mine),
        ]
        return routes, own

    return exchange(
        [attn, gate_up, down, out_rows, dq, dkv],
        [
            ((PLANE, 2, 48, PACK), BF16),
            ((PLANE, 2, 48, 1280), BF16),
            ((PLANE, 2, 48, 640), BF16),
            ((PLANE, 12, D), BF16),
            (dq.shape, BF16),
            (dkv.shape, BF16),
        ],
        7,
        plan,
    )


def final_swap(attn, gate_up, down, out_rows):
    def plan(me):
        z, place, x, y = parts_of(me[0])
        mine = z * 4 + me[1]
        pick = lambda m: m // 4
        routes = [
            column_route(me, [(0, pick, 0, lambda m: m), (1, pick, 1, lambda m: m), (2, pick, 2, lambda m: m)]),
            Route(
                4,
                lambda i: (4 * mine + place // 4, i),
                lambda i: (
                    (me[0] // 4) // 4 * PLANE + 4 * lax.rem(me[0], 4) + i,
                    lax.rem(me[0] // 4, 4),
                ),
                [(3, lambda i: slice(None), 3, lambda i: lax.rem(place, 4), lambda i: i)],
                index=lambda i: lax.rem(place, 4),
                may_be_self=True,
            ),
        ]
        own = [(0, z, 0, mine), (1, z, 1, mine), (2, z, 2, mine)]
        return routes, own

    return exchange(
        [attn, gate_up, down, out_rows],
        [((8, 48, PACK), BF16), ((8, 48, 1280), BF16), ((8, 48, 640), BF16), ((4, 12, D), BF16)],
        8,
        plan,
    )


def unpack_queries(source, target):
    for run in range(2):
        for part in range(4):
            target[:, run * RUN + part * TOK : run * RUN + (part + 1) * TOK] = source[run, part]


def unpack_keys(kv_ref, key_rows, value_lines):
    def step(j, carry):
        place = pl.ds(pl.multiple_of(j * TOK, TOK), TOK)
        block = kv_ref[j // PLANE, lax.rem(j, PLANE)]
        key_rows[place, :] = block[:HEAD_DIM].astype(F32).T.astype(BF16)
        value_lines[:, place] = block[HEAD_DIM:]
        return carry

    lax.fori_loop(0, SEQ // TOK, step, 0)


def visible_block(block, start, query):
    key = block * RUN + lax.broadcasted_iota(jnp.int32, (RUN, RUN), 0)
    return jnp.logical_and(key >= start, key <= query)


def attend_kernel(bounds, q_ref, kv_ref, start_ref, o_ref, low_ref, lse_ref, queries, key_rows, value_lines):
    unpack_queries(q_ref, queries)
    unpack_keys(kv_ref, key_rows, value_lines)
    for run in range(2):
        cols = slice(run * RUN, (run + 1) * RUN)
        start = start_ref[0:1, cols]
        query = bounds[4 + run] + lax.broadcasted_iota(jnp.int32, (1, RUN), 1)
        heads = [
            queries[h * HEAD_DIM : (h + 1) * HEAD_DIM, cols] * jnp.asarray(SCORE_SCALE, BF16)
            for h in range(GROUP)
        ]

        def step(block, carry):
            place = pl.ds(pl.multiple_of(block * RUN, RUN), RUN)
            keys, values = key_rows[place, :], value_lines[:, place]
            seen = visible_block(block, start, query)
            result = []
            for h in range(GROUP):
                peak, total, acc = carry[3 * h : 3 * h + 3]
                scores = jnp.dot(keys, heads[h], preferred_element_type=F32)
                scores = jnp.where(seen, scores, MASK_FILL)
                top = jnp.maximum(peak, jnp.max(scores, 0, keepdims=True))
                weights = jnp.exp(scores - top)
                fade = jnp.exp(peak - top)
                total = fade * total + jnp.sum(weights, 0, keepdims=True)
                acc = fade * acc + jnp.dot(values, weights.astype(BF16), preferred_element_type=F32)
                result += [top, total, acc]
            return tuple(result)

        zero = []
        for h in range(GROUP):
            zero += [
                jnp.full((1, RUN), MASK_FILL, F32),
                jnp.zeros((1, RUN), F32),
                jnp.zeros((HEAD_DIM, RUN), F32),
            ]
        done = lax.fori_loop(bounds[run], bounds[2 + run], step, tuple(zero))
        for h in range(GROUP):
            peak, total, acc = done[3 * h : 3 * h + 3]
            rows = slice(h * HEAD_DIM, (h + 1) * HEAD_DIM)
            attended = acc / total
            o_ref[rows, cols] = attended
            for part in range(4):
                low_ref[run, part, rows, :] = attended[:, part * TOK : (part + 1) * TOK].astype(BF16)
            lse_ref[h : h + 1, cols] = peak + jnp.log(total)


def attend(bounds, q, kv, start):
    vmem = pl.BlockSpec(memory_space=pltpu.VMEM)
    return pl.pallas_call(
        attend_kernel,
        out_shape=[
            jax.ShapeDtypeStruct((QROWS, 2 * RUN), F32),
            jax.ShapeDtypeStruct((2, 4, QROWS, TOK), BF16),
            jax.ShapeDtypeStruct((8, 2 * RUN), F32),
        ],
        in_specs=[pl.BlockSpec(memory_space=pltpu.SMEM), vmem, vmem, vmem],
        out_specs=[vmem, vmem, vmem],
        scratch_shapes=[
            pltpu.VMEM((QROWS, 2 * RUN), BF16),
            pltpu.VMEM((SEQ, HEAD_DIM), BF16),
            pltpu.VMEM((HEAD_DIM, SEQ), BF16),
        ],
        compiler_params=pltpu.CompilerParams(vmem_limit_bytes=VMEM_LIMIT),
    )(bounds, q, kv, start)


NT = (((1,), (1,)), ((), ()))


def attend_back_kernel(
    bounds, q_ref, kv_ref, do_ref, start_ref, o_ref, lse_ref, dq_ref, dkv_ref,
    queries, grads, key_rows, value_rows, key_lines, key_grad, value_grad,
):
    unpack_queries(q_ref, queries)
    unpack_queries(do_ref, grads)
    key_grad[...] = jnp.zeros_like(key_grad)
    value_grad[...] = jnp.zeros_like(value_grad)

    def spread(j, carry):
        place = pl.ds(pl.multiple_of(j * TOK, TOK), TOK)
        block = kv_ref[j // PLANE, lax.rem(j, PLANE)]
        turned = block.astype(F32).T.astype(BF16)
        key_rows[place, :] = turned[:, :HEAD_DIM]
        value_rows[place, :] = turned[:, HEAD_DIM:]
        key_lines[:, place] = block[:HEAD_DIM]
        return carry

    lax.fori_loop(0, SEQ // TOK, spread, 0)
    for run in range(2):
        cols = slice(run * RUN, (run + 1) * RUN)
        start = start_ref[0:1, cols]
        query = bounds[4 + run] + lax.broadcasted_iota(jnp.int32, (1, RUN), 1)
        lse = [lse_ref[h : h + 1, cols] for h in range(GROUP)]
        delta = []
        for h in range(GROUP):
            rows = slice(h * HEAD_DIM, (h + 1) * HEAD_DIM)
            delta.append(jnp.sum(grads[rows, cols].astype(F32) * o_ref[rows, cols], 0, keepdims=True))

        def step(block, carry):
            place = pl.ds(pl.multiple_of(block * RUN, RUN), RUN)
            keys, values, lines = key_rows[place, :], value_rows[place, :], key_lines[:, place]
            seen = visible_block(block, start, query)
            result = []
            dk = key_grad[place, :]
            dv = value_grad[place, :]
            for h in range(GROUP):
                rows = slice(h * HEAD_DIM, (h + 1) * HEAD_DIM)
                q = queries[rows, cols] * jnp.asarray(SCORE_SCALE, BF16)
                do = grads[rows, cols]
                scores = jnp.dot(keys, q, preferred_element_type=F32)
                weights = jnp.exp(jnp.where(seen, scores, MASK_FILL) - lse[h])
                pull = jnp.dot(values, do, preferred_element_type=F32)
                ds = (weights * (pull - delta[h])).astype(BF16)
                dv = dv + lax.dot_general(weights.astype(BF16), do, NT, preferred_element_type=F32)
                dk = dk + lax.dot_general(ds, q, NT, preferred_element_type=F32)
                result.append(carry[h] + jnp.dot(lines, ds, preferred_element_type=F32))
            key_grad[place, :] = dk
            value_grad[place, :] = dv
            return tuple(result)

        done = lax.fori_loop(
            bounds[run], bounds[2 + run], step, tuple(jnp.zeros((HEAD_DIM, RUN), F32) for h in range(GROUP))
        )
        for h in range(GROUP):
            rows = slice(h * HEAD_DIM, (h + 1) * HEAD_DIM)
            scaled = SCORE_SCALE * done[h]
            for part in range(4):
                dq_ref[run, part, rows, :] = scaled[:, part * TOK : (part + 1) * TOK].astype(BF16)

    def gather(j, carry):
        place = pl.ds(pl.multiple_of(j * TOK, TOK), TOK)
        dkv_ref[j // PLANE, lax.rem(j, PLANE), :HEAD_DIM, :] = key_grad[place, :].T.astype(BF16)
        dkv_ref[j // PLANE, lax.rem(j, PLANE), HEAD_DIM:, :] = value_grad[place, :].T.astype(BF16)
        return carry

    lax.fori_loop(0, SEQ // TOK, gather, 0)


def attend_back(bounds, q, kv, do, start, o, lse):
    vmem = pl.BlockSpec(memory_space=pltpu.VMEM)
    return pl.pallas_call(
        attend_back_kernel,
        out_shape=[
            jax.ShapeDtypeStruct((2, 4, QROWS, TOK), BF16),
            jax.ShapeDtypeStruct((2, PLANE, TOK, TOK), BF16),
        ],
        in_specs=[pl.BlockSpec(memory_space=pltpu.SMEM)] + [vmem] * 6,
        out_specs=[vmem, vmem],
        scratch_shapes=[
            pltpu.VMEM((QROWS, 2 * RUN), BF16),
            pltpu.VMEM((QROWS, 2 * RUN), BF16),
            pltpu.VMEM((SEQ, HEAD_DIM), BF16),
            pltpu.VMEM((SEQ, HEAD_DIM), BF16),
            pltpu.VMEM((HEAD_DIM, SEQ), BF16),
            pltpu.VMEM((SEQ, HEAD_DIM), F32),
            pltpu.VMEM((SEQ, HEAD_DIM), F32),
        ],
        compiler_params=pltpu.CompilerParams(vmem_limit_bytes=VMEM_LIMIT),
    )(bounds, q, kv, do, start, o, lse)


def rms_scale(values):
    return lax.rsqrt(jnp.mean(values * values, -1, keepdims=True) + NORM_EPS)


def norm_back(grad_normed, values, scale_factor, gain_values):
    weighted = grad_normed * gain_values
    return scale_factor * weighted - values * scale_factor**3 * jnp.mean(
        weighted * values, -1, keepdims=True
    )


def turn(values, cosine, sine):
    front, behind = values[..., :HALF, :], values[..., HALF:, :]
    return jnp.concatenate([front * cosine - behind * sine, behind * cosine + front * sine], -2)


def shards(
    layer_input,
    segments,
    choices,
    first_gain,
    query_weight,
    key_value_matrix,
    output_weight,
    second_gain,
    router_weight,
    gate_up_weight,
    down_weight,
    cotangent,
):
    shard, rep = my_place()
    z, place, x, y = parts_of(shard)
    dot = functools.partial(lax.dot_general, preferred_element_type=F32)

    choices_lines = choices[0].T
    ints = jnp.concatenate([choices_lines, segments, jnp.zeros((7, TOK), jnp.int32)], 0)
    gate_up_mine = lax.dynamic_index_in_dim(
        gate_up_weight.reshape(48, 2, 5, 2, 4, TOK), rep, 4, keepdims=False
    )
    gate_up_mine = jnp.moveaxis(gate_up_mine, 1, 0).reshape(2, 48, 1280)
    down_mine = lax.dynamic_index_in_dim(down_weight.reshape(48, 2, 5, 4, TOK), rep, 3, keepdims=False)
    down_mine = jnp.moveaxis(down_mine, 1, 0).reshape(2, 48, 640)
    query_mine = lax.dynamic_index_in_dim(query_weight.reshape(48, 2, 4, QROWS), rep, 2, keepdims=False)
    keyval_mine = lax.dynamic_index_in_dim(
        key_value_matrix.reshape(48, 2, 2, 4, HEAD_DIM), rep, 3, keepdims=False
    )
    small = jnp.concatenate(
        [router_weight, first_gain[:, None], second_gain[:, None], jnp.zeros((48, PACK - 332), BF16)], 1
    )
    attn_mine = jnp.stack(
        [
            jnp.concatenate([query_mine[:, k], keyval_mine[:, 0, k], keyval_mine[:, 1, k], small], 1)
            for k in range(2)
        ]
    )
    x_all, dy_all, ints_all, gate_up, down, attn = gather_start(
        layer_input[0], cotangent[0], ints, gate_up_mine, down_mine, attn_mine
    )
    output_full = lax.all_gather(output_weight, "shard", axis=0, tiled=True)
    query_full = lax.all_gather(query_weight, "shard", axis=0, tiled=True)
    keyval_full = lax.all_gather(key_value_matrix, "shard", axis=0, tiled=True)

    gain_one = attn[:, GAIN_ONE_AT].astype(F32)
    gain_two = attn[:, GAIN_TWO_AT].astype(F32)
    router = attn[:, ROUTER_AT : ROUTER_AT + EXPERTS]
    tokens_all = x_all.reshape(8 * TOK, D).astype(F32)
    normed = (tokens_all * rms_scale(tokens_all) * gain_one).astype(BF16)

    frequency = ROPE_BASE ** (-jnp.arange(0, HEAD_DIM, 2, dtype=F32) / HEAD_DIM)
    column_place = (
        (jnp.arange(2, dtype=jnp.int32)[:, None] * PLANE + place) * TOK
        + jnp.arange(TOK, dtype=jnp.int32)[None, :]
    )
    angle = column_place.astype(F32)[:, None, :] * frequency[None, :, None]
    cosine = jnp.cos(angle)[:, None, None]
    sine = jnp.sin(angle)[:, None, None]
    linear = dot(attn[:, : QROWS + 2 * HEAD_DIM], normed, (((0,), (1,)), ((), ())))
    linear = jnp.moveaxis(linear.reshape(QROWS + 2 * HEAD_DIM, 2, 4, TOK), 0, 2)
    turned = turn(linear[:, :, : QROWS + HEAD_DIM].reshape(2, 4, 4, HEAD_DIM, TOK), cosine, sine)
    query_lines = turned[:, :, :GROUP].reshape(2, 4, QROWS, TOK).astype(BF16)
    keyval_lines = jnp.concatenate([turned[:, :, GROUP], linear[:, :, QROWS + HEAD_DIM :]], 2).astype(BF16)
    segment_column = jnp.moveaxis(ints_all[:, 8].reshape(2, 4, TOK), 0, 1)
    segment_column = jnp.concatenate([segment_column, jnp.zeros((4, 6, TOK), jnp.int32)], 1)
    q_here, kv_here, segment_here = to_attention(query_lines, keyval_lines, segment_column)

    segment_all = jnp.moveaxis(segment_here[:, :2], 1, 0).reshape(SEQ)
    earlier = jnp.sum(segment_all[None, :] < jnp.arange(5, dtype=jnp.int32)[:, None], 1, dtype=jnp.int32)
    runs = jnp.stack([x, 7 - x])
    mark = jnp.concatenate(
        [lax.dynamic_slice_in_dim(segment_all, runs[k] * RUN, RUN) for k in range(2)]
    )
    start = jnp.sum(
        jnp.where(mark[None, :] == jnp.arange(5, dtype=jnp.int32)[:, None], earlier[:, None], 0), 0
    )
    first_block = jnp.min(start.reshape(2, RUN), 1) // RUN
    bounds = jnp.concatenate([first_block, runs + 1, runs * RUN, jnp.zeros((2,), jnp.int32)])
    start_lines = jnp.broadcast_to(start[None, :], (8, 2 * RUN))
    o_here, o_low, lse = attend(bounds, q_here, kv_here, start_lines)
    attended = to_owners(o_low).reshape(D, TOK)

    tokens = layer_input[0].astype(F32)
    out_grad = cotangent[0].astype(F32)
    residual = tokens + RESIDUAL_SCALE * dot(attended, output_full, (((0,), (0,)), ((), ())))
    scale_two = rms_scale(residual)
    normed_two = (residual * scale_two * gain_two).astype(BF16)
    normed_two_all = column_gather(normed_two, 3).reshape(8 * TOK, D)

    dy_rows = dy_all.reshape(8 * TOK, D)
    chosen = jnp.any(
        ints_all[:, :8, :, None] == jnp.arange(EXPERTS, dtype=jnp.int32), 1
    ).reshape(8 * TOK, EXPERTS)
    logits = jnp.where(chosen, dot(normed_two_all, router, (((1,), (0,)), ((), ()))), MASK_FILL)
    exponent = jnp.where(chosen, jnp.exp(logits - jnp.max(logits, -1, keepdims=True)), 0.0)
    shares = exponent / jnp.sum(exponent, -1, keepdims=True)
    share = lax.dynamic_slice_in_dim(shares, z * 5, 5, 1)[:, :, None]
    joined = dot(normed_two_all, gate_up, (((1,), (0,)), ((), ()))).reshape(8 * TOK, 5, 2, TOK)
    gate, up = joined[:, :, 0], joined[:, :, 1]
    sigmoid = 1.0 / (1.0 + jnp.exp(-gate))
    silu = gate * sigmoid
    hidden = (silu * up).astype(BF16).astype(F32)
    shared_hidden = (share * hidden).astype(BF16).reshape(8 * TOK, 640)
    mixture_part = dot(shared_hidden, down, (((1,), (1,)), ((), ()))).astype(BF16)
    pulled = RESIDUAL_SCALE * dot(dy_rows, down, (((1,), (0,)), ((), ()))).reshape(8 * TOK, 5, TOK)
    grad_share = jnp.sum(hidden * pulled, -1)
    grad_hidden = share * pulled
    grad_gate = grad_hidden * up * (sigmoid + silu * (1.0 - sigmoid))
    grad_up = grad_hidden * silu
    grad_joined = jnp.stack([grad_gate, grad_up], 2).astype(BF16).reshape(8 * TOK, 1280)
    grad_normed_part = dot(grad_joined, gate_up, (((1,), (1,)), ((), ()))).astype(BF16)
    share_lines = jnp.pad(jnp.moveaxis(grad_share.reshape(8, TOK, 5), 2, 1), ((0, 0), (0, 3), (0, 0)))
    normed_parts, mixture_parts, share_parts = column_swap(
        [grad_normed_part.reshape(8, TOK, D), mixture_part.reshape(8, TOK, D), share_lines], 4
    )
    grad_gate_up = dot(normed_two_all, grad_joined, (((0,), (0,)), ((), ()))).astype(BF16)
    grad_down = (RESIDUAL_SCALE * dot(dy_rows, shared_hidden, (((0,), (0,)), ((), ())))).astype(BF16)

    mixture = jnp.sum(mixture_parts.astype(F32), 0)
    layer_out = (residual + RESIDUAL_SCALE * mixture).astype(BF16)
    mine = z * 4 + rep
    own_shares = lax.dynamic_index_in_dim(shares.reshape(8, TOK, EXPERTS), mine, 0, keepdims=False)
    grad_gates = jnp.sum(share_parts.reshape(2, 4, 8, TOK), 1)[:, :5].reshape(EXPERTS, TOK).T
    grad_logits = own_shares * (grad_gates - jnp.sum(own_shares * grad_gates, -1, keepdims=True))
    grad_normed_two = jnp.sum(normed_parts.astype(F32), 0) + jnp.dot(
        grad_logits, router.astype(F32).T, precision=PRECISE
    )
    grad_router = jnp.dot(normed_two.astype(F32).T, grad_logits, precision=PRECISE)
    grad_residual = out_grad + norm_back(grad_normed_two, residual, scale_two, gain_two)
    grad_lin = (RESIDUAL_SCALE * grad_residual).astype(BF16)
    grad_attended = dot(output_full, grad_lin, (((1,), (1,)), ((), ()))).astype(BF16)
    do_here = to_heads(grad_attended.reshape(HEADS, QROWS, TOK))
    dq_here, dkv_here = attend_back(bounds, q_here, kv_here, do_here, start_lines, o_here, lse)
    dq_parts, dkv_parts = from_attention(dq_here, dkv_here)

    dkv_sum = jnp.sum(dkv_parts.reshape(4, 4, 2, 2 * HEAD_DIM, TOK).astype(F32), 0)
    dkv_sum = jnp.moveaxis(dkv_sum, 0, 1)
    dqk = jnp.concatenate([dq_parts.astype(F32), dkv_sum[:, :, :HEAD_DIM]], 2).reshape(2, 4, 4, HEAD_DIM, TOK)
    dqk = turn(dqk, cosine, -sine)
    dq_lines = dqk[:, :, :GROUP].reshape(8, QROWS, TOK).astype(BF16)
    dkv_lines = (
        jnp.concatenate([dqk[:, :, GROUP], dkv_sum[:, :, HEAD_DIM:]], 2)
        .reshape(8, 2 * HEAD_DIM, TOK)
        .astype(BF16)
    )
    dqkv_lines = jnp.moveaxis(jnp.concatenate([dq_lines, dkv_lines], 1), 0, 1).reshape(320, 8 * TOK)
    grad_attn = dot(normed, dqkv_lines, (((0,), (1,)), ((), ())))
    grad_attn = jnp.concatenate([grad_attn, grad_router, jnp.zeros((D, PACK - 330), F32)], 1).astype(BF16)
    grad_lin_all = column_gather(grad_lin, 9).reshape(8 * TOK, D)
    (attended_here,) = column_swap([attended.reshape(HEADS, QROWS, TOK)], 10)
    attended_rows = jnp.moveaxis(attended_here, 0, 1).reshape(QROWS, 8 * TOK)
    grad_out = dot(attended_rows, grad_lin_all, (((1,), (0,)), ((), ()))).astype(BF16)

    attn_parts, gate_up_parts, down_parts, out_parts, dq_mine, dkv_mine = plane_sums(
        grad_attn.reshape(2, PLANE, 48, PACK),
        grad_gate_up.reshape(2, PLANE, 48, 1280),
        grad_down.reshape(2, PLANE, 48, 640),
        grad_out.reshape(PLANE, 12, D),
        dq_lines,
        dkv_lines,
    )
    attn_sum = jnp.sum(attn_parts.astype(F32), 0).astype(BF16)
    gate_up_sum = jnp.sum(gate_up_parts.astype(F32), 0).astype(BF16)
    down_sum = jnp.sum(down_parts.astype(F32), 0).astype(BF16)
    out_sum = jnp.sum(out_parts.astype(F32), 0).astype(BF16)
    attn_own, gate_up_own, down_own, out_own = final_swap(attn_sum, gate_up_sum, down_sum, out_sum)

    dq_own = dq_mine.reshape(D, TOK)
    dk_own = dkv_mine[:, :HEAD_DIM].reshape(HEADS * HEAD_DIM, TOK)
    dv_own = dkv_mine[:, HEAD_DIM:].reshape(HEADS * HEAD_DIM, TOK)
    grad_normed = dot(dq_own, query_full, (((0,), (1,)), ((), ()))) + dot(
        jnp.concatenate([dk_own, dv_own], 0), keyval_full, (((0,), (1,)), ((), ()))
    )
    input_grad = grad_residual + norm_back(grad_normed, tokens, rms_scale(tokens), gain_one)

    attn_f32 = attn_own.astype(F32)
    query_grad = jnp.moveaxis(attn_f32[:, :, :QROWS], 0, 1).reshape(48, D)
    key_grad = jnp.moveaxis(attn_f32[:, :, QROWS : QROWS + HEAD_DIM], 0, 1).reshape(48, HEADS * HEAD_DIM)
    value_grad = jnp.moveaxis(attn_f32[:, :, QROWS + HEAD_DIM : ROUTER_AT], 0, 1).reshape(
        48, HEADS * HEAD_DIM
    )
    keyval_grad = jnp.concatenate([key_grad, value_grad], 1)
    router_grad = jnp.sum(attn_f32[:, :, ROUTER_AT : ROUTER_AT + EXPERTS], 0)
    out_grad_rows = out_own.astype(F32).reshape(48, D)
    gate_up_grad = gate_up_own.astype(F32).reshape(2, 4, 48, 5, 2, TOK)
    gate_up_grad = jnp.transpose(gate_up_grad, (2, 0, 3, 4, 1, 5)).reshape(48, EXPERTS, 2 * FF)
    down_grad = down_own.astype(F32).reshape(2, 4, 48, 5, TOK)
    down_grad = jnp.transpose(down_grad, (2, 0, 3, 1, 4)).reshape(48, EXPERTS, FF)
    first_grad = (
        jnp.sum(query_grad * query_weight.astype(F32), 1) + jnp.sum(keyval_grad * key_value_matrix.astype(F32), 1)
    ) / first_gain.astype(F32)
    second_grad = (
        jnp.sum(gate_up_grad * gate_up_weight.astype(F32), (1, 2))
        + jnp.sum(router_grad * router_weight.astype(F32), 1)
    ) / second_gain.astype(F32)
    return (
        layer_out[None],
        input_grad[None],
        first_grad,
        query_grad,
        keyval_grad,
        out_grad_rows,
        second_grad,
        router_grad,
        gate_up_grad,
        down_grad,
    )


def solution(mesh):
    row = P("shard", None)
    rows = P("shard", None, None)
    own = P("rep", "shard", None)
    in_specs = (own, P("rep", "shard"), own, P("shard"), row, row, row, P("shard"), row, rows, rows, own)
    out_specs = (own, own, P("shard"), row, row, row, P("shard"), row, rows, rows)
    return jax.shard_map(shards, mesh=mesh, in_specs=in_specs, out_specs=out_specs, check_vma=False)
```

```python
import functools

import jax
import jax.numpy as jnp
from jax import lax
from jax.experimental import pallas as pl
from jax.experimental.pallas import tpu as pltpu
from jax.sharding import PartitionSpec as P

D = 1536
HEADS = 8
GROUP = 3
HEAD_DIM = 64
HALF = HEAD_DIM // 2
FF = 512
EXPERTS = 10
TOK = 128
SEQ = 4096
PLANE = 16
RUN = 512
QROWS = GROUP * HEAD_DIM
PACK = 384
ROUTER_AT = 320
GAIN_ONE_AT = 330
GAIN_TWO_AT = 331

NORM_EPS = 1e-06
RESIDUAL_SCALE = 0.22
SCORE_SCALE = 0.015625
ROPE_BASE = 10000.0
MASK_FILL = -1e30
PRECISE = lax.Precision.HIGHEST
BF16 = jnp.bfloat16
F32 = jnp.float32
VMEM_LIMIT = 56 * 1024 * 1024


def my_place():
    return lax.axis_index("shard"), lax.axis_index("rep")


def parts_of(shard):
    place = lax.rem(shard, PLANE)
    return shard // PLANE, place, place // 4, lax.rem(place, 4)


def same(one, other):
    return jnp.logical_and(one[0] == other[0], one[1] == other[1])


class Place:
    def __init__(self, me):
        self.me = me
        self.shard, self.rep = me
        self.z_lo, self.place, self.x, self.y = parts_of(self.shard)
        self.core = lax.rem(self.rep, 2)
        self.z = (self.rep // 2) * 2 + self.z_lo
        self.member = self.z_lo * 4 + self.rep

    def device(self, z, x, y, core):
        return lax.rem(z, 2) * PLANE + 4 * x + y, (z // 2) * 2 + core

    def step(self, axis, by):
        z, x, y = self.z, self.x, self.y
        if axis == "z":
            z = lax.rem(z + by, 4)
        elif axis == "x":
            x = lax.rem(x + by, 4)
        else:
            y = lax.rem(y + by, 4)
        return self.device(z, x, y, self.core)

    def sibling(self):
        return self.shard, self.rep + 1 - 2 * self.core

    def partner(self):
        return self.shard + (1 - 2 * self.z_lo) * PLANE, self.rep

    def member_at(self, z, core):
        return lax.rem(z, 2) * 4 + (z // 2) * 2 + core

    def near(self):
        result = [self.sibling()]
        for axis in ("z", "x", "y"):
            result += [self.step(axis, 1), self.step(axis, 3)]
        return result


def mesh_id(place):
    return {"shard": place[0], "rep": place[1]}


class Net:
    def __init__(self, here, sems):
        self.here, self.sems, self.used, self.sent = here, sems, 0, []

    def take(self, count=1):
        first = self.used
        self.used += count
        return first

    def push(self, source, target, to):
        number = self.take(2)
        copy = pltpu.make_async_remote_copy(
            src_ref=source,
            dst_ref=target,
            send_sem=self.sems.at[number],
            recv_sem=self.sems.at[number + 1],
            device_id=mesh_id(to),
        )
        copy.start()
        self.sent.append(copy)
        return number + 1

    def got(self, number, region):
        pltpu.make_async_remote_copy(
            src_ref=region,
            dst_ref=region,
            send_sem=self.sems.at[number],
            recv_sem=self.sems.at[number],
            device_id=mesh_id(self.here.sibling()),
        ).wait_recv()

    def local(self, source, target):
        copy = pltpu.make_async_copy(source, target, self.sems.at[self.take()])
        copy.start()
        return copy

    def finish(self):
        for copy in self.sent:
            copy.wait_send()


class Route:
    def __init__(self, n, to, source, pieces, index=None, may_be_self=False):
        self.n, self.to, self.source, self.pieces = n, to, source, pieces
        self.index = index or (lambda i: i)
        self.may_be_self = may_be_self


def each(n, body):
    if n <= 8:
        for i in range(n):
            body(i)
    else:

        def step(i, carry):
            body(i)
            return carry

        lax.fori_loop(0, n, step, 0)


def greet_routes(routes, me, barrier):
    awaited = 0
    for route in routes:

        def greet(i, route=route):
            source = route.source(i)

            def signal():
                pl.semaphore_signal(barrier, inc=1, device_id=mesh_id(source))

            if route.may_be_self:
                pl.when(jnp.logical_not(same(source, me)))(signal)
            else:
                signal()

        each(route.n, greet)
        awaited = awaited + route.n
        if route.may_be_self:
            for i in range(route.n):
                awaited = awaited - same(route.to(i), me).astype(jnp.int32)
    return awaited


def follow_routes(net, routes, ins, outs):
    me = net.here.me
    held = []
    for route in routes:
        count = route.n * len(route.pieces)
        held.append((net.take(count), net.take(count), net.take(len(route.pieces))))

    def remote(route, base, i, k, piece):
        source_in, cut, target_out, slot, unused = piece
        return pltpu.make_async_remote_copy(
            src_ref=ins[source_in].at[cut(i)],
            dst_ref=outs[target_out].at[slot(i)],
            send_sem=net.sems.at[base[0] + i * len(route.pieces) + k],
            recv_sem=net.sems.at[base[1] + route.index(i) * len(route.pieces) + k],
            device_id=mesh_id(route.to(i)),
        )

    def within(base, i, k, piece):
        source_in, cut, target_out, slot, unused = piece
        return pltpu.make_async_copy(
            ins[source_in].at[cut(i)], outs[target_out].at[slot(i)], net.sems.at[base[2] + k]
        )

    for route, base in zip(routes, held):

        def start(i, route=route, base=base):
            for k, piece in enumerate(route.pieces):
                copy = remote(route, base, i, k, piece)
                if route.may_be_self:
                    here = same(route.to(i), me)
                    pl.when(jnp.logical_not(here))(copy.start)
                    pl.when(here)(within(base, i, k, piece).start)
                else:
                    copy.start()

        each(route.n, start)
    yield
    yield
    yield
    for route, base in zip(routes, held):

        def arrive(i, route=route, base=base):
            for k, piece in enumerate(route.pieces):
                region = outs[piece[2]].at[piece[4](i)]
                place = route.source(i)
                sem = net.sems.at[base[1] + i * len(route.pieces) + k]
                copy = pltpu.make_async_remote_copy(
                    src_ref=region, dst_ref=region, send_sem=sem, recv_sem=sem, device_id=mesh_id(place)
                )
                if route.may_be_self:
                    pl.when(jnp.logical_not(same(place, me)))(copy.wait_recv)
                else:
                    copy.wait_recv()

        each(route.n, arrive)

        def leave(i, route=route, base=base):
            for k, piece in enumerate(route.pieces):
                copy = remote(route, base, i, k, piece)
                if route.may_be_self:
                    here = same(route.to(i), me)
                    pl.when(jnp.logical_not(here))(copy.wait_send)
                    pl.when(here)(within(base, i, k, piece).wait)
                else:
                    copy.wait_send()

        each(route.n, leave)


def comm(inputs, in_vmem, outputs, scratch, n_sems, collective_id, plan):
    n_in, n_out = len(inputs), len(outputs)

    def kernel(*refs):
        ins, outs = refs[:n_in], refs[n_in : n_in + n_out]
        rest, sems = refs[n_in + n_out : -1], refs[-1]
        net = Net(Place(my_place()), sems)
        flows, routes, near = plan(net, ins, outs, rest)
        barrier = pltpu.get_barrier_semaphore()
        awaited = greet_routes(routes, net.here.me, barrier)
        if near:
            others = net.here.near()
            for other in others:
                pl.semaphore_signal(barrier, inc=1, device_id=mesh_id(other))
            awaited = awaited + len(others)
        pl.semaphore_wait(barrier, awaited)
        while flows:
            going = []
            for flow in flows:
                if next(flow, "end") != "end":
                    going.append(flow)
            flows = going
        net.finish()
        assert net.used <= n_sems, net.used

    vmem = pl.BlockSpec(memory_space=pltpu.VMEM)
    anywhere = pl.BlockSpec(memory_space=pl.ANY)
    return pl.pallas_call(
        kernel,
        out_shape=[jax.ShapeDtypeStruct(s, t) for s, t, unused in outputs],
        in_specs=[vmem if k in in_vmem else anywhere for k in range(n_in)],
        out_specs=[vmem if inside else anywhere for unused, unused2, inside in outputs],
        scratch_shapes=list(scratch) + [pltpu.SemaphoreType.DMA((n_sems,))],
        compiler_params=pltpu.CompilerParams(
            collective_id=collective_id, has_side_effects=True, vmem_limit_bytes=VMEM_LIMIT
        ),
    )(*inputs)


def column_gather(net, source, out, half_of):
    here = net.here

    def slot(by, core):
        return out.at[here.member_at(lax.rem(here.z + by, 4), core)]

    core, other = here.core, 1 - here.core
    right, left, sibling = here.step("z", 1), here.step("z", 3), here.sibling()
    keep = net.local(source, slot(0, core))
    a = net.push(source, slot(0, core), right)
    b = net.push(source, slot(0, core), left)
    s = [net.push(source, slot(0, core), sibling)]
    yield
    net.got(a, slot(3, core))
    c = net.push(half_of(slot(3, core), 0), half_of(slot(3, core), 0), right)
    s.append(net.push(slot(3, core), slot(3, core), sibling))
    net.got(b, slot(1, core))
    d = net.push(half_of(slot(1, core), 1), half_of(slot(1, core), 1), left)
    s.append(net.push(slot(1, core), slot(1, core), sibling))
    yield
    net.got(c, half_of(slot(2, core), 0))
    net.got(d, half_of(slot(2, core), 1))
    s.append(net.push(slot(2, core), slot(2, core), sibling))
    yield
    for number, by in zip(s, (0, 3, 1, 2)):
        net.got(number, slot(by, other))
    keep.wait()


def row_half(size):
    first = (size // 2 + 15) // 16 * 16

    def half(ref, k):
        return ref.at[pl.ds(0, first)] if k == 0 else ref.at[pl.ds(first, size - first)]

    return half


def ring_gather(net, axis, source, slot, half):
    right, left = net.here.step(axis, 1), net.here.step(axis, 3)
    a = net.push(source, slot(0), right)
    b = net.push(source, slot(0), left)
    yield
    net.got(a, slot(3))
    c = net.push(half(slot(3), 0), half(slot(3), 0), right)
    net.got(b, slot(1))
    d = net.push(half(slot(1), 1), half(slot(1), 1), left)
    yield
    net.got(c, half(slot(2), 0))
    net.got(d, half(slot(2), 1))


def plane_gather(net, payload, out):
    here = net.here
    z, x, y = here.z_lo, here.x, here.y
    rows = row_half(48)
    pair = lambda ref, k: ref.at[pl.ds(2 * k, 2)]

    def first():
        keep = net.local(payload.at[z], out.at[z, x, y])
        number = net.push(payload.at[1 - z], out.at[z, x, y], here.partner())
        swap.append(number)
        yield from ring_gather(net, "x", payload.at[z], lambda by: out.at[z, lax.rem(x + by, 4), y], rows)
        keep.wait()
        yield
        bundle = lambda by: out.at[z, :, lax.rem(y + by, 4)]
        yield from ring_gather(net, "y", bundle(0), bundle, pair)

    def second():
        yield
        w = 1 - z
        net.got(swap[0], out.at[w, x, y])
        yield from ring_gather(
            net, "y", out.at[w, x, y], lambda by: out.at[w, x, lax.rem(y + by, 4)], rows
        )
        yield
        bundle = lambda by: out.at[w, lax.rem(x + by, 4)]
        yield from ring_gather(net, "x", bundle(0), bundle, pair)

    swap = []
    return [first(), second()]


def add(target, *parts):
    total = parts[0][...].astype(F32)
    for part in parts[1:]:
        total = total + part[...].astype(F32)
    target[...] = total.astype(target.dtype)


def ring_sum(net, axis, block, half, halves, wholes, target, extra=None):
    right, left = net.here.step(axis, 1), net.here.step(axis, 3)
    lower, upper = halves
    a = net.push(half(block(2), 0), lower, right)
    b = net.push(half(block(2), 1), upper, left)
    yield
    net.got(a, lower)
    add(half(block(1), 0), half(block(1), 0), lower)
    c = net.push(block(1), wholes[0], right)
    net.got(b, upper)
    add(half(block(3), 1), half(block(3), 1), upper)
    d = net.push(block(3), wholes[1], left)
    yield
    net.got(c, wholes[0])
    net.got(d, wholes[1])
    add(target, block(0), wholes[0], wholes[1])


def column_sum(net, parts, out, sums, sibling_parts, halves, wholes):
    here = net.here
    half = row_half(parts.shape[1])
    at = lambda by: lax.rem(here.z + by, 4)
    numbers = {}
    for by in (2, 1, 3, 0):
        numbers[by] = net.push(
            parts.at[here.member_at(at(by), 1 - here.core)], sibling_parts.at[at(by)], here.sibling()
        )
    yield
    for by in (2, 1, 3, 0):
        net.got(numbers[by], sibling_parts.at[at(by)])
        add(sums.at[at(by)], parts.at[here.member_at(at(by), here.core)], sibling_parts.at[at(by)])
    yield from ring_sum(
        net, "z", lambda by: sums.at[at(by)], half, (halves.at[0], halves.at[1]), (wholes.at[0], wholes.at[1]), out
    )


def column_sum_scratch(rows, columns):
    return [
        pltpu.VMEM((4, rows, columns), BF16),
        pltpu.VMEM((4, rows, columns), BF16),
        pltpu.VMEM((2, rows // 2, columns), BF16),
        pltpu.VMEM((2, rows, columns), BF16),
    ]


def plane_sum(net, parts, out, held, pairs, bundles, rows_a, rows_b, blocks):
    here = net.here
    at_x = lambda by: lax.rem(here.x + by, 4)
    at_y = lambda by: lax.rem(here.y + by, 4)
    pair = lambda ref, k: ref.at[pl.ds(2 * k, 2)]
    half = row_half(48)

    def first():
        copy = net.local(parts.at[0], held.at[0])
        yield
        copy.wait()
        mine = held.at[0, :, here.y]
        yield from ring_sum(
            net, "y", lambda by: held.at[0, :, at_y(by)], pair, (pairs.at[0], pairs.at[1]),
            (bundles.at[0], bundles.at[1]), mine,
        )
        yield
        yield from ring_sum(
            net, "x", lambda by: held.at[0, at_x(by), here.y], half, (rows_a.at[0], rows_b.at[0]),
            (blocks.at[0], blocks.at[1]), out.at[0],
        )

    def second():
        copy = net.local(parts.at[1], held.at[1])
        yield
        copy.wait()
        mine = held.at[1, here.x]
        yield from ring_sum(
            net, "x", lambda by: held.at[1, at_x(by)], pair, (pairs.at[2], pairs.at[3]),
            (bundles.at[2], bundles.at[3]), mine,
        )
        yield
        yield from ring_sum(
            net, "y", lambda by: held.at[1, here.x, at_y(by)], half, (rows_a.at[1], rows_b.at[1]),
            (blocks.at[2], blocks.at[3]), out.at[1],
        )

    return [first(), second()]


def plane_sum_scratch(columns):
    return [
        pltpu.VMEM((2, 4, 4, 48, columns), BF16),
        pltpu.VMEM((4, 2, 48, columns), BF16),
        pltpu.VMEM((4, 4, 48, columns), BF16),
        pltpu.VMEM((2, 32, columns), BF16),
        pltpu.VMEM((2, 16, columns), BF16),
        pltpu.VMEM((4, 48, columns), BF16),
    ]


def column_deal(net, parts, out, passing, half):
    here = net.here
    z = here.z_lo
    core, other = here.core, 1 - here.core
    lower, upper = passing

    def slot(by, core):
        return out.at[here.member_at(lax.rem(here.z + by, 4), core)]

    right, left, sibling = here.step("z", 1), here.step("z", 3), here.sibling()
    keep = net.local(parts.at[z], slot(0, core))
    e = net.push(half(parts.at[z], 0), lower, right)
    f = net.push(half(parts.at[z], 1), upper, left)
    a = net.push(parts.at[1 - z], slot(0, core), right)
    b = net.push(parts.at[1 - z], slot(0, core), left)
    s = [net.push(parts.at[z], slot(0, core), sibling)]
    yield
    net.got(e, lower)
    c = net.push(lower, half(slot(3, core), 0), right)
    net.got(f, upper)
    d = net.push(upper, half(slot(1, core), 1), left)
    net.got(a, slot(3, core))
    s.append(net.push(slot(3, core), slot(3, core), sibling))
    net.got(b, slot(1, core))
    s.append(net.push(slot(1, core), slot(1, core), sibling))
    yield
    net.got(c, half(slot(2, core), 0))
    net.got(d, half(slot(2, core), 1))
    s.append(net.push(slot(2, core), slot(2, core), sibling))
    yield
    for number, by in zip(s, (0, 3, 1, 2)):
        net.got(number, slot(by, other))
    keep.wait()


def column_route(me, pieces):
    z, place, unused, unused2 = parts_of(me[0])
    mine = z * 4 + me[1]

    def where(member):
        return (member // 4) * PLANE + place, lax.rem(member, 4)

    def after(i):
        return lax.rem(mine + 1 + i, 8)

    def before(i):
        return lax.rem(mine + 7 - i, 8)

    return Route(
        7,
        lambda i: where(after(i)),
        lambda i: where(before(i)),
        [
            (
                a,
                lambda i, cut=cut: cut(after(i)),
                b,
                lambda i, slot=slot: slot(mine),
                lambda i, slot=slot: slot(before(i)),
            )
            for a, cut, b, slot in pieces
        ],
    )


def plane_route(me, pieces):
    z, place, unused, unused2 = parts_of(me[0])

    def after(i):
        return lax.rem(place + 1 + i, PLANE)

    def before(i):
        return lax.rem(place + 15 - i, PLANE)

    return Route(
        15,
        lambda i: (z * PLANE + after(i), me[1]),
        lambda i: (z * PLANE + before(i), me[1]),
        [
            (
                a,
                lambda i, cut=cut: cut(after(i)),
                b,
                lambda i, slot=slot: slot(place),
                lambda i, slot=slot: slot(before(i)),
            )
            for a, cut, b, slot in pieces
        ],
    )


def own_copies(net, ins, outs, copies):
    started = [net.local(ins[a].at[cut], outs[b].at[slot]) for a, cut, b, slot in copies]
    yield
    for copy in started:
        copy.wait()


ROW_HALF = row_half(TOK)


def gather_start(x, ints, attn, down):
    def plan(net, ins, outs, scratch):
        flows = [column_gather(net, ins[0], outs[0], ROW_HALF)]
        flows += plane_gather(net, ins[2], outs[2])
        flows += plane_gather(net, ins[3], outs[3])
        flows += [column_gather(net, ins[1], outs[1], lambda ref, k: ref.at[pl.ds(8 * k, 8)])]
        return flows, [], True

    x_all, ints_all, attn_all, down_all = comm(
        [x, ints, attn, down],
        (),
        [
            ((8, TOK, D), BF16, False),
            ((8, 16, TOK), jnp.int32, False),
            ((2, 4, 4, 48, PACK), BF16, False),
            ((2, 4, 4, 48, 640), BF16, False),
        ],
        [],
        112,
        0,
        plan,
    )
    return x_all, ints_all, attn_all.reshape(D, PACK), down_all.reshape(D, 640)


def gather_normed(normed, gate_up):
    def plan(net, ins, outs, scratch):
        flows = [column_gather(net, ins[0], outs[0], ROW_HALF)]
        flows += plane_gather(net, ins[1], outs[1])
        return flows, [], True

    normed_all, gate_up_all = comm(
        [normed, gate_up],
        (),
        [((8, TOK, D), BF16, False), ((2, 4, 4, 48, 1280), BF16, False)],
        [],
        64,
        3,
        plan,
    )
    return normed_all.reshape(8 * TOK, D), gate_up_all.reshape(D, 1280)


def mirrored(z, x):
    return x + z * (3 - 2 * x)


def query_routes(me, q_in, q_out):
    z_me, place, x, y = parts_of(me[0])
    base = z_me * PLANE

    def plain(i):
        return lax.rem(y + 1 + i, 4)

    def plain_before(i):
        return lax.rem(y + 3 - i, 4)

    def other(i):
        return lax.rem(y + i, 4)

    def other_before(i):
        return lax.rem(y + 4 - i, 4)

    first = Route(
        3,
        lambda i: (base + 4 * x + plain(i), me[1]),
        lambda i: (base + 4 * x + plain_before(i), me[1]),
        [(q_in, lambda i: (0, plain(i)), q_out, lambda i: (0, y), lambda i: (0, plain_before(i)))],
    )
    second = Route(
        4,
        lambda i: (base + 4 * (3 - x) + other(i), me[1]),
        lambda i: (base + 4 * (3 - x) + other_before(i), me[1]),
        [(q_in, lambda i: (1, other(i)), q_out, lambda i: (1, y), lambda i: (1, other_before(i)))],
    )
    return [first, second], [(q_in, (0, y), q_out, (0, y))]


def to_attention(q, kv, ints, dy):
    def plan(net, ins, outs, scratch):
        me = net.here.me
        z_me, place, x, y = parts_of(me[0])
        routes, own = query_routes(me, 0, 0)
        routes = [
            plane_route(
                me,
                [
                    (1, lambda p: (0, lax.rem(p, 4)), 1, lambda p: (0, p)),
                    (1, lambda p: (1, lax.rem(p, 4)), 1, lambda p: (1, p)),
                    (2, lambda p: lax.rem(p, 4), 2, lambda p: p),
                ],
            )
        ] + routes
        own = own + [
            (1, (0, y), 1, (0, place)),
            (1, (1, y), 1, (1, place)),
            (2, y, 2, place),
        ]
        flows = [
            follow_routes(net, routes, ins, outs),
            own_copies(net, ins, outs, own),
            column_gather(net, ins[3], outs[3], ROW_HALF),
        ]
        return flows, routes, True

    return comm(
        [q, kv, ints, dy],
        (),
        [
            ((2, 4, QROWS, TOK), BF16, False),
            ((2, PLANE, TOK, TOK), BF16, False),
            ((PLANE, 8, TOK), jnp.int32, False),
            ((8, TOK, D), BF16, False),
        ],
        [],
        144,
        1,
        plan,
    )


def from_attention(q, kv, grad_lin, attended, mixture):
    def plan(net, ins, outs, scratch):
        me = net.here.me
        z_me, place, x, y = parts_of(me[0])
        routes, own = query_routes(me, 0, 0)
        routes = [plane_route(me, [(1, lambda p: (slice(None), p), 1, lambda p: p)])] + routes
        routes += [column_route(me, [(3, lambda m: m, 3, lambda m: m)])]
        mine = net.here.member
        own = own + [(1, (slice(None), place), 1, place), (3, mine, 3, mine)]
        flows = [
            follow_routes(net, routes, ins, outs),
            own_copies(net, ins, outs, own),
            column_gather(net, ins[2], outs[2], ROW_HALF),
            column_sum(net, ins[4], outs[4], *scratch),
        ]
        return flows, routes, True

    return comm(
        [q, kv, grad_lin, attended, mixture],
        (4,),
        [
            ((2, 4, QROWS, TOK), BF16, False),
            ((PLANE, 2, TOK, TOK), BF16, False),
            ((8, TOK, D), BF16, False),
            ((HEADS, QROWS, TOK), BF16, False),
            ((TOK, D), F32, True),
        ],
        column_sum_scratch(TOK, D),
        144,
        6,
        plan,
    )


def head_places(me):
    z, place, x, y = parts_of(me[0])
    quarter = mirrored(z, x)

    def place_of(m):
        return (m // 4) * PLANE + 4 * quarter + me[1], lax.rem(m, 4)

    return place_of, (z, y)


def owner_places(me):
    z, place, x, y = parts_of(me[0])

    def place_of(i):
        run, other = i // 4, lax.rem(i, 4)
        return run * PLANE + 4 * mirrored(run, x) + other, y

    return place_of, z * 4 + me[1]


def to_owners(o):
    def plan(net, ins, outs, scratch):
        me = net.here.me
        owner, mine = owner_places(me)
        head, slot = head_places(me)
        route = Route(
            8,
            owner,
            head,
            [(0, lambda i: (i // 4, i % 4), 0, lambda i: mine, lambda i: i)],
            index=lambda i: mine,
            may_be_self=True,
        )
        return [follow_routes(net, [route], ins, outs)], [route], False

    return comm([o], (), [((HEADS, QROWS, TOK), BF16, False)], [], 24, 2, plan)[0]


def to_heads(do):
    def plan(net, ins, outs, scratch):
        me = net.here.me
        owner, mine = owner_places(me)
        head, slot = head_places(me)
        route = Route(
            8,
            head,
            owner,
            [(0, lambda i: i, 0, lambda i: slot, lambda i: (i // 4, i % 4))],
            index=lambda i: slot[0] * 4 + slot[1],
            may_be_self=True,
        )
        return [follow_routes(net, [route], ins, outs)], [route], False

    return comm([do], (), [((2, 4, QROWS, TOK), BF16, False)], [], 24, 5, plan)[0]


def sum_experts(normed, share, gate_up):
    def plan(net, ins, outs, scratch):
        me = net.here.me
        mine = net.here.member
        routes = [column_route(me, [(1, lambda m: m, 1, lambda m: m)])]
        flows = [
            column_sum(net, ins[0], outs[0], *scratch[:4]),
            follow_routes(net, routes, ins, outs),
            own_copies(net, ins, outs, [(1, mine, 1, mine)]),
        ]
        flows += plane_sum(net, ins[2], outs[2], *scratch[4:])
        return flows, routes, True

    return comm(
        [normed, share, gate_up],
        (0,),
        [((TOK, D), F32, True), ((8, 8, TOK), F32, False), ((2, 48, 1280), BF16, True)],
        column_sum_scratch(TOK, D) + plane_sum_scratch(1280),
        96,
        4,
        plan,
    )


def sum_planes(attn, down, out_rows, dq, dkv):
    def plan(net, ins, outs, scratch):
        me = net.here.me
        place, mine = net.here.place, net.here.member
        routes = [
            column_route(me, [(3, lambda m: m, 3, lambda m: m), (4, lambda m: m, 4, lambda m: m)]),
            plane_route(me, [(2, lambda p: p, 2, lambda p: p)]),
        ]
        own = [(2, place, 2, place), (3, mine, 3, mine), (4, mine, 4, mine)]
        flows = plane_sum(net, ins[0], outs[0], *scratch[:6]) + plane_sum(net, ins[1], outs[1], *scratch[6:])
        flows += [follow_routes(net, routes, ins, outs), own_copies(net, ins, outs, own)]
        return flows, routes, True

    return comm(
        [attn, down, out_rows, dq, dkv],
        (),
        [
            ((2, 48, PACK), BF16, True),
            ((2, 48, 640), BF16, True),
            ((PLANE, 12, D), BF16, False),
            (dq.shape, BF16, False),
            (dkv.shape, BF16, False),
        ],
        plane_sum_scratch(PACK) + plane_sum_scratch(640),
        144,
        7,
        plan,
    )


def final_deal(attn, gate_up, down, out_rows):
    def plan(net, ins, outs, scratch):
        me = net.here.me
        place, mine = net.here.place, net.here.member
        routes = [
            Route(
                4,
                lambda i: (4 * mine + place // 4, i),
                lambda i: (
                    (me[0] // 4) // 4 * PLANE + 4 * lax.rem(me[0], 4) + i,
                    lax.rem(me[0] // 4, 4),
                ),
                [(3, lambda i: slice(None), 3, lambda i: lax.rem(place, 4), lambda i: i)],
                index=lambda i: lax.rem(place, 4),
                may_be_self=True,
            ),
        ]
        half = row_half(48)
        flows = [follow_routes(net, routes, ins, outs)]
        for k in range(3):
            flows.append(column_deal(net, ins[k], outs[k], scratch[2 * k : 2 * k + 2], half))
        return flows, routes, True

    widths = (PACK, 1280, 640)
    scratch = []
    for width in widths:
        scratch += [pltpu.VMEM((32, width), BF16), pltpu.VMEM((16, width), BF16)]
    return comm(
        [attn, gate_up, down, out_rows],
        (),
        [((8, 48, width), BF16, False) for width in widths] + [((4, 12, D), BF16, False)],
        scratch,
        96,
        8,
        plan,
    )


def unpack_queries(source, target):
    for run in range(2):
        for part in range(4):
            target[:, run * RUN + part * TOK : run * RUN + (part + 1) * TOK] = source[run, part]


def unpack_keys(kv_ref, key_rows, value_lines):
    def step(j, carry):
        place = pl.ds(pl.multiple_of(j * TOK, TOK), TOK)
        block = kv_ref[j // PLANE, lax.rem(j, PLANE)]
        key_rows[place, :] = block[:HEAD_DIM].astype(F32).T.astype(BF16)
        value_lines[:, place] = block[HEAD_DIM:]
        return carry

    lax.fori_loop(0, SEQ // TOK, step, 0)


def visible_block(block, start, query):
    key = block * RUN + lax.broadcasted_iota(jnp.int32, (RUN, RUN), 0)
    return jnp.logical_and(key >= start, key <= query)


def attend_kernel(bounds, q_ref, kv_ref, start_ref, o_ref, low_ref, lse_ref, queries, key_rows, value_lines):
    unpack_queries(q_ref, queries)
    unpack_keys(kv_ref, key_rows, value_lines)
    for run in range(2):
        cols = slice(run * RUN, (run + 1) * RUN)
        start = start_ref[0:1, cols]
        query = bounds[4 + run] + lax.broadcasted_iota(jnp.int32, (1, RUN), 1)
        heads = [
            queries[h * HEAD_DIM : (h + 1) * HEAD_DIM, cols] * jnp.asarray(SCORE_SCALE, BF16)
            for h in range(GROUP)
        ]

        def step(block, carry):
            place = pl.ds(pl.multiple_of(block * RUN, RUN), RUN)
            keys, values = key_rows[place, :], value_lines[:, place]
            seen = visible_block(block, start, query)
            result = []
            for h in range(GROUP):
                peak, total, acc = carry[3 * h : 3 * h + 3]
                scores = jnp.dot(keys, heads[h], preferred_element_type=F32)
                scores = jnp.where(seen, scores, MASK_FILL)
                top = jnp.maximum(peak, jnp.max(scores, 0, keepdims=True))
                weights = jnp.exp(scores - top)
                fade = jnp.exp(peak - top)
                total = fade * total + jnp.sum(weights, 0, keepdims=True)
                acc = fade * acc + jnp.dot(values, weights.astype(BF16), preferred_element_type=F32)
                result += [top, total, acc]
            return tuple(result)

        zero = []
        for h in range(GROUP):
            zero += [
                jnp.full((1, RUN), MASK_FILL, F32),
                jnp.zeros((1, RUN), F32),
                jnp.zeros((HEAD_DIM, RUN), F32),
            ]
        done = lax.fori_loop(bounds[run], bounds[2 + run], step, tuple(zero))
        for h in range(GROUP):
            peak, total, acc = done[3 * h : 3 * h + 3]
            rows = slice(h * HEAD_DIM, (h + 1) * HEAD_DIM)
            attended = acc / total
            o_ref[rows, cols] = attended
            for part in range(4):
                low_ref[run, part, rows, :] = attended[:, part * TOK : (part + 1) * TOK].astype(BF16)
            lse_ref[h : h + 1, cols] = peak + jnp.log(total)


def attend(bounds, q, kv, start):
    vmem = pl.BlockSpec(memory_space=pltpu.VMEM)
    return pl.pallas_call(
        attend_kernel,
        out_shape=[
            jax.ShapeDtypeStruct((QROWS, 2 * RUN), F32),
            jax.ShapeDtypeStruct((2, 4, QROWS, TOK), BF16),
            jax.ShapeDtypeStruct((8, 2 * RUN), F32),
        ],
        in_specs=[pl.BlockSpec(memory_space=pltpu.SMEM), vmem, vmem, vmem],
        out_specs=[vmem, vmem, vmem],
        scratch_shapes=[
            pltpu.VMEM((QROWS, 2 * RUN), BF16),
            pltpu.VMEM((SEQ, HEAD_DIM), BF16),
            pltpu.VMEM((HEAD_DIM, SEQ), BF16),
        ],
        compiler_params=pltpu.CompilerParams(vmem_limit_bytes=VMEM_LIMIT),
    )(bounds, q, kv, start)


NT = (((1,), (1,)), ((), ()))


def attend_back_kernel(
    bounds, q_ref, kv_ref, do_ref, start_ref, o_ref, lse_ref, dq_ref, dkv_ref,
    queries, grads, key_rows, value_rows, key_lines, key_grad, value_grad,
):
    unpack_queries(q_ref, queries)
    unpack_queries(do_ref, grads)
    key_grad[...] = jnp.zeros_like(key_grad)
    value_grad[...] = jnp.zeros_like(value_grad)

    def spread(j, carry):
        place = pl.ds(pl.multiple_of(j * TOK, TOK), TOK)
        block = kv_ref[j // PLANE, lax.rem(j, PLANE)]
        turned = block.astype(F32).T.astype(BF16)
        key_rows[place, :] = turned[:, :HEAD_DIM]
        value_rows[place, :] = turned[:, HEAD_DIM:]
        key_lines[:, place] = block[:HEAD_DIM]
        return carry

    lax.fori_loop(0, SEQ // TOK, spread, 0)
    for run in range(2):
        cols = slice(run * RUN, (run + 1) * RUN)
        start = start_ref[0:1, cols]
        query = bounds[4 + run] + lax.broadcasted_iota(jnp.int32, (1, RUN), 1)
        lse = [lse_ref[h : h + 1, cols] for h in range(GROUP)]
        delta = []
        for h in range(GROUP):
            rows = slice(h * HEAD_DIM, (h + 1) * HEAD_DIM)
            delta.append(jnp.sum(grads[rows, cols].astype(F32) * o_ref[rows, cols], 0, keepdims=True))

        def step(block, carry):
            place = pl.ds(pl.multiple_of(block * RUN, RUN), RUN)
            keys, values, lines = key_rows[place, :], value_rows[place, :], key_lines[:, place]
            seen = visible_block(block, start, query)
            result = []
            dk = key_grad[place, :]
            dv = value_grad[place, :]
            for h in range(GROUP):
                rows = slice(h * HEAD_DIM, (h + 1) * HEAD_DIM)
                q = queries[rows, cols] * jnp.asarray(SCORE_SCALE, BF16)
                do = grads[rows, cols]
                scores = jnp.dot(keys, q, preferred_element_type=F32)
                weights = jnp.exp(jnp.where(seen, scores, MASK_FILL) - lse[h])
                pull = jnp.dot(values, do, preferred_element_type=F32)
                ds = (weights * (pull - delta[h])).astype(BF16)
                dv = dv + lax.dot_general(weights.astype(BF16), do, NT, preferred_element_type=F32)
                dk = dk + lax.dot_general(ds, q, NT, preferred_element_type=F32)
                result.append(carry[h] + jnp.dot(lines, ds, preferred_element_type=F32))
            key_grad[place, :] = dk
            value_grad[place, :] = dv
            return tuple(result)

        done = lax.fori_loop(
            bounds[run], bounds[2 + run], step, tuple(jnp.zeros((HEAD_DIM, RUN), F32) for h in range(GROUP))
        )
        for h in range(GROUP):
            rows = slice(h * HEAD_DIM, (h + 1) * HEAD_DIM)
            scaled = SCORE_SCALE * done[h]
            for part in range(4):
                dq_ref[run, part, rows, :] = scaled[:, part * TOK : (part + 1) * TOK].astype(BF16)

    def gather(j, carry):
        place = pl.ds(pl.multiple_of(j * TOK, TOK), TOK)
        dkv_ref[j // PLANE, lax.rem(j, PLANE), :HEAD_DIM, :] = key_grad[place, :].T.astype(BF16)
        dkv_ref[j // PLANE, lax.rem(j, PLANE), HEAD_DIM:, :] = value_grad[place, :].T.astype(BF16)
        return carry

    lax.fori_loop(0, SEQ // TOK, gather, 0)


def attend_back(bounds, q, kv, do, start, o, lse):
    vmem = pl.BlockSpec(memory_space=pltpu.VMEM)
    return pl.pallas_call(
        attend_back_kernel,
        out_shape=[
            jax.ShapeDtypeStruct((2, 4, QROWS, TOK), BF16),
            jax.ShapeDtypeStruct((2, PLANE, TOK, TOK), BF16),
        ],
        in_specs=[pl.BlockSpec(memory_space=pltpu.SMEM)] + [vmem] * 6,
        out_specs=[vmem, vmem],
        scratch_shapes=[
            pltpu.VMEM((QROWS, 2 * RUN), BF16),
            pltpu.VMEM((QROWS, 2 * RUN), BF16),
            pltpu.VMEM((SEQ, HEAD_DIM), BF16),
            pltpu.VMEM((SEQ, HEAD_DIM), BF16),
            pltpu.VMEM((HEAD_DIM, SEQ), BF16),
            pltpu.VMEM((SEQ, HEAD_DIM), F32),
            pltpu.VMEM((SEQ, HEAD_DIM), F32),
        ],
        compiler_params=pltpu.CompilerParams(vmem_limit_bytes=VMEM_LIMIT),
    )(bounds, q, kv, do, start, o, lse)


def rms_scale(values):
    return lax.rsqrt(jnp.mean(values * values, -1, keepdims=True) + NORM_EPS)


def norm_back(grad_normed, values, scale_factor, gain_values):
    weighted = grad_normed * gain_values
    return scale_factor * weighted - values * scale_factor**3 * jnp.mean(
        weighted * values, -1, keepdims=True
    )


def turn(values, cosine, sine):
    front, behind = values[..., :HALF, :], values[..., HALF:, :]
    return jnp.concatenate([front * cosine - behind * sine, behind * cosine + front * sine], -2)


def shards(
    layer_input,
    segments,
    choices,
    first_gain,
    query_weight,
    key_value_matrix,
    output_weight,
    second_gain,
    router_weight,
    gate_up_weight,
    down_weight,
    cotangent,
):
    shard, rep = my_place()
    z, place, x, y = parts_of(shard)
    dot = functools.partial(lax.dot_general, preferred_element_type=F32)

    choices_lines = choices[0].T
    ints = jnp.concatenate([choices_lines, segments, jnp.zeros((7, TOK), jnp.int32)], 0)
    gate_up_mine = lax.dynamic_index_in_dim(
        gate_up_weight.reshape(48, 2, 5, 2, 4, TOK), rep, 4, keepdims=False
    )
    gate_up_mine = jnp.moveaxis(gate_up_mine, 1, 0).reshape(2, 48, 1280)
    down_mine = lax.dynamic_index_in_dim(down_weight.reshape(48, 2, 5, 4, TOK), rep, 3, keepdims=False)
    down_mine = jnp.moveaxis(down_mine, 1, 0).reshape(2, 48, 640)
    query_mine = lax.dynamic_index_in_dim(query_weight.reshape(48, 2, 4, QROWS), rep, 2, keepdims=False)
    keyval_mine = lax.dynamic_index_in_dim(
        key_value_matrix.reshape(48, 2, 2, 4, HEAD_DIM), rep, 3, keepdims=False
    )
    small = jnp.concatenate(
        [router_weight, first_gain[:, None], second_gain[:, None], jnp.zeros((48, PACK - 332), BF16)], 1
    )
    attn_mine = jnp.stack(
        [
            jnp.concatenate([query_mine[:, k], keyval_mine[:, 0, k], keyval_mine[:, 1, k], small], 1)
            for k in range(2)
        ]
    )
    x_all, ints_all, attn, down = gather_start(layer_input[0], ints, attn_mine, down_mine)
    output_full = lax.all_gather(output_weight, "shard", axis=0, tiled=True)
    query_full = lax.all_gather(query_weight, "shard", axis=0, tiled=True)
    keyval_full = lax.all_gather(key_value_matrix, "shard", axis=0, tiled=True)

    gain_one = attn[:, GAIN_ONE_AT].astype(F32)
    gain_two = attn[:, GAIN_TWO_AT].astype(F32)
    router = attn[:, ROUTER_AT : ROUTER_AT + EXPERTS]
    tokens_all = x_all.reshape(8 * TOK, D).astype(F32)
    normed = (tokens_all * rms_scale(tokens_all) * gain_one).astype(BF16)

    frequency = ROPE_BASE ** (-jnp.arange(0, HEAD_DIM, 2, dtype=F32) / HEAD_DIM)
    column_place = (
        (jnp.arange(2, dtype=jnp.int32)[:, None] * PLANE + place) * TOK
        + jnp.arange(TOK, dtype=jnp.int32)[None, :]
    )
    angle = column_place.astype(F32)[:, None, :] * frequency[None, :, None]
    cosine = jnp.cos(angle)[:, None, None]
    sine = jnp.sin(angle)[:, None, None]
    linear = dot(attn[:, : QROWS + 2 * HEAD_DIM], normed, (((0,), (1,)), ((), ())))
    linear = jnp.moveaxis(linear.reshape(QROWS + 2 * HEAD_DIM, 2, 4, TOK), 0, 2)
    turned = turn(linear[:, :, : QROWS + HEAD_DIM].reshape(2, 4, 4, HEAD_DIM, TOK), cosine, sine)
    query_lines = turned[:, :, :GROUP].reshape(2, 4, QROWS, TOK).astype(BF16)
    keyval_lines = jnp.concatenate([turned[:, :, GROUP], linear[:, :, QROWS + HEAD_DIM :]], 2).astype(BF16)
    segment_column = jnp.moveaxis(ints_all[:, 8].reshape(2, 4, TOK), 0, 1)
    segment_column = jnp.concatenate([segment_column, jnp.zeros((4, 6, TOK), jnp.int32)], 1)
    q_here, kv_here, segment_here, dy_all = to_attention(
        query_lines, keyval_lines, segment_column, cotangent[0]
    )

    segment_all = jnp.moveaxis(segment_here[:, :2], 1, 0).reshape(SEQ)
    earlier = jnp.sum(segment_all[None, :] < jnp.arange(5, dtype=jnp.int32)[:, None], 1, dtype=jnp.int32)
    runs = jnp.stack([x, 7 - x])
    mark = jnp.concatenate(
        [lax.dynamic_slice_in_dim(segment_all, runs[k] * RUN, RUN) for k in range(2)]
    )
    start = jnp.sum(
        jnp.where(mark[None, :] == jnp.arange(5, dtype=jnp.int32)[:, None], earlier[:, None], 0), 0
    )
    first_block = jnp.min(start.reshape(2, RUN), 1) // RUN
    bounds = jnp.concatenate([first_block, runs + 1, runs * RUN, jnp.zeros((2,), jnp.int32)])
    start_lines = jnp.broadcast_to(start[None, :], (8, 2 * RUN))
    o_here, o_low, lse = attend(bounds, q_here, kv_here, start_lines)
    attended = to_owners(o_low).reshape(D, TOK)

    tokens = layer_input[0].astype(F32)
    out_grad = cotangent[0].astype(F32)
    residual = tokens + RESIDUAL_SCALE * dot(attended, output_full, (((0,), (0,)), ((), ())))
    scale_two = rms_scale(residual)
    normed_two = (residual * scale_two * gain_two).astype(BF16)
    normed_two_all, gate_up = gather_normed(normed_two, gate_up_mine)

    dy_rows = dy_all.reshape(8 * TOK, D)
    chosen = jnp.any(
        ints_all[:, :8, :, None] == jnp.arange(EXPERTS, dtype=jnp.int32), 1
    ).reshape(8 * TOK, EXPERTS)
    logits = jnp.where(chosen, dot(normed_two_all, router, (((1,), (0,)), ((), ()))), MASK_FILL)
    exponent = jnp.where(chosen, jnp.exp(logits - jnp.max(logits, -1, keepdims=True)), 0.0)
    shares = exponent / jnp.sum(exponent, -1, keepdims=True)
    share = lax.dynamic_slice_in_dim(shares, z * 5, 5, 1)[:, :, None]
    joined = dot(normed_two_all, gate_up, (((1,), (0,)), ((), ()))).reshape(8 * TOK, 5, 2, TOK)
    gate, up = joined[:, :, 0], joined[:, :, 1]
    sigmoid = 1.0 / (1.0 + jnp.exp(-gate))
    silu = gate * sigmoid
    hidden = (silu * up).astype(BF16).astype(F32)
    shared_hidden = (share * hidden).astype(BF16).reshape(8 * TOK, 640)
    mixture_part = dot(shared_hidden, down, (((1,), (1,)), ((), ()))).astype(BF16)
    pulled = RESIDUAL_SCALE * dot(dy_rows, down, (((1,), (0,)), ((), ()))).reshape(8 * TOK, 5, TOK)
    grad_share = jnp.sum(hidden * pulled, -1)
    grad_hidden = share * pulled
    grad_gate = grad_hidden * up * (sigmoid + silu * (1.0 - sigmoid))
    grad_up = grad_hidden * silu
    grad_joined = jnp.stack([grad_gate, grad_up], 2).astype(BF16).reshape(8 * TOK, 1280)
    grad_normed_part = dot(grad_joined, gate_up, (((1,), (1,)), ((), ()))).astype(BF16)
    share_lines = jnp.pad(jnp.moveaxis(grad_share.reshape(8, TOK, 5), 2, 1), ((0, 0), (0, 3), (0, 0)))
    grad_gate_up = dot(normed_two_all, grad_joined, (((0,), (0,)), ((), ()))).astype(BF16)
    grad_down = (RESIDUAL_SCALE * dot(dy_rows, shared_hidden, (((0,), (0,)), ((), ())))).astype(BF16)

    normed_sum, share_parts, gate_up_sum = sum_experts(
        grad_normed_part.reshape(8, TOK, D), share_lines, grad_gate_up.reshape(2, 4, 4, 48, 1280)
    )

    mine = z * 4 + rep
    own_shares = lax.dynamic_index_in_dim(shares.reshape(8, TOK, EXPERTS), mine, 0, keepdims=False)
    grad_gates = jnp.sum(share_parts.reshape(2, 4, 8, TOK), 1)[:, :5].reshape(EXPERTS, TOK).T
    grad_logits = own_shares * (grad_gates - jnp.sum(own_shares * grad_gates, -1, keepdims=True))
    grad_normed_two = normed_sum + jnp.dot(
        grad_logits, router.astype(F32).T, precision=PRECISE
    )
    grad_router = jnp.dot(normed_two.astype(F32).T, grad_logits, precision=PRECISE)
    grad_residual = out_grad + norm_back(grad_normed_two, residual, scale_two, gain_two)
    grad_lin = (RESIDUAL_SCALE * grad_residual).astype(BF16)
    grad_attended = dot(output_full, grad_lin, (((1,), (1,)), ((), ()))).astype(BF16)
    do_here = to_heads(grad_attended.reshape(HEADS, QROWS, TOK))
    dq_here, dkv_here = attend_back(bounds, q_here, kv_here, do_here, start_lines, o_here, lse)
    dq_parts, dkv_parts, grad_lin_all, attended_here, mixture = from_attention(
        dq_here,
        dkv_here,
        grad_lin,
        attended.reshape(HEADS, QROWS, TOK),
        mixture_part.reshape(8, TOK, D),
    )
    layer_out = (residual + RESIDUAL_SCALE * mixture).astype(BF16)

    dkv_sum = jnp.sum(dkv_parts.reshape(4, 4, 2, 2 * HEAD_DIM, TOK).astype(F32), 0)
    dkv_sum = jnp.moveaxis(dkv_sum, 0, 1)
    dqk = jnp.concatenate([dq_parts.astype(F32), dkv_sum[:, :, :HEAD_DIM]], 2).reshape(2, 4, 4, HEAD_DIM, TOK)
    dqk = turn(dqk, cosine, -sine)
    dq_lines = dqk[:, :, :GROUP].reshape(8, QROWS, TOK).astype(BF16)
    dkv_lines = (
        jnp.concatenate([dqk[:, :, GROUP], dkv_sum[:, :, HEAD_DIM:]], 2)
        .reshape(8, 2 * HEAD_DIM, TOK)
        .astype(BF16)
    )
    dqkv_lines = jnp.moveaxis(jnp.concatenate([dq_lines, dkv_lines], 1), 0, 1).reshape(320, 8 * TOK)
    grad_attn = dot(normed, dqkv_lines, (((0,), (1,)), ((), ())))
    grad_attn = jnp.concatenate([grad_attn, grad_router, jnp.zeros((D, PACK - 330), F32)], 1).astype(BF16)
    attended_rows = jnp.moveaxis(attended_here, 0, 1).reshape(QROWS, 8 * TOK)
    grad_out = dot(attended_rows, grad_lin_all.reshape(8 * TOK, D), (((1,), (0,)), ((), ()))).astype(BF16)

    attn_sum, down_sum, out_parts, dq_mine, dkv_mine = sum_planes(
        grad_attn.reshape(2, 4, 4, 48, PACK),
        grad_down.reshape(2, 4, 4, 48, 640),
        grad_out.reshape(PLANE, 12, D),
        dq_lines,
        dkv_lines,
    )
    out_sum = jnp.sum(out_parts.astype(F32), 0).astype(BF16)
    attn_own, gate_up_own, down_own, out_own = final_deal(attn_sum, gate_up_sum, down_sum, out_sum)

    dq_own = dq_mine.reshape(D, TOK)
    dk_own = dkv_mine[:, :HEAD_DIM].reshape(HEADS * HEAD_DIM, TOK)
    dv_own = dkv_mine[:, HEAD_DIM:].reshape(HEADS * HEAD_DIM, TOK)
    grad_normed = dot(dq_own, query_full, (((0,), (1,)), ((), ()))) + dot(
        jnp.concatenate([dk_own, dv_own], 0), keyval_full, (((0,), (1,)), ((), ()))
    )
    input_grad = grad_residual + norm_back(grad_normed, tokens, rms_scale(tokens), gain_one)

    attn_f32 = attn_own.astype(F32)
    query_grad = jnp.moveaxis(attn_f32[:, :, :QROWS], 0, 1).reshape(48, D)
    key_grad = jnp.moveaxis(attn_f32[:, :, QROWS : QROWS + HEAD_DIM], 0, 1).reshape(48, HEADS * HEAD_DIM)
    value_grad = jnp.moveaxis(attn_f32[:, :, QROWS + HEAD_DIM : ROUTER_AT], 0, 1).reshape(
        48, HEADS * HEAD_DIM
    )
    keyval_grad = jnp.concatenate([key_grad, value_grad], 1)
    router_grad = jnp.sum(attn_f32[:, :, ROUTER_AT : ROUTER_AT + EXPERTS], 0)
    out_grad_rows = out_own.astype(F32).reshape(48, D)
    gate_up_grad = gate_up_own.astype(F32).reshape(2, 4, 48, 5, 2, TOK)
    gate_up_grad = jnp.transpose(gate_up_grad, (2, 0, 3, 4, 1, 5)).reshape(48, EXPERTS, 2 * FF)
    down_grad = down_own.astype(F32).reshape(2, 4, 48, 5, TOK)
    down_grad = jnp.transpose(down_grad, (2, 0, 3, 1, 4)).reshape(48, EXPERTS, FF)
    first_grad = (
        jnp.sum(query_grad * query_weight.astype(F32), 1) + jnp.sum(keyval_grad * key_value_matrix.astype(F32), 1)
    ) / first_gain.astype(F32)
    second_grad = (
        jnp.sum(gate_up_grad * gate_up_weight.astype(F32), (1, 2))
        + jnp.sum(router_grad * router_weight.astype(F32), 1)
    ) / second_gain.astype(F32)
    return (
        layer_out[None],
        input_grad[None],
        first_grad,
        query_grad,
        keyval_grad,
        out_grad_rows,
        second_grad,
        router_grad,
        gate_up_grad,
        down_grad,
    )


def solution(mesh):
    row = P("shard", None)
    rows = P("shard", None, None)
    own = P("rep", "shard", None)
    in_specs = (own, P("rep", "shard"), own, P("shard"), row, row, row, P("shard"), row, rows, rows, own)
    out_specs = (own, own, P("shard"), row, row, row, P("shard"), row, rows, rows)
    return jax.shard_map(shards, mesh=mesh, in_specs=in_specs, out_specs=out_specs, check_vma=False)
```

```python
import functools

import jax
import jax.numpy as jnp
from jax import lax
from jax.experimental import pallas as pl
from jax.experimental.pallas import tpu as pltpu
from jax.sharding import PartitionSpec as P

D = 1536
HEADS = 8
GROUP = 3
HEAD_DIM = 64
HALF = HEAD_DIM // 2
FF = 512
EXPERTS = 10
TOK = 128
SEQ = 4096
PLANE = 16
RUN = 512
QROWS = GROUP * HEAD_DIM
PACK = 384
ROUTER_AT = 320
GAIN_ONE_AT = 330
GAIN_TWO_AT = 331

NORM_EPS = 1e-06
RESIDUAL_SCALE = 0.22
SCORE_SCALE = 0.015625
ROPE_BASE = 10000.0
MASK_FILL = -1e30
PRECISE = lax.Precision.HIGHEST
BF16 = jnp.bfloat16
F32 = jnp.float32
VMEM_LIMIT = 56 * 1024 * 1024


def my_place():
    return lax.axis_index("shard"), lax.axis_index("rep")


def parts_of(shard):
    place = lax.rem(shard, PLANE)
    return shard // PLANE, place, place // 4, lax.rem(place, 4)


def same(one, other):
    return jnp.logical_and(one[0] == other[0], one[1] == other[1])


class Place:
    def __init__(self, me):
        self.me = me
        self.shard, self.rep = me
        self.z_lo, self.place, self.x, self.y = parts_of(self.shard)
        self.core = lax.rem(self.rep, 2)
        self.z = (self.rep // 2) * 2 + self.z_lo
        self.member = self.z_lo * 4 + self.rep

    def device(self, z, x, y, core):
        return lax.rem(z, 2) * PLANE + 4 * x + y, (z // 2) * 2 + core

    def step(self, axis, by):
        z, x, y = self.z, self.x, self.y
        if axis == "z":
            z = lax.rem(z + by, 4)
        elif axis == "x":
            x = lax.rem(x + by, 4)
        else:
            y = lax.rem(y + by, 4)
        return self.device(z, x, y, self.core)

    def sibling(self):
        return self.shard, self.rep + 1 - 2 * self.core

    def partner(self):
        return self.shard + (1 - 2 * self.z_lo) * PLANE, self.rep

    def trader(self):
        return self.z_lo * PLANE + 4 * mirrored(self.z_lo, self.x) + self.rep, self.y

    def member_at(self, z, core):
        return lax.rem(z, 2) * 4 + (z // 2) * 2 + core

    def near(self):
        result = [self.sibling()]
        for axis in ("z", "x", "y"):
            result += [self.step(axis, 1), self.step(axis, 3)]
        return result


def mesh_id(place):
    return {"shard": place[0], "rep": place[1]}


class Net:
    def __init__(self, here, sems):
        self.here, self.sems, self.used, self.sent = here, sems, 0, []

    def take(self, count=1):
        first = self.used
        self.used += count
        return first

    def push(self, source, target, to):
        number = self.take(2)
        copy = pltpu.make_async_remote_copy(
            src_ref=source,
            dst_ref=target,
            send_sem=self.sems.at[number],
            recv_sem=self.sems.at[number + 1],
            device_id=mesh_id(to),
        )
        copy.start()
        self.sent.append(copy)
        return number + 1

    def got(self, number, region):
        pltpu.make_async_remote_copy(
            src_ref=region,
            dst_ref=region,
            send_sem=self.sems.at[number],
            recv_sem=self.sems.at[number],
            device_id=mesh_id(self.here.sibling()),
        ).wait_recv()

    def local(self, source, target):
        copy = pltpu.make_async_copy(source, target, self.sems.at[self.take()])
        copy.start()
        return copy

    def finish(self):
        for copy in self.sent:
            copy.wait_send()


class Route:
    def __init__(self, n, to, source, pieces, index=None, may_be_self=False):
        self.n, self.to, self.source, self.pieces = n, to, source, pieces
        self.index = index or (lambda i: i)
        self.may_be_self = may_be_self


def each(n, body):
    if n <= 8:
        for i in range(n):
            body(i)
    else:

        def step(i, carry):
            body(i)
            return carry

        lax.fori_loop(0, n, step, 0)


def greet_routes(routes, me, barrier):
    awaited = 0
    for route in routes:

        def greet(i, route=route):
            source = route.source(i)

            def signal():
                pl.semaphore_signal(barrier, inc=1, device_id=mesh_id(source))

            if route.may_be_self:
                pl.when(jnp.logical_not(same(source, me)))(signal)
            else:
                signal()

        each(route.n, greet)
        awaited = awaited + route.n
        if route.may_be_self:
            for i in range(route.n):
                awaited = awaited - same(route.to(i), me).astype(jnp.int32)
    return awaited


HOP = 2.0


def time_of(ref, rate=50.0):
    size = jnp.dtype(ref.dtype).itemsize / 1000.0
    for extent in ref.shape:
        size *= extent
    return HOP + size / rate


def follow_routes(net, routes, ins, outs, guess=15.0):
    me = net.here.me
    held = []
    for route in routes:
        count = route.n * len(route.pieces)
        held.append((net.take(count), net.take(count), net.take(len(route.pieces))))

    def remote(route, base, i, k, piece):
        source_in, cut, target_out, slot, unused = piece
        return pltpu.make_async_remote_copy(
            src_ref=ins[source_in].at[cut(i)],
            dst_ref=outs[target_out].at[slot(i)],
            send_sem=net.sems.at[base[0] + i * len(route.pieces) + k],
            recv_sem=net.sems.at[base[1] + route.index(i) * len(route.pieces) + k],
            device_id=mesh_id(route.to(i)),
        )

    def within(base, i, k, piece):
        source_in, cut, target_out, slot, unused = piece
        return pltpu.make_async_copy(
            ins[source_in].at[cut(i)], outs[target_out].at[slot(i)], net.sems.at[base[2] + k]
        )

    for route, base in zip(routes, held):

        def start(i, route=route, base=base):
            for k, piece in enumerate(route.pieces):
                copy = remote(route, base, i, k, piece)
                if route.may_be_self:
                    here = same(route.to(i), me)
                    pl.when(jnp.logical_not(here))(copy.start)
                    pl.when(here)(within(base, i, k, piece).start)
                else:
                    copy.start()

        each(route.n, start)
    yield guess
    for route, base in zip(routes, held):

        def arrive(i, route=route, base=base):
            for k, piece in enumerate(route.pieces):
                region = outs[piece[2]].at[piece[4](i)]
                place = route.source(i)
                sem = net.sems.at[base[1] + i * len(route.pieces) + k]
                copy = pltpu.make_async_remote_copy(
                    src_ref=region, dst_ref=region, send_sem=sem, recv_sem=sem, device_id=mesh_id(place)
                )
                if route.may_be_self:
                    pl.when(jnp.logical_not(same(place, me)))(copy.wait_recv)
                else:
                    copy.wait_recv()

        each(route.n, arrive)

        def leave(i, route=route, base=base):
            for k, piece in enumerate(route.pieces):
                copy = remote(route, base, i, k, piece)
                if route.may_be_self:
                    here = same(route.to(i), me)
                    pl.when(jnp.logical_not(here))(copy.wait_send)
                    pl.when(here)(within(base, i, k, piece).wait)
                else:
                    copy.wait_send()

        each(route.n, leave)


def trade(net, pieces):
    other = net.here.trader()
    here = same(other, net.here.me)
    copies = []
    for source, target in pieces:
        number = net.take(2)
        remote = pltpu.make_async_remote_copy(
            src_ref=source,
            dst_ref=target,
            send_sem=net.sems.at[number],
            recv_sem=net.sems.at[number + 1],
            device_id=mesh_id(other),
        )
        within = pltpu.make_async_copy(source, target, net.sems.at[net.take()])
        pl.when(jnp.logical_not(here))(remote.start)
        pl.when(here)(within.start)
        copies.append((remote, within))
    yield 30.0
    for remote, within in copies:
        pl.when(jnp.logical_not(here))(remote.wait)
        pl.when(here)(within.wait)


def greet_trader(here, barrier):
    other = here.trader()
    away = jnp.logical_not(same(other, here.me))

    @pl.when(away)
    def signal():
        pl.semaphore_signal(barrier, inc=1, device_id=mesh_id(other))

    return away.astype(jnp.int32)


def spread_rows(net, rows, out):
    here = net.here
    ahead = lax.rem(here.x - here.rep + 4, 4)
    pair = lambda k: out.at[pl.ds(2 * k, 2)]
    row_halves = row_half(48)

    def at(by):
        return out.at[lax.rem(here.y + by, 4)]

    def copy(number, source, target, to):
        return pltpu.make_async_remote_copy(
            src_ref=source,
            dst_ref=target,
            send_sem=net.sems.at[number],
            recv_sem=net.sems.at[number + 1],
            device_id=mesh_id(to),
        )

    def come(number, region):
        copy(number, region, region, here.sibling()).wait_recv()

    up, down, right, left = here.step("y", 1), here.step("y", 3), here.step("x", 1), here.step("x", 3)
    numbers = [net.take(2) for k in range(8)]
    keep = pltpu.make_async_copy(rows, at(0), net.sems.at[net.take()])
    first = [copy(numbers[0], rows, at(0), up), copy(numbers[1], rows, at(0), down)]
    second = [
        copy(numbers[2], row_halves(at(3), 0), row_halves(at(3), 0), up),
        copy(numbers[3], row_halves(at(1), 1), row_halves(at(1), 1), down),
    ]
    third = [copy(numbers[4], out, out, right), copy(numbers[5], out, out, left)]
    on_right = copy(numbers[6], pair(0), pair(0), right)
    on_left = copy(numbers[7], pair(1), pair(1), left)

    @pl.when(ahead == 0)
    def begin():
        keep.start()
        first[0].start()
        first[1].start()

    now = time_of(rows)
    yield now

    @pl.when(ahead == 0)
    def hand_on():
        come(numbers[0], at(3))
        second[0].start()
        come(numbers[1], at(1))
        second[1].start()

    now += time_of(rows, 100.0)
    yield now

    @pl.when(ahead == 0)
    def go_out():
        come(numbers[2], row_halves(at(2), 0))
        come(numbers[3], row_halves(at(2), 1))
        keep.wait()
        third[0].start()
        third[1].start()

    now += time_of(out, 70.0)
    yield now

    @pl.when(ahead == 1)
    def to_right():
        come(numbers[4], out)
        on_right.start()

    @pl.when(ahead == 3)
    def to_left():
        come(numbers[5], out)
        on_left.start()

    now += time_of(out, 140.0)
    yield now

    @pl.when(ahead == 2)
    def end():
        come(numbers[6], pair(0))
        come(numbers[7], pair(1))

    @pl.when(ahead == 0)
    def sent():
        for each_copy in first + second + third:
            each_copy.wait_send()

    pl.when(ahead == 1)(on_right.wait_send)
    pl.when(ahead == 3)(on_left.wait_send)


def comm(inputs, in_vmem, outputs, scratch, n_sems, collective_id, plan):
    n_in, n_out = len(inputs), len(outputs)

    def kernel(*refs):
        ins, outs = refs[:n_in], refs[n_in : n_in + n_out]
        rest, sems = refs[n_in + n_out : -1], refs[-1]
        net = Net(Place(my_place()), sems)
        flows, routes, near, greetings = plan(net, ins, outs, rest)
        barrier = pltpu.get_barrier_semaphore()
        awaited = greet_routes(routes, net.here.me, barrier)
        if near:
            others = net.here.near()
            for other in others:
                pl.semaphore_signal(barrier, inc=1, device_id=mesh_id(other))
            awaited = awaited + len(others)
        for greeting in greetings:
            awaited = awaited + greeting(net.here, barrier)
        pl.semaphore_wait(barrier, awaited)
        waits = [(0.0, number, flow) for number, flow in enumerate(flows)]
        while waits:
            unused, number, flow = waits.pop(0)
            when = next(flow, None)
            if when is not None:
                waits = sorted(waits + [(when, number, flow)], key=lambda wait: wait[:2])
        net.finish()
        assert net.used <= n_sems, net.used

    vmem = pl.BlockSpec(memory_space=pltpu.VMEM)
    anywhere = pl.BlockSpec(memory_space=pl.ANY)
    return pl.pallas_call(
        kernel,
        out_shape=[jax.ShapeDtypeStruct(s, t) for s, t, unused in outputs],
        in_specs=[vmem if k in in_vmem else anywhere for k in range(n_in)],
        out_specs=[vmem if inside else anywhere for unused, unused2, inside in outputs],
        scratch_shapes=list(scratch) + [pltpu.SemaphoreType.DMA((n_sems,))],
        compiler_params=pltpu.CompilerParams(
            collective_id=collective_id, has_side_effects=True, vmem_limit_bytes=VMEM_LIMIT
        ),
    )(*inputs)


def column_gather(net, source, out, half_of):
    here = net.here

    def slot(by, core):
        return out.at[here.member_at(lax.rem(here.z + by, 4), core)]

    core, other = here.core, 1 - here.core
    right, left, sibling = here.step("z", 1), here.step("z", 3), here.sibling()
    keep = net.local(source, slot(0, core))
    a = net.push(source, slot(0, core), right)
    b = net.push(source, slot(0, core), left)
    s = [net.push(source, slot(0, core), sibling)]
    now = time_of(source)
    yield now
    net.got(a, slot(3, core))
    c = net.push(half_of(slot(3, core), 0), half_of(slot(3, core), 0), right)
    s.append(net.push(slot(3, core), slot(3, core), sibling))
    net.got(b, slot(1, core))
    d = net.push(half_of(slot(1, core), 1), half_of(slot(1, core), 1), left)
    s.append(net.push(slot(1, core), slot(1, core), sibling))
    now += time_of(source, 100.0)
    yield now
    net.got(c, half_of(slot(2, core), 0))
    net.got(d, half_of(slot(2, core), 1))
    s.append(net.push(slot(2, core), slot(2, core), sibling))
    yield now + time_of(source, 200.0)
    for number, by in zip(s, (0, 3, 1, 2)):
        net.got(number, slot(by, other))
    keep.wait()


def row_half(size):
    first = (size // 2 + 15) // 16 * 16

    def half(ref, k):
        return ref.at[pl.ds(0, first)] if k == 0 else ref.at[pl.ds(first, size - first)]

    return half


def ring_gather(net, axis, source, slot, half, now, rate):
    right, left = net.here.step(axis, 1), net.here.step(axis, 3)
    a = net.push(source, slot(0), right)
    b = net.push(source, slot(0), left)
    now += time_of(source, rate)
    yield now
    net.got(a, slot(3))
    c = net.push(half(slot(3), 0), half(slot(3), 0), right)
    net.got(b, slot(1))
    d = net.push(half(slot(1), 1), half(slot(1), 1), left)
    now += time_of(source, 2 * rate)
    yield now
    net.got(c, half(slot(2), 0))
    net.got(d, half(slot(2), 1))
    return now


def swap_pair(net, payload, target):
    here = net.here
    number = net.push(payload.at[1 - here.z_lo], target, here.partner())
    yield 12.0
    net.got(number, target)


def plane_gather(net, payload, pair, out, rate=50.0):
    here = net.here
    z, x, y = here.z_lo, here.x, here.y
    rows = row_half(48)
    two = lambda ref, k: ref.at[pl.ds(2 * k, 2)]
    swap = []

    def first():
        if pair is None:
            swap.append(net.push(payload.at[1 - z], out.at[z, x, y], here.partner()))
        keep = net.local(payload.at[z], out.at[z, x, y])
        now = yield from ring_gather(
            net, "x", payload.at[z], lambda by: out.at[z, lax.rem(x + by, 4), y], rows, 0.0, rate
        )
        keep.wait()
        bundle = lambda by: out.at[z, :, lax.rem(y + by, 4)]
        yield from ring_gather(net, "y", bundle(0), bundle, two, now, rate)

    def second():
        w = 1 - z
        now, source = 0.0, pair
        if pair is None:
            now, source = time_of(payload.at[0], rate), out.at[w, x, y]
            yield now
            net.got(swap[0], source)
        else:
            keep = net.local(pair, out.at[w, x, y])
        now = yield from ring_gather(
            net, "y", source, lambda by: out.at[w, x, lax.rem(y + by, 4)], rows, now, rate
        )
        if pair is not None:
            keep.wait()
        bundle = lambda by: out.at[w, lax.rem(x + by, 4)]
        yield from ring_gather(net, "x", bundle(0), bundle, two, now, rate)

    return [first(), second()]


def add(target, *parts):
    total = parts[0][...].astype(F32)
    for part in parts[1:]:
        total = total + part[...].astype(F32)
    target[...] = total.astype(target.dtype)


def ring_sum(net, axis, block, half, halves, wholes, target, now, rate=50.0):
    right, left = net.here.step(axis, 1), net.here.step(axis, 3)
    lower, upper = halves
    a = net.push(half(block(2), 0), lower, right)
    b = net.push(half(block(2), 1), upper, left)
    now += time_of(lower, rate)
    yield now
    net.got(a, lower)
    add(half(block(1), 0), half(block(1), 0), lower)
    c = net.push(block(1), wholes[0], right)
    net.got(b, upper)
    add(half(block(3), 1), half(block(3), 1), upper)
    d = net.push(block(3), wholes[1], left)
    now += time_of(wholes[0], rate)
    yield now
    net.got(c, wholes[0])
    net.got(d, wholes[1])
    add(target, block(0), wholes[0], wholes[1])
    return now


def column_sum(net, parts, out, sums, sibling_parts, halves, wholes):
    here = net.here
    half = row_half(parts.shape[1])
    at = lambda by: lax.rem(here.z + by, 4)
    numbers = {}
    for by in (2, 1, 3, 0):
        numbers[by] = net.push(
            parts.at[here.member_at(at(by), 1 - here.core)], sibling_parts.at[at(by)], here.sibling()
        )
    now = HOP
    for by in (2, 1, 3):
        now += time_of(sums.at[0], 200.0) - HOP
        yield now
        net.got(numbers[by], sibling_parts.at[at(by)])
        add(sums.at[at(by)], parts.at[here.member_at(at(by), here.core)], sibling_parts.at[at(by)])
        if by == 2:
            ring = ring_sum(
                net, "z", lambda by: sums.at[at(by)], half, (halves.at[0], halves.at[1]),
                (wholes.at[0], wholes.at[1]), out, now,
            )
            when = next(ring)
    net.got(numbers[0], sibling_parts.at[at(0)])
    add(sums.at[at(0)], parts.at[here.member_at(at(0), here.core)], sibling_parts.at[at(0)])
    yield when
    yield from ring


def column_sum_scratch(rows, columns):
    return [
        pltpu.VMEM((4, rows, columns), BF16),
        pltpu.VMEM((4, rows, columns), BF16),
        pltpu.VMEM((2, rows // 2, columns), BF16),
        pltpu.VMEM((2, rows, columns), BF16),
    ]


def plane_sum(net, parts, out, held, pairs, bundles, rows_a, rows_b, blocks, rate=50.0):
    here = net.here
    at_x = lambda by: lax.rem(here.x + by, 4)
    at_y = lambda by: lax.rem(here.y + by, 4)
    pair = lambda ref, k: ref.at[pl.ds(2 * k, 2)]
    half = row_half(48)

    def first():
        copy = net.local(parts.at[0], held.at[0])
        yield 2.0
        copy.wait()
        mine = held.at[0, :, here.y]
        now = yield from ring_sum(
            net, "y", lambda by: held.at[0, :, at_y(by)], pair, (pairs.at[0], pairs.at[1]),
            (bundles.at[0], bundles.at[1]), mine, 2.0, rate,
        )
        yield from ring_sum(
            net, "x", lambda by: held.at[0, at_x(by), here.y], half, (rows_a.at[0], rows_b.at[0]),
            (blocks.at[0], blocks.at[1]), out.at[0], now, rate,
        )

    def second():
        copy = net.local(parts.at[1], held.at[1])
        yield 2.0
        copy.wait()
        mine = held.at[1, here.x]
        now = yield from ring_sum(
            net, "x", lambda by: held.at[1, at_x(by)], pair, (pairs.at[2], pairs.at[3]),
            (bundles.at[2], bundles.at[3]), mine, 2.0, rate,
        )
        yield from ring_sum(
            net, "y", lambda by: held.at[1, here.x, at_y(by)], half, (rows_a.at[1], rows_b.at[1]),
            (blocks.at[2], blocks.at[3]), out.at[1], now, rate,
        )

    return [first(), second()]


def plane_sum_scratch(columns):
    return [
        pltpu.VMEM((2, 4, 4, 48, columns), BF16),
        pltpu.VMEM((4, 2, 48, columns), BF16),
        pltpu.VMEM((4, 4, 48, columns), BF16),
        pltpu.VMEM((2, 32, columns), BF16),
        pltpu.VMEM((2, 16, columns), BF16),
        pltpu.VMEM((4, 48, columns), BF16),
    ]


def column_deal(net, parts, out, passing, half):
    here = net.here
    z = here.z_lo
    core, other = here.core, 1 - here.core
    lower, upper = passing

    def slot(by, core):
        return out.at[here.member_at(lax.rem(here.z + by, 4), core)]

    right, left, sibling = here.step("z", 1), here.step("z", 3), here.sibling()
    keep = net.local(parts.at[z], slot(0, core))
    e = net.push(half(parts.at[z], 0), lower, right)
    f = net.push(half(parts.at[z], 1), upper, left)
    a = net.push(parts.at[1 - z], slot(0, core), right)
    b = net.push(parts.at[1 - z], slot(0, core), left)
    s = [net.push(parts.at[z], slot(0, core), sibling)]
    now = time_of(parts.at[0])
    yield now
    net.got(e, lower)
    c = net.push(lower, half(slot(3, core), 0), right)
    net.got(f, upper)
    d = net.push(upper, half(slot(1, core), 1), left)
    net.got(a, slot(3, core))
    s.append(net.push(slot(3, core), slot(3, core), sibling))
    net.got(b, slot(1, core))
    s.append(net.push(slot(1, core), slot(1, core), sibling))
    now += time_of(parts.at[0])
    yield now
    net.got(c, half(slot(2, core), 0))
    net.got(d, half(slot(2, core), 1))
    s.append(net.push(slot(2, core), slot(2, core), sibling))
    yield now + HOP
    for number, by in zip(s, (0, 3, 1, 2)):
        net.got(number, slot(by, other))
    keep.wait()


def column_route(me, pieces):
    z, place, unused, unused2 = parts_of(me[0])
    mine = z * 4 + me[1]

    def where(member):
        return (member // 4) * PLANE + place, lax.rem(member, 4)

    def after(i):
        return lax.rem(mine + 1 + i, 8)

    def before(i):
        return lax.rem(mine + 7 - i, 8)

    return Route(
        7,
        lambda i: where(after(i)),
        lambda i: where(before(i)),
        [
            (
                a,
                lambda i, cut=cut: cut(after(i)),
                b,
                lambda i, slot=slot: slot(mine),
                lambda i, slot=slot: slot(before(i)),
            )
            for a, cut, b, slot in pieces
        ],
    )


def plane_route(me, pieces):
    z, place, unused, unused2 = parts_of(me[0])

    def after(i):
        return lax.rem(place + 1 + i, PLANE)

    def before(i):
        return lax.rem(place + 15 - i, PLANE)

    return Route(
        15,
        lambda i: (z * PLANE + after(i), me[1]),
        lambda i: (z * PLANE + before(i), me[1]),
        [
            (
                a,
                lambda i, cut=cut: cut(after(i)),
                b,
                lambda i, slot=slot: slot(place),
                lambda i, slot=slot: slot(before(i)),
            )
            for a, cut, b, slot in pieces
        ],
    )


def own_copies(net, ins, outs, copies):
    started = [net.local(ins[a].at[cut], outs[b].at[slot]) for a, cut, b, slot in copies]
    yield 100.0
    for copy in started:
        copy.wait()


ROW_HALF = row_half(TOK)


def mirrored(z, x):
    return x + z * (3 - 2 * x)


def query_routes(me, q_in, q_out):
    z_me, place, x, y = parts_of(me[0])
    base = z_me * PLANE

    def plain(i):
        return lax.rem(y + 1 + i, 4)

    def plain_before(i):
        return lax.rem(y + 3 - i, 4)

    def other(i):
        return lax.rem(y + i, 4)

    def other_before(i):
        return lax.rem(y + 4 - i, 4)

    first = Route(
        3,
        lambda i: (base + 4 * x + plain(i), me[1]),
        lambda i: (base + 4 * x + plain_before(i), me[1]),
        [(q_in, lambda i: (0, plain(i)), q_out, lambda i: (0, y), lambda i: (0, plain_before(i)))],
    )
    second = Route(
        4,
        lambda i: (base + 4 * (3 - x) + other(i), me[1]),
        lambda i: (base + 4 * (3 - x) + other_before(i), me[1]),
        [(q_in, lambda i: (1, other(i)), q_out, lambda i: (1, y), lambda i: (1, other_before(i)))],
    )
    return [first, second], [(q_in, (0, y), q_out, (0, y))]


def gather_start(x, segments, attn, out_rows, choices, dy):
    def plan(net, ins, outs, scratch):
        flows = plane_gather(net, ins[2], None, outs[2])
        flows += [
            spread_rows(net, ins[3], outs[3]),
            column_gather(net, ins[0], outs[0], ROW_HALF),
            column_gather(net, ins[1], outs[1], lambda ref, k: ref.at[pl.ds(8 * k, 8)]),
            trade(net, [(ins[4], outs[4]), (ins[5], outs[5])]),
        ]
        return flows, [], True, [greet_trader]

    return comm(
        [x, segments, attn, out_rows, choices, dy],
        (),
        [
            ((8, TOK, D), BF16, False),
            ((8, 16, TOK), jnp.int32, False),
            ((2, 4, 4, 48, PACK), BF16, False),
            ((4, 48, D), BF16, False),
            ((16, TOK), jnp.int32, False),
            ((TOK, D), BF16, False),
        ],
        [],
        112,
        0,
        plan,
    )


def to_attention(q, kv, ints, x, gate_up, down):
    def plan(net, ins, outs, scratch):
        me = net.here.me
        z_me, place, x, y = parts_of(me[0])
        routes, own = query_routes(me, 0, 0)
        routes = [
            plane_route(
                me,
                [
                    (1, lambda p: (0, lax.rem(p, 4)), 1, lambda p: (0, p)),
                    (1, lambda p: (1, lax.rem(p, 4)), 1, lambda p: (1, p)),
                    (2, lambda p: lax.rem(p, 4), 2, lambda p: p),
                ],
            )
        ] + routes
        own = own + [
            (1, (0, y), 1, (0, place)),
            (1, (1, y), 1, (1, place)),
            (2, y, 2, place),
        ]
        flows = [
            follow_routes(net, routes, ins, outs, 20.0),
            own_copies(net, ins, outs, own),
            trade(net, [(ins[3], outs[3])]),
            swap_pair(net, ins[4], outs[4]),
            swap_pair(net, ins[5], outs[5]),
        ]
        return flows, routes, True, [greet_trader]

    return comm(
        [q, kv, ints, x, gate_up, down],
        (),
        [
            ((2, 4, QROWS, TOK), BF16, False),
            ((2, PLANE, TOK, TOK), BF16, False),
            ((PLANE, 8, TOK), jnp.int32, False),
            ((TOK, D), BF16, False),
            ((48, 1280), BF16, False),
            ((48, 640), BF16, False),
        ],
        [],
        144,
        1,
        plan,
    )


def sum_attended(parts, gate_up, pair, dy, choices):
    def plan(net, ins, outs, scratch):
        flows = plane_gather(net, ins[1], ins[2], outs[1])
        flows += [
            column_sum(net, ins[0], outs[0], *scratch),
            column_gather(net, ins[3], outs[2], ROW_HALF),
            column_gather(net, ins[4], outs[3], lambda ref, k: ref.at[pl.ds(8 * k, 8)]),
        ]
        return flows, [], True, []

    total, gate_up_all, dy_all, choices_all = comm(
        [parts, gate_up, pair, dy, choices],
        (0,),
        [
            ((TOK, D), F32, True),
            ((2, 4, 4, 48, 1280), BF16, False),
            ((8, TOK, D), BF16, False),
            ((8, 16, TOK), jnp.int32, False),
        ],
        column_sum_scratch(TOK, D),
        160,
        2,
        plan,
    )
    return total, gate_up_all.reshape(D, 1280), dy_all, choices_all


def gather_normed(normed, down, pair):
    def plan(net, ins, outs, scratch):
        flows = [column_gather(net, ins[0], outs[0], ROW_HALF)]
        flows += plane_gather(net, ins[1], ins[2], outs[1])
        return flows, [], True, []

    normed_all, down_all = comm(
        [normed, down, pair],
        (),
        [((8, TOK, D), BF16, False), ((2, 4, 4, 48, 640), BF16, False)],
        [],
        64,
        3,
        plan,
    )
    return normed_all.reshape(8 * TOK, D), down_all.reshape(D, 640)


def sum_experts(normed, share, gate_up):
    def plan(net, ins, outs, scratch):
        me = net.here.me
        mine = net.here.member
        routes = [column_route(me, [(1, lambda m: m, 1, lambda m: m)])]
        flows = [
            column_sum(net, ins[0], outs[0], *scratch[:4]),
            follow_routes(net, routes, ins, outs, 10.0),
            own_copies(net, ins, outs, [(1, mine, 1, mine)]),
        ]
        flows += plane_sum(net, ins[2], outs[2], *scratch[4:])
        return flows, routes, True, []

    return comm(
        [normed, share, gate_up],
        (0,),
        [((TOK, D), F32, True), ((8, 8, TOK), F32, False), ((2, 48, 1280), BF16, True)],
        column_sum_scratch(TOK, D) + plane_sum_scratch(1280),
        96,
        4,
        plan,
    )


def gather_grad(grad_lin, down):
    def plan(net, ins, outs, scratch):
        flows = [column_gather(net, ins[0], outs[0], ROW_HALF)]
        flows += plane_sum(net, ins[1], outs[1], *scratch)
        return flows, [], True, []

    return comm(
        [grad_lin, down],
        (),
        [((8, TOK, D), BF16, False), ((2, 48, 640), BF16, True)],
        plane_sum_scratch(640),
        64,
        5,
        plan,
    )


def from_attention(q, kv, mixture, grad):
    def plan(net, ins, outs, scratch):
        me = net.here.me
        z_me, place, x, y = parts_of(me[0])
        routes, own = query_routes(me, 0, 0)
        routes = [plane_route(me, [(1, lambda p: (slice(None), p), 1, lambda p: p)])] + routes
        own = own + [(1, (slice(None), place), 1, place)]
        flows = [
            follow_routes(net, routes, ins, outs, 25.0),
            own_copies(net, ins, outs, own),
            column_sum(net, ins[2], outs[2], *scratch),
            trade(net, [(ins[3], outs[3])]),
        ]
        return flows, routes, True, [greet_trader]

    return comm(
        [q, kv, mixture, grad],
        (2,),
        [
            ((2, 4, QROWS, TOK), BF16, False),
            ((PLANE, 2, TOK, TOK), BF16, False),
            ((TOK, D), F32, True),
            ((TOK, D), BF16, False),
        ],
        column_sum_scratch(TOK, D),
        128,
        6,
        plan,
    )


def sum_planes(attn, out_rows, normed):
    def plan(net, ins, outs, scratch):
        me = net.here.me
        place = net.here.place
        routes = [plane_route(me, [(1, lambda p: p, 1, lambda p: p)])]
        flows = [column_sum(net, ins[2], outs[2], *scratch[6:])]
        flows += plane_sum(net, ins[0], outs[0], *scratch[:6])
        flows += [
            follow_routes(net, routes, ins, outs, 20.0),
            own_copies(net, ins, outs, [(1, place, 1, place)]),
        ]
        return flows, routes, True, []

    return comm(
        [attn, out_rows, normed],
        (2,),
        [
            ((2, 48, PACK), BF16, True),
            ((PLANE, 12, D), BF16, False),
            ((TOK, D), F32, True),
        ],
        plane_sum_scratch(PACK) + column_sum_scratch(TOK, D),
        128,
        7,
        plan,
    )


def final_deal(attn, gate_up, down, out_rows, layer_out):
    def plan(net, ins, outs, scratch):
        me = net.here.me
        place, mine = net.here.place, net.here.member
        routes = [
            Route(
                4,
                lambda i: (4 * mine + place // 4, i),
                lambda i: (
                    (me[0] // 4) // 4 * PLANE + 4 * lax.rem(me[0], 4) + i,
                    lax.rem(me[0] // 4, 4),
                ),
                [(3, lambda i: slice(None), 3, lambda i: lax.rem(place, 4), lambda i: i)],
                index=lambda i: lax.rem(place, 4),
                may_be_self=True,
            ),
        ]
        half = row_half(48)
        flows = [follow_routes(net, routes, ins, outs, 15.0)]
        for k in range(3):
            flows.append(column_deal(net, ins[k], outs[k], scratch[2 * k : 2 * k + 2], half))
        flows.append(trade(net, [(ins[4], outs[4])]))
        return flows, routes, True, [greet_trader]

    widths = (PACK, 1280, 640)
    scratch = []
    for width in widths:
        scratch += [pltpu.VMEM((32, width), BF16), pltpu.VMEM((16, width), BF16)]
    return comm(
        [attn, gate_up, down, out_rows, layer_out],
        (),
        [((8, 48, width), BF16, False) for width in widths]
        + [((4, 12, D), BF16, False), ((TOK, D), BF16, False)],
        scratch,
        96,
        8,
        plan,
    )


def assemble_kernel(
    attn, gate_up, down, out_rows, query_weight, keyval_weight, router_weight, gate_up_weight, gains,
    query_grad, keyval_grad, out_grad, router_grad, gate_up_grad, down_grad, gain_grads,
):
    parts = [attn[m].astype(F32) for m in range(HEADS)]
    query = jnp.concatenate([part[:, :QROWS] for part in parts], 1)
    key = jnp.concatenate([part[:, QROWS : QROWS + HEAD_DIM] for part in parts], 1)
    value = jnp.concatenate([part[:, QROWS + HEAD_DIM : ROUTER_AT] for part in parts], 1)
    query_grad[...] = query
    keyval_grad[:, : HEADS * HEAD_DIM] = key
    keyval_grad[:, HEADS * HEAD_DIM :] = value
    router = parts[0]
    for part in parts[1:]:
        router = router + part
    router = router[:, ROUTER_AT : ROUTER_AT + EXPERTS]
    router_grad[...] = router
    for k in range(4):
        out_grad[12 * k : 12 * k + 12, :] = out_rows[k].astype(F32)
    first = jnp.sum(query * query_weight[...].astype(F32), 1, keepdims=True)
    half = HEADS * HEAD_DIM
    first = first + jnp.sum(key * keyval_weight[:, :half].astype(F32), 1, keepdims=True)
    first = first + jnp.sum(value * keyval_weight[:, half:].astype(F32), 1, keepdims=True)
    second = jnp.sum(router * router_weight[...].astype(F32), 1, keepdims=True)
    for expert in range(EXPERTS):
        z, local = expert // 5, expert % 5
        rows = []
        for side in range(2):
            at = local * 256 + side * TOK
            rows += [gate_up[4 * z + q, :, at : at + TOK].astype(F32) for q in range(4)]
        whole = jnp.concatenate(rows, 1)
        gate_up_grad[:, expert, :] = whole
        second = second + jnp.sum(whole * gate_up_weight[:, expert, :].astype(F32), 1, keepdims=True)
        down_grad[:, expert, :] = jnp.concatenate(
            [down[4 * z + q, :, local * TOK : (local + 1) * TOK].astype(F32) for q in range(4)], 1
        )
    gain_grads[:, 0:1] = first / gains[:, 0:1]
    gain_grads[:, 1:2] = second / gains[:, 1:2]


def assemble(attn, gate_up, down, out_rows, query_weight, keyval_weight, router_weight, gate_up_weight, gains):
    vmem = pl.BlockSpec(memory_space=pltpu.VMEM)
    shapes = [(48, D), (48, 1024), (48, D), (48, EXPERTS), (48, EXPERTS, 2 * FF), (48, EXPERTS, FF), (48, 2)]
    return pl.pallas_call(
        assemble_kernel,
        out_shape=[jax.ShapeDtypeStruct(shape, F32) for shape in shapes],
        in_specs=[vmem] * 9,
        out_specs=[vmem] * len(shapes),
        compiler_params=pltpu.CompilerParams(vmem_limit_bytes=VMEM_LIMIT),
    )(attn, gate_up, down, out_rows, query_weight, keyval_weight, router_weight, gate_up_weight, gains)


def unpack_queries(source, target):
    for run in range(2):
        for part in range(4):
            target[:, run * RUN + part * TOK : run * RUN + (part + 1) * TOK] = source[run, part]


def unpack_keys(kv_ref, key_rows, value_lines):
    def step(j, carry):
        place = pl.ds(pl.multiple_of(j * TOK, TOK), TOK)
        block = kv_ref[j // PLANE, lax.rem(j, PLANE)]
        key_rows[place, :] = block[:HEAD_DIM].astype(F32).T.astype(BF16)
        value_lines[:, place] = block[HEAD_DIM:]
        return carry

    lax.fori_loop(0, SEQ // TOK, step, 0)


def visible_block(block, start, query):
    key = block * RUN + lax.broadcasted_iota(jnp.int32, (RUN, RUN), 0)
    return jnp.logical_and(key >= start, key <= query)


def attend_kernel(bounds, q_ref, kv_ref, start_ref, o_ref, low_ref, lse_ref, queries, key_rows, value_lines):
    unpack_queries(q_ref, queries)
    unpack_keys(kv_ref, key_rows, value_lines)
    for run in range(2):
        cols = slice(run * RUN, (run + 1) * RUN)
        start = start_ref[0:1, cols]
        query = bounds[4 + run] + lax.broadcasted_iota(jnp.int32, (1, RUN), 1)
        heads = [
            queries[h * HEAD_DIM : (h + 1) * HEAD_DIM, cols] * jnp.asarray(SCORE_SCALE, BF16)
            for h in range(GROUP)
        ]

        def step(block, carry):
            place = pl.ds(pl.multiple_of(block * RUN, RUN), RUN)
            keys, values = key_rows[place, :], value_lines[:, place]
            seen = visible_block(block, start, query)
            result = []
            for h in range(GROUP):
                peak, total, acc = carry[3 * h : 3 * h + 3]
                scores = jnp.dot(keys, heads[h], preferred_element_type=F32)
                scores = jnp.where(seen, scores, MASK_FILL)
                top = jnp.maximum(peak, jnp.max(scores, 0, keepdims=True))
                weights = jnp.exp(scores - top)
                fade = jnp.exp(peak - top)
                total = fade * total + jnp.sum(weights, 0, keepdims=True)
                acc = fade * acc + jnp.dot(values, weights.astype(BF16), preferred_element_type=F32)
                result += [top, total, acc]
            return tuple(result)

        zero = []
        for h in range(GROUP):
            zero += [
                jnp.full((1, RUN), MASK_FILL, F32),
                jnp.zeros((1, RUN), F32),
                jnp.zeros((HEAD_DIM, RUN), F32),
            ]
        done = lax.fori_loop(bounds[run], bounds[2 + run], step, tuple(zero))
        for h in range(GROUP):
            peak, total, acc = done[3 * h : 3 * h + 3]
            rows = slice(h * HEAD_DIM, (h + 1) * HEAD_DIM)
            attended = acc / total
            o_ref[rows, cols] = attended
            low_ref[rows, cols] = attended.astype(BF16)
            lse_ref[h : h + 1, cols] = peak + jnp.log(total)


def attend(bounds, q, kv, start):
    vmem = pl.BlockSpec(memory_space=pltpu.VMEM)
    return pl.pallas_call(
        attend_kernel,
        out_shape=[
            jax.ShapeDtypeStruct((QROWS, 2 * RUN), F32),
            jax.ShapeDtypeStruct((QROWS, 2 * RUN), BF16),
            jax.ShapeDtypeStruct((8, 2 * RUN), F32),
        ],
        in_specs=[pl.BlockSpec(memory_space=pltpu.SMEM), vmem, vmem, vmem],
        out_specs=[vmem, vmem, vmem],
        scratch_shapes=[
            pltpu.VMEM((QROWS, 2 * RUN), BF16),
            pltpu.VMEM((SEQ, HEAD_DIM), BF16),
            pltpu.VMEM((HEAD_DIM, SEQ), BF16),
        ],
        compiler_params=pltpu.CompilerParams(vmem_limit_bytes=VMEM_LIMIT),
    )(bounds, q, kv, start)


NT = (((1,), (1,)), ((), ()))


def attend_back_kernel(
    bounds, q_ref, kv_ref, grads, start_ref, o_ref, lse_ref, dq_ref, dkv_ref,
    queries, key_rows, value_rows, key_lines, key_grad, value_grad,
):
    unpack_queries(q_ref, queries)
    key_grad[...] = jnp.zeros_like(key_grad)
    value_grad[...] = jnp.zeros_like(value_grad)

    def spread(j, carry):
        place = pl.ds(pl.multiple_of(j * TOK, TOK), TOK)
        block = kv_ref[j // PLANE, lax.rem(j, PLANE)]
        turned = block.astype(F32).T.astype(BF16)
        key_rows[place, :] = turned[:, :HEAD_DIM]
        value_rows[place, :] = turned[:, HEAD_DIM:]
        key_lines[:, place] = block[:HEAD_DIM]
        return carry

    lax.fori_loop(0, SEQ // TOK, spread, 0)
    for run in range(2):
        cols = slice(run * RUN, (run + 1) * RUN)
        start = start_ref[0:1, cols]
        query = bounds[4 + run] + lax.broadcasted_iota(jnp.int32, (1, RUN), 1)
        lse = [lse_ref[h : h + 1, cols] for h in range(GROUP)]
        delta = []
        for h in range(GROUP):
            rows = slice(h * HEAD_DIM, (h + 1) * HEAD_DIM)
            delta.append(jnp.sum(grads[rows, cols].astype(F32) * o_ref[rows, cols], 0, keepdims=True))

        def step(block, carry):
            place = pl.ds(pl.multiple_of(block * RUN, RUN), RUN)
            keys, values, lines = key_rows[place, :], value_rows[place, :], key_lines[:, place]
            seen = visible_block(block, start, query)
            result = []
            dk = key_grad[place, :]
            dv = value_grad[place, :]
            for h in range(GROUP):
                rows = slice(h * HEAD_DIM, (h + 1) * HEAD_DIM)
                q = queries[rows, cols] * jnp.asarray(SCORE_SCALE, BF16)
                do = grads[rows, cols]
                scores = jnp.dot(keys, q, preferred_element_type=F32)
                weights = jnp.exp(jnp.where(seen, scores, MASK_FILL) - lse[h])
                pull = jnp.dot(values, do, preferred_element_type=F32)
                ds = (weights * (pull - delta[h])).astype(BF16)
                dv = dv + lax.dot_general(weights.astype(BF16), do, NT, preferred_element_type=F32)
                dk = dk + lax.dot_general(ds, q, NT, preferred_element_type=F32)
                result.append(carry[h] + jnp.dot(lines, ds, preferred_element_type=F32))
            key_grad[place, :] = dk
            value_grad[place, :] = dv
            return tuple(result)

        done = lax.fori_loop(
            bounds[run], bounds[2 + run], step, tuple(jnp.zeros((HEAD_DIM, RUN), F32) for h in range(GROUP))
        )
        for h in range(GROUP):
            rows = slice(h * HEAD_DIM, (h + 1) * HEAD_DIM)
            scaled = SCORE_SCALE * done[h]
            for part in range(4):
                dq_ref[run, part, rows, :] = scaled[:, part * TOK : (part + 1) * TOK].astype(BF16)

    def gather(j, carry):
        place = pl.ds(pl.multiple_of(j * TOK, TOK), TOK)
        dkv_ref[j // PLANE, lax.rem(j, PLANE), :HEAD_DIM, :] = key_grad[place, :].T.astype(BF16)
        dkv_ref[j // PLANE, lax.rem(j, PLANE), HEAD_DIM:, :] = value_grad[place, :].T.astype(BF16)
        return carry

    lax.fori_loop(0, SEQ // TOK, gather, 0)


def attend_back(bounds, q, kv, do, start, o, lse):
    vmem = pl.BlockSpec(memory_space=pltpu.VMEM)
    return pl.pallas_call(
        attend_back_kernel,
        out_shape=[
            jax.ShapeDtypeStruct((2, 4, QROWS, TOK), BF16),
            jax.ShapeDtypeStruct((2, PLANE, TOK, TOK), BF16),
        ],
        in_specs=[pl.BlockSpec(memory_space=pltpu.SMEM)] + [vmem] * 6,
        out_specs=[vmem, vmem],
        scratch_shapes=[
            pltpu.VMEM((QROWS, 2 * RUN), BF16),
            pltpu.VMEM((SEQ, HEAD_DIM), BF16),
            pltpu.VMEM((SEQ, HEAD_DIM), BF16),
            pltpu.VMEM((HEAD_DIM, SEQ), BF16),
            pltpu.VMEM((SEQ, HEAD_DIM), F32),
            pltpu.VMEM((SEQ, HEAD_DIM), F32),
        ],
        compiler_params=pltpu.CompilerParams(vmem_limit_bytes=VMEM_LIMIT),
    )(bounds, q, kv, do, start, o, lse)


def rms_scale(values):
    return lax.rsqrt(jnp.mean(values * values, -1, keepdims=True) + NORM_EPS)


def norm_back(grad_normed, values, scale_factor, gain_values):
    weighted = grad_normed * gain_values
    return scale_factor * weighted - values * scale_factor**3 * jnp.mean(
        weighted * values, -1, keepdims=True
    )


def turn(values, cosine, sine):
    front, behind = values[..., :HALF, :], values[..., HALF:, :]
    return jnp.concatenate([front * cosine - behind * sine, behind * cosine + front * sine], -2)


def shards(
    layer_input,
    segments,
    choices,
    first_gain,
    query_weight,
    key_value_matrix,
    output_weight,
    second_gain,
    router_weight,
    gate_up_weight,
    down_weight,
    cotangent,
):
    shard, rep = my_place()
    z, place, x, y = parts_of(shard)
    dot = functools.partial(lax.dot_general, preferred_element_type=F32)

    pad = jnp.zeros((8, TOK), jnp.int32)
    choices_lines = jnp.concatenate([choices[0].T, pad], 0)
    segment_lines = jnp.concatenate([segments, pad, pad[:7]], 0)
    gate_up_mine = lax.dynamic_index_in_dim(
        gate_up_weight.reshape(48, 2, 5, 2, 4, TOK), rep, 4, keepdims=False
    )
    gate_up_mine = jnp.moveaxis(gate_up_mine, 1, 0).reshape(2, 48, 1280)
    down_mine = lax.dynamic_index_in_dim(down_weight.reshape(48, 2, 5, 4, TOK), rep, 3, keepdims=False)
    down_mine = jnp.moveaxis(down_mine, 1, 0).reshape(2, 48, 640)
    query_mine = lax.dynamic_index_in_dim(query_weight.reshape(48, 2, 4, QROWS), rep, 2, keepdims=False)
    keyval_mine = lax.dynamic_index_in_dim(
        key_value_matrix.reshape(48, 2, 2, 4, HEAD_DIM), rep, 3, keepdims=False
    )
    small = jnp.concatenate(
        [router_weight, first_gain[:, None], second_gain[:, None], jnp.zeros((48, PACK - 332), BF16)], 1
    )
    attn_mine = jnp.stack(
        [
            jnp.concatenate([query_mine[:, k], keyval_mine[:, 0, k], keyval_mine[:, 1, k], small], 1)
            for k in range(2)
        ]
    )
    x_all, segment_members, attn, out_slice, choices_traded, dy_traded = gather_start(
        layer_input[0], segment_lines, attn_mine, output_weight, choices_lines, cotangent[0]
    )
    attn = attn.reshape(D, PACK)
    out_slice = out_slice.reshape(QROWS, D)

    gain_one = attn[:, GAIN_ONE_AT].astype(F32)
    gain_two = attn[:, GAIN_TWO_AT].astype(F32)
    router = attn[:, ROUTER_AT : ROUTER_AT + EXPERTS]
    tokens_all = x_all.reshape(8 * TOK, D).astype(F32)
    normed = (tokens_all * rms_scale(tokens_all) * gain_one).astype(BF16)

    frequency = ROPE_BASE ** (-jnp.arange(0, HEAD_DIM, 2, dtype=F32) / HEAD_DIM)
    column_place = (
        (jnp.arange(2, dtype=jnp.int32)[:, None] * PLANE + place) * TOK
        + jnp.arange(TOK, dtype=jnp.int32)[None, :]
    )
    angle = column_place.astype(F32)[:, None, :] * frequency[None, :, None]
    cosine = jnp.cos(angle)[:, None, None]
    sine = jnp.sin(angle)[:, None, None]
    linear = dot(attn[:, : QROWS + 2 * HEAD_DIM], normed, (((0,), (1,)), ((), ())))
    linear = jnp.moveaxis(linear.reshape(QROWS + 2 * HEAD_DIM, 2, 4, TOK), 0, 2)
    turned = turn(linear[:, :, : QROWS + HEAD_DIM].reshape(2, 4, 4, HEAD_DIM, TOK), cosine, sine)
    query_lines = turned[:, :, :GROUP].reshape(2, 4, QROWS, TOK).astype(BF16)
    keyval_lines = jnp.concatenate([turned[:, :, GROUP], linear[:, :, QROWS + HEAD_DIM :]], 2).astype(BF16)
    segment_column = jnp.moveaxis(segment_members[:, 0].reshape(2, 4, TOK), 0, 1)
    segment_column = jnp.concatenate([segment_column, jnp.zeros((4, 6, TOK), jnp.int32)], 1)
    q_here, kv_here, segment_here, x_traded, gate_up_pair, down_pair = to_attention(
        query_lines, keyval_lines, segment_column, layer_input[0], gate_up_mine, down_mine
    )

    segment_all = jnp.moveaxis(segment_here[:, :2], 1, 0).reshape(SEQ)
    earlier = jnp.sum(segment_all[None, :] < jnp.arange(5, dtype=jnp.int32)[:, None], 1, dtype=jnp.int32)
    runs = jnp.stack([x, 7 - x])
    mark = jnp.concatenate(
        [lax.dynamic_slice_in_dim(segment_all, runs[k] * RUN, RUN) for k in range(2)]
    )
    start = jnp.sum(
        jnp.where(mark[None, :] == jnp.arange(5, dtype=jnp.int32)[:, None], earlier[:, None], 0), 0
    )
    first_block = jnp.min(start.reshape(2, RUN), 1) // RUN
    bounds = jnp.concatenate([first_block, runs + 1, runs * RUN, jnp.zeros((2,), jnp.int32)])
    start_lines = jnp.broadcast_to(start[None, :], (8, 2 * RUN))
    o_here, o_low, lse = attend(bounds, q_here, kv_here, start_lines)
    attended_part = dot(o_low, out_slice, (((0,), (0,)), ((), ()))).astype(BF16)
    attended, gate_up, dy_all, choices_all = sum_attended(
        attended_part.reshape(8, TOK, D), gate_up_mine, gate_up_pair, dy_traded, choices_traded
    )

    tokens = x_traded.astype(F32)
    out_grad = dy_traded.astype(F32)
    residual = tokens + RESIDUAL_SCALE * attended
    scale_two = rms_scale(residual)
    normed_two = (residual * scale_two * gain_two).astype(BF16)
    normed_two_all, down = gather_normed(normed_two, down_mine, down_pair)

    dy_rows = dy_all.reshape(8 * TOK, D)
    chosen = jnp.any(
        choices_all[:, :8, :, None] == jnp.arange(EXPERTS, dtype=jnp.int32), 1
    ).reshape(8 * TOK, EXPERTS)
    logits = jnp.where(chosen, dot(normed_two_all, router, (((1,), (0,)), ((), ()))), MASK_FILL)
    exponent = jnp.where(chosen, jnp.exp(logits - jnp.max(logits, -1, keepdims=True)), 0.0)
    shares = exponent / jnp.sum(exponent, -1, keepdims=True)
    share = lax.dynamic_slice_in_dim(shares, z * 5, 5, 1)[:, :, None]
    joined = dot(normed_two_all, gate_up, (((1,), (0,)), ((), ()))).reshape(8 * TOK, 5, 2, TOK)
    gate, up = joined[:, :, 0], joined[:, :, 1]
    sigmoid = 1.0 / (1.0 + jnp.exp(-gate))
    silu = gate * sigmoid
    hidden = (silu * up).astype(BF16).astype(F32)
    shared_hidden = (share * hidden).astype(BF16).reshape(8 * TOK, 640)
    mixture_part = dot(shared_hidden, down, (((1,), (1,)), ((), ()))).astype(BF16)
    pulled = RESIDUAL_SCALE * dot(dy_rows, down, (((1,), (0,)), ((), ()))).reshape(8 * TOK, 5, TOK)
    grad_share = jnp.sum(hidden * pulled, -1)
    grad_hidden = share * pulled
    grad_gate = grad_hidden * up * (sigmoid + silu * (1.0 - sigmoid))
    grad_up = grad_hidden * silu
    grad_joined = jnp.stack([grad_gate, grad_up], 2).astype(BF16).reshape(8 * TOK, 1280)
    grad_normed_part = dot(grad_joined, gate_up, (((1,), (1,)), ((), ()))).astype(BF16)
    share_lines = jnp.pad(jnp.moveaxis(grad_share.reshape(8, TOK, 5), 2, 1), ((0, 0), (0, 3), (0, 0)))
    grad_gate_up = dot(normed_two_all, grad_joined, (((0,), (0,)), ((), ()))).astype(BF16)
    grad_down = (RESIDUAL_SCALE * dot(dy_rows, shared_hidden, (((0,), (0,)), ((), ())))).astype(BF16)

    normed_sum, share_parts, gate_up_sum = sum_experts(
        grad_normed_part.reshape(8, TOK, D), share_lines, grad_gate_up.reshape(2, 4, 4, 48, 1280)
    )

    mine = z * 4 + rep
    own_shares = lax.dynamic_index_in_dim(shares.reshape(8, TOK, EXPERTS), mine, 0, keepdims=False)
    grad_gates = jnp.sum(share_parts.reshape(2, 4, 8, TOK), 1)[:, :5].reshape(EXPERTS, TOK).T
    grad_logits = own_shares * (grad_gates - jnp.sum(own_shares * grad_gates, -1, keepdims=True))
    grad_normed_two = normed_sum + jnp.dot(
        grad_logits, router.astype(F32).T, precision=PRECISE
    )
    grad_router = jnp.dot(normed_two.astype(F32).T, grad_logits, precision=PRECISE)
    grad_residual = out_grad + norm_back(grad_normed_two, residual, scale_two, gain_two)
    grad_lin = (RESIDUAL_SCALE * grad_residual).astype(BF16)
    grad_lin_all, down_sum = gather_grad(grad_lin, grad_down.reshape(2, 4, 4, 48, 640))
    grad_lin_all = grad_lin_all.reshape(8 * TOK, D)
    do_here = dot(out_slice, grad_lin_all, (((1,), (1,)), ((), ()))).astype(BF16)
    dq_here, dkv_here = attend_back(bounds, q_here, kv_here, do_here, start_lines, o_here, lse)
    grad_out = dot(o_low, grad_lin_all, (((1,), (0,)), ((), ()))).astype(BF16)
    dq_parts, dkv_parts, mixture, grad_residual_back = from_attention(
        dq_here, dkv_here, mixture_part.reshape(8, TOK, D), grad_residual.astype(BF16)
    )
    layer_out = (residual + RESIDUAL_SCALE * mixture).astype(BF16)

    dkv_sum = jnp.sum(dkv_parts.reshape(4, 4, 2, 2 * HEAD_DIM, TOK).astype(F32), 0)
    dkv_sum = jnp.moveaxis(dkv_sum, 0, 1)
    dqk = jnp.concatenate([dq_parts.astype(F32), dkv_sum[:, :, :HEAD_DIM]], 2).reshape(2, 4, 4, HEAD_DIM, TOK)
    dqk = turn(dqk, cosine, -sine)
    dq_lines = dqk[:, :, :GROUP].reshape(8, QROWS, TOK).astype(BF16)
    dkv_lines = (
        jnp.concatenate([dqk[:, :, GROUP], dkv_sum[:, :, HEAD_DIM:]], 2)
        .reshape(8, 2 * HEAD_DIM, TOK)
        .astype(BF16)
    )
    dqkv_lines = jnp.moveaxis(jnp.concatenate([dq_lines, dkv_lines], 1), 0, 1).reshape(320, 8 * TOK)
    grad_attn = dot(normed, dqkv_lines, (((0,), (1,)), ((), ())))
    grad_attn = jnp.concatenate([grad_attn, grad_router, jnp.zeros((D, PACK - 330), F32)], 1).astype(BF16)
    grad_normed_part = dot(dqkv_lines, attn[:, : QROWS + 2 * HEAD_DIM], (((0,), (1,)), ((), ()))).astype(BF16)
    attn_sum, out_parts, grad_normed = sum_planes(
        grad_attn.reshape(2, 4, 4, 48, PACK),
        grad_out.reshape(PLANE, 12, D),
        grad_normed_part.reshape(8, TOK, D),
    )
    out_sum = jnp.sum(out_parts.astype(F32), 0).astype(BF16)
    attn_own, gate_up_own, down_own, out_own, layer_out = final_deal(
        attn_sum, gate_up_sum, down_sum, out_sum, layer_out
    )

    own_tokens = layer_input[0].astype(F32)
    input_grad = grad_residual_back.astype(F32) + norm_back(
        grad_normed, own_tokens, rms_scale(own_tokens), gain_one
    )

    query_grad, keyval_grad, out_grad_rows, router_grad, gate_up_grad, down_grad, gain_grads = assemble(
        attn_own,
        gate_up_own,
        down_own,
        out_own,
        query_weight,
        key_value_matrix,
        router_weight,
        gate_up_weight,
        jnp.stack([first_gain, second_gain], 1).astype(F32),
    )
    return (
        layer_out[None],
        input_grad[None],
        gain_grads[:, 0],
        query_grad,
        keyval_grad,
        out_grad_rows,
        gain_grads[:, 1],
        router_grad,
        gate_up_grad,
        down_grad,
    )


def solution(mesh):
    row = P("shard", None)
    rows = P("shard", None, None)
    own = P("rep", "shard", None)
    in_specs = (own, P("rep", "shard"), own, P("shard"), row, row, row, P("shard"), row, rows, rows, own)
    out_specs = (own, own, P("shard"), row, row, row, P("shard"), row, rows, rows)
    return jax.shard_map(shards, mesh=mesh, in_specs=in_specs, out_specs=out_specs, check_vma=False)
```

```python
import functools

import jax
import jax.numpy as jnp
from jax import lax
from jax.experimental import pallas as pl
from jax.experimental.pallas import tpu as pltpu
from jax.sharding import PartitionSpec as P

D = 1536
HEADS = 8
GROUP = 3
HEAD_DIM = 64
HALF = HEAD_DIM // 2
FF = 512
EXPERTS = 10
TOK = 128
SEQ = 4096
PLANE = 16
RUN = 512
QROWS = GROUP * HEAD_DIM
PACK = 384
ROUTER_AT = 320
GAIN_ONE_AT = 336
GAIN_TWO_AT = 337
COLUMN = 8 * TOK

NORM_EPS = 1e-06
RESIDUAL_SCALE = 0.22
SCORE_SCALE = 0.015625
ROPE_BASE = 10000.0
MASK_FILL = -1e30
PRECISE = lax.Precision.HIGHEST
BF16 = jnp.bfloat16
F32 = jnp.float32
VMEM_LIMIT = 56 * 1024 * 1024


def my_place():
    return lax.axis_index("shard"), lax.axis_index("rep")


def parts_of(shard):
    place = lax.rem(shard, PLANE)
    return shard // PLANE, place, place // 4, lax.rem(place, 4)


def same(one, other):
    return jnp.logical_and(one[0] == other[0], one[1] == other[1])


class Place:
    def __init__(self, me):
        self.me = me
        self.shard, self.rep = me
        self.z_lo, self.place, self.x, self.y = parts_of(self.shard)
        self.core = lax.rem(self.rep, 2)
        self.z = (self.rep // 2) * 2 + self.z_lo
        self.member = self.z_lo * 4 + self.rep

    def device(self, z, x, y, core):
        return lax.rem(z, 2) * PLANE + 4 * x + y, (z // 2) * 2 + core

    def step(self, axis, by):
        z, x, y = self.z, self.x, self.y
        if axis == "z":
            z = lax.rem(z + by, 4)
        elif axis == "x":
            x = lax.rem(x + by, 4)
        else:
            y = lax.rem(y + by, 4)
        return self.device(z, x, y, self.core)

    def sibling(self):
        return self.shard, self.rep + 1 - 2 * self.core

    def partner(self):
        return self.shard + (1 - 2 * self.z_lo) * PLANE, self.rep

    def trader(self):
        return self.z_lo * PLANE + 4 * mirrored(self.z_lo, self.x) + self.rep, self.y

    def member_at(self, z, core):
        return lax.rem(z, 2) * 4 + (z // 2) * 2 + core

    def near(self):
        result = [self.sibling()]
        for axis in ("z", "x", "y"):
            result += [self.step(axis, 1), self.step(axis, 3)]
        return result


def mesh_id(place):
    return {"shard": place[0], "rep": place[1]}


class Net:
    def __init__(self, here, sems):
        self.here, self.sems, self.used, self.sent = here, sems, 0, []

    def take(self, count=1):
        first = self.used
        self.used += count
        return first

    def push(self, source, target, to):
        number = self.take(2)
        copy = pltpu.make_async_remote_copy(
            src_ref=source,
            dst_ref=target,
            send_sem=self.sems.at[number],
            recv_sem=self.sems.at[number + 1],
            device_id=mesh_id(to),
        )
        copy.start()
        self.sent.append(copy)
        return number + 1

    def got(self, number, region):
        pltpu.make_async_remote_copy(
            src_ref=region,
            dst_ref=region,
            send_sem=self.sems.at[number],
            recv_sem=self.sems.at[number],
            device_id=mesh_id(self.here.sibling()),
        ).wait_recv()

    def local(self, source, target):
        copy = pltpu.make_async_copy(source, target, self.sems.at[self.take()])
        copy.start()
        return copy

    def finish(self):
        for copy in self.sent:
            copy.wait_send()


class Route:
    def __init__(self, n, to, source, pieces, index=None, may_be_self=False):
        self.n, self.to, self.source, self.pieces = n, to, source, pieces
        self.index = index or (lambda i: i)
        self.may_be_self = may_be_self


def each(n, body):
    if n <= 8:
        for i in range(n):
            body(i)
    else:

        def step(i, carry):
            body(i)
            return carry

        lax.fori_loop(0, n, step, 0)


def greet_routes(routes, me, barrier):
    awaited = 0
    for route in routes:

        def greet(i, route=route):
            source = route.source(i)

            def signal():
                pl.semaphore_signal(barrier, inc=1, device_id=mesh_id(source))

            if route.may_be_self:
                pl.when(jnp.logical_not(same(source, me)))(signal)
            else:
                signal()

        each(route.n, greet)
        awaited = awaited + route.n
        if route.may_be_self:
            for i in range(route.n):
                awaited = awaited - same(route.to(i), me).astype(jnp.int32)
    return awaited


HOP = 2.0


def time_of(ref, rate=50.0):
    size = jnp.dtype(ref.dtype).itemsize / 1000.0
    for extent in ref.shape:
        size *= extent
    return HOP + size / rate


def follow_routes(net, routes, ins, outs, guess=15.0):
    me = net.here.me
    held = []
    for route in routes:
        count = route.n * len(route.pieces)
        held.append((net.take(count), net.take(count), net.take(len(route.pieces))))

    def remote(route, base, i, k, piece):
        source_in, cut, target_out, slot, unused = piece
        return pltpu.make_async_remote_copy(
            src_ref=ins[source_in].at[cut(i)],
            dst_ref=outs[target_out].at[slot(i)],
            send_sem=net.sems.at[base[0] + i * len(route.pieces) + k],
            recv_sem=net.sems.at[base[1] + route.index(i) * len(route.pieces) + k],
            device_id=mesh_id(route.to(i)),
        )

    def within(base, i, k, piece):
        source_in, cut, target_out, slot, unused = piece
        return pltpu.make_async_copy(
            ins[source_in].at[cut(i)], outs[target_out].at[slot(i)], net.sems.at[base[2] + k]
        )

    for route, base in zip(routes, held):

        def start(i, route=route, base=base):
            for k, piece in enumerate(route.pieces):
                copy = remote(route, base, i, k, piece)
                if route.may_be_self:
                    here = same(route.to(i), me)
                    pl.when(jnp.logical_not(here))(copy.start)
                    pl.when(here)(within(base, i, k, piece).start)
                else:
                    copy.start()

        each(route.n, start)
    yield guess
    for route, base in zip(routes, held):

        def arrive(i, route=route, base=base):
            for k, piece in enumerate(route.pieces):
                region = outs[piece[2]].at[piece[4](i)]
                place = route.source(i)
                sem = net.sems.at[base[1] + i * len(route.pieces) + k]
                copy = pltpu.make_async_remote_copy(
                    src_ref=region, dst_ref=region, send_sem=sem, recv_sem=sem, device_id=mesh_id(place)
                )
                if route.may_be_self:
                    pl.when(jnp.logical_not(same(place, me)))(copy.wait_recv)
                else:
                    copy.wait_recv()

        each(route.n, arrive)

        def leave(i, route=route, base=base):
            for k, piece in enumerate(route.pieces):
                copy = remote(route, base, i, k, piece)
                if route.may_be_self:
                    here = same(route.to(i), me)
                    pl.when(jnp.logical_not(here))(copy.wait_send)
                    pl.when(here)(within(base, i, k, piece).wait)
                else:
                    copy.wait_send()

        each(route.n, leave)


def trade(net, pieces):
    other = net.here.trader()
    here = same(other, net.here.me)
    copies = []
    for source, target in pieces:
        number = net.take(2)
        remote = pltpu.make_async_remote_copy(
            src_ref=source,
            dst_ref=target,
            send_sem=net.sems.at[number],
            recv_sem=net.sems.at[number + 1],
            device_id=mesh_id(other),
        )
        within = pltpu.make_async_copy(source, target, net.sems.at[net.take()])
        pl.when(jnp.logical_not(here))(remote.start)
        pl.when(here)(within.start)
        copies.append((remote, within))
    yield 30.0
    for remote, within in copies:
        pl.when(jnp.logical_not(here))(remote.wait)
        pl.when(here)(within.wait)


def greet_trader(here, barrier):
    other = here.trader()
    away = jnp.logical_not(same(other, here.me))

    @pl.when(away)
    def signal():
        pl.semaphore_signal(barrier, inc=1, device_id=mesh_id(other))

    return away.astype(jnp.int32)


def spread_rows(net, rows, out):
    here = net.here
    ahead = lax.rem(here.x - here.rep + 4, 4)
    pair = lambda k: out.at[pl.ds(2 * k, 2)]
    row_halves = row_half(48)

    def at(by):
        return out.at[lax.rem(here.y + by, 4)]

    def copy(number, source, target, to):
        return pltpu.make_async_remote_copy(
            src_ref=source,
            dst_ref=target,
            send_sem=net.sems.at[number],
            recv_sem=net.sems.at[number + 1],
            device_id=mesh_id(to),
        )

    def come(number, region):
        copy(number, region, region, here.sibling()).wait_recv()

    up, down, right, left = here.step("y", 1), here.step("y", 3), here.step("x", 1), here.step("x", 3)
    numbers = [net.take(2) for k in range(8)]
    keep = pltpu.make_async_copy(rows, at(0), net.sems.at[net.take()])
    first = [copy(numbers[0], rows, at(0), up), copy(numbers[1], rows, at(0), down)]
    second = [
        copy(numbers[2], row_halves(at(3), 0), row_halves(at(3), 0), up),
        copy(numbers[3], row_halves(at(1), 1), row_halves(at(1), 1), down),
    ]
    third = [copy(numbers[4], out, out, right), copy(numbers[5], out, out, left)]
    on_right = copy(numbers[6], pair(0), pair(0), right)
    on_left = copy(numbers[7], pair(1), pair(1), left)

    @pl.when(ahead == 0)
    def begin():
        keep.start()
        first[0].start()
        first[1].start()

    now = time_of(rows)
    yield now

    @pl.when(ahead == 0)
    def hand_on():
        come(numbers[0], at(3))
        second[0].start()
        come(numbers[1], at(1))
        second[1].start()

    now += time_of(rows, 100.0)
    yield now

    @pl.when(ahead == 0)
    def go_out():
        come(numbers[2], row_halves(at(2), 0))
        come(numbers[3], row_halves(at(2), 1))
        keep.wait()
        third[0].start()
        third[1].start()

    now += time_of(out, 70.0)
    yield now

    @pl.when(ahead == 1)
    def to_right():
        come(numbers[4], out)
        on_right.start()

    @pl.when(ahead == 3)
    def to_left():
        come(numbers[5], out)
        on_left.start()

    now += time_of(out, 140.0)
    yield now

    @pl.when(ahead == 2)
    def end():
        come(numbers[6], pair(0))
        come(numbers[7], pair(1))

    @pl.when(ahead == 0)
    def sent():
        for each_copy in first + second + third:
            each_copy.wait_send()

    pl.when(ahead == 1)(on_right.wait_send)
    pl.when(ahead == 3)(on_left.wait_send)


def comm(inputs, in_vmem, outputs, scratch, n_sems, collective_id, plan):
    n_in, n_out = len(inputs), len(outputs)

    def kernel(*refs):
        ins, outs = refs[:n_in], refs[n_in : n_in + n_out]
        rest, sems = refs[n_in + n_out : -1], refs[-1]
        net = Net(Place(my_place()), sems)
        flows, routes, near, greetings = plan(net, ins, outs, rest)
        barrier = pltpu.get_barrier_semaphore()
        awaited = greet_routes(routes, net.here.me, barrier)
        if near:
            others = net.here.near()
            for other in others:
                pl.semaphore_signal(barrier, inc=1, device_id=mesh_id(other))
            awaited = awaited + len(others)
        for greeting in greetings:
            awaited = awaited + greeting(net.here, barrier)
        pl.semaphore_wait(barrier, awaited)
        waits = [(0.0, number, flow) for number, flow in enumerate(flows)]
        while waits:
            unused, number, flow = waits.pop(0)
            when = next(flow, None)
            if when is not None:
                waits = sorted(waits + [(when, number, flow)], key=lambda wait: wait[:2])
        net.finish()
        assert net.used <= n_sems, net.used

    vmem = pl.BlockSpec(memory_space=pltpu.VMEM)
    anywhere = pl.BlockSpec(memory_space=pl.ANY)
    return pl.pallas_call(
        kernel,
        out_shape=[jax.ShapeDtypeStruct(s, t) for s, t, unused in outputs],
        in_specs=[vmem if k in in_vmem else anywhere for k in range(n_in)],
        out_specs=[vmem if inside else anywhere for unused, unused2, inside in outputs],
        scratch_shapes=list(scratch) + [pltpu.SemaphoreType.DMA((n_sems,))],
        compiler_params=pltpu.CompilerParams(
            collective_id=collective_id, has_side_effects=True, vmem_limit_bytes=VMEM_LIMIT
        ),
    )(*inputs)


def column_gather(net, source, out, half_of):
    here = net.here

    def slot(by, core):
        return out.at[here.member_at(lax.rem(here.z + by, 4), core)]

    core, other = here.core, 1 - here.core
    right, left, sibling = here.step("z", 1), here.step("z", 3), here.sibling()
    keep = net.local(source, slot(0, core))
    a = net.push(source, slot(0, core), right)
    b = net.push(source, slot(0, core), left)
    s = [net.push(source, slot(0, core), sibling)]
    now = time_of(source)
    yield now
    net.got(a, slot(3, core))
    c = net.push(half_of(slot(3, core), 0), half_of(slot(3, core), 0), right)
    s.append(net.push(slot(3, core), slot(3, core), sibling))
    net.got(b, slot(1, core))
    d = net.push(half_of(slot(1, core), 1), half_of(slot(1, core), 1), left)
    s.append(net.push(slot(1, core), slot(1, core), sibling))
    now += time_of(source, 100.0)
    yield now
    net.got(c, half_of(slot(2, core), 0))
    net.got(d, half_of(slot(2, core), 1))
    s.append(net.push(slot(2, core), slot(2, core), sibling))
    yield now + time_of(source, 200.0)
    for number, by in zip(s, (0, 3, 1, 2)):
        net.got(number, slot(by, other))
    keep.wait()


def row_half(size):
    first = (size // 2 + 15) // 16 * 16

    def half(ref, k):
        return ref.at[pl.ds(0, first)] if k == 0 else ref.at[pl.ds(first, size - first)]

    return half


def ring_gather(net, axis, source, slot, half, now, rate):
    right, left = net.here.step(axis, 1), net.here.step(axis, 3)
    a = net.push(source, slot(0), right)
    b = net.push(source, slot(0), left)
    now += time_of(source, rate)
    yield now
    net.got(a, slot(3))
    c = net.push(half(slot(3), 0), half(slot(3), 0), right)
    net.got(b, slot(1))
    d = net.push(half(slot(1), 1), half(slot(1), 1), left)
    now += time_of(source, 2 * rate)
    yield now
    net.got(c, half(slot(2), 0))
    net.got(d, half(slot(2), 1))
    return now


def swap_pair(net, payload, target):
    here = net.here
    number = net.push(payload.at[1 - here.z_lo], target, here.partner())
    yield 12.0
    net.got(number, target)


def plane_gather(net, payload, pair, out, rate=50.0):
    here = net.here
    z, x, y = here.z_lo, here.x, here.y
    rows = row_half(48)
    two = lambda ref, k: ref.at[pl.ds(2 * k, 2)]
    swap = []

    def first():
        if pair is None:
            swap.append(net.push(payload.at[1 - z], out.at[z, x, y], here.partner()))
        keep = net.local(payload.at[z], out.at[z, x, y])
        now = yield from ring_gather(
            net, "x", payload.at[z], lambda by: out.at[z, lax.rem(x + by, 4), y], rows, 0.0, rate
        )
        keep.wait()
        bundle = lambda by: out.at[z, :, lax.rem(y + by, 4)]
        yield from ring_gather(net, "y", bundle(0), bundle, two, now, rate)

    def second():
        w = 1 - z
        now, source = 0.0, pair
        if pair is None:
            now, source = time_of(payload.at[0], rate), out.at[w, x, y]
            yield now
            net.got(swap[0], source)
        else:
            keep = net.local(pair, out.at[w, x, y])
        now = yield from ring_gather(
            net, "y", source, lambda by: out.at[w, x, lax.rem(y + by, 4)], rows, now, rate
        )
        if pair is not None:
            keep.wait()
        bundle = lambda by: out.at[w, lax.rem(x + by, 4)]
        yield from ring_gather(net, "x", bundle(0), bundle, two, now, rate)

    return [first(), second()]


def add(target, *parts):
    total = parts[0][...].astype(F32)
    for part in parts[1:]:
        total = total + part[...].astype(F32)
    target[...] = total.astype(target.dtype)


def ring_sum(net, axis, block, half, halves, wholes, target, now, rate=50.0):
    right, left = net.here.step(axis, 1), net.here.step(axis, 3)
    lower, upper = halves
    a = net.push(half(block(2), 0), lower, right)
    b = net.push(half(block(2), 1), upper, left)
    now += time_of(lower, rate)
    yield now
    net.got(a, lower)
    add(half(block(1), 0), half(block(1), 0), lower)
    c = net.push(block(1), wholes[0], right)
    net.got(b, upper)
    add(half(block(3), 1), half(block(3), 1), upper)
    d = net.push(block(3), wholes[1], left)
    now += time_of(wholes[0], rate)
    yield now
    net.got(c, wholes[0])
    net.got(d, wholes[1])
    add(target, block(0), wholes[0], wholes[1])
    return now


def column_sum(net, parts, out, sums, sibling_parts, halves, wholes):
    here = net.here
    half = row_half(parts.shape[1])
    at = lambda by: lax.rem(here.z + by, 4)
    numbers = {}
    for by in (2, 1, 3, 0):
        numbers[by] = net.push(
            parts.at[here.member_at(at(by), 1 - here.core)], sibling_parts.at[at(by)], here.sibling()
        )
    now = HOP
    for by in (2, 1, 3):
        now += time_of(sums.at[0], 200.0) - HOP
        yield now
        net.got(numbers[by], sibling_parts.at[at(by)])
        add(sums.at[at(by)], parts.at[here.member_at(at(by), here.core)], sibling_parts.at[at(by)])
        if by == 2:
            ring = ring_sum(
                net, "z", lambda by: sums.at[at(by)], half, (halves.at[0], halves.at[1]),
                (wholes.at[0], wholes.at[1]), out, now,
            )
            when = next(ring)
    net.got(numbers[0], sibling_parts.at[at(0)])
    add(sums.at[at(0)], parts.at[here.member_at(at(0), here.core)], sibling_parts.at[at(0)])
    yield when
    yield from ring


def column_sum_scratch(rows, columns):
    return [
        pltpu.VMEM((4, rows, columns), BF16),
        pltpu.VMEM((4, rows, columns), BF16),
        pltpu.VMEM((2, rows // 2, columns), BF16),
        pltpu.VMEM((2, rows, columns), BF16),
    ]


def plane_sum(net, parts, out, held, pairs, bundles, rows_a, rows_b, blocks, rate=50.0):
    here = net.here
    at_x = lambda by: lax.rem(here.x + by, 4)
    at_y = lambda by: lax.rem(here.y + by, 4)
    pair = lambda ref, k: ref.at[pl.ds(2 * k, 2)]
    half = row_half(48)

    def first():
        copy = net.local(parts.at[0], held.at[0])
        yield 2.0
        copy.wait()
        mine = held.at[0, :, here.y]
        now = yield from ring_sum(
            net, "y", lambda by: held.at[0, :, at_y(by)], pair, (pairs.at[0], pairs.at[1]),
            (bundles.at[0], bundles.at[1]), mine, 2.0, rate,
        )
        yield from ring_sum(
            net, "x", lambda by: held.at[0, at_x(by), here.y], half, (rows_a.at[0], rows_b.at[0]),
            (blocks.at[0], blocks.at[1]), out.at[0], now, rate,
        )

    def second():
        copy = net.local(parts.at[1], held.at[1])
        yield 2.0
        copy.wait()
        mine = held.at[1, here.x]
        now = yield from ring_sum(
            net, "x", lambda by: held.at[1, at_x(by)], pair, (pairs.at[2], pairs.at[3]),
            (bundles.at[2], bundles.at[3]), mine, 2.0, rate,
        )
        yield from ring_sum(
            net, "y", lambda by: held.at[1, here.x, at_y(by)], half, (rows_a.at[1], rows_b.at[1]),
            (blocks.at[2], blocks.at[3]), out.at[1], now, rate,
        )

    return [first(), second()]


def plane_sum_scratch(columns):
    return [
        pltpu.VMEM((2, 4, 4, 48, columns), BF16),
        pltpu.VMEM((4, 2, 48, columns), BF16),
        pltpu.VMEM((4, 4, 48, columns), BF16),
        pltpu.VMEM((2, 32, columns), BF16),
        pltpu.VMEM((2, 16, columns), BF16),
        pltpu.VMEM((4, 48, columns), BF16),
    ]


def column_deal(net, parts, out, passing, half):
    here = net.here
    z = here.z_lo
    core, other = here.core, 1 - here.core
    lower, upper = passing

    def slot(by, core):
        return out.at[here.member_at(lax.rem(here.z + by, 4), core)]

    right, left, sibling = here.step("z", 1), here.step("z", 3), here.sibling()
    keep = net.local(parts.at[z], slot(0, core))
    e = net.push(half(parts.at[z], 0), lower, right)
    f = net.push(half(parts.at[z], 1), upper, left)
    a = net.push(parts.at[1 - z], slot(0, core), right)
    b = net.push(parts.at[1 - z], slot(0, core), left)
    s = [net.push(parts.at[z], slot(0, core), sibling)]
    now = time_of(parts.at[0])
    yield now
    net.got(e, lower)
    c = net.push(lower, half(slot(3, core), 0), right)
    net.got(f, upper)
    d = net.push(upper, half(slot(1, core), 1), left)
    net.got(a, slot(3, core))
    s.append(net.push(slot(3, core), slot(3, core), sibling))
    net.got(b, slot(1, core))
    s.append(net.push(slot(1, core), slot(1, core), sibling))
    now += time_of(parts.at[0])
    yield now
    net.got(c, half(slot(2, core), 0))
    net.got(d, half(slot(2, core), 1))
    s.append(net.push(slot(2, core), slot(2, core), sibling))
    yield now + HOP
    for number, by in zip(s, (0, 3, 1, 2)):
        net.got(number, slot(by, other))
    keep.wait()


def column_route(me, pieces):
    z, place, unused, unused2 = parts_of(me[0])
    mine = z * 4 + me[1]

    def where(member):
        return (member // 4) * PLANE + place, lax.rem(member, 4)

    def after(i):
        return lax.rem(mine + 1 + i, 8)

    def before(i):
        return lax.rem(mine + 7 - i, 8)

    return Route(
        7,
        lambda i: where(after(i)),
        lambda i: where(before(i)),
        [
            (
                a,
                lambda i, cut=cut: cut(after(i)),
                b,
                lambda i, slot=slot: slot(mine),
                lambda i, slot=slot: slot(before(i)),
            )
            for a, cut, b, slot in pieces
        ],
    )


def plane_route(me, pieces):
    z, place, unused, unused2 = parts_of(me[0])

    def after(i):
        return lax.rem(place + 1 + i, PLANE)

    def before(i):
        return lax.rem(place + 15 - i, PLANE)

    return Route(
        15,
        lambda i: (z * PLANE + after(i), me[1]),
        lambda i: (z * PLANE + before(i), me[1]),
        [
            (
                a,
                lambda i, cut=cut: cut(after(i)),
                b,
                lambda i, slot=slot: slot(place),
                lambda i, slot=slot: slot(before(i)),
            )
            for a, cut, b, slot in pieces
        ],
    )


def own_copies(net, ins, outs, copies):
    started = [net.local(ins[a].at[cut], outs[b].at[slot]) for a, cut, b, slot in copies]
    yield 100.0
    for copy in started:
        copy.wait()


ROW_HALF = row_half(TOK)


def mirrored(z, x):
    return x + z * (3 - 2 * x)


def query_routes(me, q_in, q_out):
    z_me, place, x, y = parts_of(me[0])
    base = z_me * PLANE

    def plain(i):
        return lax.rem(y + 1 + i, 4)

    def plain_before(i):
        return lax.rem(y + 3 - i, 4)

    def other(i):
        return lax.rem(y + i, 4)

    def other_before(i):
        return lax.rem(y + 4 - i, 4)

    first = Route(
        3,
        lambda i: (base + 4 * x + plain(i), me[1]),
        lambda i: (base + 4 * x + plain_before(i), me[1]),
        [(q_in, lambda i: (0, plain(i)), q_out, lambda i: (0, y), lambda i: (0, plain_before(i)))],
    )
    second = Route(
        4,
        lambda i: (base + 4 * (3 - x) + other(i), me[1]),
        lambda i: (base + 4 * (3 - x) + other_before(i), me[1]),
        [(q_in, lambda i: (1, other(i)), q_out, lambda i: (1, y), lambda i: (1, other_before(i)))],
    )
    return [first, second], [(q_in, (0, y), q_out, (0, y))]


def gather_start(x, segments, attn, out_rows, choices, dy):
    def plan(net, ins, outs, scratch):
        flows = plane_gather(net, ins[2], None, outs[2])
        flows += [
            spread_rows(net, ins[3], outs[3]),
            column_gather(net, ins[0], outs[0], ROW_HALF),
            column_gather(net, ins[1], outs[1], lambda ref, k: ref.at[pl.ds(8 * k, 8)]),
            trade(net, [(ins[4], outs[4]), (ins[5], outs[5])]),
        ]
        return flows, [], True, [greet_trader]

    return comm(
        [x, segments, attn, out_rows, choices, dy],
        (),
        [
            ((8, TOK, D), BF16, False),
            ((8, 16, TOK), jnp.int32, False),
            ((2, 4, 4, 48, PACK), BF16, False),
            ((4, 48, D), BF16, False),
            ((16, TOK), jnp.int32, False),
            ((TOK, D), BF16, False),
        ],
        [],
        112,
        0,
        plan,
    )


def to_attention(q, kv, ints, x, gate_up, down):
    def plan(net, ins, outs, scratch):
        me = net.here.me
        z_me, place, x, y = parts_of(me[0])
        routes, own = query_routes(me, 0, 0)
        routes = [
            plane_route(
                me,
                [
                    (1, lambda p: (0, lax.rem(p, 4)), 1, lambda p: (0, p)),
                    (1, lambda p: (1, lax.rem(p, 4)), 1, lambda p: (1, p)),
                    (2, lambda p: lax.rem(p, 4), 2, lambda p: p),
                ],
            )
        ] + routes
        own = own + [
            (1, (0, y), 1, (0, place)),
            (1, (1, y), 1, (1, place)),
            (2, y, 2, place),
        ]
        flows = [
            follow_routes(net, routes, ins, outs, 20.0),
            own_copies(net, ins, outs, own),
            trade(net, [(ins[3], outs[3])]),
            swap_pair(net, ins[4], outs[4]),
            swap_pair(net, ins[5], outs[5]),
        ]
        return flows, routes, True, [greet_trader]

    return comm(
        [q, kv, ints, x, gate_up, down],
        (),
        [
            ((2, 4, QROWS, TOK), BF16, False),
            ((2, PLANE, TOK, TOK), BF16, False),
            ((PLANE, 8, TOK), jnp.int32, False),
            ((TOK, D), BF16, False),
            ((48, 1280), BF16, False),
            ((48, 640), BF16, False),
        ],
        [],
        144,
        1,
        plan,
    )


def sum_attended(parts, gate_up, pair, dy, choices):
    def plan(net, ins, outs, scratch):
        flows = plane_gather(net, ins[1], ins[2], outs[1])
        flows += [
            column_sum(net, ins[0], outs[0], *scratch),
            column_gather(net, ins[3], outs[2], ROW_HALF),
            column_gather(net, ins[4], outs[3], lambda ref, k: ref.at[pl.ds(8 * k, 8)]),
        ]
        return flows, [], True, []

    total, gate_up_all, dy_all, choices_all = comm(
        [parts, gate_up, pair, dy, choices],
        (0,),
        [
            ((TOK, D), F32, True),
            ((2, 4, 4, 48, 1280), BF16, False),
            ((8, TOK, D), BF16, False),
            ((8, 16, TOK), jnp.int32, False),
        ],
        column_sum_scratch(TOK, D),
        160,
        2,
        plan,
    )
    return total, gate_up_all.reshape(D, 1280), dy_all, choices_all


def gather_normed(normed, down, pair):
    def plan(net, ins, outs, scratch):
        flows = [column_gather(net, ins[0], outs[0], ROW_HALF)]
        flows += plane_gather(net, ins[1], ins[2], outs[1])
        return flows, [], True, []

    normed_all, down_all = comm(
        [normed, down, pair],
        (),
        [((8, TOK, D), BF16, False), ((2, 4, 4, 48, 640), BF16, False)],
        [],
        64,
        3,
        plan,
    )
    return normed_all.reshape(8 * TOK, D), down_all.reshape(D, 640)


def sum_experts(normed, share, gate_up):
    def plan(net, ins, outs, scratch):
        me = net.here.me
        mine = net.here.member
        routes = [column_route(me, [(1, lambda m: m, 1, lambda m: m)])]
        flows = [
            column_sum(net, ins[0], outs[0], *scratch[:4]),
            follow_routes(net, routes, ins, outs, 10.0),
            own_copies(net, ins, outs, [(1, mine, 1, mine)]),
        ]
        flows += plane_sum(net, ins[2], outs[2], *scratch[4:])
        return flows, routes, True, []

    return comm(
        [normed, share, gate_up],
        (0,),
        [((TOK, D), F32, True), ((8, 8, TOK), F32, False), ((2, 48, 1280), BF16, True)],
        column_sum_scratch(TOK, D) + plane_sum_scratch(1280),
        96,
        4,
        plan,
    )


def gather_grad(grad_lin, down):
    def plan(net, ins, outs, scratch):
        flows = [column_gather(net, ins[0], outs[0], ROW_HALF)]
        flows += plane_sum(net, ins[1], outs[1], *scratch)
        return flows, [], True, []

    return comm(
        [grad_lin, down],
        (),
        [((8, TOK, D), BF16, False), ((2, 48, 640), BF16, True)],
        plane_sum_scratch(640),
        64,
        5,
        plan,
    )


def from_attention(q, kv, mixture, grad):
    def plan(net, ins, outs, scratch):
        me = net.here.me
        z_me, place, x, y = parts_of(me[0])
        routes, own = query_routes(me, 0, 0)
        routes = [plane_route(me, [(1, lambda p: (slice(None), p), 1, lambda p: p)])] + routes
        own = own + [(1, (slice(None), place), 1, place)]
        flows = [
            follow_routes(net, routes, ins, outs, 25.0),
            own_copies(net, ins, outs, own),
            column_sum(net, ins[2], outs[2], *scratch),
            trade(net, [(ins[3], outs[3])]),
        ]
        return flows, routes, True, [greet_trader]

    return comm(
        [q, kv, mixture, grad],
        (2,),
        [
            ((2, 4, QROWS, TOK), BF16, False),
            ((PLANE, 2, TOK, TOK), BF16, False),
            ((TOK, D), F32, True),
            ((TOK, D), BF16, False),
        ],
        column_sum_scratch(TOK, D),
        128,
        6,
        plan,
    )


def sum_planes(attn, out_rows, normed):
    def plan(net, ins, outs, scratch):
        me = net.here.me
        place = net.here.place
        routes = [plane_route(me, [(1, lambda p: p, 1, lambda p: p)])]
        flows = [column_sum(net, ins[2], outs[2], *scratch[6:])]
        flows += plane_sum(net, ins[0], outs[0], *scratch[:6])
        flows += [
            follow_routes(net, routes, ins, outs, 20.0),
            own_copies(net, ins, outs, [(1, place, 1, place)]),
        ]
        return flows, routes, True, []

    return comm(
        [attn, out_rows, normed],
        (2,),
        [
            ((2, 48, PACK), BF16, True),
            ((PLANE, 12, D), BF16, False),
            ((TOK, D), F32, True),
        ],
        plane_sum_scratch(PACK) + column_sum_scratch(TOK, D),
        128,
        7,
        plan,
    )


def final_deal(attn, gate_up, down, out_rows, layer_out):
    def plan(net, ins, outs, scratch):
        me = net.here.me
        place, mine = net.here.place, net.here.member
        routes = [
            Route(
                4,
                lambda i: (4 * mine + place // 4, i),
                lambda i: (
                    (me[0] // 4) // 4 * PLANE + 4 * lax.rem(me[0], 4) + i,
                    lax.rem(me[0] // 4, 4),
                ),
                [(3, lambda i: slice(None), 3, lambda i: lax.rem(place, 4), lambda i: i)],
                index=lambda i: lax.rem(place, 4),
                may_be_self=True,
            ),
        ]
        half = row_half(48)
        flows = [follow_routes(net, routes, ins, outs, 15.0)]
        for k in range(3):
            flows.append(column_deal(net, ins[k], outs[k], scratch[2 * k : 2 * k + 2], half))
        flows.append(trade(net, [(ins[4], outs[4])]))
        return flows, routes, True, [greet_trader]

    widths = (PACK, 1280, 640)
    scratch = []
    for width in widths:
        scratch += [pltpu.VMEM((32, width), BF16), pltpu.VMEM((16, width), BF16)]
    return comm(
        [attn, gate_up, down, out_rows, layer_out],
        (),
        [((8, 48, width), BF16, False) for width in widths]
        + [((4, 12, D), BF16, False), ((TOK, D), BF16, False)],
        scratch,
        96,
        8,
        plan,
    )


NT = (((1,), (1,)), ((), ()))


def product_nt(one, other):
    return lax.dot_general(one, other, NT, preferred_element_type=F32)


def unit(size):
    rows = lax.broadcasted_iota(jnp.int32, (size, size), 0)
    return (rows == lax.broadcasted_iota(jnp.int32, (size, size), 1)).astype(BF16)


def turn_into(target, source, block=256):
    ones = unit(block)

    def step(k, carry):
        place = pl.ds(pl.multiple_of(k * block, block), block)
        target[place, :] = product_nt(ones, source[:, place]).astype(BF16)
        return carry

    lax.fori_loop(0, source.shape[1] // block, step, 0)


def project_kernel(x_ref, attn_ref, cos_ref, sin_ref, q_ref, kv_ref, lines_ref, turned_ref, normed, linear):
    ones = unit(PACK)

    def turn_weights(k, carry):
        place = pl.ds(pl.multiple_of(k * 256, 256), 256)
        turned_ref[:, place] = product_nt(ones, attn_ref[place, :]).astype(BF16)
        return carry

    lax.fori_loop(0, D // 256, turn_weights, 0)
    gain = turned_ref[GAIN_ONE_AT : GAIN_ONE_AT + 1, :].astype(F32)

    def norm(k, carry):
        place = pl.ds(pl.multiple_of(k * TOK, TOK), TOK)
        values = x_ref[place, :].astype(F32)
        scale = lax.rsqrt(jnp.sum(values * values, -1, keepdims=True) * (1.0 / D) + NORM_EPS)
        normed[place, :] = (values * scale * gain).astype(BF16)
        return carry

    lax.fori_loop(0, 8, norm, 0)
    for part in range(2):
        place = slice(part * 512, (part + 1) * 512)
        linear[:, place] = product_nt(turned_ref[:ROUTER_AT, :], normed[place, :])
    for z in range(2):
        cosine, sine = cos_ref[z], sin_ref[z]
        for sequence in range(4):
            at = (4 * z + sequence) * TOK
            for head in range(GROUP + 1):
                rows = head * HEAD_DIM
                front = linear[rows : rows + HALF, at : at + TOK]
                behind = linear[rows + HALF : rows + HEAD_DIM, at : at + TOK]
                one = (front * cosine - behind * sine).astype(BF16)
                two = (behind * cosine + front * sine).astype(BF16)
                if head < GROUP:
                    q_ref[z, sequence, rows : rows + HALF, :] = one
                    q_ref[z, sequence, rows + HALF : rows + HEAD_DIM, :] = two
                else:
                    kv_ref[z, sequence, :HALF, :] = one
                    kv_ref[z, sequence, HALF:HEAD_DIM, :] = two
            kv_ref[z, sequence, HEAD_DIM:, :] = linear[QROWS + HEAD_DIM : ROUTER_AT, at : at + TOK].astype(BF16)
    turn_into(lines_ref, normed)


def local_kernel(kernel, inputs, smem, anywhere_in, outputs, scratch):
    vmem = pl.BlockSpec(memory_space=pltpu.VMEM)
    anywhere = pl.BlockSpec(memory_space=pl.ANY)
    scalars = pl.BlockSpec(memory_space=pltpu.SMEM)
    return pl.pallas_call(
        kernel,
        out_shape=[jax.ShapeDtypeStruct(shape, dtype) for shape, dtype, unused in outputs],
        in_specs=[
            scalars if k in smem else anywhere if k in anywhere_in else vmem for k in range(len(inputs))
        ],
        out_specs=[vmem if inside else anywhere for unused, unused2, inside in outputs],
        scratch_shapes=scratch,
        compiler_params=pltpu.CompilerParams(vmem_limit_bytes=VMEM_LIMIT),
    )(*inputs)


def project(x_all, attn, cosine, sine):
    return local_kernel(
        project_kernel,
        [x_all, attn, cosine, sine],
        (),
        (),
        [
            ((2, 4, QROWS, TOK), BF16, True),
            ((2, 4, TOK, TOK), BF16, True),
            ((D, COLUMN), BF16, True),
            ((PACK, D), BF16, True),
        ],
        [pltpu.VMEM((COLUMN, D), BF16), pltpu.VMEM((ROUTER_AT, COLUMN), F32)],
    )


def experts_kernel(
    hn_any, dy_any, gate_up_any, down_any, router_ref, choices_ref,
    mixture_any, back_any, gate_up_grad_any, down_grad_any, pull_ref, share_ref,
    hn, dy, gate_up, down, hn_lines, dy_lines, hidden, joined, share_rows, pull_rows,
    mixture, back, gate_up_grad, down_grad, sems,
):
    z = lax.axis_index("shard") // PLANE
    loads = [
        pltpu.make_async_copy(source, target, sems.at[k])
        for k, (source, target) in enumerate(
            [(hn_any, hn), (gate_up_any, gate_up), (down_any, down), (dy_any, dy)]
        )
    ]
    for load in loads:
        load.start()
    loads[0].wait()

    row = lax.broadcasted_iota(jnp.int32, (16, TOK), 0)

    def route(block, carry):
        place = pl.ds(pl.multiple_of(block * TOK, TOK), TOK)
        logits = product_nt(router_ref[...], hn[place, :])
        named = choices_ref[block]
        named = named + jnp.where(named >= 5, 3, 0)
        chosen = row == named[0:1]
        for k in range(1, 8):
            chosen = jnp.logical_or(chosen, row == named[k : k + 1])
        logits = jnp.where(chosen, logits, MASK_FILL)
        exponent = jnp.where(chosen, jnp.exp(logits - jnp.max(logits, 0, keepdims=True)), 0.0)
        share_ref[block] = exponent / jnp.sum(exponent, 0, keepdims=True)
        mine = share_ref[block, pl.ds(pl.multiple_of(z * 8, 8), 8), :]
        share_rows[place, :] = mine.T
        return carry

    lax.fori_loop(0, 8, route, 0)
    turn_into(hn_lines, hn)
    for load in loads[1:]:
        load.wait()
    turn_into(dy_lines, dy)

    for expert in range(5):

        def work(block, carry, expert=expert):
            place = pl.ds(pl.multiple_of(block * 512, 512), 512)
            both = jnp.dot(
                hn[place, :], gate_up[:, expert * 256 : expert * 256 + 256], preferred_element_type=F32
            )
            gate, up = both[:, :TOK], both[:, TOK:]
            pulled = RESIDUAL_SCALE * jnp.dot(
                dy[place, :], down[:, expert * TOK : (expert + 1) * TOK], preferred_element_type=F32
            )
            share = share_rows[place, expert : expert + 1]
            sigmoid = 1.0 / (1.0 + jnp.exp(-gate))
            silu = gate * sigmoid
            act = (silu * up).astype(BF16).astype(F32)
            hidden[place, expert * TOK : (expert + 1) * TOK] = (share * act).astype(BF16)
            pull_rows[place, expert : expert + 1] = jnp.sum(act * pulled, 1, keepdims=True)
            grad = share * pulled
            joined[place, expert * 256 : expert * 256 + TOK] = (
                grad * up * (sigmoid + silu * (1.0 - sigmoid))
            ).astype(BF16)
            joined[place, expert * 256 + TOK : expert * 256 + 256] = (grad * silu).astype(BF16)
            return carry

        lax.fori_loop(0, 2, work, 0)

    def back_step(k, carry):
        place = pl.ds(pl.multiple_of(k * 256, 256), 256)
        back[:, place] = product_nt(joined[...], gate_up[place, :]).astype(BF16)
        return carry

    lax.fori_loop(0, D // 256, back_step, 0)
    stores = [pltpu.make_async_copy(back, back_any, sems.at[4])]
    stores[0].start()

    def gate_up_step(k, carry):
        place = pl.ds(pl.multiple_of(k * 256, 256), 256)
        gate_up_grad[:, place] = jnp.dot(
            hn_lines[...], joined[:, place], preferred_element_type=F32
        ).astype(BF16)
        return carry

    lax.fori_loop(0, 5, gate_up_step, 0)
    stores.append(pltpu.make_async_copy(gate_up_grad, gate_up_grad_any, sems.at[5]))
    stores[1].start()

    def mixture_step(k, carry):
        place = pl.ds(pl.multiple_of(k * 256, 256), 256)
        mixture[:, place] = product_nt(hidden[...], down[place, :]).astype(BF16)
        return carry

    lax.fori_loop(0, D // 256, mixture_step, 0)
    stores.append(pltpu.make_async_copy(mixture, mixture_any, sems.at[6]))
    stores[2].start()
    for first, size in ((0, 256), (256, 256), (512, 128)):
        down_grad[:, first : first + size] = (
            RESIDUAL_SCALE
            * jnp.dot(dy_lines[...], hidden[:, first : first + size], preferred_element_type=F32)
        ).astype(BF16)
    stores.append(pltpu.make_async_copy(down_grad, down_grad_any, sems.at[7]))
    stores[3].start()

    def turn_pull(block, carry):
        place = pl.ds(pl.multiple_of(block * TOK, TOK), TOK)
        pull_ref[block] = pull_rows[place, :].T
        return carry

    pull_rows[:, 5:8] = jnp.zeros((COLUMN, 3), F32)
    lax.fori_loop(0, 8, turn_pull, 0)
    for store in stores:
        store.wait()


def experts(hn, dy, gate_up, down, router, choices):
    wide = lambda rows, columns: pltpu.VMEM((rows, columns), BF16)
    return local_kernel(
        experts_kernel,
        [hn, dy, gate_up, down, router, choices],
        (),
        (0, 1, 2, 3),
        [
            ((COLUMN, D), BF16, False),
            ((COLUMN, D), BF16, False),
            ((D, 1280), BF16, False),
            ((D, 640), BF16, False),
            ((8, 8, TOK), F32, True),
            ((8, 16, TOK), F32, True),
        ],
        [
            wide(COLUMN, D), wide(COLUMN, D), wide(D, 1280), wide(D, 640), wide(D, COLUMN), wide(D, COLUMN),
            wide(COLUMN, 640), wide(COLUMN, 1280), pltpu.VMEM((COLUMN, 8), F32), pltpu.VMEM((COLUMN, 8), F32),
            wide(COLUMN, D), wide(COLUMN, D), wide(D, 1280), wide(D, 640), pltpu.SemaphoreType.DMA((8,)),
        ],
    )


def residual_grad_kernel(
    sum_ref, residual_ref, dy_ref, pull_ref, share_ref, turned_ref, grad_ref, low_ref, logit_ref
):
    shard, rep = my_place()
    mine = (shard // PLANE) * 4 + rep
    shares = share_ref[mine]
    pulls = []
    for z in range(2):
        total = pull_ref[4 * z]
        for k in range(1, 4):
            total = total + pull_ref[4 * z + k]
        pulls.append(total)
    pull = jnp.concatenate(pulls, 0)
    logits = shares * (pull - jnp.sum(shares * pull, 0, keepdims=True))
    logit_ref[...] = logits
    router = turned_ref[ROUTER_AT : ROUTER_AT + 16, :].astype(F32)
    gain = turned_ref[GAIN_TWO_AT : GAIN_TWO_AT + 1, :].astype(F32)
    grad_normed = sum_ref[...] + jnp.dot(logits.T, router, precision=PRECISE, preferred_element_type=F32)
    residual = residual_ref[...]
    scale = lax.rsqrt(jnp.sum(residual * residual, -1, keepdims=True) * (1.0 / D) + NORM_EPS)
    weighted = grad_normed * gain
    mean = jnp.sum(weighted * residual, -1, keepdims=True) * (1.0 / D)
    grad = dy_ref[...].astype(F32) + scale * weighted - residual * (scale * scale * scale * mean)
    grad_ref[...] = grad.astype(BF16)
    low_ref[...] = (RESIDUAL_SCALE * grad).astype(BF16)


def residual_grad(normed_sum, residual, dy, pull, shares, turned):
    return local_kernel(
        residual_grad_kernel,
        [normed_sum, residual, dy, pull, shares, turned],
        (),
        (),
        [((TOK, D), BF16, True), ((TOK, D), BF16, True), ((16, TOK), F32, True)],
        [],
    )


def project_grad_kernel(
    dq_ref, dkv_ref, lines_ref, turned_ref, hn_ref, logit_ref, cos_ref, sin_ref, weight_ref, normed_ref,
    grads, rows_of_grads, routed,
):
    grads[ROUTER_AT:, :] = jnp.zeros((PACK - ROUTER_AT, COLUMN), BF16)
    for z in range(2):
        cosine, sine = cos_ref[z], sin_ref[z]
        for sequence in range(4):
            at = (4 * z + sequence) * TOK
            total = dkv_ref[sequence, z].astype(F32)
            for quarter in range(1, 4):
                total = total + dkv_ref[4 * quarter + sequence, z].astype(F32)
            for head in range(GROUP + 1):
                rows = head * HEAD_DIM
                if head < GROUP:
                    front = dq_ref[z, sequence, rows : rows + HALF, :].astype(F32)
                    behind = dq_ref[z, sequence, rows + HALF : rows + HEAD_DIM, :].astype(F32)
                else:
                    front, behind = total[:HALF], total[HALF:HEAD_DIM]
                grads[rows : rows + HALF, at : at + TOK] = (front * cosine + behind * sine).astype(BF16)
                grads[rows + HALF : rows + HEAD_DIM, at : at + TOK] = (behind * cosine - front * sine).astype(BF16)
            grads[QROWS + HEAD_DIM : ROUTER_AT, at : at + TOK] = total[HEAD_DIM:].astype(BF16)
    routed[...] = jnp.zeros_like(routed)
    routed[ROUTER_AT : ROUTER_AT + 16, :] = logit_ref[...].astype(BF16)
    ones = unit(256)

    def weight_step(k, carry):
        place = pl.ds(pl.multiple_of(k * 256, 256), 256)
        hn_lines = product_nt(ones, hn_ref[:, place]).astype(BF16)
        weight_ref[place, :] = (
            product_nt(lines_ref[place, :], grads[...]) + product_nt(hn_lines, routed[...])
        ).astype(BF16)
        return carry

    lax.fori_loop(0, D // 256, weight_step, 0)
    turn_into(rows_of_grads, grads)

    def normed_step(k, carry):
        place = pl.ds(pl.multiple_of(k * 256, 256), 256)
        normed_ref[:, place] = jnp.dot(
            rows_of_grads[...], turned_ref[:, place], preferred_element_type=F32
        ).astype(BF16)
        return carry

    lax.fori_loop(0, D // 256, normed_step, 0)


def project_grad(dq, dkv, lines, turned, hn, logits, cosine, sine):
    return local_kernel(
        project_grad_kernel,
        [dq, dkv, lines, turned, hn, logits, cosine, sine],
        (),
        (),
        [((D, PACK), BF16, True), ((COLUMN, D), BF16, True)],
        [pltpu.VMEM((PACK, COLUMN), BF16), pltpu.VMEM((COLUMN, PACK), BF16), pltpu.VMEM((PACK, TOK), BF16)],
    )


def assemble_kernel(
    attn, gate_up, down, out_rows, query_weight, keyval_weight, router_weight, gate_up_weight, gains,
    query_grad, keyval_grad, out_grad, router_grad, gate_up_grad, down_grad, gain_grads,
):
    parts = [attn[m].astype(F32) for m in range(HEADS)]
    query = jnp.concatenate([part[:, :QROWS] for part in parts], 1)
    key = jnp.concatenate([part[:, QROWS : QROWS + HEAD_DIM] for part in parts], 1)
    value = jnp.concatenate([part[:, QROWS + HEAD_DIM : ROUTER_AT] for part in parts], 1)
    query_grad[...] = query
    keyval_grad[:, : HEADS * HEAD_DIM] = key
    keyval_grad[:, HEADS * HEAD_DIM :] = value
    router = parts[0]
    for part in parts[1:]:
        router = router + part
    router = jnp.concatenate([router[:, ROUTER_AT : ROUTER_AT + 5], router[:, ROUTER_AT + 8 : ROUTER_AT + 13]], 1)
    router_grad[...] = router
    for k in range(4):
        out_grad[12 * k : 12 * k + 12, :] = out_rows[k].astype(F32)
    first = jnp.sum(query * query_weight[...].astype(F32), 1, keepdims=True)
    half = HEADS * HEAD_DIM
    first = first + jnp.sum(key * keyval_weight[:, :half].astype(F32), 1, keepdims=True)
    first = first + jnp.sum(value * keyval_weight[:, half:].astype(F32), 1, keepdims=True)
    second = jnp.sum(router * router_weight[...].astype(F32), 1, keepdims=True)
    for expert in range(EXPERTS):
        z, local = expert // 5, expert % 5
        rows = []
        for side in range(2):
            at = local * 256 + side * TOK
            rows += [gate_up[4 * z + q, :, at : at + TOK].astype(F32) for q in range(4)]
        whole = jnp.concatenate(rows, 1)
        gate_up_grad[expert] = whole
        second = second + jnp.sum(whole * gate_up_weight[expert].astype(F32), 1, keepdims=True)
        down_grad[expert] = jnp.concatenate(
            [down[4 * z + q, :, local * TOK : (local + 1) * TOK].astype(F32) for q in range(4)], 1
        )
    gain_grads[:, 0:1] = first / gains[:, 0:1]
    gain_grads[:, 1:2] = second / gains[:, 1:2]


def assemble(attn, gate_up, down, out_rows, query_weight, keyval_weight, router_weight, gate_up_weight, gains):
    vmem = pl.BlockSpec(memory_space=pltpu.VMEM)
    shapes = [(48, D), (48, 1024), (48, D), (48, EXPERTS), (EXPERTS, 48, 2 * FF), (EXPERTS, 48, FF), (48, 2)]
    return pl.pallas_call(
        assemble_kernel,
        out_shape=[jax.ShapeDtypeStruct(shape, F32) for shape in shapes],
        in_specs=[vmem] * 9,
        out_specs=[vmem] * len(shapes),
        compiler_params=pltpu.CompilerParams(vmem_limit_bytes=VMEM_LIMIT),
    )(attn, gate_up, down, out_rows, query_weight, keyval_weight, router_weight, gate_up_weight, gains)


def unpack_queries(source, target):
    for run in range(2):
        for part in range(4):
            target[:, run * RUN + part * TOK : run * RUN + (part + 1) * TOK] = source[run, part]


def unpack_keys(kv_ref, key_rows, value_lines):
    def step(j, carry):
        place = pl.ds(pl.multiple_of(j * TOK, TOK), TOK)
        block = kv_ref[j // PLANE, lax.rem(j, PLANE)]
        key_rows[place, :] = block[:HEAD_DIM].astype(F32).T.astype(BF16)
        value_lines[:, place] = block[HEAD_DIM:]
        return carry

    lax.fori_loop(0, SEQ // TOK, step, 0)


def visible_block(block, start, query):
    key = block * RUN + lax.broadcasted_iota(jnp.int32, (RUN, RUN), 0)
    return jnp.logical_and(key >= start, key <= query)


def attend_kernel(bounds, q_ref, kv_ref, start_ref, o_ref, low_ref, lse_ref, queries, key_rows, value_lines):
    unpack_queries(q_ref, queries)
    unpack_keys(kv_ref, key_rows, value_lines)
    for run in range(2):
        cols = slice(run * RUN, (run + 1) * RUN)
        start = start_ref[0:1, cols]
        query = bounds[4 + run] + lax.broadcasted_iota(jnp.int32, (1, RUN), 1)
        heads = [
            queries[h * HEAD_DIM : (h + 1) * HEAD_DIM, cols] * jnp.asarray(SCORE_SCALE, BF16)
            for h in range(GROUP)
        ]

        def step(block, carry):
            place = pl.ds(pl.multiple_of(block * RUN, RUN), RUN)
            keys, values = key_rows[place, :], value_lines[:, place]
            seen = visible_block(block, start, query)
            result = []
            for h in range(GROUP):
                peak, total, acc = carry[3 * h : 3 * h + 3]
                scores = jnp.dot(keys, heads[h], preferred_element_type=F32)
                scores = jnp.where(seen, scores, MASK_FILL)
                top = jnp.maximum(peak, jnp.max(scores, 0, keepdims=True))
                weights = jnp.exp(scores - top)
                fade = jnp.exp(peak - top)
                total = fade * total + jnp.sum(weights, 0, keepdims=True)
                acc = fade * acc + jnp.dot(values, weights.astype(BF16), preferred_element_type=F32)
                result += [top, total, acc]
            return tuple(result)

        zero = []
        for h in range(GROUP):
            zero += [
                jnp.full((1, RUN), MASK_FILL, F32),
                jnp.zeros((1, RUN), F32),
                jnp.zeros((HEAD_DIM, RUN), F32),
            ]
        done = lax.fori_loop(bounds[run], bounds[2 + run], step, tuple(zero))
        for h in range(GROUP):
            peak, total, acc = done[3 * h : 3 * h + 3]
            rows = slice(h * HEAD_DIM, (h + 1) * HEAD_DIM)
            attended = acc / total
            o_ref[rows, cols] = attended
            low_ref[rows, cols] = attended.astype(BF16)
            lse_ref[h : h + 1, cols] = peak + jnp.log(total)


def attend(bounds, q, kv, start):
    vmem = pl.BlockSpec(memory_space=pltpu.VMEM)
    return pl.pallas_call(
        attend_kernel,
        out_shape=[
            jax.ShapeDtypeStruct((QROWS, 2 * RUN), F32),
            jax.ShapeDtypeStruct((QROWS, 2 * RUN), BF16),
            jax.ShapeDtypeStruct((8, 2 * RUN), F32),
        ],
        in_specs=[pl.BlockSpec(memory_space=pltpu.SMEM), vmem, vmem, vmem],
        out_specs=[vmem, vmem, vmem],
        scratch_shapes=[
            pltpu.VMEM((QROWS, 2 * RUN), BF16),
            pltpu.VMEM((SEQ, HEAD_DIM), BF16),
            pltpu.VMEM((HEAD_DIM, SEQ), BF16),
        ],
        compiler_params=pltpu.CompilerParams(vmem_limit_bytes=VMEM_LIMIT),
    )(bounds, q, kv, start)


def attend_back_kernel(
    bounds, q_ref, kv_ref, grads, start_ref, o_ref, lse_ref, dq_ref, dkv_ref,
    queries, key_rows, value_rows, key_lines, key_grad, value_grad,
):
    unpack_queries(q_ref, queries)
    key_grad[...] = jnp.zeros_like(key_grad)
    value_grad[...] = jnp.zeros_like(value_grad)

    def spread(j, carry):
        place = pl.ds(pl.multiple_of(j * TOK, TOK), TOK)
        block = kv_ref[j // PLANE, lax.rem(j, PLANE)]
        turned = block.astype(F32).T.astype(BF16)
        key_rows[place, :] = turned[:, :HEAD_DIM]
        value_rows[place, :] = turned[:, HEAD_DIM:]
        key_lines[:, place] = block[:HEAD_DIM]
        return carry

    lax.fori_loop(0, SEQ // TOK, spread, 0)
    for run in range(2):
        cols = slice(run * RUN, (run + 1) * RUN)
        start = start_ref[0:1, cols]
        query = bounds[4 + run] + lax.broadcasted_iota(jnp.int32, (1, RUN), 1)
        lse = [lse_ref[h : h + 1, cols] for h in range(GROUP)]
        delta = []
        for h in range(GROUP):
            rows = slice(h * HEAD_DIM, (h + 1) * HEAD_DIM)
            delta.append(jnp.sum(grads[rows, cols].astype(F32) * o_ref[rows, cols], 0, keepdims=True))

        def step(block, carry):
            place = pl.ds(pl.multiple_of(block * RUN, RUN), RUN)
            keys, values, lines = key_rows[place, :], value_rows[place, :], key_lines[:, place]
            seen = visible_block(block, start, query)
            result = []
            dk = key_grad[place, :]
            dv = value_grad[place, :]
            for h in range(GROUP):
                rows = slice(h * HEAD_DIM, (h + 1) * HEAD_DIM)
                q = queries[rows, cols] * jnp.asarray(SCORE_SCALE, BF16)
                do = grads[rows, cols]
                scores = jnp.dot(keys, q, preferred_element_type=F32)
                weights = jnp.exp(jnp.where(seen, scores, MASK_FILL) - lse[h])
                pull = jnp.dot(values, do, preferred_element_type=F32)
                ds = (weights * (pull - delta[h])).astype(BF16)
                dv = dv + lax.dot_general(weights.astype(BF16), do, NT, preferred_element_type=F32)
                dk = dk + lax.dot_general(ds, q, NT, preferred_element_type=F32)
                result.append(carry[h] + jnp.dot(lines, ds, preferred_element_type=F32))
            key_grad[place, :] = dk
            value_grad[place, :] = dv
            return tuple(result)

        done = lax.fori_loop(
            bounds[run], bounds[2 + run], step, tuple(jnp.zeros((HEAD_DIM, RUN), F32) for h in range(GROUP))
        )
        for h in range(GROUP):
            rows = slice(h * HEAD_DIM, (h + 1) * HEAD_DIM)
            scaled = SCORE_SCALE * done[h]
            for part in range(4):
                dq_ref[run, part, rows, :] = scaled[:, part * TOK : (part + 1) * TOK].astype(BF16)

    def gather(j, carry):
        place = pl.ds(pl.multiple_of(j * TOK, TOK), TOK)
        dkv_ref[j // PLANE, lax.rem(j, PLANE), :HEAD_DIM, :] = key_grad[place, :].T.astype(BF16)
        dkv_ref[j // PLANE, lax.rem(j, PLANE), HEAD_DIM:, :] = value_grad[place, :].T.astype(BF16)
        return carry

    lax.fori_loop(0, SEQ // TOK, gather, 0)


def attend_back(bounds, q, kv, do, start, o, lse):
    vmem = pl.BlockSpec(memory_space=pltpu.VMEM)
    return pl.pallas_call(
        attend_back_kernel,
        out_shape=[
            jax.ShapeDtypeStruct((2, 4, QROWS, TOK), BF16),
            jax.ShapeDtypeStruct((2, PLANE, TOK, TOK), BF16),
        ],
        in_specs=[pl.BlockSpec(memory_space=pltpu.SMEM)] + [vmem] * 6,
        out_specs=[vmem, vmem],
        scratch_shapes=[
            pltpu.VMEM((QROWS, 2 * RUN), BF16),
            pltpu.VMEM((SEQ, HEAD_DIM), BF16),
            pltpu.VMEM((SEQ, HEAD_DIM), BF16),
            pltpu.VMEM((HEAD_DIM, SEQ), BF16),
            pltpu.VMEM((SEQ, HEAD_DIM), F32),
            pltpu.VMEM((SEQ, HEAD_DIM), F32),
        ],
        compiler_params=pltpu.CompilerParams(vmem_limit_bytes=VMEM_LIMIT),
    )(bounds, q, kv, do, start, o, lse)


def rms_scale(values):
    return lax.rsqrt(jnp.mean(values * values, -1, keepdims=True) + NORM_EPS)


def norm_back(grad_normed, values, scale_factor, gain_values):
    weighted = grad_normed * gain_values
    return scale_factor * weighted - values * scale_factor**3 * jnp.mean(
        weighted * values, -1, keepdims=True
    )


def shards(
    layer_input,
    segments,
    choices,
    first_gain,
    query_weight,
    key_value_matrix,
    output_weight,
    second_gain,
    router_weight,
    gate_up_weight,
    down_weight,
    cotangent,
):
    shard, rep = my_place()
    z, place, x, y = parts_of(shard)
    dot = functools.partial(lax.dot_general, preferred_element_type=F32)

    pad = jnp.zeros((8, TOK), jnp.int32)
    choices_lines = jnp.concatenate([choices[0].T, pad], 0)
    segment_lines = jnp.concatenate([segments, pad, pad[:7]], 0)
    gate_up_mine = lax.dynamic_index_in_dim(
        gate_up_weight.reshape(48, 2, 5, 2, 4, TOK), rep, 4, keepdims=False
    )
    gate_up_mine = jnp.moveaxis(gate_up_mine, 1, 0).reshape(2, 48, 1280)
    down_mine = lax.dynamic_index_in_dim(down_weight.reshape(48, 2, 5, 4, TOK), rep, 3, keepdims=False)
    down_mine = jnp.moveaxis(down_mine, 1, 0).reshape(2, 48, 640)
    query_mine = lax.dynamic_index_in_dim(query_weight.reshape(48, 2, 4, QROWS), rep, 2, keepdims=False)
    keyval_mine = lax.dynamic_index_in_dim(
        key_value_matrix.reshape(48, 2, 2, 4, HEAD_DIM), rep, 3, keepdims=False
    )
    gap = jnp.zeros((48, 3), BF16)
    small = jnp.concatenate(
        [
            router_weight[:, :5], gap, router_weight[:, 5:], gap, first_gain[:, None], second_gain[:, None],
            jnp.zeros((48, PACK - GAIN_TWO_AT - 1), BF16),
        ],
        1,
    )
    attn_mine = jnp.stack(
        [
            jnp.concatenate([query_mine[:, k], keyval_mine[:, 0, k], keyval_mine[:, 1, k], small], 1)
            for k in range(2)
        ]
    )
    x_all, segment_members, attn, out_slice, choices_traded, dy_traded = gather_start(
        layer_input[0], segment_lines, attn_mine, output_weight, choices_lines, cotangent[0]
    )
    attn = attn.reshape(D, PACK)
    out_slice = out_slice.reshape(QROWS, D)

    frequency = ROPE_BASE ** (-jnp.arange(0, HEAD_DIM, 2, dtype=F32) / HEAD_DIM)
    column_place = (
        (jnp.arange(2, dtype=jnp.int32)[:, None] * PLANE + place) * TOK
        + jnp.arange(TOK, dtype=jnp.int32)[None, :]
    )
    angle = column_place.astype(F32)[:, None, :] * frequency[None, :, None]
    cosine, sine = jnp.cos(angle), jnp.sin(angle)
    query_lines, keyval_lines, normed_lines, turned = project(x_all.reshape(COLUMN, D), attn, cosine, sine)
    gain_one = turned[GAIN_ONE_AT].astype(F32)
    gain_two = turned[GAIN_TWO_AT].astype(F32)
    segment_column = jnp.moveaxis(segment_members[:, 0].reshape(2, 4, TOK), 0, 1)
    segment_column = jnp.concatenate([segment_column, jnp.zeros((4, 6, TOK), jnp.int32)], 1)
    q_here, kv_here, segment_here, x_traded, gate_up_pair, down_pair = to_attention(
        query_lines, keyval_lines, segment_column, layer_input[0], gate_up_mine, down_mine
    )

    segment_all = jnp.moveaxis(segment_here[:, :2], 1, 0).reshape(SEQ)
    earlier = jnp.sum(segment_all[None, :] < jnp.arange(5, dtype=jnp.int32)[:, None], 1, dtype=jnp.int32)
    runs = jnp.stack([x, 7 - x])
    mark = jnp.concatenate(
        [lax.dynamic_slice_in_dim(segment_all, runs[k] * RUN, RUN) for k in range(2)]
    )
    start = jnp.sum(
        jnp.where(mark[None, :] == jnp.arange(5, dtype=jnp.int32)[:, None], earlier[:, None], 0), 0
    )
    first_block = jnp.min(start.reshape(2, RUN), 1) // RUN
    bounds = jnp.concatenate([first_block, runs + 1, runs * RUN, jnp.zeros((2,), jnp.int32)])
    start_lines = jnp.broadcast_to(start[None, :], (8, 2 * RUN))
    o_here, o_low, lse = attend(bounds, q_here, kv_here, start_lines)
    attended_part = dot(o_low, out_slice, (((0,), (0,)), ((), ()))).astype(BF16)
    attended, gate_up, dy_all, choices_all = sum_attended(
        attended_part.reshape(8, TOK, D), gate_up_mine, gate_up_pair, dy_traded, choices_traded
    )

    tokens = x_traded.astype(F32)
    residual = tokens + RESIDUAL_SCALE * attended
    scale_two = rms_scale(residual)
    normed_two = (residual * scale_two * gain_two).astype(BF16)
    normed_two_all, down = gather_normed(normed_two, down_mine, down_pair)

    mixture_part, normed_part, grad_gate_up, grad_down, pull, shares = experts(
        normed_two_all,
        dy_all.reshape(COLUMN, D),
        gate_up,
        down,
        turned[ROUTER_AT : ROUTER_AT + 16],
        choices_all,
    )
    normed_sum, pull_parts, gate_up_sum = sum_experts(
        normed_part.reshape(8, TOK, D), pull, grad_gate_up.reshape(2, 4, 4, 48, 1280)
    )
    grad_residual, grad_lin, grad_logits = residual_grad(
        normed_sum, residual, dy_traded, pull_parts, shares, turned
    )
    grad_lin_all, down_sum = gather_grad(grad_lin, grad_down.reshape(2, 4, 4, 48, 640))
    grad_lin_all = grad_lin_all.reshape(8 * TOK, D)
    do_here = dot(out_slice, grad_lin_all, (((1,), (1,)), ((), ()))).astype(BF16)
    dq_here, dkv_here = attend_back(bounds, q_here, kv_here, do_here, start_lines, o_here, lse)
    grad_out = dot(o_low, grad_lin_all, (((1,), (0,)), ((), ()))).astype(BF16)
    dq_parts, dkv_parts, mixture, grad_residual_back = from_attention(
        dq_here, dkv_here, mixture_part.reshape(8, TOK, D), grad_residual
    )
    layer_out = (residual + RESIDUAL_SCALE * mixture).astype(BF16)

    grad_attn, grad_normed_part = project_grad(
        dq_parts, dkv_parts, normed_lines, turned, normed_two, grad_logits, cosine, sine
    )
    attn_sum, out_parts, grad_normed = sum_planes(
        grad_attn.reshape(2, 4, 4, 48, PACK),
        grad_out.reshape(PLANE, 12, D),
        grad_normed_part.reshape(8, TOK, D),
    )
    out_sum = jnp.sum(out_parts.astype(F32), 0).astype(BF16)
    attn_own, gate_up_own, down_own, out_own, layer_out = final_deal(
        attn_sum, gate_up_sum, down_sum, out_sum, layer_out
    )

    own_tokens = layer_input[0].astype(F32)
    input_grad = grad_residual_back.astype(F32) + norm_back(
        grad_normed, own_tokens, rms_scale(own_tokens), gain_one
    )

    query_grad, keyval_grad, out_grad_rows, router_grad, gate_up_grad, down_grad, gain_grads = assemble(
        attn_own,
        gate_up_own,
        down_own,
        out_own,
        query_weight,
        key_value_matrix,
        router_weight,
        jnp.swapaxes(gate_up_weight, 0, 1),
        jnp.stack([first_gain, second_gain], 1).astype(F32),
    )
    return (
        layer_out[None],
        input_grad[None],
        gain_grads[:, 0],
        query_grad,
        keyval_grad,
        out_grad_rows,
        gain_grads[:, 1],
        router_grad,
        jnp.swapaxes(gate_up_grad, 0, 1),
        jnp.swapaxes(down_grad, 0, 1),
    )


def solution(mesh):
    row = P("shard", None)
    rows = P("shard", None, None)
    own = P("rep", "shard", None)
    in_specs = (own, P("rep", "shard"), own, P("shard"), row, row, row, P("shard"), row, rows, rows, own)
    out_specs = (own, own, P("shard"), row, row, row, P("shard"), row, rows, rows)
    return jax.shard_map(shards, mesh=mesh, in_specs=in_specs, out_specs=out_specs, check_vma=False)
```

```python
import functools

import jax
import jax.numpy as jnp
from jax import lax
from jax.experimental import pallas as pl
from jax.experimental.pallas import tpu as pltpu
from jax.sharding import PartitionSpec as P

D = 1536
HEADS = 8
GROUP = 3
HEAD_DIM = 64
HALF = HEAD_DIM // 2
FF = 512
EXPERTS = 10
TOK = 128
SEQ = 4096
PLANE = 16
RUN = 512
QROWS = GROUP * HEAD_DIM
PACK = 384
ROUTER_AT = 320
GAIN_ONE_AT = 336
GAIN_TWO_AT = 337
COLUMN = 8 * TOK
GATE_UP = 1280
EXPERT_PACK = 1920

NORM_EPS = 1e-06
RESIDUAL_SCALE = 0.22
SCORE_SCALE = 0.015625
ROPE_BASE = 10000.0
MASK_FILL = -1e30
PRECISE = lax.Precision.HIGHEST
BF16 = jnp.bfloat16
F32 = jnp.float32
VMEM_LIMIT = 56 * 1024 * 1024


def my_place():
    return lax.axis_index("shard"), lax.axis_index("rep")


def parts_of(shard):
    place = lax.rem(shard, PLANE)
    return shard // PLANE, place, place // 4, lax.rem(place, 4)


def same(one, other):
    return jnp.logical_and(one[0] == other[0], one[1] == other[1])


class Place:
    def __init__(self, me):
        self.me = me
        self.shard, self.rep = me
        self.z_lo, self.place, self.x, self.y = parts_of(self.shard)
        self.core = lax.rem(self.rep, 2)
        self.z = (self.rep // 2) * 2 + self.z_lo
        self.member = self.z_lo * 4 + self.rep

    def device(self, z, x, y, core):
        return lax.rem(z, 2) * PLANE + 4 * x + y, (z // 2) * 2 + core

    def step(self, axis, by):
        z, x, y = self.z, self.x, self.y
        if axis == "z":
            z = lax.rem(z + by, 4)
        elif axis == "x":
            x = lax.rem(x + by, 4)
        else:
            y = lax.rem(y + by, 4)
        return self.device(z, x, y, self.core)

    def sibling(self):
        return self.shard, self.rep + 1 - 2 * self.core

    def partner(self):
        return self.shard + (1 - 2 * self.z_lo) * PLANE, self.rep

    def trader(self):
        return self.z_lo * PLANE + 4 * mirrored(self.z_lo, self.x) + self.rep, self.y

    def member_at(self, z, core):
        return lax.rem(z, 2) * 4 + (z // 2) * 2 + core

    def near(self):
        result = [self.sibling()]
        for axis in ("z", "x", "y"):
            result += [self.step(axis, 1), self.step(axis, 3)]
        return result


def mesh_id(place):
    return {"shard": place[0], "rep": place[1]}


class Net:
    def __init__(self, here, sems):
        self.here, self.sems, self.used, self.sent = here, sems, 0, []

    def take(self, count=1):
        first = self.used
        self.used += count
        return first

    def push(self, source, target, to):
        number = self.take(2)
        copy = pltpu.make_async_remote_copy(
            src_ref=source,
            dst_ref=target,
            send_sem=self.sems.at[number],
            recv_sem=self.sems.at[number + 1],
            device_id=mesh_id(to),
        )
        copy.start()
        self.sent.append(copy)
        return number + 1

    def got(self, number, region):
        pltpu.make_async_remote_copy(
            src_ref=region,
            dst_ref=region,
            send_sem=self.sems.at[number],
            recv_sem=self.sems.at[number],
            device_id=mesh_id(self.here.sibling()),
        ).wait_recv()

    def local(self, source, target):
        copy = pltpu.make_async_copy(source, target, self.sems.at[self.take()])
        copy.start()
        return copy

    def finish(self):
        for copy in self.sent:
            copy.wait_send()


class Route:
    def __init__(self, n, to, source, pieces, index=None, may_be_self=False):
        self.n, self.to, self.source, self.pieces = n, to, source, pieces
        self.index = index or (lambda i: i)
        self.may_be_self = may_be_self


def each(n, body):
    if n <= 8:
        for i in range(n):
            body(i)
    else:

        def step(i, carry):
            body(i)
            return carry

        lax.fori_loop(0, n, step, 0)


def greet_routes(routes, me, barrier):
    awaited = 0
    for route in routes:

        def greet(i, route=route):
            source = route.source(i)

            def signal():
                pl.semaphore_signal(barrier, inc=1, device_id=mesh_id(source))

            if route.may_be_self:
                pl.when(jnp.logical_not(same(source, me)))(signal)
            else:
                signal()

        each(route.n, greet)
        awaited = awaited + route.n
        if route.may_be_self:
            for i in range(route.n):
                awaited = awaited - same(route.to(i), me).astype(jnp.int32)
    return awaited


HOP = 2.0


def time_of(ref, rate=50.0):
    size = jnp.dtype(ref.dtype).itemsize / 1000.0
    for extent in ref.shape:
        size *= extent
    return HOP + size / rate


def follow_routes(net, routes, ins, outs, guess=15.0):
    me = net.here.me
    held = []
    for route in routes:
        count = route.n * len(route.pieces)
        held.append((net.take(count), net.take(count), net.take(len(route.pieces))))

    def remote(route, base, i, k, piece):
        source_in, cut, target_out, slot, unused = piece
        return pltpu.make_async_remote_copy(
            src_ref=ins[source_in].at[cut(i)],
            dst_ref=outs[target_out].at[slot(i)],
            send_sem=net.sems.at[base[0] + i * len(route.pieces) + k],
            recv_sem=net.sems.at[base[1] + route.index(i) * len(route.pieces) + k],
            device_id=mesh_id(route.to(i)),
        )

    def within(base, i, k, piece):
        source_in, cut, target_out, slot, unused = piece
        return pltpu.make_async_copy(
            ins[source_in].at[cut(i)], outs[target_out].at[slot(i)], net.sems.at[base[2] + k]
        )

    for route, base in zip(routes, held):

        def start(i, route=route, base=base):
            for k, piece in enumerate(route.pieces):
                copy = remote(route, base, i, k, piece)
                if route.may_be_self:
                    here = same(route.to(i), me)
                    pl.when(jnp.logical_not(here))(copy.start)
                    pl.when(here)(within(base, i, k, piece).start)
                else:
                    copy.start()

        each(route.n, start)
    yield guess
    for route, base in zip(routes, held):

        def arrive(i, route=route, base=base):
            for k, piece in enumerate(route.pieces):
                region = outs[piece[2]].at[piece[4](i)]
                place = route.source(i)
                sem = net.sems.at[base[1] + i * len(route.pieces) + k]
                copy = pltpu.make_async_remote_copy(
                    src_ref=region, dst_ref=region, send_sem=sem, recv_sem=sem, device_id=mesh_id(place)
                )
                if route.may_be_self:
                    pl.when(jnp.logical_not(same(place, me)))(copy.wait_recv)
                else:
                    copy.wait_recv()

        each(route.n, arrive)

        def leave(i, route=route, base=base):
            for k, piece in enumerate(route.pieces):
                copy = remote(route, base, i, k, piece)
                if route.may_be_self:
                    here = same(route.to(i), me)
                    pl.when(jnp.logical_not(here))(copy.wait_send)
                    pl.when(here)(within(base, i, k, piece).wait)
                else:
                    copy.wait_send()

        each(route.n, leave)


def trade(net, pieces, begin=0.0, now=30.0):
    other = net.here.trader()
    here = same(other, net.here.me)
    if begin:
        yield begin
    copies = []
    for source, target in pieces:
        number = net.take(2)
        remote = pltpu.make_async_remote_copy(
            src_ref=source,
            dst_ref=target,
            send_sem=net.sems.at[number],
            recv_sem=net.sems.at[number + 1],
            device_id=mesh_id(other),
        )
        within = pltpu.make_async_copy(source, target, net.sems.at[net.take()])
        pl.when(jnp.logical_not(here))(remote.start)
        pl.when(here)(within.start)
        copies.append((remote, within))
    yield now
    for remote, within in copies:
        pl.when(jnp.logical_not(here))(remote.wait)
        pl.when(here)(within.wait)


def greet_trader(here, barrier):
    other = here.trader()
    away = jnp.logical_not(same(other, here.me))

    @pl.when(away)
    def signal():
        pl.semaphore_signal(barrier, inc=1, device_id=mesh_id(other))

    return away.astype(jnp.int32)


def spread_rows(net, rows, out):
    here = net.here
    ahead = lax.rem(here.x - here.rep + 4, 4)
    pair = lambda k: out.at[pl.ds(2 * k, 2)]
    row_halves = row_half(48)

    def at(by):
        return out.at[lax.rem(here.y + by, 4)]

    def copy(number, source, target, to):
        return pltpu.make_async_remote_copy(
            src_ref=source,
            dst_ref=target,
            send_sem=net.sems.at[number],
            recv_sem=net.sems.at[number + 1],
            device_id=mesh_id(to),
        )

    def come(number, region):
        copy(number, region, region, here.sibling()).wait_recv()

    up, down, right, left = here.step("y", 1), here.step("y", 3), here.step("x", 1), here.step("x", 3)
    numbers = [net.take(2) for k in range(8)]
    keep = pltpu.make_async_copy(rows, at(0), net.sems.at[net.take()])
    first = [copy(numbers[0], rows, at(0), up), copy(numbers[1], rows, at(0), down)]
    second = [
        copy(numbers[2], row_halves(at(3), 0), row_halves(at(3), 0), up),
        copy(numbers[3], row_halves(at(1), 1), row_halves(at(1), 1), down),
    ]
    third = [copy(numbers[4], out, out, right), copy(numbers[5], out, out, left)]
    on_right = copy(numbers[6], pair(0), pair(0), right)
    on_left = copy(numbers[7], pair(1), pair(1), left)

    @pl.when(ahead == 0)
    def begin():
        keep.start()
        first[0].start()
        first[1].start()

    now = time_of(rows)
    yield now

    @pl.when(ahead == 0)
    def hand_on():
        come(numbers[0], at(3))
        second[0].start()
        come(numbers[1], at(1))
        second[1].start()

    now += time_of(rows, 100.0)
    yield now

    @pl.when(ahead == 0)
    def go_out():
        come(numbers[2], row_halves(at(2), 0))
        come(numbers[3], row_halves(at(2), 1))
        keep.wait()
        third[0].start()
        third[1].start()

    now += time_of(out, 70.0)
    yield now

    @pl.when(ahead == 1)
    def to_right():
        come(numbers[4], out)
        on_right.start()

    @pl.when(ahead == 3)
    def to_left():
        come(numbers[5], out)
        on_left.start()

    now += time_of(out, 140.0)
    yield now

    @pl.when(ahead == 2)
    def end():
        come(numbers[6], pair(0))
        come(numbers[7], pair(1))

    @pl.when(ahead == 0)
    def sent():
        for each_copy in first + second + third:
            each_copy.wait_send()

    pl.when(ahead == 1)(on_right.wait_send)
    pl.when(ahead == 3)(on_left.wait_send)


def comm(inputs, in_vmem, outputs, scratch, n_sems, collective_id, plan):
    n_in, n_out = len(inputs), len(outputs)

    def kernel(*refs):
        ins, outs = refs[:n_in], refs[n_in : n_in + n_out]
        rest, sems = refs[n_in + n_out : -1], refs[-1]
        net = Net(Place(my_place()), sems)
        flows, routes, near, greetings = plan(net, ins, outs, rest)
        barrier = pltpu.get_barrier_semaphore()
        awaited = greet_routes(routes, net.here.me, barrier)
        if near:
            others = net.here.near()
            for other in others:
                pl.semaphore_signal(barrier, inc=1, device_id=mesh_id(other))
            awaited = awaited + len(others)
        for greeting in greetings:
            awaited = awaited + greeting(net.here, barrier)
        pl.semaphore_wait(barrier, awaited)
        waits = [(0.0, number, flow) for number, flow in enumerate(flows)]
        while waits:
            unused, number, flow = waits.pop(0)
            when = next(flow, None)
            if when is not None:
                waits = sorted(waits + [(when, number, flow)], key=lambda wait: wait[:2])
        net.finish()
        assert net.used <= n_sems, net.used

    vmem = pl.BlockSpec(memory_space=pltpu.VMEM)
    anywhere = pl.BlockSpec(memory_space=pl.ANY)
    return pl.pallas_call(
        kernel,
        out_shape=[jax.ShapeDtypeStruct(s, t) for s, t, unused in outputs],
        in_specs=[vmem if k in in_vmem else anywhere for k in range(n_in)],
        out_specs=[vmem if inside else anywhere for unused, unused2, inside in outputs],
        scratch_shapes=list(scratch) + [pltpu.SemaphoreType.DMA((n_sems,))],
        compiler_params=pltpu.CompilerParams(
            collective_id=collective_id, has_side_effects=True, vmem_limit_bytes=VMEM_LIMIT
        ),
    )(*inputs)


def together(flows):
    waits, now = [(next(flow), number, flow) for number, flow in enumerate(flows)], 0.0
    while waits:
        waits = sorted(waits, key=lambda wait: wait[:2])
        now, number, flow = waits.pop(0)
        yield now
        when = next(flow, None)
        if when is not None:
            waits.append((when, number, flow))
    return now


def column_gather(net, source, out, half_of, now=0.0):
    here = net.here

    def slot(by, core):
        return out.at[here.member_at(lax.rem(here.z + by, 4), core)]

    core, other = here.core, 1 - here.core
    right, left, sibling = here.step("z", 1), here.step("z", 3), here.sibling()
    keep = net.local(source, slot(0, core))
    a = net.push(source, slot(0, core), right)
    b = net.push(source, slot(0, core), left)
    s = [net.push(source, slot(0, core), sibling)]
    now += time_of(source)
    yield now
    net.got(a, slot(3, core))
    c = net.push(half_of(slot(3, core), 0), half_of(slot(3, core), 0), right)
    s.append(net.push(slot(3, core), slot(3, core), sibling))
    net.got(b, slot(1, core))
    d = net.push(half_of(slot(1, core), 1), half_of(slot(1, core), 1), left)
    s.append(net.push(slot(1, core), slot(1, core), sibling))
    now += time_of(source, 100.0)
    yield now
    net.got(c, half_of(slot(2, core), 0))
    net.got(d, half_of(slot(2, core), 1))
    s.append(net.push(slot(2, core), slot(2, core), sibling))
    yield now + time_of(source, 200.0)
    for number, by in zip(s, (0, 3, 1, 2)):
        net.got(number, slot(by, other))
    keep.wait()


def row_half(size):
    first = (size // 2 + 15) // 16 * 16

    def half(ref, k):
        return ref.at[pl.ds(0, first)] if k == 0 else ref.at[pl.ds(first, size - first)]

    return half


def ring_gather(net, axis, source, slot, half, now, rate):
    right, left = net.here.step(axis, 1), net.here.step(axis, 3)
    a = net.push(source, slot(0), right)
    b = net.push(source, slot(0), left)
    now += time_of(source, rate)
    yield now
    net.got(a, slot(3))
    c = net.push(half(slot(3), 0), half(slot(3), 0), right)
    net.got(b, slot(1))
    d = net.push(half(slot(1), 1), half(slot(1), 1), left)
    now += time_of(source, 2 * rate)
    yield now
    net.got(c, half(slot(2), 0))
    net.got(d, half(slot(2), 1))
    return now


def swap_pair(net, payload, target, begin, now):
    here = net.here
    yield begin
    number = net.push(payload.at[1 - here.z_lo], target, here.partner())
    yield now
    net.got(number, target)


def plane_gather(net, payload, pair, out, rate=50.0):
    here = net.here
    z, x, y = here.z_lo, here.x, here.y
    rows = row_half(48)
    two = lambda ref, k: ref.at[pl.ds(2 * k, 2)]
    swap = []

    def first():
        if pair is None:
            swap.append(net.push(payload.at[1 - z], out.at[z, x, y], here.partner()))
        keep = net.local(payload.at[z], out.at[z, x, y])
        now = yield from ring_gather(
            net, "x", payload.at[z], lambda by: out.at[z, lax.rem(x + by, 4), y], rows, 0.0, rate
        )
        keep.wait()
        bundle = lambda by: out.at[z, :, lax.rem(y + by, 4)]
        yield from ring_gather(net, "y", bundle(0), bundle, two, now, rate)

    def second():
        w = 1 - z
        now, source = 0.0, pair
        if pair is None:
            now, source = time_of(payload.at[0], rate), out.at[w, x, y]
            yield now
            net.got(swap[0], source)
        else:
            keep = net.local(pair, out.at[w, x, y])
        now = yield from ring_gather(
            net, "y", source, lambda by: out.at[w, x, lax.rem(y + by, 4)], rows, now, rate
        )
        if pair is not None:
            keep.wait()
        bundle = lambda by: out.at[w, lax.rem(x + by, 4)]
        yield from ring_gather(net, "x", bundle(0), bundle, two, now, rate)

    return [first(), second()]


def add(target, *parts):
    total = parts[0][...].astype(F32)
    for part in parts[1:]:
        total = total + part[...].astype(F32)
    target[...] = total.astype(target.dtype)


def ring_sum(net, axis, block, half, halves, wholes, target, now, rate=50.0):
    right, left = net.here.step(axis, 1), net.here.step(axis, 3)
    lower, upper = halves
    a = net.push(half(block(2), 0), lower, right)
    b = net.push(half(block(2), 1), upper, left)
    now += time_of(lower, rate)
    yield now
    net.got(a, lower)
    add(half(block(1), 0), half(block(1), 0), lower)
    c = net.push(block(1), wholes[0], right)
    net.got(b, upper)
    add(half(block(3), 1), half(block(3), 1), upper)
    d = net.push(block(3), wholes[1], left)
    now += time_of(wholes[0], rate)
    yield now
    net.got(c, wholes[0])
    net.got(d, wholes[1])
    add(target, block(0), wholes[0], wholes[1])
    return now


def column_sum(net, parts, out, sums, sibling_parts, halves, wholes, now=0.0):
    here = net.here
    half = row_half(parts.shape[1])
    at = lambda by: lax.rem(here.z + by, 4)
    numbers = {}
    for by in (2, 1, 3, 0):
        numbers[by] = net.push(
            parts.at[here.member_at(at(by), 1 - here.core)], sibling_parts.at[at(by)], here.sibling()
        )
    now += HOP
    for by in (2, 1, 3):
        now += time_of(sums.at[0], 200.0) - HOP
        yield now
        net.got(numbers[by], sibling_parts.at[at(by)])
        add(sums.at[at(by)], parts.at[here.member_at(at(by), here.core)], sibling_parts.at[at(by)])
        if by == 2:
            ring = ring_sum(
                net, "z", lambda by: sums.at[at(by)], half, (halves.at[0], halves.at[1]),
                (wholes.at[0], wholes.at[1]), out, now,
            )
            when = next(ring)
    net.got(numbers[0], sibling_parts.at[at(0)])
    add(sums.at[at(0)], parts.at[here.member_at(at(0), here.core)], sibling_parts.at[at(0)])
    yield when
    now = yield from ring
    return now


def column_sum_scratch(rows, columns):
    return [
        pltpu.VMEM((4, rows, columns), BF16),
        pltpu.VMEM((4, rows, columns), BF16),
        pltpu.VMEM((2, rows // 2, columns), BF16),
        pltpu.VMEM((2, rows, columns), BF16),
    ]


def plane_sum(net, parts, out, held, pairs, bundles, rows_a, rows_b, blocks, rate=50.0, now=2.0):
    here = net.here
    at_x = lambda by: lax.rem(here.x + by, 4)
    at_y = lambda by: lax.rem(here.y + by, 4)
    pair = lambda ref, k: ref.at[pl.ds(2 * k, 2)]
    half = row_half(48)

    def first():
        if parts is not None:
            copy = net.local(parts.at[0], held.at[0])
            yield now
            copy.wait()
        mine = held.at[0, :, here.y]
        then = yield from ring_sum(
            net, "y", lambda by: held.at[0, :, at_y(by)], pair, (pairs.at[0], pairs.at[1]),
            (bundles.at[0], bundles.at[1]), mine, now, rate,
        )
        yield from ring_sum(
            net, "x", lambda by: held.at[0, at_x(by), here.y], half, (rows_a.at[0], rows_b.at[0]),
            (blocks.at[0], blocks.at[1]), out.at[0], then, rate,
        )

    def second():
        if parts is not None:
            copy = net.local(parts.at[1], held.at[1])
            yield now
            copy.wait()
        mine = held.at[1, here.x]
        then = yield from ring_sum(
            net, "x", lambda by: held.at[1, at_x(by)], pair, (pairs.at[2], pairs.at[3]),
            (bundles.at[2], bundles.at[3]), mine, now, rate,
        )
        yield from ring_sum(
            net, "y", lambda by: held.at[1, here.x, at_y(by)], half, (rows_a.at[1], rows_b.at[1]),
            (blocks.at[2], blocks.at[3]), out.at[1], then, rate,
        )

    return [first(), second()]


def plane_sum_scratch(columns):
    return [
        pltpu.VMEM((2, 4, 4, 48, columns), BF16),
        pltpu.VMEM((4, 2, 48, columns), BF16),
        pltpu.VMEM((4, 4, 48, columns), BF16),
        pltpu.VMEM((2, 32, columns), BF16),
        pltpu.VMEM((2, 16, columns), BF16),
        pltpu.VMEM((4, 48, columns), BF16),
    ]


def column_deal(net, parts, out, passing, half, now=0.0):
    here = net.here
    z = here.z_lo
    core, other = here.core, 1 - here.core
    lower, upper = passing

    def slot(by, core):
        return out.at[here.member_at(lax.rem(here.z + by, 4), core)]

    right, left, sibling = here.step("z", 1), here.step("z", 3), here.sibling()
    keep = net.local(parts.at[z], slot(0, core))
    e = net.push(half(parts.at[z], 0), lower, right)
    f = net.push(half(parts.at[z], 1), upper, left)
    a = net.push(parts.at[1 - z], slot(0, core), right)
    b = net.push(parts.at[1 - z], slot(0, core), left)
    s = [net.push(parts.at[z], slot(0, core), sibling)]
    now += time_of(parts.at[0])
    yield now
    net.got(e, lower)
    c = net.push(lower, half(slot(3, core), 0), right)
    net.got(f, upper)
    d = net.push(upper, half(slot(1, core), 1), left)
    net.got(a, slot(3, core))
    s.append(net.push(slot(3, core), slot(3, core), sibling))
    net.got(b, slot(1, core))
    s.append(net.push(slot(1, core), slot(1, core), sibling))
    now += time_of(parts.at[0])
    yield now
    net.got(c, half(slot(2, core), 0))
    net.got(d, half(slot(2, core), 1))
    s.append(net.push(slot(2, core), slot(2, core), sibling))
    yield now + HOP
    for number, by in zip(s, (0, 3, 1, 2)):
        net.got(number, slot(by, other))
    keep.wait()


def column_route(me, pieces):
    z, place, unused, unused2 = parts_of(me[0])
    mine = z * 4 + me[1]

    def where(member):
        return (member // 4) * PLANE + place, lax.rem(member, 4)

    def after(i):
        return lax.rem(mine + 1 + i, 8)

    def before(i):
        return lax.rem(mine + 7 - i, 8)

    return Route(
        7,
        lambda i: where(after(i)),
        lambda i: where(before(i)),
        [
            (
                a,
                lambda i, cut=cut: cut(after(i)),
                b,
                lambda i, slot=slot: slot(mine),
                lambda i, slot=slot: slot(before(i)),
            )
            for a, cut, b, slot in pieces
        ],
    )


def plane_route(me, pieces):
    z, place, unused, unused2 = parts_of(me[0])

    def after(i):
        return lax.rem(place + 1 + i, PLANE)

    def before(i):
        return lax.rem(place + 15 - i, PLANE)

    return Route(
        15,
        lambda i: (z * PLANE + after(i), me[1]),
        lambda i: (z * PLANE + before(i), me[1]),
        [
            (
                a,
                lambda i, cut=cut: cut(after(i)),
                b,
                lambda i, slot=slot: slot(place),
                lambda i, slot=slot: slot(before(i)),
            )
            for a, cut, b, slot in pieces
        ],
    )


def own_copies(net, ins, outs, copies):
    started = [net.local(ins[a].at[cut], outs[b].at[slot]) for a, cut, b, slot in copies]
    yield 100.0
    for copy in started:
        copy.wait()


ROW_HALF = row_half(TOK)


def mirrored(z, x):
    return x + z * (3 - 2 * x)


def query_routes(me, q_in, q_out):
    z_me, place, x, y = parts_of(me[0])
    base = z_me * PLANE

    def plain(i):
        return lax.rem(y + 1 + i, 4)

    def plain_before(i):
        return lax.rem(y + 3 - i, 4)

    def other(i):
        return lax.rem(y + i, 4)

    def other_before(i):
        return lax.rem(y + 4 - i, 4)

    first = Route(
        3,
        lambda i: (base + 4 * x + plain(i), me[1]),
        lambda i: (base + 4 * x + plain_before(i), me[1]),
        [(q_in, lambda i: (0, plain(i)), q_out, lambda i: (0, y), lambda i: (0, plain_before(i)))],
    )
    second = Route(
        4,
        lambda i: (base + 4 * (3 - x) + other(i), me[1]),
        lambda i: (base + 4 * (3 - x) + other_before(i), me[1]),
        [(q_in, lambda i: (1, other(i)), q_out, lambda i: (1, y), lambda i: (1, other_before(i)))],
    )
    return [first, second], [(q_in, (0, y), q_out, (0, y))]


def begin_layer(x, segments, attn, out_rows, choices, dy, pack, cosine, sine):
    def plan(net, ins, outs, scratch):
        me = net.here.me
        z_me, place, x_at, y_at = parts_of(me[0])
        x_all, attn_all, segment_all, q, kv, ints, normed, linear = scratch
        routes, own = query_routes(me, 0, 0)
        routes = [
            plane_route(
                me,
                [
                    (1, lambda p: (0, lax.rem(p, 4)), 1, lambda p: (0, p)),
                    (1, lambda p: (1, lax.rem(p, 4)), 1, lambda p: (1, p)),
                    (2, lambda p: lax.rem(p, 4), 2, lambda p: p),
                ],
            )
        ] + routes
        own = own + [
            (1, (0, y_at), 1, (0, place)),
            (1, (1, y_at), 1, (1, place)),
            (2, y_at, 2, place),
        ]
        eight = lambda ref, k: ref.at[pl.ds(8 * k, 8)]

        def chain():
            now = yield from together(
                plane_gather(net, ins[2], None, attn_all)
                + [column_gather(net, ins[0], x_all, ROW_HALF), column_gather(net, ins[1], segment_all, eight)]
            )
            project(x_all, attn_all, ins[7], ins[8], q, kv, outs[10], normed, linear)
            for sequence in range(4):
                ints[sequence] = jnp.concatenate(
                    [
                        segment_all[sequence, 0:1, :],
                        segment_all[4 + sequence, 0:1, :],
                        jnp.zeros((6, TOK), jnp.int32),
                    ],
                    0,
                )
            going = follow_routes(net, routes, [q, kv, ints], outs, now + 30.0)
            copies = own_copies(net, [q, kv, ints], outs, own)
            when = next(going)
            next(copies)
            turn_into(outs[9], normed)
            yield when
            for unused in going:
                pass
            for unused in copies:
                pass

        def trade_and_gather():
            yield from trade(net, [(ins[5], outs[5]), (ins[4], outs[4])], 8.0, 36.0)
            yield from together(
                [
                    column_gather(net, outs[5], outs[6], ROW_HALF, 36.0),
                    column_gather(net, outs[4], outs[11], eight, 36.0),
                ]
            )

        flows = [
            chain(),
            spread_rows(net, ins[3], outs[8]),
            trade_and_gather(),
            trade(net, [(ins[0], outs[3])], 20.0, 50.0),
            swap_pair(net, ins[6], outs[7], 20.0, 45.0),
        ]
        return flows, routes, True, [greet_trader]

    return comm(
        [x, segments, attn, out_rows, choices, dy, pack, cosine, sine],
        (7, 8),
        [
            ((2, 4, QROWS, TOK), BF16, False),
            ((2, PLANE, TOK, TOK), BF16, False),
            ((PLANE, 8, TOK), jnp.int32, False),
            ((TOK, D), BF16, False),
            ((16, TOK), jnp.int32, False),
            ((TOK, D), BF16, False),
            ((8, TOK, D), BF16, False),
            ((48, EXPERT_PACK), BF16, False),
            ((4, 48, D), BF16, False),
            ((D, COLUMN), BF16, True),
            ((PACK, D), BF16, True),
            ((8, 16, TOK), jnp.int32, False),
        ],
        [
            pltpu.VMEM((8, TOK, D), BF16),
            pltpu.VMEM((2, 4, 4, 48, PACK), BF16),
            pltpu.VMEM((8, 16, TOK), jnp.int32),
            pltpu.VMEM((2, 4, QROWS, TOK), BF16),
            pltpu.VMEM((2, 4, TOK, TOK), BF16),
            pltpu.VMEM((4, 8, TOK), jnp.int32),
            pltpu.VMEM((COLUMN, D), BF16),
            pltpu.VMEM((ROUTER_AT, COLUMN), F32),
        ],
        256,
        0,
        plan,
    )


def attended_to_experts(parts, pack, pair, x, turned):
    def plan(net, ins, outs, scratch):
        total, held = scratch[0], scratch[1:]

        def chain():
            now = yield from column_sum(net, ins[0], total, *held)
            gain = ins[4][GAIN_TWO_AT : GAIN_TWO_AT + 1, :].astype(F32)
            residual = ins[3][...].astype(F32) + RESIDUAL_SCALE * total[...]
            scale = lax.rsqrt(jnp.sum(residual * residual, -1, keepdims=True) * (1.0 / D) + NORM_EPS)
            outs[0][...] = residual
            outs[1][...] = (residual * scale * gain).astype(BF16)
            yield from column_gather(net, outs[1], outs[2], ROW_HALF, now)

        return plane_gather(net, ins[1], ins[2], outs[3]) + [chain()], [], True, []

    return comm(
        [parts, pack, pair, x, turned],
        (0, 3, 4),
        [
            ((TOK, D), F32, True),
            ((TOK, D), BF16, True),
            ((8, TOK, D), BF16, False),
            ((2, 4, 4, 48, EXPERT_PACK), BF16, False),
        ],
        [pltpu.VMEM((TOK, D), F32)] + column_sum_scratch(TOK, D),
        112,
        2,
        plan,
    )


def experts_to_attention(normed, pull, pack, residual, dy, shares, turned):
    def plan(net, ins, outs, scratch):
        total, low, pulls = scratch[:3]
        routes = [column_route(net.here.me, [(1, lambda m: m, 0, lambda m: m)])]

        def chain():
            pulled = follow_routes(net, routes, ins, [pulls])
            next(pulled)
            own = net.local(ins[1].at[net.here.member], pulls.at[net.here.member])
            now = yield from column_sum(net, ins[0], total, *scratch[3:7])
            for unused in pulled:
                pass
            own.wait()
            residual_grad(total, ins[3], ins[4], pulls, ins[5], ins[6], outs[0], low, outs[1])
            yield from column_gather(net, low, outs[2], ROW_HALF, now)

        flows = [chain()] + plane_sum(net, ins[2], outs[3], *scratch[7:])
        return flows, routes, True, []

    return comm(
        [normed, pull, pack, residual, dy, shares, turned],
        (0, 3, 4, 5, 6),
        [
            ((TOK, D), BF16, True),
            ((16, TOK), F32, True),
            ((8, TOK, D), BF16, False),
            ((2, 48, EXPERT_PACK), BF16, True),
        ],
        [pltpu.VMEM((TOK, D), F32), pltpu.VMEM((TOK, D), BF16), pltpu.VMEM((8, 8, TOK), F32)]
        + column_sum_scratch(TOK, D)
        + plane_sum_scratch(EXPERT_PACK),
        112,
        3,
        plan,
    )


def finish_layer(q, kv, mixture, residual, lines, turned, hn, logits, cosine, sine, o_low, grad_lin, pack, grad):
    def plan(net, ins, outs, scratch):
        me = net.here.me
        z_me, place, x_at, y_at = parts_of(me[0])
        mine = net.here.member
        (dq, dkv, lines_here, grad_lin_here, row_send, row_parts, row_sum, lower, upper, lower_pack, upper_pack,
         attn_sum, grads, rows_of_grads, routed, hn_lines, normed_parts, mixture_sum, low_out) = scratch[:19]
        held = scratch[19:25]
        one_sum, other_sum = scratch[25:29], scratch[29:33]
        routes, own = query_routes(me, 0, 0)
        routes = [plane_route(me, [(1, lambda p: (slice(None), p), 1, lambda p: p)])] + routes
        own = own + [(1, (slice(None), place), 1, place)]
        rows_in = [plane_route(me, [(0, lambda p: p, 0, lambda p: p)])]
        rows_out = [
            Route(
                4,
                lambda i: (4 * mine + place // 4, i),
                lambda i: (
                    (me[0] // 4) // 4 * PLANE + 4 * lax.rem(me[0], 4) + i,
                    lax.rem(me[0] // 4, 4),
                ),
                [(0, lambda i: slice(None), 3, lambda i: lax.rem(place, 4), lambda i: i)],
                index=lambda i: lax.rem(place, 4),
                may_be_self=True,
            ),
        ]
        half = row_half(48)

        def chain():
            loads = [net.local(ins[4], lines_here), net.local(ins[11], grad_lin_here)]
            going = follow_routes(net, routes, [ins[0], ins[1]], [dq, dkv], 25.0)
            copies = own_copies(net, [ins[0], ins[1]], [dq, dkv], own)
            when = next(going)
            next(copies)
            turn_into(hn_lines, ins[6])
            loads[1].wait()
            total = jnp.dot(ins[10][...], grad_lin_here[...], preferred_element_type=F32)
            for k in range(PLANE):
                row_send[k] = total[12 * k : 12 * k + 12].astype(BF16)
            yield when
            for unused in going:
                pass
            for unused in copies:
                pass
            loads[0].wait()
            weight_grads(dq, dkv, lines_here, hn_lines, ins[7], ins[8], ins[9], held[0], grads, routed)
            now = when + 10.0

            def weights():
                then = yield from together(plane_sum(net, None, attn_sum, *held, now=now))
                yield from column_deal(net, attn_sum, outs[1], (lower, upper), half, then)

            def normed():
                normed_grads(grads, rows_of_grads, ins[5], normed_parts)
                yield from column_sum(net, normed_parts, outs[0], *one_sum, now=now + 6.0)

            def rows():
                keep = net.local(row_send.at[place], row_parts.at[place])
                yield from follow_routes(net, rows_in, [row_send], [row_parts], now + 18.0)
                keep.wait()
                total = row_parts[0].astype(F32)
                for k in range(1, PLANE):
                    total = total + row_parts[k].astype(F32)
                row_sum[...] = total.astype(BF16)
                yield from follow_routes(net, rows_out, [row_sum], outs, now + 40.0)

            yield from together([weights(), rows(), normed()])

        def layer_output():
            now = yield from column_sum(net, ins[2], mixture_sum, *other_sum)
            low_out[...] = (ins[3][...] + RESIDUAL_SCALE * mixture_sum[...]).astype(BF16)
            yield from trade(net, [(low_out, outs[4])], 0.0, now + 30.0)

        flows = [
            chain(),
            layer_output(),
            column_deal(net, ins[12], outs[2], (lower_pack, upper_pack), half, 10.0),
            trade(net, [(ins[13], outs[5])], 24.0, 60.0),
        ]
        return flows, routes + rows_in + rows_out, True, [greet_trader]

    return comm(
        [q, kv, mixture, residual, lines, turned, hn, logits, cosine, sine, o_low, grad_lin, pack, grad],
        (2, 3, 5, 6, 7, 8, 9, 10),
        [
            ((TOK, D), F32, True),
            ((8, 48, PACK), BF16, False),
            ((8, 48, EXPERT_PACK), BF16, False),
            ((4, 12, D), BF16, False),
            ((TOK, D), BF16, False),
            ((TOK, D), BF16, False),
        ],
        [
            pltpu.VMEM((2, 4, QROWS, TOK), BF16),
            pltpu.VMEM((PLANE, 2, TOK, TOK), BF16),
            pltpu.VMEM((D, COLUMN), BF16),
            pltpu.VMEM((COLUMN, D), BF16),
            pltpu.VMEM((PLANE, 12, D), BF16),
            pltpu.VMEM((PLANE, 12, D), BF16),
            pltpu.VMEM((12, D), BF16),
            pltpu.VMEM((32, PACK), BF16),
            pltpu.VMEM((16, PACK), BF16),
            pltpu.VMEM((32, EXPERT_PACK), BF16),
            pltpu.VMEM((16, EXPERT_PACK), BF16),
            pltpu.VMEM((2, 48, PACK), BF16),
            pltpu.VMEM((PACK, COLUMN), BF16),
            pltpu.VMEM((COLUMN, PACK), BF16),
            pltpu.VMEM((PACK, TOK), BF16),
            pltpu.VMEM((D, TOK), BF16),
            pltpu.VMEM((8, TOK, D), BF16),
            pltpu.VMEM((TOK, D), F32),
            pltpu.VMEM((TOK, D), BF16),
        ]
        + plane_sum_scratch(PACK)
        + column_sum_scratch(TOK, D)
        + column_sum_scratch(TOK, D),
        320,
        4,
        plan,
    )


NT = (((1,), (1,)), ((), ()))


def product_nt(one, other):
    return lax.dot_general(one, other, NT, preferred_element_type=F32)


def unit(size):
    rows = lax.broadcasted_iota(jnp.int32, (size, size), 0)
    return (rows == lax.broadcasted_iota(jnp.int32, (size, size), 1)).astype(BF16)


def turn_into(target, source, block=256):
    ones = unit(block)

    def step(k, carry):
        place = pl.ds(pl.multiple_of(k * block, block), block)
        target[place, :] = product_nt(ones, source[:, place]).astype(BF16)
        return carry

    lax.fori_loop(0, source.shape[1] // block, step, 0)


def project(x_ref, attn_ref, cos_ref, sin_ref, q_ref, kv_ref, turned_ref, normed, linear):
    ones = unit(PACK)
    for z in range(2):
        weights = attn_ref[z].reshape(D // 2, PACK)
        turned_ref[:, z * (D // 2) : (z + 1) * (D // 2)] = product_nt(ones, weights).astype(BF16)
    gain = turned_ref[GAIN_ONE_AT : GAIN_ONE_AT + 1, :].astype(F32)

    def norm(k, carry):
        place = pl.ds(pl.multiple_of(k * TOK, TOK), TOK)
        values = x_ref[k].astype(F32)
        scale = lax.rsqrt(jnp.sum(values * values, -1, keepdims=True) * (1.0 / D) + NORM_EPS)
        normed[place, :] = (values * scale * gain).astype(BF16)
        return carry

    lax.fori_loop(0, 8, norm, 0)
    for part in range(2):
        place = slice(part * 512, (part + 1) * 512)
        linear[:, place] = product_nt(turned_ref[:ROUTER_AT, :], normed[place, :])
    for z in range(2):
        cosine, sine = cos_ref[z], sin_ref[z]
        for sequence in range(4):
            at = (4 * z + sequence) * TOK
            for head in range(GROUP + 1):
                rows = head * HEAD_DIM
                front = linear[rows : rows + HALF, at : at + TOK]
                behind = linear[rows + HALF : rows + HEAD_DIM, at : at + TOK]
                one = (front * cosine - behind * sine).astype(BF16)
                two = (behind * cosine + front * sine).astype(BF16)
                if head < GROUP:
                    q_ref[z, sequence, rows : rows + HALF, :] = one
                    q_ref[z, sequence, rows + HALF : rows + HEAD_DIM, :] = two
                else:
                    kv_ref[z, sequence, :HALF, :] = one
                    kv_ref[z, sequence, HALF:HEAD_DIM, :] = two
            kv_ref[z, sequence, HEAD_DIM:, :] = linear[QROWS + HEAD_DIM : ROUTER_AT, at : at + TOK].astype(BF16)


def local_kernel(kernel, inputs, smem, anywhere_in, outputs, scratch):
    vmem = pl.BlockSpec(memory_space=pltpu.VMEM)
    anywhere = pl.BlockSpec(memory_space=pl.ANY)
    scalars = pl.BlockSpec(memory_space=pltpu.SMEM)
    return pl.pallas_call(
        kernel,
        out_shape=[jax.ShapeDtypeStruct(shape, dtype) for shape, dtype, unused in outputs],
        in_specs=[
            scalars if k in smem else anywhere if k in anywhere_in else vmem for k in range(len(inputs))
        ],
        out_specs=[vmem if inside else anywhere for unused, unused2, inside in outputs],
        scratch_shapes=scratch,
        compiler_params=pltpu.CompilerParams(vmem_limit_bytes=VMEM_LIMIT),
    )(*inputs)


def experts_kernel(
    hn_any, dy_any, pack_any, router_ref, choices_ref,
    mixture_any, back_any, grad_any, pull_ref, share_ref,
    hn, dy, pack, hn_lines, dy_lines, hidden, joined, share_rows, pull_rows,
    mixture, back, grad, sems,
):
    gate_up, down = pack.at[:, :GATE_UP], pack.at[:, GATE_UP:]
    z = lax.axis_index("shard") // PLANE
    loads = [
        pltpu.make_async_copy(source, target, sems.at[k])
        for k, (source, target) in enumerate(
            [(hn_any, hn), (pack_any, pack), (dy_any, dy)]
        )
    ]
    for load in loads:
        load.start()
    loads[0].wait()

    row = lax.broadcasted_iota(jnp.int32, (16, TOK), 0)

    def route(block, carry):
        place = pl.ds(pl.multiple_of(block * TOK, TOK), TOK)
        logits = product_nt(router_ref[...], hn[place, :])
        named = choices_ref[block]
        named = named + jnp.where(named >= 5, 3, 0)
        chosen = row == named[0:1]
        for k in range(1, 8):
            chosen = jnp.logical_or(chosen, row == named[k : k + 1])
        logits = jnp.where(chosen, logits, MASK_FILL)
        exponent = jnp.where(chosen, jnp.exp(logits - jnp.max(logits, 0, keepdims=True)), 0.0)
        share_ref[block] = exponent / jnp.sum(exponent, 0, keepdims=True)
        mine = share_ref[block, pl.ds(pl.multiple_of(z * 8, 8), 8), :]
        share_rows[place, :] = mine.T
        return carry

    lax.fori_loop(0, 8, route, 0)
    turn_into(hn_lines, hn)
    for load in loads[1:]:
        load.wait()
    turn_into(dy_lines, dy)

    for expert in range(5):

        def work(block, carry, expert=expert):
            place = pl.ds(pl.multiple_of(block * 512, 512), 512)
            both = jnp.dot(
                hn[place, :], gate_up[:, expert * 256 : expert * 256 + 256], preferred_element_type=F32
            )
            gate, up = both[:, :TOK], both[:, TOK:]
            pulled = RESIDUAL_SCALE * jnp.dot(
                dy[place, :], down[:, expert * TOK : (expert + 1) * TOK], preferred_element_type=F32
            )
            share = share_rows[place, expert : expert + 1]
            sigmoid = 1.0 / (1.0 + jnp.exp(-gate))
            silu = gate * sigmoid
            act = (silu * up).astype(BF16).astype(F32)
            hidden[place, expert * TOK : (expert + 1) * TOK] = (share * act).astype(BF16)
            pull_rows[place, expert : expert + 1] = jnp.sum(act * pulled, 1, keepdims=True)
            grad = share * pulled
            joined[place, expert * 256 : expert * 256 + TOK] = (
                grad * up * (sigmoid + silu * (1.0 - sigmoid))
            ).astype(BF16)
            joined[place, expert * 256 + TOK : expert * 256 + 256] = (grad * silu).astype(BF16)
            return carry

        lax.fori_loop(0, 2, work, 0)

    def back_step(k, carry):
        place = pl.ds(pl.multiple_of(k * 256, 256), 256)
        back[:, place] = product_nt(joined[...], gate_up[place, :]).astype(BF16)
        return carry

    lax.fori_loop(0, D // 256, back_step, 0)
    stores = [pltpu.make_async_copy(back, back_any, sems.at[4])]
    stores[0].start()

    def gate_up_step(k, carry):
        place = pl.ds(pl.multiple_of(k * 256, 256), 256)
        grad[:, place] = jnp.dot(
            hn_lines[...], joined[:, place], preferred_element_type=F32
        ).astype(BF16)
        return carry

    lax.fori_loop(0, 5, gate_up_step, 0)

    def mixture_step(k, carry):
        place = pl.ds(pl.multiple_of(k * 256, 256), 256)
        mixture[:, place] = product_nt(hidden[...], down[place, :]).astype(BF16)
        return carry

    lax.fori_loop(0, D // 256, mixture_step, 0)
    stores.append(pltpu.make_async_copy(mixture, mixture_any, sems.at[5]))
    stores[1].start()
    for first, size in ((0, 256), (256, 256), (512, 128)):
        grad[:, GATE_UP + first : GATE_UP + first + size] = (
            RESIDUAL_SCALE
            * jnp.dot(dy_lines[...], hidden[:, first : first + size], preferred_element_type=F32)
        ).astype(BF16)
    stores.append(pltpu.make_async_copy(grad, grad_any, sems.at[6]))
    stores[2].start()

    def turn_pull(block, carry):
        place = pl.ds(pl.multiple_of(block * TOK, TOK), TOK)
        pull_ref[block] = pull_rows[place, :].T
        return carry

    pull_rows[:, 5:8] = jnp.zeros((COLUMN, 3), F32)
    lax.fori_loop(0, 8, turn_pull, 0)
    for store in stores:
        store.wait()


def experts(hn, dy, pack, router, choices):
    wide = lambda rows, columns: pltpu.VMEM((rows, columns), BF16)
    return local_kernel(
        experts_kernel,
        [hn, dy, pack, router, choices],
        (),
        (0, 1, 2),
        [
            ((COLUMN, D), BF16, False),
            ((COLUMN, D), BF16, False),
            ((D, EXPERT_PACK), BF16, False),
            ((8, 8, TOK), F32, True),
            ((8, 16, TOK), F32, True),
        ],
        [
            wide(COLUMN, D), wide(COLUMN, D), wide(D, EXPERT_PACK), wide(D, COLUMN), wide(D, COLUMN),
            wide(COLUMN, 640), wide(COLUMN, GATE_UP), pltpu.VMEM((COLUMN, 8), F32), pltpu.VMEM((COLUMN, 8), F32),
            wide(COLUMN, D), wide(COLUMN, D), wide(D, EXPERT_PACK), pltpu.SemaphoreType.DMA((8,)),
        ],
    )


def residual_grad(
    sum_ref, residual_ref, dy_ref, pull_ref, share_ref, turned_ref, grad_ref, low_ref, logit_ref
):
    shard, rep = my_place()
    mine = (shard // PLANE) * 4 + rep
    shares = share_ref[mine]
    pulls = []
    for z in range(2):
        total = pull_ref[4 * z]
        for k in range(1, 4):
            total = total + pull_ref[4 * z + k]
        pulls.append(total)
    pull = jnp.concatenate(pulls, 0)
    logits = shares * (pull - jnp.sum(shares * pull, 0, keepdims=True))
    logit_ref[...] = logits
    router = turned_ref[ROUTER_AT : ROUTER_AT + 16, :].astype(F32)
    gain = turned_ref[GAIN_TWO_AT : GAIN_TWO_AT + 1, :].astype(F32)
    grad_normed = sum_ref[...] + jnp.dot(logits.T, router, precision=PRECISE, preferred_element_type=F32)
    residual = residual_ref[...]
    scale = lax.rsqrt(jnp.sum(residual * residual, -1, keepdims=True) * (1.0 / D) + NORM_EPS)
    weighted = grad_normed * gain
    mean = jnp.sum(weighted * residual, -1, keepdims=True) * (1.0 / D)
    grad = dy_ref[...].astype(F32) + scale * weighted - residual * (scale * scale * scale * mean)
    grad_ref[...] = grad.astype(BF16)
    low_ref[...] = (RESIDUAL_SCALE * grad).astype(BF16)


def weight_grads(dq_ref, dkv_ref, lines_ref, hn_lines, logit_ref, cos_ref, sin_ref, weight_ref, grads, routed):
    grads[ROUTER_AT:, :] = jnp.zeros((PACK - ROUTER_AT, COLUMN), BF16)
    for z in range(2):
        cosine, sine = cos_ref[z], sin_ref[z]
        for sequence in range(4):
            at = (4 * z + sequence) * TOK
            total = dkv_ref[sequence, z].astype(F32)
            for quarter in range(1, 4):
                total = total + dkv_ref[4 * quarter + sequence, z].astype(F32)
            for head in range(GROUP + 1):
                rows = head * HEAD_DIM
                if head < GROUP:
                    front = dq_ref[z, sequence, rows : rows + HALF, :].astype(F32)
                    behind = dq_ref[z, sequence, rows + HALF : rows + HEAD_DIM, :].astype(F32)
                else:
                    front, behind = total[:HALF], total[HALF:HEAD_DIM]
                grads[rows : rows + HALF, at : at + TOK] = (front * cosine + behind * sine).astype(BF16)
                grads[rows + HALF : rows + HEAD_DIM, at : at + TOK] = (behind * cosine - front * sine).astype(BF16)
            grads[QROWS + HEAD_DIM : ROUTER_AT, at : at + TOK] = total[HEAD_DIM:].astype(BF16)
    routed[...] = jnp.zeros_like(routed)
    routed[ROUTER_AT : ROUTER_AT + 16, :] = logit_ref[...].astype(BF16)

    def weight_step(k, carry):
        place = pl.ds(pl.multiple_of(k * 192, 192), 192)
        total = product_nt(lines_ref[place, :], grads[...]) + product_nt(hn_lines[place, :], routed[...])
        weight_ref[k // 4, lax.rem(k, 4)] = total.astype(BF16).reshape(4, 48, PACK)
        return carry

    lax.fori_loop(0, 8, weight_step, 0)


def normed_grads(grads, rows_of_grads, turned_ref, normed_ref):
    turn_into(rows_of_grads, grads)

    def step(k, carry):
        place = pl.ds(pl.multiple_of(k * 256, 256), 256)
        total = jnp.dot(rows_of_grads[...], turned_ref[:, place], preferred_element_type=F32)
        normed_ref[:, :, place] = total.astype(BF16).reshape(8, TOK, 256)
        return carry

    lax.fori_loop(0, D // 256, step, 0)


def assemble_kernel(
    attn, pack, out_rows, query_weight, keyval_weight, router_weight, gate_up_weight, gains,
    normed_grad, traded_grad, x, turned, traded_out, input_grad, layer_out,
    query_grad, keyval_grad, out_grad, router_grad, gate_up_grad, down_grad, gain_grads,
):
    layer_out[...] = traded_out[...]
    values = x[...].astype(F32)
    scale = lax.rsqrt(jnp.sum(values * values, -1, keepdims=True) * (1.0 / D) + NORM_EPS)
    weighted = normed_grad[...] * turned[GAIN_ONE_AT : GAIN_ONE_AT + 1, :].astype(F32)
    mean = jnp.sum(weighted * values, -1, keepdims=True) * (1.0 / D)
    input_grad[...] = traded_grad[...].astype(F32) + scale * weighted - values * (scale * scale * scale * mean)
    parts = [attn[m].astype(F32) for m in range(HEADS)]
    query = jnp.concatenate([part[:, :QROWS] for part in parts], 1)
    key = jnp.concatenate([part[:, QROWS : QROWS + HEAD_DIM] for part in parts], 1)
    value = jnp.concatenate([part[:, QROWS + HEAD_DIM : ROUTER_AT] for part in parts], 1)
    query_grad[...] = query
    keyval_grad[:, : HEADS * HEAD_DIM] = key
    keyval_grad[:, HEADS * HEAD_DIM :] = value
    router = parts[0]
    for part in parts[1:]:
        router = router + part
    router = jnp.concatenate([router[:, ROUTER_AT : ROUTER_AT + 5], router[:, ROUTER_AT + 8 : ROUTER_AT + 13]], 1)
    router_grad[...] = router
    for k in range(4):
        out_grad[12 * k : 12 * k + 12, :] = out_rows[k].astype(F32)
    first = jnp.sum(query * query_weight[...].astype(F32), 1, keepdims=True)
    half = HEADS * HEAD_DIM
    first = first + jnp.sum(key * keyval_weight[:, :half].astype(F32), 1, keepdims=True)
    first = first + jnp.sum(value * keyval_weight[:, half:].astype(F32), 1, keepdims=True)
    second = jnp.sum(router * router_weight[...].astype(F32), 1, keepdims=True)
    for expert in range(EXPERTS):
        z, local = expert // 5, expert % 5
        rows = []
        for side in range(2):
            at = local * 256 + side * TOK
            rows += [pack[4 * z + q, :, at : at + TOK].astype(F32) for q in range(4)]
        whole = jnp.concatenate(rows, 1)
        gate_up_grad[expert] = whole
        second = second + jnp.sum(whole * gate_up_weight[expert].astype(F32), 1, keepdims=True)
        at = GATE_UP + local * TOK
        down_grad[expert] = jnp.concatenate(
            [pack[4 * z + q, :, at : at + TOK].astype(F32) for q in range(4)], 1
        )
    gain_grads[:, 0:1] = first / gains[:, 0:1]
    gain_grads[:, 1:2] = second / gains[:, 1:2]


def assemble(*inputs):
    shapes = [(48, D), (48, 1024), (48, D), (48, EXPERTS), (EXPERTS, 48, 2 * FF), (EXPERTS, 48, FF), (48, 2)]
    outputs = [((TOK, D), F32, True), ((TOK, D), BF16, True)] + [(shape, F32, True) for shape in shapes]
    return local_kernel(assemble_kernel, inputs, (), (), outputs, [])


def unpack_queries(source, target):
    for run in range(2):
        for part in range(4):
            target[:, run * RUN + part * TOK : run * RUN + (part + 1) * TOK] = source[run, part]


def unpack_keys(kv_ref, key_rows, value_lines):
    def step(j, carry):
        place = pl.ds(pl.multiple_of(j * TOK, TOK), TOK)
        block = kv_ref[j // PLANE, lax.rem(j, PLANE)]
        key_rows[place, :] = block[:HEAD_DIM].astype(F32).T.astype(BF16)
        value_lines[:, place] = block[HEAD_DIM:]
        return carry

    lax.fori_loop(0, SEQ // TOK, step, 0)


def visible_block(block, start, query):
    key = block * RUN + lax.broadcasted_iota(jnp.int32, (RUN, RUN), 0)
    return jnp.logical_and(key >= start, key <= query)


def attend_kernel(bounds, q_ref, kv_ref, start_ref, o_ref, low_ref, lse_ref, queries, key_rows, value_lines):
    unpack_queries(q_ref, queries)
    unpack_keys(kv_ref, key_rows, value_lines)
    for run in range(2):
        cols = slice(run * RUN, (run + 1) * RUN)
        start = start_ref[0:1, cols]
        query = bounds[4 + run] + lax.broadcasted_iota(jnp.int32, (1, RUN), 1)
        heads = [
            queries[h * HEAD_DIM : (h + 1) * HEAD_DIM, cols] * jnp.asarray(SCORE_SCALE, BF16)
            for h in range(GROUP)
        ]

        def step(block, carry):
            place = pl.ds(pl.multiple_of(block * RUN, RUN), RUN)
            keys, values = key_rows[place, :], value_lines[:, place]
            seen = visible_block(block, start, query)
            result = []
            for h in range(GROUP):
                peak, total, acc = carry[3 * h : 3 * h + 3]
                scores = jnp.dot(keys, heads[h], preferred_element_type=F32)
                scores = jnp.where(seen, scores, MASK_FILL)
                top = jnp.maximum(peak, jnp.max(scores, 0, keepdims=True))
                weights = jnp.exp(scores - top)
                fade = jnp.exp(peak - top)
                total = fade * total + jnp.sum(weights, 0, keepdims=True)
                acc = fade * acc + jnp.dot(values, weights.astype(BF16), preferred_element_type=F32)
                result += [top, total, acc]
            return tuple(result)

        zero = []
        for h in range(GROUP):
            zero += [
                jnp.full((1, RUN), MASK_FILL, F32),
                jnp.zeros((1, RUN), F32),
                jnp.zeros((HEAD_DIM, RUN), F32),
            ]
        done = lax.fori_loop(bounds[run], bounds[2 + run], step, tuple(zero))
        for h in range(GROUP):
            peak, total, acc = done[3 * h : 3 * h + 3]
            rows = slice(h * HEAD_DIM, (h + 1) * HEAD_DIM)
            attended = acc / total
            o_ref[rows, cols] = attended
            low_ref[rows, cols] = attended.astype(BF16)
            lse_ref[h : h + 1, cols] = peak + jnp.log(total)


def attend(bounds, q, kv, start):
    vmem = pl.BlockSpec(memory_space=pltpu.VMEM)
    return pl.pallas_call(
        attend_kernel,
        out_shape=[
            jax.ShapeDtypeStruct((QROWS, 2 * RUN), F32),
            jax.ShapeDtypeStruct((QROWS, 2 * RUN), BF16),
            jax.ShapeDtypeStruct((8, 2 * RUN), F32),
        ],
        in_specs=[pl.BlockSpec(memory_space=pltpu.SMEM), vmem, vmem, vmem],
        out_specs=[vmem, vmem, vmem],
        scratch_shapes=[
            pltpu.VMEM((QROWS, 2 * RUN), BF16),
            pltpu.VMEM((SEQ, HEAD_DIM), BF16),
            pltpu.VMEM((HEAD_DIM, SEQ), BF16),
        ],
        compiler_params=pltpu.CompilerParams(vmem_limit_bytes=VMEM_LIMIT),
    )(bounds, q, kv, start)


def attend_back_kernel(
    bounds, q_ref, kv_ref, grads, start_ref, o_ref, lse_ref, dq_ref, dkv_ref,
    queries, key_rows, value_rows, key_lines, key_grad, value_grad,
):
    unpack_queries(q_ref, queries)
    key_grad[...] = jnp.zeros_like(key_grad)
    value_grad[...] = jnp.zeros_like(value_grad)

    def spread(j, carry):
        place = pl.ds(pl.multiple_of(j * TOK, TOK), TOK)
        block = kv_ref[j // PLANE, lax.rem(j, PLANE)]
        turned = block.astype(F32).T.astype(BF16)
        key_rows[place, :] = turned[:, :HEAD_DIM]
        value_rows[place, :] = turned[:, HEAD_DIM:]
        key_lines[:, place] = block[:HEAD_DIM]
        return carry

    lax.fori_loop(0, SEQ // TOK, spread, 0)
    for run in range(2):
        cols = slice(run * RUN, (run + 1) * RUN)
        start = start_ref[0:1, cols]
        query = bounds[4 + run] + lax.broadcasted_iota(jnp.int32, (1, RUN), 1)
        lse = [lse_ref[h : h + 1, cols] for h in range(GROUP)]
        delta = []
        for h in range(GROUP):
            rows = slice(h * HEAD_DIM, (h + 1) * HEAD_DIM)
            delta.append(jnp.sum(grads[rows, cols].astype(F32) * o_ref[rows, cols], 0, keepdims=True))

        def step(block, carry):
            place = pl.ds(pl.multiple_of(block * RUN, RUN), RUN)
            keys, values, lines = key_rows[place, :], value_rows[place, :], key_lines[:, place]
            seen = visible_block(block, start, query)
            result = []
            dk = key_grad[place, :]
            dv = value_grad[place, :]
            for h in range(GROUP):
                rows = slice(h * HEAD_DIM, (h + 1) * HEAD_DIM)
                q = queries[rows, cols] * jnp.asarray(SCORE_SCALE, BF16)
                do = grads[rows, cols]
                scores = jnp.dot(keys, q, preferred_element_type=F32)
                weights = jnp.exp(jnp.where(seen, scores, MASK_FILL) - lse[h])
                pull = jnp.dot(values, do, preferred_element_type=F32)
                ds = (weights * (pull - delta[h])).astype(BF16)
                dv = dv + lax.dot_general(weights.astype(BF16), do, NT, preferred_element_type=F32)
                dk = dk + lax.dot_general(ds, q, NT, preferred_element_type=F32)
                result.append(carry[h] + jnp.dot(lines, ds, preferred_element_type=F32))
            key_grad[place, :] = dk
            value_grad[place, :] = dv
            return tuple(result)

        done = lax.fori_loop(
            bounds[run], bounds[2 + run], step, tuple(jnp.zeros((HEAD_DIM, RUN), F32) for h in range(GROUP))
        )
        for h in range(GROUP):
            rows = slice(h * HEAD_DIM, (h + 1) * HEAD_DIM)
            scaled = SCORE_SCALE * done[h]
            for part in range(4):
                dq_ref[run, part, rows, :] = scaled[:, part * TOK : (part + 1) * TOK].astype(BF16)

    def gather(j, carry):
        place = pl.ds(pl.multiple_of(j * TOK, TOK), TOK)
        dkv_ref[j // PLANE, lax.rem(j, PLANE), :HEAD_DIM, :] = key_grad[place, :].T.astype(BF16)
        dkv_ref[j // PLANE, lax.rem(j, PLANE), HEAD_DIM:, :] = value_grad[place, :].T.astype(BF16)
        return carry

    lax.fori_loop(0, SEQ // TOK, gather, 0)


def attend_back(bounds, q, kv, do, start, o, lse):
    vmem = pl.BlockSpec(memory_space=pltpu.VMEM)
    return pl.pallas_call(
        attend_back_kernel,
        out_shape=[
            jax.ShapeDtypeStruct((2, 4, QROWS, TOK), BF16),
            jax.ShapeDtypeStruct((2, PLANE, TOK, TOK), BF16),
        ],
        in_specs=[pl.BlockSpec(memory_space=pltpu.SMEM)] + [vmem] * 6,
        out_specs=[vmem, vmem],
        scratch_shapes=[
            pltpu.VMEM((QROWS, 2 * RUN), BF16),
            pltpu.VMEM((SEQ, HEAD_DIM), BF16),
            pltpu.VMEM((SEQ, HEAD_DIM), BF16),
            pltpu.VMEM((HEAD_DIM, SEQ), BF16),
            pltpu.VMEM((SEQ, HEAD_DIM), F32),
            pltpu.VMEM((SEQ, HEAD_DIM), F32),
        ],
        compiler_params=pltpu.CompilerParams(vmem_limit_bytes=VMEM_LIMIT),
    )(bounds, q, kv, do, start, o, lse)


def shards(
    layer_input,
    segments,
    choices,
    first_gain,
    query_weight,
    key_value_matrix,
    output_weight,
    second_gain,
    router_weight,
    gate_up_weight,
    down_weight,
    cotangent,
):
    shard, rep = my_place()
    z, place, x, y = parts_of(shard)
    dot = functools.partial(lax.dot_general, preferred_element_type=F32)

    pad = jnp.zeros((8, TOK), jnp.int32)
    choices_lines = jnp.concatenate([choices[0].T, pad], 0)
    segment_lines = jnp.concatenate([segments, pad, pad[:7]], 0)
    gate_up_mine = lax.dynamic_index_in_dim(
        gate_up_weight.reshape(48, 2, 5, 2, 4, TOK), rep, 4, keepdims=False
    )
    gate_up_mine = jnp.moveaxis(gate_up_mine, 1, 0).reshape(2, 48, 1280)
    down_mine = lax.dynamic_index_in_dim(down_weight.reshape(48, 2, 5, 4, TOK), rep, 3, keepdims=False)
    down_mine = jnp.moveaxis(down_mine, 1, 0).reshape(2, 48, 640)
    expert_mine = jnp.concatenate([gate_up_mine, down_mine], 2)
    query_mine = lax.dynamic_index_in_dim(query_weight.reshape(48, 2, 4, QROWS), rep, 2, keepdims=False)
    keyval_mine = lax.dynamic_index_in_dim(
        key_value_matrix.reshape(48, 2, 2, 4, HEAD_DIM), rep, 3, keepdims=False
    )
    gap = jnp.zeros((48, 3), BF16)
    small = jnp.concatenate(
        [
            router_weight[:, :5], gap, router_weight[:, 5:], gap, first_gain[:, None], second_gain[:, None],
            jnp.zeros((48, PACK - GAIN_TWO_AT - 1), BF16),
        ],
        1,
    )
    attn_mine = jnp.stack(
        [
            jnp.concatenate([query_mine[:, k], keyval_mine[:, 0, k], keyval_mine[:, 1, k], small], 1)
            for k in range(2)
        ]
    )
    frequency = ROPE_BASE ** (-jnp.arange(0, HEAD_DIM, 2, dtype=F32) / HEAD_DIM)
    column_place = (
        (jnp.arange(2, dtype=jnp.int32)[:, None] * PLANE + place) * TOK
        + jnp.arange(TOK, dtype=jnp.int32)[None, :]
    )
    angle = column_place.astype(F32)[:, None, :] * frequency[None, :, None]
    cosine, sine = jnp.cos(angle), jnp.sin(angle)
    (
        q_here, kv_here, segment_here, x_traded, choices_traded, dy_traded, dy_all, expert_pair, out_slice,
        normed_lines, turned, choices_all,
    ) = begin_layer(
        layer_input[0], segment_lines, attn_mine, output_weight, choices_lines, cotangent[0], expert_mine,
        cosine, sine,
    )
    out_slice = out_slice.reshape(QROWS, D)

    segment_all = jnp.moveaxis(segment_here[:, :2], 1, 0).reshape(SEQ)
    earlier = jnp.sum(segment_all[None, :] < jnp.arange(5, dtype=jnp.int32)[:, None], 1, dtype=jnp.int32)
    runs = jnp.stack([x, 7 - x])
    mark = jnp.concatenate(
        [lax.dynamic_slice_in_dim(segment_all, runs[k] * RUN, RUN) for k in range(2)]
    )
    start = jnp.sum(
        jnp.where(mark[None, :] == jnp.arange(5, dtype=jnp.int32)[:, None], earlier[:, None], 0), 0
    )
    first_block = jnp.min(start.reshape(2, RUN), 1) // RUN
    bounds = jnp.concatenate([first_block, runs + 1, runs * RUN, jnp.zeros((2,), jnp.int32)])
    start_lines = jnp.broadcast_to(start[None, :], (8, 2 * RUN))
    o_here, o_low, lse = attend(bounds, q_here, kv_here, start_lines)
    attended_part = dot(o_low, out_slice, (((0,), (0,)), ((), ()))).astype(BF16)

    residual, normed_two, normed_two_all, expert_pack = attended_to_experts(
        attended_part.reshape(8, TOK, D), expert_mine, expert_pair, x_traded, turned
    )

    mixture_part, normed_part, grad_pack, pull, shares = experts(
        normed_two_all.reshape(COLUMN, D),
        dy_all.reshape(COLUMN, D),
        expert_pack.reshape(D, EXPERT_PACK),
        turned[ROUTER_AT : ROUTER_AT + 16],
        choices_all,
    )
    grad_residual, grad_logits, grad_lin_all, pack_sum = experts_to_attention(
        normed_part.reshape(8, TOK, D),
        pull,
        grad_pack.reshape(2, 4, 4, 48, EXPERT_PACK),
        residual,
        dy_traded,
        shares,
        turned,
    )
    grad_lin_all = grad_lin_all.reshape(8 * TOK, D)
    do_here = dot(out_slice, grad_lin_all, (((1,), (1,)), ((), ()))).astype(BF16)
    dq_here, dkv_here = attend_back(bounds, q_here, kv_here, do_here, start_lines, o_here, lse)
    grad_normed, attn_own, pack_own, out_own, layer_out, grad_back = finish_layer(
        dq_here, dkv_here, mixture_part.reshape(8, TOK, D), residual, normed_lines, turned, normed_two, grad_logits,
        cosine, sine, o_low, grad_lin_all, pack_sum, grad_residual,
    )
    (
        input_grad, layer_out, query_grad, keyval_grad, out_grad_rows, router_grad, gate_up_grad, down_grad, gain_grads,
    ) = assemble(
        attn_own,
        pack_own,
        out_own,
        query_weight,
        key_value_matrix,
        router_weight,
        jnp.swapaxes(gate_up_weight, 0, 1),
        jnp.stack([first_gain, second_gain], 1).astype(F32),
        grad_normed,
        grad_back,
        layer_input[0],
        turned,
        layer_out,
    )
    return (
        layer_out[None],
        input_grad[None],
        gain_grads[:, 0],
        query_grad,
        keyval_grad,
        out_grad_rows,
        gain_grads[:, 1],
        router_grad,
        jnp.swapaxes(gate_up_grad, 0, 1),
        jnp.swapaxes(down_grad, 0, 1),
    )


def solution(mesh):
    row = P("shard", None)
    rows = P("shard", None, None)
    own = P("rep", "shard", None)
    in_specs = (own, P("rep", "shard"), own, P("shard"), row, row, row, P("shard"), row, rows, rows, own)
    out_specs = (own, own, P("shard"), row, row, row, P("shard"), row, rows, rows)
    return jax.shard_map(shards, mesh=mesh, in_specs=in_specs, out_specs=out_specs, check_vma=False)
```

```python
import jax
import jax.numpy as jnp
from jax import lax
from jax.experimental import pallas as pl
from jax.experimental.pallas import tpu as pltpu
from jax.sharding import PartitionSpec as P

D = 1536
HEADS = 8
GROUP = 3
HEAD_DIM = 64
HALF = HEAD_DIM // 2
FF = 512
EXPERTS = 10
TOK = 128
SEQ = 4096
PLANE = 16
RUN = 512
QROWS = GROUP * HEAD_DIM
PACK = 384
ROUTER_AT = 320
GAIN_ONE_AT = 336
GAIN_TWO_AT = 337
COLUMN = 8 * TOK
GATE_UP = 1280
EXPERT_PACK = 1920

NORM_EPS = 1e-06
RESIDUAL_SCALE = 0.22
SCORE_SCALE = 0.015625
ROPE_BASE = 10000.0
MASK_FILL = -1e30
PRECISE = lax.Precision.HIGHEST
BF16 = jnp.bfloat16
F32 = jnp.float32
VMEM_LIMIT = 56 * 1024 * 1024


def my_place():
    return lax.axis_index("shard"), lax.axis_index("rep")


def parts_of(shard):
    place = lax.rem(shard, PLANE)
    return shard // PLANE, place, place // 4, lax.rem(place, 4)


def same(one, other):
    return jnp.logical_and(one[0] == other[0], one[1] == other[1])


class Place:
    def __init__(self, me):
        self.me = me
        self.shard, self.rep = me
        self.z_lo, self.place, self.x, self.y = parts_of(self.shard)
        self.core = lax.rem(self.rep, 2)
        self.z = (self.rep // 2) * 2 + self.z_lo
        self.member = self.z_lo * 4 + self.rep

    def device(self, z, x, y, core):
        return lax.rem(z, 2) * PLANE + 4 * x + y, (z // 2) * 2 + core

    def step(self, axis, by):
        z, x, y = self.z, self.x, self.y
        if axis == "z":
            z = lax.rem(z + by, 4)
        elif axis == "x":
            x = lax.rem(x + by, 4)
        else:
            y = lax.rem(y + by, 4)
        return self.device(z, x, y, self.core)

    def sibling(self):
        return self.shard, self.rep + 1 - 2 * self.core

    def partner(self):
        return self.shard + (1 - 2 * self.z_lo) * PLANE, self.rep

    def trader(self):
        return self.z_lo * PLANE + 4 * mirrored(self.z_lo, self.x) + self.rep, self.y

    def member_at(self, z, core):
        return lax.rem(z, 2) * 4 + (z // 2) * 2 + core

    def near(self):
        result = [self.sibling()]
        for axis in ("z", "x", "y"):
            result += [self.step(axis, 1), self.step(axis, 3)]
        return result


def mesh_id(place):
    return {"shard": place[0], "rep": place[1]}


class Net:
    def __init__(self, here, sems):
        self.here, self.sems, self.used, self.sent = here, sems, 0, []

    def take(self, count=1):
        first = self.used
        self.used += count
        return first

    def push(self, source, target, to):
        number = self.take(2)
        copy = pltpu.make_async_remote_copy(
            src_ref=source,
            dst_ref=target,
            send_sem=self.sems.at[number],
            recv_sem=self.sems.at[number + 1],
            device_id=mesh_id(to),
        )
        copy.start()
        self.sent.append(copy)
        return number + 1

    def got(self, number, region):
        pltpu.make_async_remote_copy(
            src_ref=region,
            dst_ref=region,
            send_sem=self.sems.at[number],
            recv_sem=self.sems.at[number],
            device_id=mesh_id(self.here.sibling()),
        ).wait_recv()

    def local(self, source, target):
        copy = pltpu.make_async_copy(source, target, self.sems.at[self.take()])
        copy.start()
        return copy

    def finish(self):
        for copy in self.sent:
            copy.wait_send()


class Route:
    def __init__(self, n, to, source, pieces, index=None, may_be_self=False):
        self.n, self.to, self.source, self.pieces = n, to, source, pieces
        self.index = index or (lambda i: i)
        self.may_be_self = may_be_self


def each(n, body):
    if n <= 8:
        for i in range(n):
            body(i)
    else:

        def step(i, carry):
            body(i)
            return carry

        lax.fori_loop(0, n, step, 0)


def greet_routes(routes, me, barrier):
    awaited = 0
    for route in routes:

        def greet(i, route=route):
            source = route.source(i)

            def signal():
                pl.semaphore_signal(barrier, inc=1, device_id=mesh_id(source))

            if route.may_be_self:
                pl.when(jnp.logical_not(same(source, me)))(signal)
            else:
                signal()

        each(route.n, greet)
        awaited = awaited + route.n
        if route.may_be_self:
            for i in range(route.n):
                awaited = awaited - same(route.to(i), me).astype(jnp.int32)
    return awaited


HOP = 2.0


def time_of(ref, rate=50.0):
    size = jnp.dtype(ref.dtype).itemsize / 1000.0
    for extent in ref.shape:
        size *= extent
    return HOP + size / rate


def follow_routes(net, routes, ins, outs, guess=15.0):
    me = net.here.me
    held = []
    for route in routes:
        count = route.n * len(route.pieces)
        held.append((net.take(count), net.take(count), net.take(len(route.pieces))))

    def remote(route, base, i, k, piece):
        source_in, cut, target_out, slot, unused = piece
        return pltpu.make_async_remote_copy(
            src_ref=ins[source_in].at[cut(i)],
            dst_ref=outs[target_out].at[slot(i)],
            send_sem=net.sems.at[base[0] + i * len(route.pieces) + k],
            recv_sem=net.sems.at[base[1] + route.index(i) * len(route.pieces) + k],
            device_id=mesh_id(route.to(i)),
        )

    def within(base, i, k, piece):
        source_in, cut, target_out, slot, unused = piece
        return pltpu.make_async_copy(
            ins[source_in].at[cut(i)], outs[target_out].at[slot(i)], net.sems.at[base[2] + k]
        )

    for route, base in zip(routes, held):

        def start(i, route=route, base=base):
            for k, piece in enumerate(route.pieces):
                copy = remote(route, base, i, k, piece)
                if route.may_be_self:
                    here = same(route.to(i), me)
                    pl.when(jnp.logical_not(here))(copy.start)
                    pl.when(here)(within(base, i, k, piece).start)
                else:
                    copy.start()

        each(route.n, start)
    yield guess
    for route, base in zip(routes, held):

        def arrive(i, route=route, base=base):
            for k, piece in enumerate(route.pieces):
                region = outs[piece[2]].at[piece[4](i)]
                place = route.source(i)
                sem = net.sems.at[base[1] + i * len(route.pieces) + k]
                copy = pltpu.make_async_remote_copy(
                    src_ref=region, dst_ref=region, send_sem=sem, recv_sem=sem, device_id=mesh_id(place)
                )
                if route.may_be_self:
                    pl.when(jnp.logical_not(same(place, me)))(copy.wait_recv)
                else:
                    copy.wait_recv()

        each(route.n, arrive)

        def leave(i, route=route, base=base):
            for k, piece in enumerate(route.pieces):
                copy = remote(route, base, i, k, piece)
                if route.may_be_self:
                    here = same(route.to(i), me)
                    pl.when(jnp.logical_not(here))(copy.wait_send)
                    pl.when(here)(within(base, i, k, piece).wait)
                else:
                    copy.wait_send()

        each(route.n, leave)


def trade(net, pieces, begin=0.0, now=30.0):
    other = net.here.trader()
    here = same(other, net.here.me)
    if begin:
        yield begin
    copies = []
    for source, target in pieces:
        number = net.take(2)
        remote = pltpu.make_async_remote_copy(
            src_ref=source,
            dst_ref=target,
            send_sem=net.sems.at[number],
            recv_sem=net.sems.at[number + 1],
            device_id=mesh_id(other),
        )
        within = pltpu.make_async_copy(source, target, net.sems.at[net.take()])
        pl.when(jnp.logical_not(here))(remote.start)
        pl.when(here)(within.start)
        copies.append((remote, within))
    yield now
    for remote, within in copies:
        pl.when(jnp.logical_not(here))(remote.wait)
        pl.when(here)(within.wait)


def greet_trader(here, barrier):
    other = here.trader()
    away = jnp.logical_not(same(other, here.me))

    @pl.when(away)
    def signal():
        pl.semaphore_signal(barrier, inc=1, device_id=mesh_id(other))

    return away.astype(jnp.int32)


def spread_rows(net, rows, out):
    here = net.here
    ahead = lax.rem(here.x - here.rep + 4, 4)
    pair = lambda k: out.at[pl.ds(2 * k, 2)]
    row_halves = row_half(48)

    def at(by):
        return out.at[lax.rem(here.y + by, 4)]

    def copy(number, source, target, to):
        return pltpu.make_async_remote_copy(
            src_ref=source,
            dst_ref=target,
            send_sem=net.sems.at[number],
            recv_sem=net.sems.at[number + 1],
            device_id=mesh_id(to),
        )

    def come(number, region):
        copy(number, region, region, here.sibling()).wait_recv()

    up, down, right, left = here.step("y", 1), here.step("y", 3), here.step("x", 1), here.step("x", 3)
    numbers = [net.take(2) for k in range(8)]
    keep = pltpu.make_async_copy(rows, at(0), net.sems.at[net.take()])
    first = [copy(numbers[0], rows, at(0), up), copy(numbers[1], rows, at(0), down)]
    second = [
        copy(numbers[2], row_halves(at(3), 0), row_halves(at(3), 0), up),
        copy(numbers[3], row_halves(at(1), 1), row_halves(at(1), 1), down),
    ]
    third = [copy(numbers[4], out, out, right), copy(numbers[5], out, out, left)]
    on_right = copy(numbers[6], pair(0), pair(0), right)
    on_left = copy(numbers[7], pair(1), pair(1), left)

    @pl.when(ahead == 0)
    def begin():
        keep.start()
        first[0].start()
        first[1].start()

    now = time_of(rows)
    yield now

    @pl.when(ahead == 0)
    def hand_on():
        come(numbers[0], at(3))
        second[0].start()
        come(numbers[1], at(1))
        second[1].start()

    now += time_of(rows, 100.0)
    yield now

    @pl.when(ahead == 0)
    def go_out():
        come(numbers[2], row_halves(at(2), 0))
        come(numbers[3], row_halves(at(2), 1))
        keep.wait()
        third[0].start()
        third[1].start()

    now += time_of(out, 70.0)
    yield now

    @pl.when(ahead == 1)
    def to_right():
        come(numbers[4], out)
        on_right.start()

    @pl.when(ahead == 3)
    def to_left():
        come(numbers[5], out)
        on_left.start()

    now += time_of(out, 140.0)
    yield now

    @pl.when(ahead == 2)
    def end():
        come(numbers[6], pair(0))
        come(numbers[7], pair(1))

    @pl.when(ahead == 0)
    def sent():
        for each_copy in first + second + third:
            each_copy.wait_send()

    pl.when(ahead == 1)(on_right.wait_send)
    pl.when(ahead == 3)(on_left.wait_send)


def comm(inputs, in_vmem, outputs, scratch, n_sems, collective_id, plan):
    n_in, n_out = len(inputs), len(outputs)

    def kernel(*refs):
        ins, outs = refs[:n_in], refs[n_in : n_in + n_out]
        rest, sems = refs[n_in + n_out : -1], refs[-1]
        net = Net(Place(my_place()), sems)
        flows, routes, near, greetings = plan(net, ins, outs, rest)
        barrier = pltpu.get_barrier_semaphore()
        awaited = greet_routes(routes, net.here.me, barrier)
        if near:
            others = net.here.near()
            for other in others:
                pl.semaphore_signal(barrier, inc=1, device_id=mesh_id(other))
            awaited = awaited + len(others)
        for greeting in greetings:
            awaited = awaited + greeting(net.here, barrier)
        pl.semaphore_wait(barrier, awaited)
        waits = [(0.0, number, flow) for number, flow in enumerate(flows)]
        while waits:
            unused, number, flow = waits.pop(0)
            when = next(flow, None)
            if when is not None:
                waits = sorted(waits + [(when, number, flow)], key=lambda wait: wait[:2])
        net.finish()
        assert net.used <= n_sems, net.used

    vmem = pl.BlockSpec(memory_space=pltpu.VMEM)
    anywhere = pl.BlockSpec(memory_space=pl.ANY)
    return pl.pallas_call(
        kernel,
        out_shape=[jax.ShapeDtypeStruct(s, t) for s, t, unused in outputs],
        in_specs=[vmem if k in in_vmem else anywhere for k in range(n_in)],
        out_specs=[vmem if inside else anywhere for unused, unused2, inside in outputs],
        scratch_shapes=list(scratch) + [pltpu.SemaphoreType.DMA((n_sems,))],
        compiler_params=pltpu.CompilerParams(
            collective_id=collective_id, has_side_effects=True, vmem_limit_bytes=VMEM_LIMIT
        ),
    )(*inputs)


def together(flows):
    waits, now = [(next(flow), number, flow) for number, flow in enumerate(flows)], 0.0
    while waits:
        waits = sorted(waits, key=lambda wait: wait[:2])
        now, number, flow = waits.pop(0)
        yield now
        when = next(flow, None)
        if when is not None:
            waits.append((when, number, flow))
    return now


def resumed(when, flow):
    yield when
    yield from flow


def column_gather(net, source, out, half_of, now=0.0):
    here = net.here

    def slot(by, core):
        return out.at[here.member_at(lax.rem(here.z + by, 4), core)]

    core, other = here.core, 1 - here.core
    right, left, sibling = here.step("z", 1), here.step("z", 3), here.sibling()
    keep = net.local(source, slot(0, core))
    a = net.push(source, slot(0, core), right)
    b = net.push(source, slot(0, core), left)
    s = [net.push(source, slot(0, core), sibling)]
    now += time_of(source)
    yield now
    net.got(a, slot(3, core))
    c = net.push(half_of(slot(3, core), 0), half_of(slot(3, core), 0), right)
    s.append(net.push(slot(3, core), slot(3, core), sibling))
    net.got(b, slot(1, core))
    d = net.push(half_of(slot(1, core), 1), half_of(slot(1, core), 1), left)
    s.append(net.push(slot(1, core), slot(1, core), sibling))
    now += time_of(source, 100.0)
    yield now
    net.got(c, half_of(slot(2, core), 0))
    net.got(d, half_of(slot(2, core), 1))
    s.append(net.push(slot(2, core), slot(2, core), sibling))
    yield now + time_of(source, 200.0)
    for number, by in zip(s, (0, 3, 1, 2)):
        net.got(number, slot(by, other))
    keep.wait()


def row_half(size):
    first = (size // 2 + 15) // 16 * 16

    def half(ref, k):
        return ref.at[pl.ds(0, first)] if k == 0 else ref.at[pl.ds(first, size - first)]

    return half


def ring_gather(net, axis, source, slot, half, now, rate):
    right, left = net.here.step(axis, 1), net.here.step(axis, 3)
    a = net.push(source, slot(0), right)
    b = net.push(source, slot(0), left)
    now += time_of(source, rate)
    yield now
    net.got(a, slot(3))
    c = net.push(half(slot(3), 0), half(slot(3), 0), right)
    net.got(b, slot(1))
    d = net.push(half(slot(1), 1), half(slot(1), 1), left)
    now += time_of(source, 2 * rate)
    yield now
    net.got(c, half(slot(2), 0))
    net.got(d, half(slot(2), 1))
    return now


def swap_pair(net, payload, target, begin, now):
    here = net.here
    yield begin
    number = net.push(payload.at[1 - here.z_lo], target, here.partner())
    yield now
    net.got(number, target)


def plane_gather(net, payload, pair, out, rate=50.0, now=0.0):
    here = net.here
    z, x, y = here.z_lo, here.x, here.y
    rows = row_half(48)
    two = lambda ref, k: ref.at[pl.ds(2 * k, 2)]
    swap = []

    def first():
        if pair is None:
            swap.append(net.push(payload.at[1 - z], out.at[z, x, y], here.partner()))
        keep = net.local(payload.at[z], out.at[z, x, y])
        then = yield from ring_gather(
            net, "x", payload.at[z], lambda by: out.at[z, lax.rem(x + by, 4), y], rows, now, rate
        )
        keep.wait()
        bundle = lambda by: out.at[z, :, lax.rem(y + by, 4)]
        yield from ring_gather(net, "y", bundle(0), bundle, two, then, rate)

    def second():
        w = 1 - z
        then, source = now, pair
        if pair is None:
            then, source = now + time_of(payload.at[0], rate), out.at[w, x, y]
            yield then
            net.got(swap[0], source)
        else:
            keep = net.local(pair, out.at[w, x, y])
        then = yield from ring_gather(
            net, "y", source, lambda by: out.at[w, x, lax.rem(y + by, 4)], rows, then, rate
        )
        if pair is not None:
            keep.wait()
        bundle = lambda by: out.at[w, lax.rem(x + by, 4)]
        yield from ring_gather(net, "x", bundle(0), bundle, two, then, rate)

    return [first(), second()]


def add(target, *parts):
    total = parts[0][...].astype(F32)
    for part in parts[1:]:
        total = total + part[...].astype(F32)
    target[...] = total.astype(target.dtype)


def ring_sum(net, axis, block, half, halves, wholes, target, now, rate=50.0):
    right, left = net.here.step(axis, 1), net.here.step(axis, 3)
    lower, upper = halves
    a = net.push(half(block(2), 0), lower, right)
    b = net.push(half(block(2), 1), upper, left)
    now += time_of(lower, rate)
    yield now
    net.got(a, lower)
    add(half(block(1), 0), half(block(1), 0), lower)
    c = net.push(block(1), wholes[0], right)
    net.got(b, upper)
    add(half(block(3), 1), half(block(3), 1), upper)
    d = net.push(block(3), wholes[1], left)
    now += time_of(wholes[0], rate)
    yield now
    net.got(c, wholes[0])
    net.got(d, wholes[1])
    add(target, block(0), wholes[0], wholes[1])
    return now


def column_sum(net, parts, out, sums, sibling_parts, halves, wholes, now=0.0):
    here = net.here
    half = row_half(parts.shape[1])
    at = lambda by: lax.rem(here.z + by, 4)
    numbers = {}
    for by in (2, 1, 3, 0):
        numbers[by] = net.push(
            parts.at[here.member_at(at(by), 1 - here.core)], sibling_parts.at[at(by)], here.sibling()
        )
    now += HOP
    for by in (2, 1, 3):
        now += time_of(sums.at[0], 200.0) - HOP
        yield now
        net.got(numbers[by], sibling_parts.at[at(by)])
        add(sums.at[at(by)], parts.at[here.member_at(at(by), here.core)], sibling_parts.at[at(by)])
        if by == 2:
            ring = ring_sum(
                net, "z", lambda by: sums.at[at(by)], half, (halves.at[0], halves.at[1]),
                (wholes.at[0], wholes.at[1]), out, now,
            )
            when = next(ring)
    net.got(numbers[0], sibling_parts.at[at(0)])
    add(sums.at[at(0)], parts.at[here.member_at(at(0), here.core)], sibling_parts.at[at(0)])
    yield when
    now = yield from ring
    return now


def column_sum_rows(net, parts, out, scratch, k, now):
    sums, sibling_parts, halves, wholes = scratch
    rows, half_rows = pl.ds(k * 64, 64), pl.ds(k * 32, 32)
    now = yield from column_sum(
        net, parts.at[:, rows], out.at[rows], sums.at[:, rows], sibling_parts.at[:, rows], halves.at[:, half_rows],
        wholes.at[:, rows], now=now,
    )
    return now


def column_sum_scratch(rows, columns):
    return [
        pltpu.VMEM((4, rows, columns), BF16),
        pltpu.VMEM((4, rows, columns), BF16),
        pltpu.VMEM((2, rows // 2, columns), BF16),
        pltpu.VMEM((2, rows, columns), BF16),
    ]


def plane_sum(net, parts, out, held, pairs, bundles, rows_a, rows_b, blocks, rate=50.0, now=2.0):
    here = net.here
    at_x = lambda by: lax.rem(here.x + by, 4)
    at_y = lambda by: lax.rem(here.y + by, 4)
    pair = lambda ref, k: ref.at[pl.ds(2 * k, 2)]
    half = row_half(48)

    def first():
        if parts is not None:
            copy = net.local(parts.at[0], held.at[0])
            yield now
            copy.wait()
        mine = held.at[0, :, here.y]
        then = yield from ring_sum(
            net, "y", lambda by: held.at[0, :, at_y(by)], pair, (pairs.at[0], pairs.at[1]),
            (bundles.at[0], bundles.at[1]), mine, now, rate,
        )
        yield from ring_sum(
            net, "x", lambda by: held.at[0, at_x(by), here.y], half, (rows_a.at[0], rows_b.at[0]),
            (blocks.at[0], blocks.at[1]), out.at[0], then, rate,
        )

    def second():
        if parts is not None:
            copy = net.local(parts.at[1], held.at[1])
            yield now
            copy.wait()
        mine = held.at[1, here.x]
        then = yield from ring_sum(
            net, "x", lambda by: held.at[1, at_x(by)], pair, (pairs.at[2], pairs.at[3]),
            (bundles.at[2], bundles.at[3]), mine, now, rate,
        )
        yield from ring_sum(
            net, "y", lambda by: held.at[1, here.x, at_y(by)], half, (rows_a.at[1], rows_b.at[1]),
            (blocks.at[2], blocks.at[3]), out.at[1], then, rate,
        )

    return [first(), second()]


def plane_sum_scratch(columns):
    return [
        pltpu.VMEM((2, 4, 4, 48, columns), BF16),
        pltpu.VMEM((4, 2, 48, columns), BF16),
        pltpu.VMEM((4, 4, 48, columns), BF16),
        pltpu.VMEM((2, 32, columns), BF16),
        pltpu.VMEM((2, 16, columns), BF16),
        pltpu.VMEM((4, 48, columns), BF16),
    ]


def column_deal(net, parts, out, passing, half, now=0.0, begin=0.0):
    here = net.here
    z = here.z_lo
    if begin:
        yield begin
        now = max(now, begin)
    core, other = here.core, 1 - here.core
    lower, upper = passing

    def slot(by, core):
        return out.at[here.member_at(lax.rem(here.z + by, 4), core)]

    right, left, sibling = here.step("z", 1), here.step("z", 3), here.sibling()
    keep = net.local(parts.at[z], slot(0, core))
    e = net.push(half(parts.at[z], 0), lower, right)
    f = net.push(half(parts.at[z], 1), upper, left)
    a = net.push(parts.at[1 - z], slot(0, core), right)
    b = net.push(parts.at[1 - z], slot(0, core), left)
    s = [net.push(parts.at[z], slot(0, core), sibling)]
    now += time_of(parts.at[0])
    yield now
    net.got(e, lower)
    c = net.push(lower, half(slot(3, core), 0), right)
    net.got(f, upper)
    d = net.push(upper, half(slot(1, core), 1), left)
    net.got(a, slot(3, core))
    s.append(net.push(slot(3, core), slot(3, core), sibling))
    net.got(b, slot(1, core))
    s.append(net.push(slot(1, core), slot(1, core), sibling))
    now += time_of(parts.at[0])
    yield now
    net.got(c, half(slot(2, core), 0))
    net.got(d, half(slot(2, core), 1))
    s.append(net.push(slot(2, core), slot(2, core), sibling))
    yield now + HOP
    for number, by in zip(s, (0, 3, 1, 2)):
        net.got(number, slot(by, other))
    keep.wait()


def column_route(me, pieces):
    z, place, unused, unused2 = parts_of(me[0])
    mine = z * 4 + me[1]

    def where(member):
        return (member // 4) * PLANE + place, lax.rem(member, 4)

    def after(i):
        return lax.rem(mine + 1 + i, 8)

    def before(i):
        return lax.rem(mine + 7 - i, 8)

    return Route(
        7,
        lambda i: where(after(i)),
        lambda i: where(before(i)),
        [
            (
                a,
                lambda i, cut=cut: cut(after(i)),
                b,
                lambda i, slot=slot: slot(mine),
                lambda i, slot=slot: slot(before(i)),
            )
            for a, cut, b, slot in pieces
        ],
    )


def plane_route(me, pieces):
    z, place, unused, unused2 = parts_of(me[0])

    def after(i):
        return lax.rem(place + 1 + i, PLANE)

    def before(i):
        return lax.rem(place + 15 - i, PLANE)

    return Route(
        15,
        lambda i: (z * PLANE + after(i), me[1]),
        lambda i: (z * PLANE + before(i), me[1]),
        [
            (
                a,
                lambda i, cut=cut: cut(after(i)),
                b,
                lambda i, slot=slot: slot(place),
                lambda i, slot=slot: slot(before(i)),
            )
            for a, cut, b, slot in pieces
        ],
    )


def own_copies(net, ins, outs, copies):
    started = [net.local(ins[a].at[cut], outs[b].at[slot]) for a, cut, b, slot in copies]
    yield 100.0
    for copy in started:
        copy.wait()


ROW_HALF = row_half(TOK)


def mirrored(z, x):
    return x + z * (3 - 2 * x)


def query_routes(me, q_in, q_out):
    z_me, place, x, y = parts_of(me[0])
    base = z_me * PLANE

    def plain(i):
        return lax.rem(y + 1 + i, 4)

    def plain_before(i):
        return lax.rem(y + 3 - i, 4)

    def other(i):
        return lax.rem(y + i, 4)

    def other_before(i):
        return lax.rem(y + 4 - i, 4)

    first = Route(
        3,
        lambda i: (base + 4 * x + plain(i), me[1]),
        lambda i: (base + 4 * x + plain_before(i), me[1]),
        [(q_in, lambda i: (0, plain(i)), q_out, lambda i: (0, y), lambda i: (0, plain_before(i)))],
    )
    second = Route(
        4,
        lambda i: (base + 4 * (3 - x) + other(i), me[1]),
        lambda i: (base + 4 * (3 - x) + other_before(i), me[1]),
        [(q_in, lambda i: (1, other(i)), q_out, lambda i: (1, y), lambda i: (1, other_before(i)))],
    )
    return [first, second], [(q_in, (0, y), q_out, (0, y))]


def forward(x, segments, attn, out_rows, choices, dy, pack, cosine, sine):
    def plan(net, ins, outs, scratch):
        here = net.here
        me = here.me
        place, x_at, y_at = here.place, here.x, here.y
        (x_all, attn_all, segment_all, q, kv, ints, normed, linear, out_slice, x_traded, pair, low_rows, parts,
         total) = scratch[:14]
        attending, summing = scratch[14:20], scratch[20:24]
        (q_here, kv_here, starts, o_here, o_low, lse, lines, turned, residual, own_normed, normed_all, pack_all,
         dy_all, choices_all, dy_traded, choices_traded, out_given) = outs[:17]
        segment_here = scratch[24]
        routes, own = query_routes(me, 0, 0)
        routes = [
            plane_route(
                me,
                [
                    (1, lambda p: (0, lax.rem(p, 4)), 1, lambda p: (0, p)),
                    (1, lambda p: (1, lax.rem(p, 4)), 1, lambda p: (1, p)),
                    (2, lambda p: lax.rem(p, 4), 2, lambda p: p),
                ],
            )
        ] + routes
        own = own + [
            (1, (0, y_at), 1, (0, place)),
            (1, (1, y_at), 1, (1, place)),
            (2, y_at, 2, place),
        ]
        segment_routes = [column_route(me, [(0, lambda m: slice(None), 0, lambda m: m)])]
        eight = lambda ref, k: ref.at[pl.ds(8 * k, 8)]
        spreading = spread_rows(net, ins[3], out_slice)
        trading = trade(net, [(ins[0], x_traded)], 45.0, 66.0)

        def chain():
            marked = follow_routes(net, segment_routes, [ins[1]], [segment_all])
            next(marked)
            own_mark = net.local(ins[1], segment_all.at[here.member])
            now = yield from together(
                plane_gather(net, ins[2], None, attn_all) + [column_gather(net, ins[0], x_all, ROW_HALF)]
            )
            for unused in marked:
                pass
            own_mark.wait()
            project(x_all, attn_all, ins[7], ins[8], q, kv, turned, normed, linear)
            for sequence in range(4):
                ints[sequence] = jnp.concatenate(
                    [
                        segment_all[sequence, 0:1, :],
                        segment_all[4 + sequence, 0:1, :],
                        jnp.zeros((6, TOK), jnp.int32),
                    ],
                    0,
                )
            targets = [q_here, kv_here, segment_here]
            going = follow_routes(net, routes, [q, kv, ints], targets, now + 22.0)
            copies = own_copies(net, [q, kv, ints], targets, own)
            now = next(going)
            next(copies)
            turn_into(lines, normed)
            yield now
            for unused in going:
                pass
            for unused in copies:
                pass
            document_starts(segment_here, starts, x_at)
            unpack_queries(q_here, attending[0])
            unpack_keys(kv_here, attending[1], attending[2], x_at)
            for third in range(3):

                def step(k, carry):
                    attend_step(x_at, k, *attending[:3], starts, *attending[3:], o_here, o_low, lse)
                    return carry

                lax.fori_loop(3 * third, 3 * third + 3, step, 0)
                now += 7.0
                yield now
            for unused in spreading:
                pass
            turn_into(low_rows, o_low)
            for block in range(4):
                columns = slice(block * 384, (block + 1) * 384)
                weights = out_slice[:, :, columns].reshape(QROWS, 384)
                product = jnp.dot(low_rows[...], weights, preferred_element_type=F32)
                parts[:, :, columns] = product.astype(BF16).reshape(8, TOK, 384)
            given = net.local(out_slice, out_given)

            def tail(k, now):
                rows = pl.ds(k * 64, 64)
                now = yield from column_sum_rows(net, parts, total, summing, k, now)
                for unused in trading:
                    pass
                gain = turned[GAIN_TWO_AT : GAIN_TWO_AT + 1, :].astype(F32)
                hidden = x_traded[rows, :].astype(F32) + RESIDUAL_SCALE * total[rows, :]
                scale = lax.rsqrt(jnp.sum(hidden * hidden, -1, keepdims=True) * (1.0 / D) + NORM_EPS)
                residual[rows, :] = hidden
                own_normed[rows, :] = (hidden * scale * gain).astype(BF16)
                yield from column_gather(net, own_normed.at[rows], normed_all.at[:, rows], row_half(64), now)

            yield from together([tail(0, now + 3.0), tail(1, now + 7.0)])
            given.wait()

        def gather_dy():
            yield from trade(net, [(ins[4], choices_traded), (ins[5], dy_traded)], 0.0, 24.0)
            yield from together(
                [
                    column_gather(net, choices_traded, choices_all, eight, 27.0),
                    column_gather(net, dy_traded, dy_all, ROW_HALF, 27.0),
                ]
            )

        def gather_experts():
            yield from swap_pair(net, ins[6], pair, 22.0, 43.0)
            yield 46.0
            yield from together(plane_gather(net, ins[6], pair, pack_all, rate=30.0, now=46.0))

        flows = [chain(), spreading, gather_dy(), trading, gather_experts()]
        return flows, routes + segment_routes, True, [greet_trader]

    return comm(
        [x, segments, attn, out_rows, choices, dy, pack, cosine, sine],
        (7, 8),
        [
            ((2, 4, QROWS, TOK), BF16, True),
            ((2, PLANE, TOK, TOK), BF16, True),
            ((2, 8, RUN), F32, True),
            ((QROWS, 2 * RUN), F32, True),
            ((QROWS, 2 * RUN), BF16, True),
            ((8, 2 * RUN), F32, True),
            ((D, COLUMN), BF16, True),
            ((PACK, D), BF16, True),
            ((TOK, D), F32, True),
            ((TOK, D), BF16, True),
            ((8, TOK, D), BF16, False),
            ((2, 4, 4, 48, EXPERT_PACK), BF16, False),
            ((8, TOK, D), BF16, False),
            ((8, 16, TOK), jnp.int32, False),
            ((TOK, D), BF16, False),
            ((16, TOK), jnp.int32, False),
            ((4, 48, D), BF16, False),
        ],
        [
            pltpu.VMEM((8, TOK, D), BF16),
            pltpu.VMEM((2, 4, 4, 48, PACK), BF16),
            pltpu.VMEM((8, 8, TOK), jnp.int32),
            pltpu.VMEM((2, 4, QROWS, TOK), BF16),
            pltpu.VMEM((2, 4, TOK, TOK), BF16),
            pltpu.VMEM((4, 8, TOK), jnp.int32),
            pltpu.VMEM((COLUMN, D), BF16),
            pltpu.VMEM((ROUTER_AT, COLUMN), F32),
            pltpu.VMEM((4, 48, D), BF16),
            pltpu.VMEM((TOK, D), BF16),
            pltpu.VMEM((48, EXPERT_PACK), BF16),
            pltpu.VMEM((COLUMN, QROWS), BF16),
            pltpu.VMEM((8, TOK, D), BF16),
            pltpu.VMEM((TOK, D), F32),
        ]
        + attend_scratch()
        + column_sum_scratch(TOK, D)
        + [pltpu.VMEM((PLANE, 8, TOK), jnp.int32)],
        384,
        0,
        plan,
    )


def experts(hn_all, dy_all, pack_all, choices, residual, dy, turned):
    def plan(net, ins, outs, scratch):
        (hn, dy_here, pack, hn_lines, dy_lines, hidden, joined, shares, share_rows, pull_rows, pulls, back, mixture,
         total, low, pull_parts) = scratch[:16]
        summing, held = scratch[16:20], scratch[20:26]
        gate_up, down = pack.at[:, :GATE_UP], pack.at[:, GATE_UP:]
        routes = [column_route(net.here.me, [(0, lambda m: m, 0, lambda m: m)])]
        mixture_out, grad_out, logits_out, low_all, pack_sum = outs

        def z_chain():
            pulled = follow_routes(net, routes, [pulls], [pull_parts])
            next(pulled)
            own = net.local(pulls.at[net.here.member], pull_parts.at[net.here.member])
            now = yield from column_sum(net, back, total, *summing)
            for unused in pulled:
                pass
            own.wait()
            residual_grad(total, ins[4], ins[5], pull_parts, shares, ins[6], grad_out, low, logits_out)
            yield from column_gather(net, low, low_all, ROW_HALF, now)

        def grads():
            def gate_up_step(k, carry):
                place = pl.ds(pl.multiple_of(k * 256, 256), 256)
                product = jnp.dot(hn_lines[...], joined[:, place], preferred_element_type=F32)
                held[0][:, :, :, :, place] = product.astype(BF16).reshape(2, 4, 4, 48, 256)
                return carry

            lax.fori_loop(0, 5, gate_up_step, 0)
            first = pl.ds(0, GATE_UP)
            one = together(plane_sum(net, None, pack_sum.at[:, :, first], *columns_of(held, first), now=6.0))
            one_when = next(one)
            for at, size in ((0, 256), (256, 256), (512, 128)):
                product = RESIDUAL_SCALE * jnp.dot(
                    dy_lines[...], hidden[:, at : at + size], preferred_element_type=F32
                )
                held[0][:, :, :, :, GATE_UP + at : GATE_UP + at + size] = product.astype(BF16).reshape(
                    2, 4, 4, 48, size
                )
            last = pl.ds(GATE_UP, EXPERT_PACK - GATE_UP)
            two = together(plane_sum(net, None, pack_sum.at[:, :, last], *columns_of(held, last), now=20.0))
            two_when = next(two)

            def mixture_step(k, carry):
                place = pl.ds(pl.multiple_of(k * 256, 256), 256)
                product = product_nt(hidden[...], down[place, :])
                mixture[:, :, place] = product.astype(BF16).reshape(8, TOK, 256)
                return carry

            lax.fori_loop(0, D // 256, mixture_step, 0)
            store = net.local(mixture, mixture_out)
            yield from together([resumed(one_when, one), resumed(two_when, two)])
            store.wait()

        def chain():
            experts_forward(
                net, ins[0], ins[1], ins[2], ins[6], ins[3], hn, dy_here, pack, hn_lines, dy_lines, hidden, joined,
                shares, share_rows, pull_rows, pulls, net.here.z_lo,
            )

            def back_step(k, carry):
                place = pl.ds(pl.multiple_of(k * 256, 256), 256)
                product = product_nt(joined[...], gate_up[place, :])
                back[:, :, place] = product.astype(BF16).reshape(8, TOK, 256)
                return carry

            lax.fori_loop(0, D // 256, back_step, 0)
            yield 0.0
            yield from together([z_chain(), grads()])

        return [chain()], routes, True, []

    wide = lambda rows, columns: pltpu.VMEM((rows, columns), BF16)
    return comm(
        [hn_all, dy_all, pack_all, choices, residual, dy, turned],
        (3, 4, 5, 6),
        [
            ((8, TOK, D), BF16, False),
            ((TOK, D), BF16, True),
            ((16, TOK), F32, True),
            ((8, TOK, D), BF16, False),
            ((2, 48, EXPERT_PACK), BF16, True),
        ],
        [
            wide(COLUMN, D), wide(COLUMN, D), wide(D, EXPERT_PACK), wide(D, COLUMN), wide(D, COLUMN),
            wide(COLUMN, 640), wide(COLUMN, GATE_UP), pltpu.VMEM((8, 16, TOK), F32), pltpu.VMEM((COLUMN, 8), F32),
            pltpu.VMEM((COLUMN, 8), F32), pltpu.VMEM((8, 8, TOK), F32), pltpu.VMEM((8, TOK, D), BF16),
            pltpu.VMEM((8, TOK, D), BF16), pltpu.VMEM((TOK, D), F32), wide(TOK, D), pltpu.VMEM((8, 8, TOK), F32),
        ]
        + column_sum_scratch(TOK, D)
        + plane_sum_scratch(EXPERT_PACK),
        144,
        3,
        plan,
    )


def columns_of(refs, columns):
    return [ref.at[(slice(None),) * (len(ref.shape) - 1) + (columns,)] for ref in refs]


def backward(
    q_here, kv_here, mixture, residual, lines, turned, hn, logits, cosine, sine, o_low, grad_lin, pack, grad,
    o_here, lse, starts, out_rows,
):
    def plan(net, ins, outs, scratch):
        me = net.here.me
        place, x_at, y_at = net.here.place, net.here.x, net.here.y
        mine = net.here.member
        (dq, dkv, lines_here, grad_lin_here, row_send, row_parts, row_sum, lower, upper, lower_pack, upper_pack,
         attn_sum, grads, rows_of_grads, routed, hn_lines, normed_parts, mixture_sum, low_out) = scratch[:19]
        held = scratch[19:25]
        one_sum, other_sum = scratch[25:29], scratch[29:33]
        queries, do, key_rows, value_rows, key_lines, key_grad, value_grad, query_grad, delta = scratch[33:42]
        dq_send, dkv_send = scratch[42:44]
        routes, own = query_routes(me, 0, 0)
        routes = [plane_route(me, [(1, lambda p: (slice(None), p), 1, lambda p: p)])] + routes
        own = own + [(1, (slice(None), place), 1, place)]
        rows_in = [plane_route(me, [(0, lambda p: p, 0, lambda p: p)])]
        rows_out = [
            Route(
                4,
                lambda i: (4 * mine + place // 4, i),
                lambda i: (
                    (me[0] // 4) // 4 * PLANE + 4 * lax.rem(me[0], 4) + i,
                    lax.rem(me[0] // 4, 4),
                ),
                [(0, lambda i: slice(None), 3, lambda i: lax.rem(place, 4), lambda i: i)],
                index=lambda i: lax.rem(place, 4),
                may_be_self=True,
            ),
        ]
        half = row_half(48)

        def rows():
            keep = net.local(row_send.at[place], row_parts.at[place])
            yield from follow_routes(net, rows_in, [row_send], [row_parts], 20.0)
            keep.wait()
            total = row_parts[0].astype(F32)
            for k in range(1, PLANE):
                total = total + row_parts[k].astype(F32)
            row_sum[...] = total.astype(BF16)
            yield from follow_routes(net, rows_out, [row_sum], outs, 45.0)

        def chain():
            loads = [net.local(ins[4], lines_here), net.local(ins[11], grad_lin_here)]
            unpack_queries(ins[0], queries)
            spread_keys(ins[1], key_rows, value_rows, key_lines, x_at)
            key_grad[...] = jnp.zeros_like(key_grad)
            value_grad[...] = jnp.zeros_like(value_grad)
            loads[1].wait()
            weights = ins[17][...].reshape(QROWS, D)
            do[...] = product_nt(weights, grad_lin_here[...]).astype(BF16)
            total = jnp.dot(ins[10][...], grad_lin_here[...], preferred_element_type=F32)
            for k in range(PLANE):
                row_send[k] = total[12 * k : 12 * k + 12].astype(BF16)
            row_flow = rows()
            row_when = next(row_flow)
            now = 6.0
            for third in range(3):

                def step(k, carry):
                    attend_back_step(
                        x_at, k, queries, do, ins[14], ins[15], ins[16], key_rows, value_rows, key_lines,
                        key_grad, value_grad, query_grad, delta, dq_send,
                    )
                    return carry

                lax.fori_loop(3 * third, 3 * third + 3, step, 0)
                now += 5.0
                yield now
            collect_keys(key_grad, value_grad, dkv_send)
            going = follow_routes(net, routes, [dq_send, dkv_send], [dq, dkv], now + 22.0)
            copies = own_copies(net, [dq_send, dkv_send], [dq, dkv], own)
            when = next(going)
            next(copies)
            turn_into(hn_lines, ins[6])
            yield row_when
            row_when = next(row_flow)
            yield when
            for unused in going:
                pass
            for unused in copies:
                pass
            loads[0].wait()
            weight_grads(dq, dkv, lines_here, hn_lines, ins[7], ins[8], ins[9], held[0], grads, routed)
            now = when + 10.0

            def weights():
                then = yield from together(plane_sum(net, None, attn_sum, *held, now=now))
                yield from column_deal(net, attn_sum, outs[1], (lower, upper), half, then)

            def normed():
                normed_grads(grads, rows_of_grads, ins[5], normed_parts)
                yield from together(
                    [column_sum_rows(net, normed_parts, outs[0], one_sum, k, now + 6.0 + 4.0 * k) for k in range(2)]
                )

            yield from together([weights(), normed(), resumed(row_when, row_flow)])

        def layer_output():
            now = yield from column_sum(net, ins[2], mixture_sum, *other_sum)
            low_out[...] = (ins[3][...] + RESIDUAL_SCALE * mixture_sum[...]).astype(BF16)
            yield from trade(net, [(low_out, outs[4])], 48.0, 75.0)

        flows = [
            trade(net, [(ins[13], outs[5])], 0.0, 30.0),
            layer_output(),
            chain(),
            column_deal(net, ins[12], outs[2], (lower_pack, upper_pack), half, begin=24.0),
        ]
        return flows, routes + rows_in + rows_out, True, [greet_trader]

    return comm(
        [
            q_here, kv_here, mixture, residual, lines, turned, hn, logits, cosine, sine, o_low, grad_lin, pack, grad,
            o_here, lse, starts, out_rows,
        ],
        (0, 1, 2, 3, 5, 6, 7, 8, 9, 10, 14, 15, 16, 17),
        [
            ((TOK, D), F32, True),
            ((8, 48, PACK), BF16, False),
            ((8, 48, EXPERT_PACK), BF16, False),
            ((4, 12, D), BF16, False),
            ((TOK, D), BF16, False),
            ((TOK, D), BF16, False),
        ],
        [
            pltpu.VMEM((2, 4, QROWS, TOK), BF16),
            pltpu.VMEM((PLANE, 2, TOK, TOK), BF16),
            pltpu.VMEM((D, COLUMN), BF16),
            pltpu.VMEM((COLUMN, D), BF16),
            pltpu.VMEM((PLANE, 12, D), BF16),
            pltpu.VMEM((PLANE, 12, D), BF16),
            pltpu.VMEM((12, D), BF16),
            pltpu.VMEM((32, PACK), BF16),
            pltpu.VMEM((16, PACK), BF16),
            pltpu.VMEM((32, EXPERT_PACK), BF16),
            pltpu.VMEM((16, EXPERT_PACK), BF16),
            pltpu.VMEM((2, 48, PACK), BF16),
            pltpu.VMEM((PACK, COLUMN), BF16),
            pltpu.VMEM((COLUMN, PACK), BF16),
            pltpu.VMEM((PACK, TOK), BF16),
            pltpu.VMEM((D, TOK), BF16),
            pltpu.VMEM((8, TOK, D), BF16),
            pltpu.VMEM((TOK, D), F32),
            pltpu.VMEM((TOK, D), BF16),
        ]
        + plane_sum_scratch(PACK)
        + column_sum_scratch(TOK, D)
        + column_sum_scratch(TOK, D)
        + attend_back_scratch()
        + [pltpu.VMEM((2, 4, QROWS, TOK), BF16), pltpu.VMEM((2, PLANE, TOK, TOK), BF16)],
        384,
        4,
        plan,
    )


NT = (((1,), (1,)), ((), ()))


def product_nt(one, other):
    return lax.dot_general(one, other, NT, preferred_element_type=F32)


def unit(size):
    rows = lax.broadcasted_iota(jnp.int32, (size, size), 0)
    return (rows == lax.broadcasted_iota(jnp.int32, (size, size), 1)).astype(BF16)


def turn_into(target, source, block=256):
    ones = unit(block)

    def step(k, carry):
        place = pl.ds(pl.multiple_of(k * block, block), block)
        target[place, :] = product_nt(ones, source[:, place]).astype(BF16)
        return carry

    lax.fori_loop(0, source.shape[1] // block, step, 0)


def project(x_ref, attn_ref, cos_ref, sin_ref, q_ref, kv_ref, turned_ref, normed, linear):
    ones = unit(PACK)
    for z in range(2):
        weights = attn_ref[z].reshape(D // 2, PACK)
        turned_ref[:, z * (D // 2) : (z + 1) * (D // 2)] = product_nt(ones, weights).astype(BF16)
    gain = turned_ref[GAIN_ONE_AT : GAIN_ONE_AT + 1, :].astype(F32)

    def norm(k, carry):
        place = pl.ds(pl.multiple_of(k * TOK, TOK), TOK)
        values = x_ref[k].astype(F32)
        scale = lax.rsqrt(jnp.sum(values * values, -1, keepdims=True) * (1.0 / D) + NORM_EPS)
        normed[place, :] = (values * scale * gain).astype(BF16)
        return carry

    lax.fori_loop(0, 8, norm, 0)
    for part in range(2):
        place = slice(part * 512, (part + 1) * 512)
        linear[:, place] = product_nt(turned_ref[:ROUTER_AT, :], normed[place, :])
    for z in range(2):
        cosine, sine = cos_ref[z], sin_ref[z]
        for sequence in range(4):
            at = (4 * z + sequence) * TOK
            for head in range(GROUP + 1):
                rows = head * HEAD_DIM
                front = linear[rows : rows + HALF, at : at + TOK]
                behind = linear[rows + HALF : rows + HEAD_DIM, at : at + TOK]
                one = (front * cosine - behind * sine).astype(BF16)
                two = (behind * cosine + front * sine).astype(BF16)
                if head < GROUP:
                    q_ref[z, sequence, rows : rows + HALF, :] = one
                    q_ref[z, sequence, rows + HALF : rows + HEAD_DIM, :] = two
                else:
                    kv_ref[z, sequence, :HALF, :] = one
                    kv_ref[z, sequence, HALF:HEAD_DIM, :] = two
            kv_ref[z, sequence, HEAD_DIM:, :] = linear[QROWS + HEAD_DIM : ROUTER_AT, at : at + TOK].astype(BF16)


def local_kernel(kernel, inputs, smem, anywhere_in, outputs, scratch):
    vmem = pl.BlockSpec(memory_space=pltpu.VMEM)
    anywhere = pl.BlockSpec(memory_space=pl.ANY)
    scalars = pl.BlockSpec(memory_space=pltpu.SMEM)
    return pl.pallas_call(
        kernel,
        out_shape=[jax.ShapeDtypeStruct(shape, dtype) for shape, dtype, unused in outputs],
        in_specs=[
            scalars if k in smem else anywhere if k in anywhere_in else vmem for k in range(len(inputs))
        ],
        out_specs=[vmem if inside else anywhere for unused, unused2, inside in outputs],
        scratch_shapes=scratch,
        compiler_params=pltpu.CompilerParams(vmem_limit_bytes=VMEM_LIMIT),
    )(*inputs)


def experts_forward(
    net, hn_any, dy_any, pack_any, turned_ref, choices_ref, hn, dy, pack, hn_lines, dy_lines, hidden, joined,
    share_ref, share_rows, pull_rows, pull_ref, z,
):
    gate_up, down = pack.at[:, :GATE_UP], pack.at[:, GATE_UP:]
    loads = [net.local(hn_any, hn), net.local(dy_any, dy), net.local(pack_any, pack)]
    loads[0].wait()

    row = lax.broadcasted_iota(jnp.int32, (16, TOK), 0)
    router = turned_ref[ROUTER_AT : ROUTER_AT + 16, :]

    def route(block, carry):
        place = pl.ds(pl.multiple_of(block * TOK, TOK), TOK)
        logits = product_nt(router, hn[place, :])
        named = choices_ref[block]
        named = named + jnp.where(named >= 5, 3, 0)
        chosen = row == named[0:1]
        for k in range(1, 8):
            chosen = jnp.logical_or(chosen, row == named[k : k + 1])
        logits = jnp.where(chosen, logits, MASK_FILL)
        exponent = jnp.where(chosen, jnp.exp(logits - jnp.max(logits, 0, keepdims=True)), 0.0)
        share_ref[block] = exponent / jnp.sum(exponent, 0, keepdims=True)
        mine = share_ref[block, pl.ds(pl.multiple_of(z * 8, 8), 8), :]
        share_rows[place, :] = mine.T
        return carry

    lax.fori_loop(0, 8, route, 0)
    turn_into(hn_lines, hn)
    loads[1].wait()
    turn_into(dy_lines, dy)
    loads[2].wait()

    for expert in range(5):

        def work(block, carry, expert=expert):
            place = pl.ds(pl.multiple_of(block * 512, 512), 512)
            both = jnp.dot(
                hn[place, :], gate_up[:, expert * 256 : expert * 256 + 256], preferred_element_type=F32
            )
            gate, up = both[:, :TOK], both[:, TOK:]
            pulled = RESIDUAL_SCALE * jnp.dot(
                dy[place, :], down[:, expert * TOK : (expert + 1) * TOK], preferred_element_type=F32
            )
            share = share_rows[place, expert : expert + 1]
            sigmoid = 1.0 / (1.0 + jnp.exp(-gate))
            silu = gate * sigmoid
            act = (silu * up).astype(BF16).astype(F32)
            hidden[place, expert * TOK : (expert + 1) * TOK] = (share * act).astype(BF16)
            pull_rows[place, expert : expert + 1] = jnp.sum(act * pulled, 1, keepdims=True)
            grad = share * pulled
            joined[place, expert * 256 : expert * 256 + TOK] = (
                grad * up * (sigmoid + silu * (1.0 - sigmoid))
            ).astype(BF16)
            joined[place, expert * 256 + TOK : expert * 256 + 256] = (grad * silu).astype(BF16)
            return carry

        lax.fori_loop(0, 2, work, 0)

    def turn_pull(block, carry):
        place = pl.ds(pl.multiple_of(block * TOK, TOK), TOK)
        pull_ref[block] = pull_rows[place, :].T
        return carry

    pull_rows[:, 5:8] = jnp.zeros((COLUMN, 3), F32)
    lax.fori_loop(0, 8, turn_pull, 0)


def residual_grad(
    sum_ref, residual_ref, dy_ref, pull_ref, share_ref, turned_ref, grad_ref, low_ref, logit_ref
):
    shard, rep = my_place()
    mine = (shard // PLANE) * 4 + rep
    shares = share_ref[mine]
    pulls = []
    for z in range(2):
        total = pull_ref[4 * z]
        for k in range(1, 4):
            total = total + pull_ref[4 * z + k]
        pulls.append(total)
    pull = jnp.concatenate(pulls, 0)
    logits = shares * (pull - jnp.sum(shares * pull, 0, keepdims=True))
    logit_ref[...] = logits
    router = turned_ref[ROUTER_AT : ROUTER_AT + 16, :].astype(F32)
    gain = turned_ref[GAIN_TWO_AT : GAIN_TWO_AT + 1, :].astype(F32)
    grad_normed = sum_ref[...] + jnp.dot(logits.T, router, precision=PRECISE, preferred_element_type=F32)
    residual = residual_ref[...]
    scale = lax.rsqrt(jnp.sum(residual * residual, -1, keepdims=True) * (1.0 / D) + NORM_EPS)
    weighted = grad_normed * gain
    mean = jnp.sum(weighted * residual, -1, keepdims=True) * (1.0 / D)
    grad = dy_ref[...].astype(F32) + scale * weighted - residual * (scale * scale * scale * mean)
    grad_ref[...] = grad.astype(BF16)
    low_ref[...] = (RESIDUAL_SCALE * grad).astype(BF16)


def weight_grads(dq_ref, dkv_ref, lines_ref, hn_lines, logit_ref, cos_ref, sin_ref, weight_ref, grads, routed):
    grads[ROUTER_AT:, :] = jnp.zeros((PACK - ROUTER_AT, COLUMN), BF16)
    for z in range(2):
        cosine, sine = cos_ref[z], sin_ref[z]
        for sequence in range(4):
            at = (4 * z + sequence) * TOK
            total = dkv_ref[sequence, z].astype(F32)
            for quarter in range(1, 4):
                total = total + dkv_ref[4 * quarter + sequence, z].astype(F32)
            for head in range(GROUP + 1):
                rows = head * HEAD_DIM
                if head < GROUP:
                    front = dq_ref[z, sequence, rows : rows + HALF, :].astype(F32)
                    behind = dq_ref[z, sequence, rows + HALF : rows + HEAD_DIM, :].astype(F32)
                else:
                    front, behind = total[:HALF], total[HALF:HEAD_DIM]
                grads[rows : rows + HALF, at : at + TOK] = (front * cosine + behind * sine).astype(BF16)
                grads[rows + HALF : rows + HEAD_DIM, at : at + TOK] = (behind * cosine - front * sine).astype(BF16)
            grads[QROWS + HEAD_DIM : ROUTER_AT, at : at + TOK] = total[HEAD_DIM:].astype(BF16)
    routed[...] = jnp.zeros_like(routed)
    routed[ROUTER_AT : ROUTER_AT + 16, :] = logit_ref[...].astype(BF16)

    def weight_step(k, carry):
        place = pl.ds(pl.multiple_of(k * 192, 192), 192)
        total = product_nt(lines_ref[place, :], grads[...]) + product_nt(hn_lines[place, :], routed[...])
        weight_ref[k // 4, lax.rem(k, 4)] = total.astype(BF16).reshape(4, 48, PACK)
        return carry

    lax.fori_loop(0, 8, weight_step, 0)


def normed_grads(grads, rows_of_grads, turned_ref, normed_ref):
    turn_into(rows_of_grads, grads)

    def step(k, carry):
        place = pl.ds(pl.multiple_of(k * 256, 256), 256)
        total = jnp.dot(rows_of_grads[...], turned_ref[:, place], preferred_element_type=F32)
        normed_ref[:, :, place] = total.astype(BF16).reshape(8, TOK, 256)
        return carry

    lax.fori_loop(0, D // 256, step, 0)


def assemble_kernel(
    attn, pack, out_rows, query_weight, keyval_weight, router_weight, gate_up_weight, gains,
    normed_grad, traded_grad, x, turned, traded_out, input_grad, layer_out,
    query_grad, keyval_grad, out_grad, router_grad, gate_up_grad, down_grad, gain_grads,
):
    layer_out[...] = traded_out[...]
    values = x[...].astype(F32)
    scale = lax.rsqrt(jnp.sum(values * values, -1, keepdims=True) * (1.0 / D) + NORM_EPS)
    weighted = normed_grad[...] * turned[GAIN_ONE_AT : GAIN_ONE_AT + 1, :].astype(F32)
    mean = jnp.sum(weighted * values, -1, keepdims=True) * (1.0 / D)
    input_grad[...] = traded_grad[...].astype(F32) + scale * weighted - values * (scale * scale * scale * mean)
    parts = [attn[m].astype(F32) for m in range(HEADS)]
    query = jnp.concatenate([part[:, :QROWS] for part in parts], 1)
    key = jnp.concatenate([part[:, QROWS : QROWS + HEAD_DIM] for part in parts], 1)
    value = jnp.concatenate([part[:, QROWS + HEAD_DIM : ROUTER_AT] for part in parts], 1)
    query_grad[...] = query
    keyval_grad[:, : HEADS * HEAD_DIM] = key
    keyval_grad[:, HEADS * HEAD_DIM :] = value
    router = parts[0]
    for part in parts[1:]:
        router = router + part
    router = jnp.concatenate([router[:, ROUTER_AT : ROUTER_AT + 5], router[:, ROUTER_AT + 8 : ROUTER_AT + 13]], 1)
    router_grad[...] = router
    for k in range(4):
        out_grad[12 * k : 12 * k + 12, :] = out_rows[k].astype(F32)
    first = jnp.sum(query * query_weight[...].astype(F32), 1, keepdims=True)
    half = HEADS * HEAD_DIM
    first = first + jnp.sum(key * keyval_weight[:, :half].astype(F32), 1, keepdims=True)
    first = first + jnp.sum(value * keyval_weight[:, half:].astype(F32), 1, keepdims=True)
    second = jnp.sum(router * router_weight[...].astype(F32), 1, keepdims=True)
    for expert in range(EXPERTS):
        z, local = expert // 5, expert % 5
        rows = []
        for side in range(2):
            at = local * 256 + side * TOK
            rows += [pack[4 * z + q, :, at : at + TOK].astype(F32) for q in range(4)]
        whole = jnp.concatenate(rows, 1)
        gate_up_grad[expert] = whole
        second = second + jnp.sum(whole * gate_up_weight[expert].astype(F32), 1, keepdims=True)
        at = GATE_UP + local * TOK
        down_grad[expert] = jnp.concatenate(
            [pack[4 * z + q, :, at : at + TOK].astype(F32) for q in range(4)], 1
        )
    gain_grads[:, 0:1] = first / gains[:, 0:1]
    gain_grads[:, 1:2] = second / gains[:, 1:2]


def assemble(*inputs):
    shapes = [(48, D), (48, 1024), (48, D), (48, EXPERTS), (EXPERTS, 48, 2 * FF), (EXPERTS, 48, FF), (48, 2)]
    outputs = [((TOK, D), F32, True), ((TOK, D), BF16, True)] + [(shape, F32, True) for shape in shapes]
    return local_kernel(assemble_kernel, inputs, (), (), outputs, [])


def run_of(x, step):
    run = (step > x).astype(jnp.int32)
    block = step - run * (x + 1)
    return run, block, block == 0, jnp.logical_or(step == x, step == 8)


def run_base(x, run):
    return (x + run * (7 - 2 * x)) * RUN


def unpack_queries(source, target):
    for run in range(2):
        for part in range(4):
            target[run, :, part * TOK : (part + 1) * TOK] = source[run, part]


def document_starts(segment_ref, starts, x):
    segments = [segment_ref[:, z, :].astype(F32) for z in range(2)]
    earlier = []
    for number in range(1, 5):
        count = [
            jnp.sum(
                jnp.sum((part < number).astype(F32), 0, keepdims=True), 1, keepdims=True
            )
            for part in segments
        ]
        earlier.append(count[0] + count[1])
    for run in range(2):
        first = 4 * (x + run * (3 - 2 * x))
        mark = jnp.concatenate([segment_ref[first + k, run : run + 1, :] for k in range(4)], 1)
        start = jnp.zeros((1, RUN), F32)
        for number in range(1, 5):
            start = jnp.where(mark == number, earlier[number - 1], start)
        starts[run, 0:1, :] = start


def visible_block(starts, x, run, block):
    key = lax.broadcasted_iota(jnp.int32, (RUN, RUN), 0).astype(F32)
    shift = (block * RUN).astype(F32)
    start = starts[run, 0:1, :] - shift
    query = lax.broadcasted_iota(jnp.int32, (1, RUN), 1).astype(F32) + (run_base(x, run).astype(F32) - shift)
    return jnp.logical_and(key >= start, key <= query)


def unpack_keys(kv_ref, key_rows, value_lines, x):
    ones = unit(TOK)

    def step(j, carry):
        place = pl.ds(pl.multiple_of(j * TOK, TOK), TOK)
        block = kv_ref.at[j // PLANE, lax.rem(j, PLANE)]
        key_rows[place, :] = product_nt(ones, block[:HEAD_DIM, :]).astype(BF16)
        value_lines[:, place] = block[HEAD_DIM:, :]
        return carry

    lax.fori_loop(0, (8 - x) * 4, step, 0)


def attend_step(x, step, queries, key_rows, value_lines, starts, peak, total, acc, o_ref, low_ref, lse_ref):
    run, block, first, last = run_of(x, step)

    @pl.when(first)
    def begin():
        peak[...] = jnp.full_like(peak, MASK_FILL)
        total[...] = jnp.zeros_like(total)
        acc[...] = jnp.zeros_like(acc)

    place = pl.ds(pl.multiple_of(block * RUN, RUN), RUN)
    keys, values = key_rows[place, :], value_lines[:, place]
    seen = visible_block(starts, x, run, block)
    for h in range(GROUP):
        rows = slice(h * HEAD_DIM, (h + 1) * HEAD_DIM)
        scores = jnp.dot(
            keys, queries[run, rows, :] * jnp.asarray(SCORE_SCALE, BF16), preferred_element_type=F32
        )
        scores = jnp.where(seen, scores, MASK_FILL)
        before = peak[h : h + 1, :]
        top = jnp.maximum(before, jnp.max(scores, 0, keepdims=True))
        weights = jnp.exp(scores - top)
        fade = jnp.exp(before - top)
        peak[h : h + 1, :] = top
        total[h : h + 1, :] = fade * total[h : h + 1, :] + jnp.sum(weights, 0, keepdims=True)
        acc[rows, :] = fade * acc[rows, :] + jnp.dot(
            values, weights.astype(BF16), preferred_element_type=F32
        )

    @pl.when(last)
    def end():
        cols = pl.ds(pl.multiple_of(run * RUN, RUN), RUN)
        for h in range(GROUP):
            rows = slice(h * HEAD_DIM, (h + 1) * HEAD_DIM)
            attended = acc[rows, :] / total[h : h + 1, :]
            o_ref[rows, cols] = attended
            low_ref[rows, cols] = attended.astype(BF16)
            lse_ref[h : h + 1, cols] = peak[h : h + 1, :] + jnp.log(total[h : h + 1, :])


def attend_scratch():
    return [
        pltpu.VMEM((2, QROWS, RUN), BF16),
        pltpu.VMEM((SEQ, HEAD_DIM), BF16),
        pltpu.VMEM((HEAD_DIM, SEQ), BF16),
        pltpu.VMEM((8, RUN), F32),
        pltpu.VMEM((8, RUN), F32),
        pltpu.VMEM((QROWS, RUN), F32),
    ]


def spread_keys(kv_ref, key_rows, value_rows, key_lines, x):
    ones = unit(TOK)

    def step(j, carry):
        place = pl.ds(pl.multiple_of(j * TOK, TOK), TOK)
        block = kv_ref[j // PLANE, lax.rem(j, PLANE)]
        turned = product_nt(ones, block).astype(BF16)
        key_rows[place, :] = turned[:, :HEAD_DIM]
        value_rows[place, :] = turned[:, HEAD_DIM:]
        key_lines[:, place] = block[:HEAD_DIM]
        return carry

    lax.fori_loop(0, (8 - x) * 4, step, 0)


def attend_back_step(
    x, step, queries, do_ref, o_ref, lse_ref, starts, key_rows, value_rows, key_lines,
    key_grad, value_grad, query_grad, delta, dq_ref,
):
    run, block, first, last = run_of(x, step)
    cols = pl.ds(pl.multiple_of(run * RUN, RUN), RUN)

    @pl.when(first)
    def begin():
        query_grad[...] = jnp.zeros_like(query_grad)
        for h in range(GROUP):
            rows = slice(h * HEAD_DIM, (h + 1) * HEAD_DIM)
            delta[h : h + 1, :] = jnp.sum(
                do_ref[rows, cols].astype(F32) * o_ref[rows, cols], 0, keepdims=True
            )

    place = pl.ds(pl.multiple_of(block * RUN, RUN), RUN)
    keys, values, lines = key_rows[place, :], value_rows[place, :], key_lines[:, place]
    seen = visible_block(starts, x, run, block)
    dk, dv = key_grad[place, :], value_grad[place, :]
    for h in range(GROUP):
        rows = slice(h * HEAD_DIM, (h + 1) * HEAD_DIM)
        q = queries[run, rows, :] * jnp.asarray(SCORE_SCALE, BF16)
        do = do_ref[rows, cols]
        scores = jnp.dot(keys, q, preferred_element_type=F32)
        weights = jnp.exp(jnp.where(seen, scores, MASK_FILL) - lse_ref[h : h + 1, cols])
        pull = jnp.dot(values, do, preferred_element_type=F32)
        ds = (weights * (pull - delta[h : h + 1, :])).astype(BF16)
        dv = dv + product_nt(weights.astype(BF16), do)
        dk = dk + product_nt(ds, q)
        query_grad[rows, :] += jnp.dot(lines, ds, preferred_element_type=F32)
    key_grad[place, :] = dk
    value_grad[place, :] = dv

    @pl.when(last)
    def end():
        scaled = (SCORE_SCALE * query_grad[...]).astype(BF16)
        for part in range(4):
            dq_ref[run, part] = scaled[:, part * TOK : (part + 1) * TOK]


def collect_keys(key_grad, value_grad, dkv_ref):
    ones = unit(HEAD_DIM)

    def step(j, carry):
        place = pl.ds(pl.multiple_of(j * TOK, TOK), TOK)
        dkv_ref[j // PLANE, lax.rem(j, PLANE), :HEAD_DIM, :] = product_nt(
            ones, key_grad[place, :].astype(BF16)
        ).astype(BF16)
        dkv_ref[j // PLANE, lax.rem(j, PLANE), HEAD_DIM:, :] = product_nt(
            ones, value_grad[place, :].astype(BF16)
        ).astype(BF16)
        return carry

    lax.fori_loop(0, SEQ // TOK, step, 0)


def attend_back_scratch():
    return [
        pltpu.VMEM((2, QROWS, RUN), BF16),
        pltpu.VMEM((QROWS, 2 * RUN), BF16),
        pltpu.VMEM((SEQ, HEAD_DIM), BF16),
        pltpu.VMEM((SEQ, HEAD_DIM), BF16),
        pltpu.VMEM((HEAD_DIM, SEQ), BF16),
        pltpu.VMEM((SEQ, HEAD_DIM), F32),
        pltpu.VMEM((SEQ, HEAD_DIM), F32),
        pltpu.VMEM((QROWS, RUN), F32),
        pltpu.VMEM((8, RUN), F32),
    ]


def shards(
    layer_input,
    segments,
    choices,
    first_gain,
    query_weight,
    key_value_matrix,
    output_weight,
    second_gain,
    router_weight,
    gate_up_weight,
    down_weight,
    cotangent,
):
    shard, rep = my_place()
    z, place, x, y = parts_of(shard)

    pad = jnp.zeros((8, TOK), jnp.int32)
    choices_lines = jnp.concatenate([choices[0].T, pad], 0)
    segment_lines = jnp.concatenate([segments, pad[:7]], 0)
    gate_up_mine = lax.dynamic_index_in_dim(
        gate_up_weight.reshape(48, 2, 5, 2, 4, TOK), rep, 4, keepdims=False
    )
    gate_up_mine = jnp.moveaxis(gate_up_mine, 1, 0).reshape(2, 48, 1280)
    down_mine = lax.dynamic_index_in_dim(down_weight.reshape(48, 2, 5, 4, TOK), rep, 3, keepdims=False)
    down_mine = jnp.moveaxis(down_mine, 1, 0).reshape(2, 48, 640)
    expert_mine = jnp.concatenate([gate_up_mine, down_mine], 2)
    query_mine = lax.dynamic_index_in_dim(query_weight.reshape(48, 2, 4, QROWS), rep, 2, keepdims=False)
    keyval_mine = lax.dynamic_index_in_dim(
        key_value_matrix.reshape(48, 2, 2, 4, HEAD_DIM), rep, 3, keepdims=False
    )
    gap = jnp.zeros((48, 3), BF16)
    small = jnp.concatenate(
        [
            router_weight[:, :5], gap, router_weight[:, 5:], gap, first_gain[:, None], second_gain[:, None],
            jnp.zeros((48, PACK - GAIN_TWO_AT - 1), BF16),
        ],
        1,
    )
    attn_mine = jnp.stack(
        [
            jnp.concatenate([query_mine[:, k], keyval_mine[:, 0, k], keyval_mine[:, 1, k], small], 1)
            for k in range(2)
        ]
    )
    frequency = ROPE_BASE ** (-jnp.arange(0, HEAD_DIM, 2, dtype=F32) / HEAD_DIM)
    column_place = (
        (jnp.arange(2, dtype=jnp.int32)[:, None] * PLANE + place) * TOK
        + jnp.arange(TOK, dtype=jnp.int32)[None, :]
    )
    angle = column_place.astype(F32)[:, None, :] * frequency[None, :, None]
    cosine, sine = jnp.cos(angle), jnp.sin(angle)
    (
        q_here, kv_here, starts, o_here, o_low, lse, normed_lines, turned, residual, normed_two, normed_two_all,
        expert_pack, dy_all, choices_all, dy_traded, choices_traded, out_slice,
    ) = forward(
        layer_input[0], segment_lines, attn_mine, output_weight, choices_lines, cotangent[0], expert_mine,
        cosine, sine,
    )

    mixture_part, grad_residual, grad_logits, grad_lin_all, pack_sum = experts(
        normed_two_all.reshape(COLUMN, D),
        dy_all.reshape(COLUMN, D),
        expert_pack.reshape(D, EXPERT_PACK),
        choices_all,
        residual,
        dy_traded,
        turned,
    )
    grad_normed, attn_own, pack_own, out_own, layer_out, grad_back = backward(
        q_here, kv_here, mixture_part, residual, normed_lines, turned, normed_two, grad_logits,
        cosine, sine, o_low, grad_lin_all.reshape(COLUMN, D), pack_sum, grad_residual, o_here, lse, starts, out_slice,
    )
    (
        input_grad, layer_out, query_grad, keyval_grad, out_grad_rows, router_grad, gate_up_grad, down_grad, gain_grads,
    ) = assemble(
        attn_own,
        pack_own,
        out_own,
        query_weight,
        key_value_matrix,
        router_weight,
        jnp.swapaxes(gate_up_weight, 0, 1),
        jnp.stack([first_gain, second_gain], 1).astype(F32),
        grad_normed,
        grad_back,
        layer_input[0],
        turned,
        layer_out,
    )
    return (
        layer_out[None],
        input_grad[None],
        gain_grads[:, 0],
        query_grad,
        keyval_grad,
        out_grad_rows,
        gain_grads[:, 1],
        router_grad,
        jnp.swapaxes(gate_up_grad, 0, 1),
        jnp.swapaxes(down_grad, 0, 1),
    )


def solution(mesh):
    row = P("shard", None)
    rows = P("shard", None, None)
    own = P("rep", "shard", None)
    in_specs = (own, P("rep", "shard"), own, P("shard"), row, row, row, P("shard"), row, rows, rows, own)
    out_specs = (own, own, P("shard"), row, row, row, P("shard"), row, rows, rows)
    return jax.shard_map(shards, mesh=mesh, in_specs=in_specs, out_specs=out_specs, check_vma=False)
```

```python
import jax
import jax.numpy as jnp
from jax import lax
from jax.experimental import pallas as pl
from jax.experimental.pallas import tpu as pltpu
from jax.sharding import PartitionSpec as P

D = 1536
HEADS = 8
GROUP = 3
HEAD_DIM = 64
HALF = HEAD_DIM // 2
FF = 512
EXPERTS = 10
TOK = 128
SEQ = 4096
PLANE = 16
RUN = 512
QROWS = GROUP * HEAD_DIM
PACK = 384
ROUTER_AT = 320
GAIN_ONE_AT = 336
GAIN_TWO_AT = 337
COLUMN = 8 * TOK
GATE_UP = 1280
EXPERT_PACK = 1920

NORM_EPS = 1e-06
RESIDUAL_SCALE = 0.22
SCORE_SCALE = 0.015625
ROPE_BASE = 10000.0
MASK_FILL = -1e30
PRECISE = lax.Precision.HIGHEST
BF16 = jnp.bfloat16
F32 = jnp.float32
VMEM_LIMIT = 56 * 1024 * 1024


def my_place():
    return lax.axis_index("shard"), lax.axis_index("rep")


def parts_of(shard):
    place = lax.rem(shard, PLANE)
    return shard // PLANE, place, place // 4, lax.rem(place, 4)


def same(one, other):
    return jnp.logical_and(one[0] == other[0], one[1] == other[1])


class Place:
    def __init__(self, me):
        self.me = me
        self.shard, self.rep = me
        self.z_lo, self.place, self.x, self.y = parts_of(self.shard)
        self.core = lax.rem(self.rep, 2)
        self.z = (self.rep // 2) * 2 + self.z_lo
        self.member = self.z_lo * 4 + self.rep

    def device(self, z, x, y, core):
        return lax.rem(z, 2) * PLANE + 4 * x + y, (z // 2) * 2 + core

    def step(self, axis, by):
        z, x, y = self.z, self.x, self.y
        if axis == "z":
            z = lax.rem(z + by, 4)
        elif axis == "x":
            x = lax.rem(x + by, 4)
        else:
            y = lax.rem(y + by, 4)
        return self.device(z, x, y, self.core)

    def sibling(self):
        return self.shard, self.rep + 1 - 2 * self.core

    def partner(self):
        return self.shard + (1 - 2 * self.z_lo) * PLANE, self.rep

    def trader(self):
        return self.z_lo * PLANE + 4 * mirrored(self.z_lo, self.x) + self.rep, self.y

    def member_at(self, z, core):
        return lax.rem(z, 2) * 4 + (z // 2) * 2 + core

    def near(self):
        result = [self.sibling()]
        for axis in ("z", "x", "y"):
            result += [self.step(axis, 1), self.step(axis, 3)]
        return result


def mesh_id(place):
    return {"shard": place[0], "rep": place[1]}


class Net:
    def __init__(self, here, sems):
        self.here, self.sems, self.used, self.sent = here, sems, 0, []

    def take(self, count=1):
        first = self.used
        self.used += count
        return first

    def push(self, source, target, to):
        number = self.take(2)
        copy = pltpu.make_async_remote_copy(
            src_ref=source,
            dst_ref=target,
            send_sem=self.sems.at[number],
            recv_sem=self.sems.at[number + 1],
            device_id=mesh_id(to),
        )
        copy.start()
        self.sent.append(copy)
        return number + 1

    def got(self, number, region):
        pltpu.make_async_remote_copy(
            src_ref=region,
            dst_ref=region,
            send_sem=self.sems.at[number],
            recv_sem=self.sems.at[number],
            device_id=mesh_id(self.here.sibling()),
        ).wait_recv()

    def local(self, source, target):
        copy = pltpu.make_async_copy(source, target, self.sems.at[self.take()])
        copy.start()
        return copy

    def finish(self):
        for copy in self.sent:
            copy.wait_send()


class Route:
    def __init__(self, n, to, source, pieces, index=None, may_be_self=False):
        self.n, self.to, self.source, self.pieces = n, to, source, pieces
        self.index = index or (lambda i: i)
        self.may_be_self = may_be_self


def each(n, body):
    if n <= 8:
        for i in range(n):
            body(i)
    else:

        def step(i, carry):
            body(i)
            return carry

        lax.fori_loop(0, n, step, 0)


def greet_routes(routes, me, barrier):
    awaited = 0
    for route in routes:

        def greet(i, route=route):
            source = route.source(i)

            def signal():
                pl.semaphore_signal(barrier, inc=1, device_id=mesh_id(source))

            if route.may_be_self:
                pl.when(jnp.logical_not(same(source, me)))(signal)
            else:
                signal()

        each(route.n, greet)
        awaited = awaited + route.n
        if route.may_be_self:
            for i in range(route.n):
                awaited = awaited - same(route.to(i), me).astype(jnp.int32)
    return awaited


HOP = 2.0


def time_of(ref, rate=50.0):
    size = jnp.dtype(ref.dtype).itemsize / 1000.0
    for extent in ref.shape:
        size *= extent
    return HOP + size / rate


def follow_routes(net, routes, ins, outs, guess=15.0):
    me = net.here.me
    held = []
    for route in routes:
        count = route.n * len(route.pieces)
        held.append((net.take(count), net.take(count), net.take(len(route.pieces))))

    def remote(route, base, i, k, piece):
        source_in, cut, target_out, slot, unused = piece
        return pltpu.make_async_remote_copy(
            src_ref=ins[source_in].at[cut(i)],
            dst_ref=outs[target_out].at[slot(i)],
            send_sem=net.sems.at[base[0] + i * len(route.pieces) + k],
            recv_sem=net.sems.at[base[1] + route.index(i) * len(route.pieces) + k],
            device_id=mesh_id(route.to(i)),
        )

    def within(base, i, k, piece):
        source_in, cut, target_out, slot, unused = piece
        return pltpu.make_async_copy(
            ins[source_in].at[cut(i)], outs[target_out].at[slot(i)], net.sems.at[base[2] + k]
        )

    for route, base in zip(routes, held):

        def start(i, route=route, base=base):
            for k, piece in enumerate(route.pieces):
                copy = remote(route, base, i, k, piece)
                if route.may_be_self:
                    here = same(route.to(i), me)
                    pl.when(jnp.logical_not(here))(copy.start)
                    pl.when(here)(within(base, i, k, piece).start)
                else:
                    copy.start()

        each(route.n, start)
    yield guess
    for route, base in zip(routes, held):

        def arrive(i, route=route, base=base):
            for k, piece in enumerate(route.pieces):
                region = outs[piece[2]].at[piece[4](i)]
                place = route.source(i)
                sem = net.sems.at[base[1] + i * len(route.pieces) + k]
                copy = pltpu.make_async_remote_copy(
                    src_ref=region, dst_ref=region, send_sem=sem, recv_sem=sem, device_id=mesh_id(place)
                )
                if route.may_be_self:
                    pl.when(jnp.logical_not(same(place, me)))(copy.wait_recv)
                else:
                    copy.wait_recv()

        each(route.n, arrive)

        def leave(i, route=route, base=base):
            for k, piece in enumerate(route.pieces):
                copy = remote(route, base, i, k, piece)
                if route.may_be_self:
                    here = same(route.to(i), me)
                    pl.when(jnp.logical_not(here))(copy.wait_send)
                    pl.when(here)(within(base, i, k, piece).wait)
                else:
                    copy.wait_send()

        each(route.n, leave)


def trade(net, pieces, begin=0.0, now=30.0):
    other = net.here.trader()
    here = same(other, net.here.me)
    if begin:
        yield begin
    copies = []
    for source, target in pieces:
        number = net.take(2)
        remote = pltpu.make_async_remote_copy(
            src_ref=source,
            dst_ref=target,
            send_sem=net.sems.at[number],
            recv_sem=net.sems.at[number + 1],
            device_id=mesh_id(other),
        )
        within = pltpu.make_async_copy(source, target, net.sems.at[net.take()])
        pl.when(jnp.logical_not(here))(remote.start)
        pl.when(here)(within.start)
        copies.append((remote, within))
    yield now
    for remote, within in copies:
        pl.when(jnp.logical_not(here))(remote.wait)
        pl.when(here)(within.wait)


def greet_trader(here, barrier):
    other = here.trader()
    away = jnp.logical_not(same(other, here.me))

    @pl.when(away)
    def signal():
        pl.semaphore_signal(barrier, inc=1, device_id=mesh_id(other))

    return away.astype(jnp.int32)


def spread_rows(net, rows, out):
    here = net.here
    ahead = lax.rem(here.x - here.rep + 4, 4)
    pair = lambda k: out.at[pl.ds(2 * k, 2)]
    row_halves = row_half(48)

    def at(by):
        return out.at[lax.rem(here.y + by, 4)]

    def copy(number, source, target, to):
        return pltpu.make_async_remote_copy(
            src_ref=source,
            dst_ref=target,
            send_sem=net.sems.at[number],
            recv_sem=net.sems.at[number + 1],
            device_id=mesh_id(to),
        )

    def come(number, region):
        copy(number, region, region, here.sibling()).wait_recv()

    up, down, right, left = here.step("y", 1), here.step("y", 3), here.step("x", 1), here.step("x", 3)
    numbers = [net.take(2) for k in range(8)]
    keep = pltpu.make_async_copy(rows, at(0), net.sems.at[net.take()])
    first = [copy(numbers[0], rows, at(0), up), copy(numbers[1], rows, at(0), down)]
    second = [
        copy(numbers[2], row_halves(at(3), 0), row_halves(at(3), 0), up),
        copy(numbers[3], row_halves(at(1), 1), row_halves(at(1), 1), down),
    ]
    third = [copy(numbers[4], out, out, right), copy(numbers[5], out, out, left)]
    on_right = copy(numbers[6], pair(0), pair(0), right)
    on_left = copy(numbers[7], pair(1), pair(1), left)

    @pl.when(ahead == 0)
    def begin():
        keep.start()
        first[0].start()
        first[1].start()

    now = time_of(rows)
    yield now

    @pl.when(ahead == 0)
    def hand_on():
        come(numbers[0], at(3))
        second[0].start()
        come(numbers[1], at(1))
        second[1].start()

    now += time_of(rows, 100.0)
    yield now

    @pl.when(ahead == 0)
    def go_out():
        come(numbers[2], row_halves(at(2), 0))
        come(numbers[3], row_halves(at(2), 1))
        keep.wait()
        third[0].start()
        third[1].start()

    now += time_of(out, 70.0)
    yield now

    @pl.when(ahead == 1)
    def to_right():
        come(numbers[4], out)
        on_right.start()

    @pl.when(ahead == 3)
    def to_left():
        come(numbers[5], out)
        on_left.start()

    now += time_of(out, 140.0)
    yield now

    @pl.when(ahead == 2)
    def end():
        come(numbers[6], pair(0))
        come(numbers[7], pair(1))

    @pl.when(ahead == 0)
    def sent():
        for each_copy in first + second + third:
            each_copy.wait_send()

    pl.when(ahead == 1)(on_right.wait_send)
    pl.when(ahead == 3)(on_left.wait_send)


def comm(inputs, in_vmem, outputs, scratch, n_sems, collective_id, plan):
    n_in, n_out = len(inputs), len(outputs)

    def kernel(*refs):
        ins, outs = refs[:n_in], refs[n_in : n_in + n_out]
        rest, sems = refs[n_in + n_out : -1], refs[-1]
        net = Net(Place(my_place()), sems)
        flows, routes, near, greetings = plan(net, ins, outs, rest)
        barrier = pltpu.get_barrier_semaphore()
        awaited = greet_routes(routes, net.here.me, barrier)
        if near:
            others = net.here.near()
            for other in others:
                pl.semaphore_signal(barrier, inc=1, device_id=mesh_id(other))
            awaited = awaited + len(others)
        for greeting in greetings:
            awaited = awaited + greeting(net.here, barrier)
        pl.semaphore_wait(barrier, awaited)
        waits = [(0.0, number, flow) for number, flow in enumerate(flows)]
        while waits:
            unused, number, flow = waits.pop(0)
            when = next(flow, None)
            if when is not None:
                waits = sorted(waits + [(when, number, flow)], key=lambda wait: wait[:2])
        net.finish()
        assert net.used <= n_sems, net.used

    vmem = pl.BlockSpec(memory_space=pltpu.VMEM)
    anywhere = pl.BlockSpec(memory_space=pl.ANY)
    return pl.pallas_call(
        kernel,
        out_shape=[jax.ShapeDtypeStruct(s, t) for s, t, unused in outputs],
        in_specs=[vmem if k in in_vmem else anywhere for k in range(n_in)],
        out_specs=[vmem if inside else anywhere for unused, unused2, inside in outputs],
        scratch_shapes=list(scratch) + [pltpu.SemaphoreType.DMA((n_sems,))],
        compiler_params=pltpu.CompilerParams(
            collective_id=collective_id, has_side_effects=True, vmem_limit_bytes=VMEM_LIMIT
        ),
    )(*inputs)


def together(flows):
    waits, now = [(next(flow), number, flow) for number, flow in enumerate(flows)], 0.0
    while waits:
        waits = sorted(waits, key=lambda wait: wait[:2])
        now, number, flow = waits.pop(0)
        yield now
        when = next(flow, None)
        if when is not None:
            waits.append((when, number, flow))
    return now


def resumed(when, flow):
    yield when
    yield from flow


def column_gather(net, source, out, half_of, now=0.0):
    here = net.here

    def slot(by, core):
        return out.at[here.member_at(lax.rem(here.z + by, 4), core)]

    core, other = here.core, 1 - here.core
    right, left, sibling = here.step("z", 1), here.step("z", 3), here.sibling()
    keep = net.local(source, slot(0, core))
    a = net.push(source, slot(0, core), right)
    b = net.push(source, slot(0, core), left)
    s = [net.push(source, slot(0, core), sibling)]
    now += time_of(source)
    yield now
    net.got(a, slot(3, core))
    c = net.push(half_of(slot(3, core), 0), half_of(slot(3, core), 0), right)
    s.append(net.push(slot(3, core), slot(3, core), sibling))
    net.got(b, slot(1, core))
    d = net.push(half_of(slot(1, core), 1), half_of(slot(1, core), 1), left)
    s.append(net.push(slot(1, core), slot(1, core), sibling))
    now += time_of(source, 100.0)
    yield now
    net.got(c, half_of(slot(2, core), 0))
    net.got(d, half_of(slot(2, core), 1))
    s.append(net.push(slot(2, core), slot(2, core), sibling))
    yield now + time_of(source, 200.0)
    for number, by in zip(s, (0, 3, 1, 2)):
        net.got(number, slot(by, other))
    keep.wait()


def row_half(size):
    first = (size // 2 + 15) // 16 * 16

    def half(ref, k):
        return ref.at[pl.ds(0, first)] if k == 0 else ref.at[pl.ds(first, size - first)]

    return half


def ring_gather(net, axis, source, slot, half, now, rate):
    right, left = net.here.step(axis, 1), net.here.step(axis, 3)
    a = net.push(source, slot(0), right)
    b = net.push(source, slot(0), left)
    now += time_of(source, rate)
    yield now
    net.got(a, slot(3))
    c = net.push(half(slot(3), 0), half(slot(3), 0), right)
    net.got(b, slot(1))
    d = net.push(half(slot(1), 1), half(slot(1), 1), left)
    now += time_of(source, 2 * rate)
    yield now
    net.got(c, half(slot(2), 0))
    net.got(d, half(slot(2), 1))
    return now


def swap_pair(net, payload, target, begin, now):
    here = net.here
    yield begin
    number = net.push(payload.at[1 - here.z_lo], target, here.partner())
    yield now
    net.got(number, target)


def plane_gather(net, payload, pair, out, rate=50.0, now=0.0):
    here = net.here
    z, x, y = here.z_lo, here.x, here.y
    rows = row_half(48)
    two = lambda ref, k: ref.at[pl.ds(2 * k, 2)]
    swap = []

    def first():
        if pair is None:
            swap.append(net.push(payload.at[1 - z], out.at[z, x, y], here.partner()))
        keep = net.local(payload.at[z], out.at[z, x, y])
        then = yield from ring_gather(
            net, "x", payload.at[z], lambda by: out.at[z, lax.rem(x + by, 4), y], rows, now, rate
        )
        keep.wait()
        bundle = lambda by: out.at[z, :, lax.rem(y + by, 4)]
        yield from ring_gather(net, "y", bundle(0), bundle, two, then, rate)

    def second():
        w = 1 - z
        then, source = now, pair
        if pair is None:
            then, source = now + time_of(payload.at[0], rate), out.at[w, x, y]
            yield then
            net.got(swap[0], source)
        else:
            keep = net.local(pair, out.at[w, x, y])
        then = yield from ring_gather(
            net, "y", source, lambda by: out.at[w, x, lax.rem(y + by, 4)], rows, then, rate
        )
        if pair is not None:
            keep.wait()
        bundle = lambda by: out.at[w, lax.rem(x + by, 4)]
        yield from ring_gather(net, "x", bundle(0), bundle, two, then, rate)

    return [first(), second()]


def add(target, *parts):
    total = parts[0][...].astype(F32)
    for part in parts[1:]:
        total = total + part[...].astype(F32)
    target[...] = total.astype(target.dtype)


def ring_sum(net, axis, block, half, halves, wholes, target, now, rate=50.0):
    right, left = net.here.step(axis, 1), net.here.step(axis, 3)
    lower, upper = halves
    a = net.push(half(block(2), 0), lower, right)
    b = net.push(half(block(2), 1), upper, left)
    now += time_of(lower, rate)
    yield now
    net.got(a, lower)
    add(half(block(1), 0), half(block(1), 0), lower)
    c = net.push(block(1), wholes[0], right)
    net.got(b, upper)
    add(half(block(3), 1), half(block(3), 1), upper)
    d = net.push(block(3), wholes[1], left)
    now += time_of(wholes[0], rate)
    yield now
    net.got(c, wholes[0])
    net.got(d, wholes[1])
    add(target, block(0), wholes[0], wholes[1])
    return now


def column_sum(net, parts, out, sums, sibling_parts, halves, wholes, now=0.0):
    here = net.here
    half = row_half(parts.shape[1])
    at = lambda by: lax.rem(here.z + by, 4)
    numbers = {}
    for by in (2, 1, 3, 0):
        numbers[by] = net.push(
            parts.at[here.member_at(at(by), 1 - here.core)], sibling_parts.at[at(by)], here.sibling()
        )
    now += HOP
    for by in (2, 1, 3):
        now += time_of(sums.at[0], 200.0) - HOP
        yield now
        net.got(numbers[by], sibling_parts.at[at(by)])
        add(sums.at[at(by)], parts.at[here.member_at(at(by), here.core)], sibling_parts.at[at(by)])
        if by == 2:
            ring = ring_sum(
                net, "z", lambda by: sums.at[at(by)], half, (halves.at[0], halves.at[1]),
                (wholes.at[0], wholes.at[1]), out, now,
            )
            when = next(ring)
    net.got(numbers[0], sibling_parts.at[at(0)])
    add(sums.at[at(0)], parts.at[here.member_at(at(0), here.core)], sibling_parts.at[at(0)])
    yield when
    now = yield from ring
    return now


def column_sum_rows(net, parts, out, scratch, k, now):
    sums, sibling_parts, halves, wholes = scratch
    rows, half_rows = pl.ds(k * 64, 64), pl.ds(k * 32, 32)
    now = yield from column_sum(
        net, parts.at[:, rows], out.at[rows], sums.at[:, rows], sibling_parts.at[:, rows], halves.at[:, half_rows],
        wholes.at[:, rows], now=now,
    )
    return now


def column_sum_scratch(rows, columns):
    return [
        pltpu.VMEM((4, rows, columns), BF16),
        pltpu.VMEM((4, rows, columns), BF16),
        pltpu.VMEM((2, rows // 2, columns), BF16),
        pltpu.VMEM((2, rows, columns), BF16),
    ]


def plane_sum(net, parts, out, held, pairs, bundles, rows_a, rows_b, blocks, rate=50.0, now=2.0):
    here = net.here
    at_x = lambda by: lax.rem(here.x + by, 4)
    at_y = lambda by: lax.rem(here.y + by, 4)
    pair = lambda ref, k: ref.at[pl.ds(2 * k, 2)]
    half = row_half(48)

    def first():
        if parts is not None:
            copy = net.local(parts.at[0], held.at[0])
            yield now
            copy.wait()
        mine = held.at[0, :, here.y]
        then = yield from ring_sum(
            net, "y", lambda by: held.at[0, :, at_y(by)], pair, (pairs.at[0], pairs.at[1]),
            (bundles.at[0], bundles.at[1]), mine, now, rate,
        )
        yield from ring_sum(
            net, "x", lambda by: held.at[0, at_x(by), here.y], half, (rows_a.at[0], rows_b.at[0]),
            (blocks.at[0], blocks.at[1]), out.at[0], then, rate,
        )

    def second():
        if parts is not None:
            copy = net.local(parts.at[1], held.at[1])
            yield now
            copy.wait()
        mine = held.at[1, here.x]
        then = yield from ring_sum(
            net, "x", lambda by: held.at[1, at_x(by)], pair, (pairs.at[2], pairs.at[3]),
            (bundles.at[2], bundles.at[3]), mine, now, rate,
        )
        yield from ring_sum(
            net, "y", lambda by: held.at[1, here.x, at_y(by)], half, (rows_a.at[1], rows_b.at[1]),
            (blocks.at[2], blocks.at[3]), out.at[1], then, rate,
        )

    return [first(), second()]


def plane_sum_scratch(columns):
    return [
        pltpu.VMEM((2, 4, 4, 48, columns), BF16),
        pltpu.VMEM((4, 2, 48, columns), BF16),
        pltpu.VMEM((4, 4, 48, columns), BF16),
        pltpu.VMEM((2, 32, columns), BF16),
        pltpu.VMEM((2, 16, columns), BF16),
        pltpu.VMEM((4, 48, columns), BF16),
    ]


def column_deal(net, parts, out, passing, half, now=0.0, begin=0.0):
    here = net.here
    z = here.z_lo
    if begin:
        yield begin
        now = max(now, begin)
    core, other = here.core, 1 - here.core
    lower, upper = passing

    def slot(by, core):
        return out.at[here.member_at(lax.rem(here.z + by, 4), core)]

    right, left, sibling = here.step("z", 1), here.step("z", 3), here.sibling()
    keep = net.local(parts.at[z], slot(0, core))
    e = net.push(half(parts.at[z], 0), lower, right)
    f = net.push(half(parts.at[z], 1), upper, left)
    a = net.push(parts.at[1 - z], slot(0, core), right)
    b = net.push(parts.at[1 - z], slot(0, core), left)
    s = [net.push(parts.at[z], slot(0, core), sibling)]
    now += time_of(parts.at[0])
    yield now
    net.got(e, lower)
    c = net.push(lower, half(slot(3, core), 0), right)
    net.got(f, upper)
    d = net.push(upper, half(slot(1, core), 1), left)
    net.got(a, slot(3, core))
    s.append(net.push(slot(3, core), slot(3, core), sibling))
    net.got(b, slot(1, core))
    s.append(net.push(slot(1, core), slot(1, core), sibling))
    now += time_of(parts.at[0])
    yield now
    net.got(c, half(slot(2, core), 0))
    net.got(d, half(slot(2, core), 1))
    s.append(net.push(slot(2, core), slot(2, core), sibling))
    yield now + HOP
    for number, by in zip(s, (0, 3, 1, 2)):
        net.got(number, slot(by, other))
    keep.wait()


def column_route(me, pieces):
    z, place, unused, unused2 = parts_of(me[0])
    mine = z * 4 + me[1]

    def where(member):
        return (member // 4) * PLANE + place, lax.rem(member, 4)

    def after(i):
        return lax.rem(mine + 1 + i, 8)

    def before(i):
        return lax.rem(mine + 7 - i, 8)

    return Route(
        7,
        lambda i: where(after(i)),
        lambda i: where(before(i)),
        [
            (
                a,
                lambda i, cut=cut: cut(after(i)),
                b,
                lambda i, slot=slot: slot(mine),
                lambda i, slot=slot: slot(before(i)),
            )
            for a, cut, b, slot in pieces
        ],
    )


def plane_route(me, pieces):
    z, place, unused, unused2 = parts_of(me[0])

    def after(i):
        return lax.rem(place + 1 + i, PLANE)

    def before(i):
        return lax.rem(place + 15 - i, PLANE)

    return Route(
        15,
        lambda i: (z * PLANE + after(i), me[1]),
        lambda i: (z * PLANE + before(i), me[1]),
        [
            (
                a,
                lambda i, cut=cut: cut(after(i)),
                b,
                lambda i, slot=slot: slot(place),
                lambda i, slot=slot: slot(before(i)),
            )
            for a, cut, b, slot in pieces
        ],
    )


def own_copies(net, ins, outs, copies):
    started = [net.local(ins[a].at[cut], outs[b].at[slot]) for a, cut, b, slot in copies]
    yield 100.0
    for copy in started:
        copy.wait()


ROW_HALF = row_half(TOK)


def mirrored(z, x):
    return x + z * (3 - 2 * x)


def query_routes(me, q_in, q_out):
    z_me, place, x, y = parts_of(me[0])
    base = z_me * PLANE

    def plain(i):
        return lax.rem(y + 1 + i, 4)

    def plain_before(i):
        return lax.rem(y + 3 - i, 4)

    def other(i):
        return lax.rem(y + i, 4)

    def other_before(i):
        return lax.rem(y + 4 - i, 4)

    first = Route(
        3,
        lambda i: (base + 4 * x + plain(i), me[1]),
        lambda i: (base + 4 * x + plain_before(i), me[1]),
        [(q_in, lambda i: (0, plain(i)), q_out, lambda i: (0, y), lambda i: (0, plain_before(i)))],
    )
    second = Route(
        4,
        lambda i: (base + 4 * (3 - x) + other(i), me[1]),
        lambda i: (base + 4 * (3 - x) + other_before(i), me[1]),
        [(q_in, lambda i: (1, other(i)), q_out, lambda i: (1, y), lambda i: (1, other_before(i)))],
    )
    return [first, second], [(q_in, (0, y), q_out, (0, y))]


def pack_attention(pack, query_weight, keyval_weight, router_lines, gain_lines, rep):
    blank = jnp.zeros((3, 48), F32)
    lines = router_lines[...].astype(F32)
    small = jnp.concatenate(
        [lines[:5], blank, lines[5:], blank, gain_lines[...].astype(F32), jnp.zeros((6, 48), F32)], 0
    ).T.astype(BF16)
    fill = jnp.zeros((48, PACK - ROUTER_AT - 24), BF16)
    for k in range(4):

        @pl.when(rep == k)
        def fill_in(k=k):
            for z in range(2):
                m = 4 * z + k
                pack[z] = jnp.concatenate(
                    [
                        query_weight[:, m * QROWS : (m + 1) * QROWS],
                        keyval_weight[:, m * HEAD_DIM : (m + 1) * HEAD_DIM],
                        keyval_weight[:, (HEADS + m) * HEAD_DIM : (HEADS + m + 1) * HEAD_DIM],
                        small,
                        fill,
                    ],
                    1,
                )


def pack_experts(net, pack, gate_up_weight, down_weight):
    copies = []
    for z in range(2):
        for expert in range(5):
            for side in range(2):
                source = pl.ds(pl.multiple_of(side * FF + net.here.rep * TOK, TOK), TOK)
                target = pl.ds(expert * 256 + side * TOK, TOK)
                copies.append((gate_up_weight.at[5 * z + expert, :, source], pack.at[z, :, target]))
            source = pl.ds(pl.multiple_of(net.here.rep * TOK, TOK), TOK)
            target = pl.ds(GATE_UP + expert * TOK, TOK)
            copies.append((down_weight.at[5 * z + expert, :, source], pack.at[z, :, target]))
    return [net.local(source, target) for source, target in copies]


def forward(
    x, segments, query_weight, keyval_weight, router_lines, gain_lines, out_rows, choices, dy, gate_up_weight,
    down_weight, cosine, sine,
):
    def plan(net, ins, outs, scratch):
        here = net.here
        me = here.me
        place, x_at, y_at = here.place, here.x, here.y
        (x_all, attn_all, segment_all, q, kv, ints, normed, linear, out_slice, x_traded, pair, low_rows, parts,
         total) = scratch[:14]
        attending, summing = scratch[14:20], scratch[20:24]
        segment_here, attn, pack, segment_rows, lines, q_here, kv_here, o_here = scratch[24:32]
        (q_kept, kv_kept, starts, o_kept, o_low, lse, lines_kept, turned, residual, own_normed, normed_all, pack_all,
         dy_all, choices_all, dy_traded, choices_traded, out_given) = outs[:17]
        x, segments, out_rows, choices, dy, cosine, sine = ins[0], ins[1], ins[6], ins[7], ins[8], ins[11], ins[12]
        routes, own = query_routes(me, 0, 0)
        routes = [
            plane_route(
                me,
                [
                    (1, lambda p: (0, lax.rem(p, 4)), 1, lambda p: (0, p)),
                    (1, lambda p: (1, lax.rem(p, 4)), 1, lambda p: (1, p)),
                    (2, lambda p: lax.rem(p, 4), 2, lambda p: p),
                ],
            )
        ] + routes
        own = own + [
            (1, (0, y_at), 1, (0, place)),
            (1, (1, y_at), 1, (1, place)),
            (2, y_at, 2, place),
        ]
        segment_routes = [column_route(me, [(0, lambda m: slice(None), 0, lambda m: m)])]
        choice_routes = [column_route(me, [(0, lambda m: slice(None), 0, lambda m: m)])]
        spreading = spread_rows(net, out_rows, out_slice)
        trading = trade(net, [(x, x_traded)], 45.0, 66.0)

        def chain():
            pack_attention(attn, ins[2], ins[3], ins[4], ins[5], here.rep)
            segment_rows[...] = jnp.broadcast_to(segments[...], (8, TOK))
            marked = follow_routes(net, segment_routes, [segment_rows], [segment_all])
            next(marked)
            own_mark = net.local(segment_rows, segment_all.at[here.member])
            now = yield from together(plane_gather(net, attn, None, attn_all) + [column_gather(net, x, x_all, ROW_HALF)])
            for unused in marked:
                pass
            own_mark.wait()
            project(x_all, attn_all, cosine, sine, q, kv, turned, normed, linear)
            for sequence in range(4):
                ints[sequence] = jnp.concatenate(
                    [
                        segment_all[sequence, 0:1, :],
                        segment_all[4 + sequence, 0:1, :],
                        jnp.zeros((6, TOK), jnp.int32),
                    ],
                    0,
                )
            targets = [q_here, kv_here, segment_here]
            going = follow_routes(net, routes, [q, kv, ints], targets, now + 22.0)
            copies = own_copies(net, [q, kv, ints], targets, own)
            now = next(going)
            next(copies)
            turn_into(lines, normed)
            kept = [net.local(lines, lines_kept)]
            yield now
            for unused in going:
                pass
            for unused in copies:
                pass
            kept += [net.local(q_here, q_kept), net.local(kv_here, kv_kept)]
            document_starts(segment_here, starts, x_at)
            unpack_queries(q_here, attending[0])
            unpack_keys(kv_here, attending[1], attending[2], x_at)
            for third in range(3):

                def step(k, carry):
                    attend_step(x_at, k, *attending[:3], starts, *attending[3:], o_here, o_low, lse)
                    return carry

                lax.fori_loop(3 * third, 3 * third + 3, step, 0)
                now += 7.0
                yield now
            for unused in spreading:
                pass
            turn_into(low_rows, o_low)
            for block in range(4):
                columns = slice(block * 384, (block + 1) * 384)
                weights = out_slice[:, :, columns].reshape(QROWS, 384)
                product = jnp.dot(low_rows[...], weights, preferred_element_type=F32)
                parts[:, :, columns] = product.astype(BF16).reshape(8, TOK, 384)
            kept += [net.local(out_slice, out_given), net.local(o_here, o_kept)]

            def tail(k, now):
                rows = pl.ds(k * 64, 64)
                now = yield from column_sum_rows(net, parts, total, summing, k, now)
                for unused in trading:
                    pass
                gain = turned[GAIN_TWO_AT : GAIN_TWO_AT + 1, :].astype(F32)
                hidden = x_traded[rows, :].astype(F32) + RESIDUAL_SCALE * total[rows, :]
                scale = lax.rsqrt(jnp.sum(hidden * hidden, -1, keepdims=True) * (1.0 / D) + NORM_EPS)
                residual[rows, :] = hidden
                own_normed[rows, :] = (hidden * scale * gain).astype(BF16)
                yield from column_gather(net, own_normed.at[rows], normed_all.at[:, rows], row_half(64), now)

            yield from together([tail(0, now + 3.0), tail(1, now + 7.0)])
            for copy in kept:
                copy.wait()

        def gather_dy():
            yield from trade(net, [(choices, choices_traded), (dy, dy_traded)], 0.0, 24.0)
            sent = follow_routes(net, choice_routes, [choices_traded], [choices_all], 50.0)
            when = next(sent)
            own_choices = net.local(choices_traded, choices_all.at[here.member])
            yield from together([resumed(when, sent), column_gather(net, dy_traded, dy_all, ROW_HALF, 27.0)])
            own_choices.wait()

        def gather_experts():
            packing = pack_experts(net, pack, ins[9], ins[10])
            yield 22.0
            for copy in packing:
                copy.wait()
            yield from swap_pair(net, pack, pair, 22.0, 43.0)
            yield 46.0
            yield from together(plane_gather(net, pack, pair, pack_all, rate=30.0, now=46.0))

        flows = [chain(), spreading, gather_dy(), trading, gather_experts()]
        return flows, routes + segment_routes + choice_routes, True, [greet_trader]

    return comm(
        [
            x, segments, query_weight, keyval_weight, router_lines, gain_lines, out_rows, choices, dy, gate_up_weight,
            down_weight, cosine, sine,
        ],
        (1, 2, 3, 4, 5, 11, 12),
        [
            ((2, 4, QROWS, TOK), BF16, False),
            ((2, PLANE, TOK, TOK), BF16, False),
            ((2, 8, RUN), F32, True),
            ((QROWS, 2 * RUN), F32, False),
            ((QROWS, 2 * RUN), BF16, True),
            ((8, 2 * RUN), F32, True),
            ((D, COLUMN), BF16, False),
            ((PACK, D), BF16, True),
            ((TOK, D), F32, True),
            ((TOK, D), BF16, True),
            ((8, TOK, D), BF16, False),
            ((2, 4, 4, 48, EXPERT_PACK), BF16, False),
            ((8, TOK, D), BF16, False),
            ((8, 8, TOK), jnp.int32, False),
            ((TOK, D), BF16, False),
            ((8, TOK), jnp.int32, False),
            ((4, 48, D), BF16, False),
        ],
        [
            pltpu.VMEM((8, TOK, D), BF16),
            pltpu.VMEM((2, 4, 4, 48, PACK), BF16),
            pltpu.VMEM((8, 8, TOK), jnp.int32),
            pltpu.VMEM((2, 4, QROWS, TOK), BF16),
            pltpu.VMEM((2, 4, TOK, TOK), BF16),
            pltpu.VMEM((4, 8, TOK), jnp.int32),
            pltpu.VMEM((COLUMN, D), BF16),
            pltpu.VMEM((ROUTER_AT, COLUMN), F32),
            pltpu.VMEM((4, 48, D), BF16),
            pltpu.VMEM((TOK, D), BF16),
            pltpu.VMEM((48, EXPERT_PACK), BF16),
            pltpu.VMEM((COLUMN, QROWS), BF16),
            pltpu.VMEM((8, TOK, D), BF16),
            pltpu.VMEM((TOK, D), F32),
        ]
        + attend_scratch()
        + column_sum_scratch(TOK, D)
        + [
            pltpu.VMEM((PLANE, 8, TOK), jnp.int32),
            pltpu.VMEM((2, 48, PACK), BF16),
            pltpu.VMEM((2, 48, EXPERT_PACK), BF16),
            pltpu.VMEM((8, TOK), jnp.int32),
            pltpu.VMEM((D, COLUMN), BF16),
            pltpu.VMEM((2, 4, QROWS, TOK), BF16),
            pltpu.VMEM((2, PLANE, TOK, TOK), BF16),
            pltpu.VMEM((QROWS, 2 * RUN), F32),
        ],
        416,
        0,
        plan,
    )


def experts(hn_all, dy_all, pack_all, choices, residual, dy, turned):
    def plan(net, ins, outs, scratch):
        (hn, dy_here, pack, hn_lines, dy_lines, hidden, joined, shares, share_rows, pull_rows, pulls, back, mixture,
         total, low, pull_parts) = scratch[:16]
        summing, held = scratch[16:20], scratch[20:26]
        gate_up, down = pack.at[:, :GATE_UP], pack.at[:, GATE_UP:]
        routes = [column_route(net.here.me, [(0, lambda m, k=k: (k, m), 0, lambda m, k=k: (k, m))]) for k in range(2)]
        mixture_out, grad_out, logits_out, low_all, pack_sum = outs
        mine = net.here.member

        def z_chain(k, now):
            rows = pl.ds(k * 64, 64)
            pulled = follow_routes(net, [routes[k]], [pulls], [pull_parts])
            next(pulled)
            own = net.local(pulls.at[k, mine], pull_parts.at[k, mine])
            now = yield from column_sum_rows(net, back, total, summing, k, now)
            for unused in pulled:
                pass
            own.wait()
            residual_grad(total, ins[4], ins[5], pull_parts, shares, ins[6], grad_out, low, logits_out, k)
            yield from column_gather(net, low.at[rows], low_all.at[:, rows], row_half(64), now)

        def grads(now):
            sums = []

            def weights(first, size, at):
                part = pl.ds(first, size)
                flow = together(plane_sum(net, None, pack_sum.at[:, :, part], *columns_of(held, part), now=at))
                sums.append(resumed(next(flow), flow))

            turn_into(hn_lines, hn)

            def gate_up_step(j, carry):
                place = pl.ds(pl.multiple_of(j * 256, 256), 256)
                product = jnp.dot(
                    hn_lines[...], joined[:, :, place].reshape(COLUMN, 256), preferred_element_type=F32
                )
                held[0][:, :, :, :, place] = product.astype(BF16).reshape(2, 4, 4, 48, 256)
                return carry

            lax.fori_loop(0, 5, gate_up_step, 0)
            weights(0, GATE_UP, now)

            def back_step(j, carry):
                place = pl.ds(pl.multiple_of(j * 256, 256), 256)
                product = product_nt(joined[...].reshape(COLUMN, GATE_UP), gate_up[place, :])
                back[:, :, place] = product.astype(BF16).reshape(8, TOK, 256)
                return carry

            lax.fori_loop(0, D // 256, back_step, 0)
            chains = [z_chain(0, now + 5.0), z_chain(1, now + 8.0)]
            sums += [resumed(next(flow), flow) for flow in chains]

            def after():
                turn_into(dy_lines, dy_here)
                yield now + 8.0
                for at, size in ((0, 256), (256, 256), (512, 128)):
                    product = RESIDUAL_SCALE * jnp.dot(
                        dy_lines[...], hidden[:, :, at : at + size].reshape(COLUMN, size), preferred_element_type=F32
                    )
                    held[0][:, :, :, :, GATE_UP + at : GATE_UP + at + size] = product.astype(BF16).reshape(
                        2, 4, 4, 48, size
                    )
                part = pl.ds(GATE_UP, EXPERT_PACK - GATE_UP)
                flow = together(
                    plane_sum(net, None, pack_sum.at[:, :, part], *columns_of(held, part), rate=35.0, now=now + 14.0)
                )
                when = next(flow)

                def mixture_step(j, carry):
                    place = pl.ds(pl.multiple_of(j * 256, 256), 256)
                    product = product_nt(hidden[...].reshape(COLUMN, 640), down[place, :])
                    mixture[:, :, place] = product.astype(BF16).reshape(8, TOK, 256)
                    return carry

                def mix():
                    yield now + 20.0
                    lax.fori_loop(0, D // 256, mixture_step, 0)
                    store = net.local(mixture, mixture_out)
                    yield now + 60.0
                    store.wait()

                yield from together([resumed(when, flow), mix()])

            yield from together(sums + [after()])

        def chain():
            loads = [net.local(ins[0], hn), net.local(ins[2], pack), net.local(ins[1], dy_here)]
            loads[0].wait()
            expert_shares(hn, ins[6], ins[3], shares, share_rows, net.here.z_lo)
            for load in loads[1:]:
                load.wait()
            for k in range(2):
                for unused in experts_forward(
                    hn, dy_here, gate_up, down, hidden, joined, share_rows, pull_rows, pulls, k, 0.0
                ):
                    pass
            yield 0.0
            yield from grads(1.0)

        return [chain()], routes, True, []

    wide = lambda rows, columns: pltpu.VMEM((rows, columns), BF16)
    blocks = lambda columns, dtype=BF16: pltpu.VMEM((8, TOK, columns), dtype)
    return comm(
        [hn_all, dy_all, pack_all, choices, residual, dy, turned],
        (3, 4, 5, 6),
        [
            ((8, TOK, D), BF16, False),
            ((TOK, D), BF16, True),
            ((16, TOK), F32, True),
            ((8, TOK, D), BF16, False),
            ((2, 48, EXPERT_PACK), BF16, True),
        ],
        [
            blocks(D), blocks(D), wide(D, EXPERT_PACK), wide(D, COLUMN), wide(D, COLUMN), blocks(640),
            blocks(GATE_UP), pltpu.VMEM((8, 16, TOK), F32), blocks(8, F32), blocks(8, F32),
            pltpu.VMEM((2, 8, 8, TOK), F32), blocks(D), blocks(D), pltpu.VMEM((TOK, D), F32), wide(TOK, D),
            pltpu.VMEM((2, 8, 8, TOK), F32),
        ]
        + column_sum_scratch(TOK, D)
        + plane_sum_scratch(EXPERT_PACK),
        256,
        3,
        plan,
    )


def columns_of(refs, columns):
    return [ref.at[(slice(None),) * (len(ref.shape) - 1) + (columns,)] for ref in refs]


def backward(
    q_here, kv_here, mixture, residual, lines, turned, hn, logits, cosine, sine, o_low, grad_lin, pack, grad,
    o_here, lse, starts, out_rows,
):
    def plan(net, ins, outs, scratch):
        me = net.here.me
        place, x_at, y_at = net.here.place, net.here.x, net.here.y
        mine = net.here.member
        (dq, dkv, lines_here, grad_lin_here, row_send, row_parts, row_sum, lower, upper, lower_pack, upper_pack,
         attn_sum, grads, rows_of_grads, routed, hn_lines, normed_parts, mixture_sum, low_out) = scratch[:19]
        held = scratch[19:25]
        one_sum, other_sum = scratch[25:29], scratch[29:33]
        queries, do, key_rows, value_rows, key_lines, key_grad, value_grad, query_grad, delta = scratch[33:42]
        dq_send, dkv_send = scratch[42:44]
        routes, own = query_routes(me, 0, 0)
        routes = [plane_route(me, [(1, lambda p: (slice(None), p), 1, lambda p: p)])] + routes
        own = own + [(1, (slice(None), place), 1, place)]
        rows_in = [plane_route(me, [(0, lambda p: p, 0, lambda p: p)])]
        rows_out = [
            Route(
                4,
                lambda i: (4 * mine + place // 4, i),
                lambda i: (
                    (me[0] // 4) // 4 * PLANE + 4 * lax.rem(me[0], 4) + i,
                    lax.rem(me[0] // 4, 4),
                ),
                [(0, lambda i: slice(None), 3, lambda i: lax.rem(place, 4), lambda i: i)],
                index=lambda i: lax.rem(place, 4),
                may_be_self=True,
            ),
        ]
        half = row_half(48)

        def rows():
            keep = net.local(row_send.at[place], row_parts.at[place])
            yield from follow_routes(net, rows_in, [row_send], [row_parts], 20.0)
            keep.wait()
            total = row_parts[0].astype(F32)
            for k in range(1, PLANE):
                total = total + row_parts[k].astype(F32)
            row_sum[...] = total.astype(BF16)
            yield from follow_routes(net, rows_out, [row_sum], outs, 45.0)

        def chain():
            loads = [net.local(ins[4], lines_here), net.local(ins[11], grad_lin_here)]
            unpack_queries(ins[0], queries)
            spread_keys(ins[1], key_rows, value_rows, key_lines, x_at)
            key_grad[...] = jnp.zeros_like(key_grad)
            value_grad[...] = jnp.zeros_like(value_grad)
            loads[1].wait()
            weights = ins[17][...].reshape(QROWS, D)
            do[...] = product_nt(weights, grad_lin_here[...]).astype(BF16)
            total = jnp.dot(ins[10][...], grad_lin_here[...], preferred_element_type=F32)
            for k in range(PLANE):
                row_send[k] = total[12 * k : 12 * k + 12].astype(BF16)
            row_flow = rows()
            row_when = next(row_flow)
            now = 6.0
            for third in range(3):

                def step(k, carry):
                    attend_back_step(
                        x_at, k, queries, do, ins[14], ins[15], ins[16], key_rows, value_rows, key_lines,
                        key_grad, value_grad, query_grad, delta, dq_send,
                    )
                    return carry

                lax.fori_loop(3 * third, 3 * third + 3, step, 0)
                now += 5.0
                yield now
            collect_keys(key_grad, value_grad, dkv_send)
            going = follow_routes(net, routes, [dq_send, dkv_send], [dq, dkv], now + 22.0)
            copies = own_copies(net, [dq_send, dkv_send], [dq, dkv], own)
            when = next(going)
            next(copies)
            turn_into(hn_lines, ins[6])
            yield row_when
            row_when = next(row_flow)
            yield when
            for unused in going:
                pass
            for unused in copies:
                pass
            loads[0].wait()
            weight_grads(dq, dkv, lines_here, hn_lines, ins[7], ins[8], ins[9], held[0], grads, routed)
            now = when + 10.0

            def weights():
                then = yield from together(plane_sum(net, None, attn_sum, *held, now=now))
                yield from column_deal(net, attn_sum, outs[1], (lower, upper), half, then)

            def normed():
                normed_grads(grads, rows_of_grads, ins[5], normed_parts)
                yield from together(
                    [column_sum_rows(net, normed_parts, outs[0], one_sum, k, now + 6.0 + 4.0 * k) for k in range(2)]
                )

            yield from together([weights(), normed(), resumed(row_when, row_flow)])

        def layer_output():
            now = yield from column_sum(net, ins[2], mixture_sum, *other_sum)
            low_out[...] = (ins[3][...] + RESIDUAL_SCALE * mixture_sum[...]).astype(BF16)
            yield from trade(net, [(low_out, outs[4])], 48.0, 75.0)

        flows = [
            trade(net, [(ins[13], outs[5])], 0.0, 30.0),
            layer_output(),
            chain(),
            column_deal(net, ins[12], outs[2], (lower_pack, upper_pack), half, begin=24.0),
        ]
        return flows, routes + rows_in + rows_out, True, [greet_trader]

    return comm(
        [
            q_here, kv_here, mixture, residual, lines, turned, hn, logits, cosine, sine, o_low, grad_lin, pack, grad,
            o_here, lse, starts, out_rows,
        ],
        (0, 1, 2, 3, 5, 6, 7, 8, 9, 10, 14, 15, 16, 17),
        [
            ((TOK, D), F32, True),
            ((8, 48, PACK), BF16, False),
            ((8, 48, EXPERT_PACK), BF16, False),
            ((4, 12, D), BF16, False),
            ((TOK, D), BF16, False),
            ((TOK, D), BF16, False),
        ],
        [
            pltpu.VMEM((2, 4, QROWS, TOK), BF16),
            pltpu.VMEM((PLANE, 2, TOK, TOK), BF16),
            pltpu.VMEM((D, COLUMN), BF16),
            pltpu.VMEM((COLUMN, D), BF16),
            pltpu.VMEM((PLANE, 12, D), BF16),
            pltpu.VMEM((PLANE, 12, D), BF16),
            pltpu.VMEM((12, D), BF16),
            pltpu.VMEM((32, PACK), BF16),
            pltpu.VMEM((16, PACK), BF16),
            pltpu.VMEM((32, EXPERT_PACK), BF16),
            pltpu.VMEM((16, EXPERT_PACK), BF16),
            pltpu.VMEM((2, 48, PACK), BF16),
            pltpu.VMEM((PACK, COLUMN), BF16),
            pltpu.VMEM((COLUMN, PACK), BF16),
            pltpu.VMEM((PACK, TOK), BF16),
            pltpu.VMEM((D, TOK), BF16),
            pltpu.VMEM((8, TOK, D), BF16),
            pltpu.VMEM((TOK, D), F32),
            pltpu.VMEM((TOK, D), BF16),
        ]
        + plane_sum_scratch(PACK)
        + column_sum_scratch(TOK, D)
        + column_sum_scratch(TOK, D)
        + attend_back_scratch()
        + [pltpu.VMEM((2, 4, QROWS, TOK), BF16), pltpu.VMEM((2, PLANE, TOK, TOK), BF16)],
        384,
        4,
        plan,
    )


NT = (((1,), (1,)), ((), ()))


def product_nt(one, other):
    return lax.dot_general(one, other, NT, preferred_element_type=F32)


def unit(size):
    rows = lax.broadcasted_iota(jnp.int32, (size, size), 0)
    return (rows == lax.broadcasted_iota(jnp.int32, (size, size), 1)).astype(BF16)


def turn_into(target, source, block=256):
    ones = unit(block)

    def step(k, carry):
        place = pl.ds(pl.multiple_of(k * block, block), block)
        if len(source.shape) == 3:
            part = source[:, :, place].reshape(target.shape[1], block)
        else:
            part = source[:, place]
        target[place, :] = product_nt(ones, part).astype(BF16)
        return carry

    lax.fori_loop(0, source.shape[-1] // block, step, 0)


def project(x_ref, attn_ref, cos_ref, sin_ref, q_ref, kv_ref, turned_ref, normed, linear):
    ones = unit(PACK)
    for z in range(2):
        weights = attn_ref[z].reshape(D // 2, PACK)
        turned_ref[:, z * (D // 2) : (z + 1) * (D // 2)] = product_nt(ones, weights).astype(BF16)
    gain = turned_ref[GAIN_ONE_AT : GAIN_ONE_AT + 1, :].astype(F32)

    def norm(k, carry):
        place = pl.ds(pl.multiple_of(k * TOK, TOK), TOK)
        values = x_ref[k].astype(F32)
        scale = lax.rsqrt(jnp.sum(values * values, -1, keepdims=True) * (1.0 / D) + NORM_EPS)
        normed[place, :] = (values * scale * gain).astype(BF16)
        return carry

    lax.fori_loop(0, 8, norm, 0)
    for part in range(2):
        place = slice(part * 512, (part + 1) * 512)
        linear[:, place] = product_nt(turned_ref[:ROUTER_AT, :], normed[place, :])
    for z in range(2):
        cosine, sine = cos_ref[z], sin_ref[z]
        for sequence in range(4):
            at = (4 * z + sequence) * TOK
            for head in range(GROUP + 1):
                rows = head * HEAD_DIM
                front = linear[rows : rows + HALF, at : at + TOK]
                behind = linear[rows + HALF : rows + HEAD_DIM, at : at + TOK]
                one = (front * cosine - behind * sine).astype(BF16)
                two = (behind * cosine + front * sine).astype(BF16)
                if head < GROUP:
                    q_ref[z, sequence, rows : rows + HALF, :] = one
                    q_ref[z, sequence, rows + HALF : rows + HEAD_DIM, :] = two
                else:
                    kv_ref[z, sequence, :HALF, :] = one
                    kv_ref[z, sequence, HALF:HEAD_DIM, :] = two
            kv_ref[z, sequence, HEAD_DIM:, :] = linear[QROWS + HEAD_DIM : ROUTER_AT, at : at + TOK].astype(BF16)


def local_kernel(kernel, inputs, smem, anywhere_in, outputs, scratch):
    vmem = pl.BlockSpec(memory_space=pltpu.VMEM)
    anywhere = pl.BlockSpec(memory_space=pl.ANY)
    scalars = pl.BlockSpec(memory_space=pltpu.SMEM)
    return pl.pallas_call(
        kernel,
        out_shape=[jax.ShapeDtypeStruct(shape, dtype) for shape, dtype, unused in outputs],
        in_specs=[
            scalars if k in smem else anywhere if k in anywhere_in else vmem for k in range(len(inputs))
        ],
        out_specs=[vmem if inside else anywhere for unused, unused2, inside in outputs],
        scratch_shapes=scratch,
        compiler_params=pltpu.CompilerParams(vmem_limit_bytes=VMEM_LIMIT),
    )(*inputs)


def expert_shares(hn, turned_ref, choices_ref, share_ref, share_rows, z):
    row = lax.broadcasted_iota(jnp.int32, (16, TOK), 0)
    router = turned_ref[ROUTER_AT : ROUTER_AT + 16, :]

    def route(block, carry):
        logits = product_nt(router, hn[block])
        named = choices_ref[block]
        named = named + jnp.where(named >= 5, 3, 0)
        chosen = row == named[0:1]
        for k in range(1, 8):
            chosen = jnp.logical_or(chosen, row == named[k : k + 1])
        logits = jnp.where(chosen, logits, MASK_FILL)
        exponent = jnp.where(chosen, jnp.exp(logits - jnp.max(logits, 0, keepdims=True)), 0.0)
        share_ref[block] = exponent / jnp.sum(exponent, 0, keepdims=True)
        mine = share_ref[block, pl.ds(pl.multiple_of(z * 8, 8), 8), :]
        share_rows[block] = mine.T
        return carry

    lax.fori_loop(0, 8, route, 0)


def experts_forward(hn, dy, gate_up, down, hidden, joined, share_rows, pull_rows, pull_ref, k, now):
    rows = pl.ds(k * 64, 64)
    for expert in range(5):
        both = jnp.dot(
            hn[:, rows, :].reshape(512, D),
            gate_up[:, expert * 256 : expert * 256 + 256],
            preferred_element_type=F32,
        )
        gate, up = both[:, :TOK], both[:, TOK:]
        pulled = RESIDUAL_SCALE * jnp.dot(
            dy[:, rows, :].reshape(512, D),
            down[:, expert * TOK : (expert + 1) * TOK],
            preferred_element_type=F32,
        )
        share = share_rows[:, rows, expert : expert + 1].reshape(512, 1)
        sigmoid = 1.0 / (1.0 + jnp.exp(-gate))
        silu = gate * sigmoid
        act = (silu * up).astype(BF16).astype(F32)
        hidden[:, rows, expert * TOK : (expert + 1) * TOK] = (share * act).astype(BF16).reshape(8, 64, TOK)
        pull_rows[:, rows, expert : expert + 1] = jnp.sum(act * pulled, 1, keepdims=True).reshape(8, 64, 1)
        grad = share * pulled
        left = (grad * up * (sigmoid + silu * (1.0 - sigmoid))).astype(BF16)
        joined[:, rows, expert * 256 : expert * 256 + TOK] = left.reshape(8, 64, TOK)
        joined[:, rows, expert * 256 + TOK : expert * 256 + 256] = (grad * silu).astype(BF16).reshape(8, 64, TOK)
        if expert in (1, 3):
            yield now + 2.2 * (expert + 1)

    pull_rows[:, rows, 5:8] = jnp.zeros((8, 64, 3), F32)

    def turn_pull(block, carry):
        part = pull_rows[block, rows, :].T
        pull_ref[k, block] = jnp.concatenate([part, part], 1)
        return carry

    lax.fori_loop(0, 8, turn_pull, 0)


def residual_grad(
    sum_ref, residual_ref, dy_ref, pull_ref, share_ref, turned_ref, grad_ref, low_ref, logit_ref, k
):
    rows, tokens = pl.ds(k * 64, 64), slice(k * 64, k * 64 + 64)
    shard, rep = my_place()
    mine = (shard // PLANE) * 4 + rep
    shares = share_ref[mine]
    pulls = []
    for z in range(2):
        total = pull_ref[k, 4 * z]
        for quarter in range(1, 4):
            total = total + pull_ref[k, 4 * z + quarter]
        pulls.append(total)
    pull = jnp.concatenate(pulls, 0)
    logits = shares * (pull - jnp.sum(shares * pull, 0, keepdims=True))
    logit_ref[:, tokens] = logits[:, tokens]
    router = turned_ref[ROUTER_AT : ROUTER_AT + 16, :].astype(F32)
    gain = turned_ref[GAIN_TWO_AT : GAIN_TWO_AT + 1, :].astype(F32)
    grad_normed = sum_ref[rows, :] + jnp.dot(
        logits.T[tokens], router, precision=PRECISE, preferred_element_type=F32
    )
    residual = residual_ref[rows, :]
    scale = lax.rsqrt(jnp.sum(residual * residual, -1, keepdims=True) * (1.0 / D) + NORM_EPS)
    weighted = grad_normed * gain
    mean = jnp.sum(weighted * residual, -1, keepdims=True) * (1.0 / D)
    grad = dy_ref[rows, :].astype(F32) + scale * weighted - residual * (scale * scale * scale * mean)
    grad_ref[rows, :] = grad.astype(BF16)
    low_ref[rows, :] = (RESIDUAL_SCALE * grad).astype(BF16)


def weight_grads(dq_ref, dkv_ref, lines_ref, hn_lines, logit_ref, cos_ref, sin_ref, weight_ref, grads, routed):
    grads[ROUTER_AT:, :] = jnp.zeros((PACK - ROUTER_AT, COLUMN), BF16)
    for z in range(2):
        cosine, sine = cos_ref[z], sin_ref[z]
        for sequence in range(4):
            at = (4 * z + sequence) * TOK
            total = dkv_ref[sequence, z].astype(F32)
            for quarter in range(1, 4):
                total = total + dkv_ref[4 * quarter + sequence, z].astype(F32)
            for head in range(GROUP + 1):
                rows = head * HEAD_DIM
                if head < GROUP:
                    front = dq_ref[z, sequence, rows : rows + HALF, :].astype(F32)
                    behind = dq_ref[z, sequence, rows + HALF : rows + HEAD_DIM, :].astype(F32)
                else:
                    front, behind = total[:HALF], total[HALF:HEAD_DIM]
                grads[rows : rows + HALF, at : at + TOK] = (front * cosine + behind * sine).astype(BF16)
                grads[rows + HALF : rows + HEAD_DIM, at : at + TOK] = (behind * cosine - front * sine).astype(BF16)
            grads[QROWS + HEAD_DIM : ROUTER_AT, at : at + TOK] = total[HEAD_DIM:].astype(BF16)
    routed[...] = jnp.zeros_like(routed)
    routed[ROUTER_AT : ROUTER_AT + 16, :] = logit_ref[...].astype(BF16)

    def weight_step(k, carry):
        place = pl.ds(pl.multiple_of(k * 192, 192), 192)
        total = product_nt(lines_ref[place, :], grads[...]) + product_nt(hn_lines[place, :], routed[...])
        weight_ref[k // 4, lax.rem(k, 4)] = total.astype(BF16).reshape(4, 48, PACK)
        return carry

    lax.fori_loop(0, 8, weight_step, 0)


def normed_grads(grads, rows_of_grads, turned_ref, normed_ref):
    turn_into(rows_of_grads, grads)

    def step(k, carry):
        place = pl.ds(pl.multiple_of(k * 256, 256), 256)
        total = jnp.dot(rows_of_grads[...], turned_ref[:, place], preferred_element_type=F32)
        normed_ref[:, :, place] = total.astype(BF16).reshape(8, TOK, 256)
        return carry

    lax.fori_loop(0, D // 256, step, 0)


def assemble_kernel(
    attn, pack, out_rows, query_weight, keyval_weight, router_weight, gate_up_weight, gains,
    normed_grad, traded_grad, x, turned, traded_out, input_grad, layer_out,
    query_grad, keyval_grad, out_grad, router_grad, gate_up_grad, down_grad, first_grad, second_grad,
):
    layer_out[...] = traded_out[...]
    values = x[...].astype(F32)
    scale = lax.rsqrt(jnp.sum(values * values, -1, keepdims=True) * (1.0 / D) + NORM_EPS)
    weighted = normed_grad[...] * turned[GAIN_ONE_AT : GAIN_ONE_AT + 1, :].astype(F32)
    mean = jnp.sum(weighted * values, -1, keepdims=True) * (1.0 / D)
    input_grad[...] = traded_grad[...].astype(F32) + scale * weighted - values * (scale * scale * scale * mean)
    parts = [attn[m].astype(F32) for m in range(HEADS)]
    query = jnp.concatenate([part[:, :QROWS] for part in parts], 1)
    key = jnp.concatenate([part[:, QROWS : QROWS + HEAD_DIM] for part in parts], 1)
    value = jnp.concatenate([part[:, QROWS + HEAD_DIM : ROUTER_AT] for part in parts], 1)
    query_grad[...] = query
    keyval_grad[:, : HEADS * HEAD_DIM] = key
    keyval_grad[:, HEADS * HEAD_DIM :] = value
    router = parts[0]
    for part in parts[1:]:
        router = router + part
    router = jnp.concatenate([router[:, ROUTER_AT : ROUTER_AT + 5], router[:, ROUTER_AT + 8 : ROUTER_AT + 13]], 1)
    blank = jnp.zeros((48, TOK - EXPERTS - 2), F32)
    for k in range(4):
        out_grad[12 * k : 12 * k + 12, :] = out_rows[k].astype(F32)
    first = jnp.sum(query * query_weight[...].astype(F32), 1, keepdims=True)
    half = HEADS * HEAD_DIM
    first = first + jnp.sum(key * keyval_weight[:, :half].astype(F32), 1, keepdims=True)
    first = first + jnp.sum(value * keyval_weight[:, half:].astype(F32), 1, keepdims=True)
    second = jnp.sum(router * router_weight[...].astype(F32).T, 1, keepdims=True)
    for expert in range(EXPERTS):
        z, local = expert // 5, expert % 5
        rows = []
        for side in range(2):
            at = local * 256 + side * TOK
            rows += [pack[4 * z + q, :, at : at + TOK].astype(F32) for q in range(4)]
        whole = jnp.concatenate(rows, 1)
        gate_up_grad[expert] = whole
        second = second + jnp.sum(whole * gate_up_weight[expert].astype(F32), 1, keepdims=True)
        at = GATE_UP + local * TOK
        down_grad[expert] = jnp.concatenate(
            [pack[4 * z + q, :, at : at + TOK].astype(F32) for q in range(4)], 1
        )
    lines = jnp.concatenate([router, first, second, blank], 1).T
    router_grad[...] = lines[:EXPERTS]
    first_grad[...] = lines[EXPERTS : EXPERTS + 1] / gains[0:1].astype(F32)
    second_grad[...] = lines[EXPERTS + 1 : EXPERTS + 2] / gains[1:2].astype(F32)


def assemble(*inputs):
    shapes = [(48, D), (48, 1024), (48, D), (EXPERTS, 48), (EXPERTS, 48, 2 * FF), (EXPERTS, 48, FF), (1, 48), (1, 48)]
    outputs = [((TOK, D), F32, True), ((TOK, D), BF16, True)] + [(shape, F32, True) for shape in shapes]
    return local_kernel(assemble_kernel, inputs, (), (), outputs, [])


def run_of(x, step):
    run = (step > x).astype(jnp.int32)
    block = step - run * (x + 1)
    return run, block, block == 0, jnp.logical_or(step == x, step == 8)


def run_base(x, run):
    return (x + run * (7 - 2 * x)) * RUN


def unpack_queries(source, target):
    for run in range(2):
        for part in range(4):
            target[run, :, part * TOK : (part + 1) * TOK] = source[run, part]


def document_starts(segment_ref, starts, x):
    segments = [segment_ref[:, z, :].astype(F32) for z in range(2)]
    earlier = []
    for number in range(1, 5):
        count = [
            jnp.sum(
                jnp.sum((part < number).astype(F32), 0, keepdims=True), 1, keepdims=True
            )
            for part in segments
        ]
        earlier.append(count[0] + count[1])
    for run in range(2):
        first = 4 * (x + run * (3 - 2 * x))
        mark = jnp.concatenate([segment_ref[first + k, run : run + 1, :] for k in range(4)], 1)
        start = jnp.zeros((1, RUN), F32)
        for number in range(1, 5):
            start = jnp.where(mark == number, earlier[number - 1], start)
        starts[run, 0:1, :] = start


def visible_block(starts, x, run, block):
    key = lax.broadcasted_iota(jnp.int32, (RUN, RUN), 0).astype(F32)
    shift = (block * RUN).astype(F32)
    start = starts[run, 0:1, :] - shift
    query = lax.broadcasted_iota(jnp.int32, (1, RUN), 1).astype(F32) + (run_base(x, run).astype(F32) - shift)
    return jnp.logical_and(key >= start, key <= query)


def unpack_keys(kv_ref, key_rows, value_lines, x):
    ones = unit(TOK)

    def step(j, carry):
        place = pl.ds(pl.multiple_of(j * TOK, TOK), TOK)
        block = kv_ref.at[j // PLANE, lax.rem(j, PLANE)]
        key_rows[place, :] = product_nt(ones, block[:HEAD_DIM, :]).astype(BF16)
        value_lines[:, place] = block[HEAD_DIM:, :]
        return carry

    lax.fori_loop(0, (8 - x) * 4, step, 0)


def attend_step(x, step, queries, key_rows, value_lines, starts, peak, total, acc, o_ref, low_ref, lse_ref):
    run, block, first, last = run_of(x, step)

    @pl.when(first)
    def begin():
        peak[...] = jnp.full_like(peak, MASK_FILL)
        total[...] = jnp.zeros_like(total)
        acc[...] = jnp.zeros_like(acc)

    place = pl.ds(pl.multiple_of(block * RUN, RUN), RUN)
    keys, values = key_rows[place, :], value_lines[:, place]
    seen = visible_block(starts, x, run, block)
    for h in range(GROUP):
        rows = slice(h * HEAD_DIM, (h + 1) * HEAD_DIM)
        scores = jnp.dot(
            keys, queries[run, rows, :] * jnp.asarray(SCORE_SCALE, BF16), preferred_element_type=F32
        )
        scores = jnp.where(seen, scores, MASK_FILL)
        before = peak[h : h + 1, :]
        top = jnp.maximum(before, jnp.max(scores, 0, keepdims=True))
        weights = jnp.exp(scores - top)
        fade = jnp.exp(before - top)
        peak[h : h + 1, :] = top
        total[h : h + 1, :] = fade * total[h : h + 1, :] + jnp.sum(weights, 0, keepdims=True)
        acc[rows, :] = fade * acc[rows, :] + jnp.dot(
            values, weights.astype(BF16), preferred_element_type=F32
        )

    @pl.when(last)
    def end():
        cols = pl.ds(pl.multiple_of(run * RUN, RUN), RUN)
        for h in range(GROUP):
            rows = slice(h * HEAD_DIM, (h + 1) * HEAD_DIM)
            attended = acc[rows, :] / total[h : h + 1, :]
            o_ref[rows, cols] = attended
            low_ref[rows, cols] = attended.astype(BF16)
            lse_ref[h : h + 1, cols] = peak[h : h + 1, :] + jnp.log(total[h : h + 1, :])


def attend_scratch():
    return [
        pltpu.VMEM((2, QROWS, RUN), BF16),
        pltpu.VMEM((SEQ, HEAD_DIM), BF16),
        pltpu.VMEM((HEAD_DIM, SEQ), BF16),
        pltpu.VMEM((8, RUN), F32),
        pltpu.VMEM((8, RUN), F32),
        pltpu.VMEM((QROWS, RUN), F32),
    ]


def spread_keys(kv_ref, key_rows, value_rows, key_lines, x):
    ones = unit(TOK)

    def step(j, carry):
        place = pl.ds(pl.multiple_of(j * TOK, TOK), TOK)
        block = kv_ref[j // PLANE, lax.rem(j, PLANE)]
        turned = product_nt(ones, block).astype(BF16)
        key_rows[place, :] = turned[:, :HEAD_DIM]
        value_rows[place, :] = turned[:, HEAD_DIM:]
        key_lines[:, place] = block[:HEAD_DIM]
        return carry

    lax.fori_loop(0, (8 - x) * 4, step, 0)


def attend_back_step(
    x, step, queries, do_ref, o_ref, lse_ref, starts, key_rows, value_rows, key_lines,
    key_grad, value_grad, query_grad, delta, dq_ref,
):
    run, block, first, last = run_of(x, step)
    cols = pl.ds(pl.multiple_of(run * RUN, RUN), RUN)

    @pl.when(first)
    def begin():
        query_grad[...] = jnp.zeros_like(query_grad)
        for h in range(GROUP):
            rows = slice(h * HEAD_DIM, (h + 1) * HEAD_DIM)
            delta[h : h + 1, :] = jnp.sum(
                do_ref[rows, cols].astype(F32) * o_ref[rows, cols], 0, keepdims=True
            )

    place = pl.ds(pl.multiple_of(block * RUN, RUN), RUN)
    keys, values, lines = key_rows[place, :], value_rows[place, :], key_lines[:, place]
    seen = visible_block(starts, x, run, block)
    dk, dv = key_grad[place, :], value_grad[place, :]
    for h in range(GROUP):
        rows = slice(h * HEAD_DIM, (h + 1) * HEAD_DIM)
        q = queries[run, rows, :] * jnp.asarray(SCORE_SCALE, BF16)
        do = do_ref[rows, cols]
        scores = jnp.dot(keys, q, preferred_element_type=F32)
        weights = jnp.exp(jnp.where(seen, scores, MASK_FILL) - lse_ref[h : h + 1, cols])
        pull = jnp.dot(values, do, preferred_element_type=F32)
        ds = (weights * (pull - delta[h : h + 1, :])).astype(BF16)
        dv = dv + product_nt(weights.astype(BF16), do)
        dk = dk + product_nt(ds, q)
        query_grad[rows, :] += jnp.dot(lines, ds, preferred_element_type=F32)
    key_grad[place, :] = dk
    value_grad[place, :] = dv

    @pl.when(last)
    def end():
        scaled = (SCORE_SCALE * query_grad[...]).astype(BF16)
        for part in range(4):
            dq_ref[run, part] = scaled[:, part * TOK : (part + 1) * TOK]


def collect_keys(key_grad, value_grad, dkv_ref):
    ones = unit(HEAD_DIM)

    def step(j, carry):
        place = pl.ds(pl.multiple_of(j * TOK, TOK), TOK)
        dkv_ref[j // PLANE, lax.rem(j, PLANE), :HEAD_DIM, :] = product_nt(
            ones, key_grad[place, :].astype(BF16)
        ).astype(BF16)
        dkv_ref[j // PLANE, lax.rem(j, PLANE), HEAD_DIM:, :] = product_nt(
            ones, value_grad[place, :].astype(BF16)
        ).astype(BF16)
        return carry

    lax.fori_loop(0, SEQ // TOK, step, 0)


def attend_back_scratch():
    return [
        pltpu.VMEM((2, QROWS, RUN), BF16),
        pltpu.VMEM((QROWS, 2 * RUN), BF16),
        pltpu.VMEM((SEQ, HEAD_DIM), BF16),
        pltpu.VMEM((SEQ, HEAD_DIM), BF16),
        pltpu.VMEM((HEAD_DIM, SEQ), BF16),
        pltpu.VMEM((SEQ, HEAD_DIM), F32),
        pltpu.VMEM((SEQ, HEAD_DIM), F32),
        pltpu.VMEM((QROWS, RUN), F32),
        pltpu.VMEM((8, RUN), F32),
    ]


def shards(
    layer_input,
    segments,
    choices,
    first_gain,
    query_weight,
    key_value_matrix,
    output_weight,
    second_gain,
    router_weight,
    gate_up_weight,
    down_weight,
    cotangent,
):
    shard, rep = my_place()
    z, place, x, y = parts_of(shard)

    gain_lines = jnp.stack([first_gain, second_gain])
    frequency = ROPE_BASE ** (-jnp.arange(0, HEAD_DIM, 2, dtype=F32) / HEAD_DIM)
    column_place = (
        (jnp.arange(2, dtype=jnp.int32)[:, None] * PLANE + place) * TOK
        + jnp.arange(TOK, dtype=jnp.int32)[None, :]
    )
    angle = column_place.astype(F32)[:, None, :] * frequency[None, :, None]
    cosine, sine = jnp.cos(angle), jnp.sin(angle)
    (
        q_here, kv_here, starts, o_here, o_low, lse, normed_lines, turned, residual, normed_two, normed_two_all,
        expert_pack, dy_all, choices_all, dy_traded, choices_traded, out_slice,
    ) = forward(
        layer_input[0],
        segments,
        query_weight,
        key_value_matrix,
        router_weight.T,
        gain_lines,
        output_weight,
        choices[0].T,
        cotangent[0],
        jnp.swapaxes(gate_up_weight, 0, 1),
        jnp.swapaxes(down_weight, 0, 1),
        cosine,
        sine,
    )

    mixture_part, grad_residual, grad_logits, grad_lin_all, pack_sum = experts(
        normed_two_all,
        dy_all,
        expert_pack.reshape(D, EXPERT_PACK),
        choices_all,
        residual,
        dy_traded,
        turned,
    )
    grad_normed, attn_own, pack_own, out_own, layer_out, grad_back = backward(
        q_here, kv_here, mixture_part, residual, normed_lines, turned, normed_two, grad_logits,
        cosine, sine, o_low, grad_lin_all.reshape(COLUMN, D), pack_sum, grad_residual, o_here, lse, starts, out_slice,
    )
    (
        input_grad, layer_out, query_grad, keyval_grad, out_grad_rows, router_grad, gate_up_grad, down_grad,
        first_grad, second_grad,
    ) = assemble(
        attn_own,
        pack_own,
        out_own,
        query_weight,
        key_value_matrix,
        router_weight.T,
        jnp.swapaxes(gate_up_weight, 0, 1),
        gain_lines,
        grad_normed,
        grad_back,
        layer_input[0],
        turned,
        layer_out,
    )
    return (
        layer_out[None],
        input_grad[None],
        first_grad[0],
        query_grad,
        keyval_grad,
        out_grad_rows,
        second_grad[0],
        router_grad.T,
        jnp.swapaxes(gate_up_grad, 0, 1),
        jnp.swapaxes(down_grad, 0, 1),
    )


def solution(mesh):
    row = P("shard", None)
    rows = P("shard", None, None)
    own = P("rep", "shard", None)
    in_specs = (own, P("rep", "shard"), own, P("shard"), row, row, row, P("shard"), row, rows, rows, own)
    out_specs = (own, own, P("shard"), row, row, row, P("shard"), row, rows, rows)
    return jax.shard_map(shards, mesh=mesh, in_specs=in_specs, out_specs=out_specs, check_vma=False)
```

```python
import jax
import jax.numpy as jnp
from jax import lax
from jax.experimental import pallas as pl
from jax.experimental.pallas import tpu as pltpu
from jax.sharding import PartitionSpec as P

D = 1536
HEADS = 8
GROUP = 3
HEAD_DIM = 64
HALF = HEAD_DIM // 2
FF = 512
EXPERTS = 10
TOK = 128
SEQ = 4096
PLANE = 16
RUN = 512
QROWS = GROUP * HEAD_DIM
PACK = 384
ROUTER_AT = 320
GAIN_ONE_AT = 336
GAIN_TWO_AT = 337
COLUMN = 8 * TOK
PARTS = 2
PART = TOK // PARTS
GATE_UP = 1280
EXPERT_PACK = 1920

NORM_EPS = 1e-06
RESIDUAL_SCALE = 0.22
SCORE_SCALE = 0.015625
ROPE_BASE = 10000.0
MASK_FILL = -1e30
PRECISE = lax.Precision.HIGHEST
BF16 = jnp.bfloat16
F32 = jnp.float32
VMEM_LIMIT = 56 * 1024 * 1024


def my_place():
    return lax.axis_index("shard"), lax.axis_index("rep")


def parts_of(shard):
    place = lax.rem(shard, PLANE)
    return shard // PLANE, place, place // 4, lax.rem(place, 4)


def same(one, other):
    return jnp.logical_and(one[0] == other[0], one[1] == other[1])


def crossed(number):
    if isinstance(number, int):
        return (0, 2, 1, 3)[number]
    return number + (number == 1).astype(jnp.int32) - (number == 2).astype(jnp.int32)


class Place:
    def __init__(self, me):
        self.me = me
        self.shard, self.rep = me
        self.z_lo, self.place, self.x, self.y = parts_of(self.shard)
        self.core = lax.rem(self.rep, 2)
        self.z = (self.rep // 2) * 2 + self.z_lo
        self.member = self.z_lo * 4 + self.rep

    def device(self, z, x, y, core):
        return lax.rem(z, 2) * PLANE + 4 * x + y, (z // 2) * 2 + core

    def step(self, axis, by):
        z, x, y = self.z, self.x, self.y
        if axis == "z":
            z = lax.rem(z + by, 4)
        elif axis == "x":
            x = lax.rem(x + by, 4)
        else:
            y = lax.rem(y + by, 4)
        return self.device(z, x, y, self.core)

    def sibling(self):
        return self.shard, self.rep + 1 - 2 * self.core

    def partner(self):
        return self.shard + (1 - 2 * self.z_lo) * PLANE, self.rep

    def trader(self):
        return self.z_lo * PLANE + 4 * mirrored(self.z_lo, self.x) + crossed(self.rep), crossed(self.y)

    def member_at(self, z, core):
        return lax.rem(z, 2) * 4 + (z // 2) * 2 + core

    def near(self):
        result = [self.sibling()]
        for axis in ("z", "x", "y"):
            result += [self.step(axis, 1), self.step(axis, 3)]
        return result


def mesh_id(place):
    return {"shard": place[0], "rep": place[1]}


class Net:
    def __init__(self, here, sems):
        self.here, self.sems, self.used, self.sent = here, sems, 0, []

    def take(self, count=1):
        first = self.used
        self.used += count
        return first

    def push(self, source, target, to):
        number = self.take(2)
        copy = pltpu.make_async_remote_copy(
            src_ref=source,
            dst_ref=target,
            send_sem=self.sems.at[number],
            recv_sem=self.sems.at[number + 1],
            device_id=mesh_id(to),
        )
        copy.start()
        self.sent.append(copy)
        return number + 1

    def got(self, number, region):
        pltpu.make_async_remote_copy(
            src_ref=region,
            dst_ref=region,
            send_sem=self.sems.at[number],
            recv_sem=self.sems.at[number],
            device_id=mesh_id(self.here.sibling()),
        ).wait_recv()

    def local(self, source, target):
        copy = pltpu.make_async_copy(source, target, self.sems.at[self.take()])
        copy.start()
        return copy

    def finish(self):
        for copy in self.sent:
            copy.wait_send()


class Route:
    def __init__(self, n, to, source, pieces, index=None, may_be_self=False):
        self.n, self.to, self.source, self.pieces = n, to, source, pieces
        self.index = index or (lambda i: i)
        self.may_be_self = may_be_self


def each(n, body):
    if n <= 8:
        for i in range(n):
            body(i)
    else:

        def step(i, carry):
            body(i)
            return carry

        lax.fori_loop(0, n, step, 0)


def greet_routes(routes, me, barrier):
    awaited = 0
    for route in routes:

        def greet(i, route=route):
            source = route.source(i)

            def signal():
                pl.semaphore_signal(barrier, inc=1, device_id=mesh_id(source))

            if route.may_be_self:
                pl.when(jnp.logical_not(same(source, me)))(signal)
            else:
                signal()

        each(route.n, greet)
        awaited = awaited + route.n
        if route.may_be_self:
            for i in range(route.n):
                awaited = awaited - same(route.to(i), me).astype(jnp.int32)
    return awaited


HOP = 2.0


def time_of(ref, rate=50.0):
    size = jnp.dtype(ref.dtype).itemsize / 1000.0
    for extent in ref.shape:
        size *= extent
    return HOP + size / rate


def follow_routes(net, routes, ins, outs, guess=15.0):
    me = net.here.me
    held = []
    for route in routes:
        count = route.n * len(route.pieces)
        held.append((net.take(count), net.take(count), net.take(len(route.pieces))))

    def remote(route, base, i, k, piece):
        source_in, cut, target_out, slot, unused = piece
        return pltpu.make_async_remote_copy(
            src_ref=ins[source_in].at[cut(i)],
            dst_ref=outs[target_out].at[slot(i)],
            send_sem=net.sems.at[base[0] + i * len(route.pieces) + k],
            recv_sem=net.sems.at[base[1] + route.index(i) * len(route.pieces) + k],
            device_id=mesh_id(route.to(i)),
        )

    def within(base, i, k, piece):
        source_in, cut, target_out, slot, unused = piece
        return pltpu.make_async_copy(
            ins[source_in].at[cut(i)], outs[target_out].at[slot(i)], net.sems.at[base[2] + k]
        )

    for route, base in zip(routes, held):

        def start(i, route=route, base=base):
            for k, piece in enumerate(route.pieces):
                copy = remote(route, base, i, k, piece)
                if route.may_be_self:
                    here = same(route.to(i), me)
                    pl.when(jnp.logical_not(here))(copy.start)
                    pl.when(here)(within(base, i, k, piece).start)
                else:
                    copy.start()

        each(route.n, start)
    yield guess
    for route, base in zip(routes, held):

        def arrive(i, route=route, base=base):
            for k, piece in enumerate(route.pieces):
                region = outs[piece[2]].at[piece[4](i)]
                place = route.source(i)
                sem = net.sems.at[base[1] + i * len(route.pieces) + k]
                copy = pltpu.make_async_remote_copy(
                    src_ref=region, dst_ref=region, send_sem=sem, recv_sem=sem, device_id=mesh_id(place)
                )
                if route.may_be_self:
                    pl.when(jnp.logical_not(same(place, me)))(copy.wait_recv)
                else:
                    copy.wait_recv()

        each(route.n, arrive)

        def leave(i, route=route, base=base):
            for k, piece in enumerate(route.pieces):
                copy = remote(route, base, i, k, piece)
                if route.may_be_self:
                    here = same(route.to(i), me)
                    pl.when(jnp.logical_not(here))(copy.wait_send)
                    pl.when(here)(within(base, i, k, piece).wait)
                else:
                    copy.wait_send()

        each(route.n, leave)


def trade(net, pieces, begin=0.0, now=30.0):
    other = net.here.trader()
    here = same(other, net.here.me)
    if begin:
        yield begin
    copies = []
    for source, target in pieces:
        number = net.take(2)
        remote = pltpu.make_async_remote_copy(
            src_ref=source,
            dst_ref=target,
            send_sem=net.sems.at[number],
            recv_sem=net.sems.at[number + 1],
            device_id=mesh_id(other),
        )
        within = pltpu.make_async_copy(source, target, net.sems.at[net.take()])
        pl.when(jnp.logical_not(here))(remote.start)
        pl.when(here)(within.start)
        copies.append((remote, within))
    yield now
    for remote, within in copies:
        pl.when(jnp.logical_not(here))(remote.wait)
        pl.when(here)(within.wait)


def greet_trader(here, barrier):
    other = here.trader()
    away = jnp.logical_not(same(other, here.me))

    @pl.when(away)
    def signal():
        pl.semaphore_signal(barrier, inc=1, device_id=mesh_id(other))

    return away.astype(jnp.int32)


def spread_rows(net, rows, out):
    here = net.here
    ahead = lax.rem(here.x - here.rep + 4, 4)
    pair = lambda k: out.at[pl.ds(2 * k, 2)]
    row_halves = row_half(48)

    def at(by):
        return out.at[lax.rem(here.y + by, 4)]

    def copy(number, source, target, to):
        return pltpu.make_async_remote_copy(
            src_ref=source,
            dst_ref=target,
            send_sem=net.sems.at[number],
            recv_sem=net.sems.at[number + 1],
            device_id=mesh_id(to),
        )

    def come(number, region):
        copy(number, region, region, here.sibling()).wait_recv()

    up, down, right, left = here.step("y", 1), here.step("y", 3), here.step("x", 1), here.step("x", 3)
    numbers = [net.take(2) for k in range(8)]
    keep = pltpu.make_async_copy(rows, at(0), net.sems.at[net.take()])
    first = [copy(numbers[0], rows, at(0), up), copy(numbers[1], rows, at(0), down)]
    second = [
        copy(numbers[2], row_halves(at(3), 0), row_halves(at(3), 0), up),
        copy(numbers[3], row_halves(at(1), 1), row_halves(at(1), 1), down),
    ]
    third = [copy(numbers[4], out, out, right), copy(numbers[5], out, out, left)]
    on_right = copy(numbers[6], pair(0), pair(0), right)
    on_left = copy(numbers[7], pair(1), pair(1), left)

    @pl.when(ahead == 0)
    def begin():
        keep.start()
        first[0].start()
        first[1].start()

    now = time_of(rows)
    yield now

    @pl.when(ahead == 0)
    def hand_on():
        come(numbers[0], at(3))
        second[0].start()
        come(numbers[1], at(1))
        second[1].start()

    now += time_of(rows, 100.0)
    yield now

    @pl.when(ahead == 0)
    def go_out():
        come(numbers[2], row_halves(at(2), 0))
        come(numbers[3], row_halves(at(2), 1))
        keep.wait()
        third[0].start()
        third[1].start()

    now += time_of(out, 70.0)
    yield now

    @pl.when(ahead == 1)
    def to_right():
        come(numbers[4], out)
        on_right.start()

    @pl.when(ahead == 3)
    def to_left():
        come(numbers[5], out)
        on_left.start()

    now += time_of(out, 140.0)
    yield now

    @pl.when(ahead == 2)
    def end():
        come(numbers[6], pair(0))
        come(numbers[7], pair(1))

    @pl.when(ahead == 0)
    def sent():
        for each_copy in first + second + third:
            each_copy.wait_send()

    pl.when(ahead == 1)(on_right.wait_send)
    pl.when(ahead == 3)(on_left.wait_send)


def comm(inputs, in_vmem, outputs, scratch, n_sems, collective_id, plan):
    n_in, n_out = len(inputs), len(outputs)

    def kernel(*refs):
        ins, outs = refs[:n_in], refs[n_in : n_in + n_out]
        rest, sems = refs[n_in + n_out : -1], refs[-1]
        net = Net(Place(my_place()), sems)
        flows, routes, near, greetings = plan(net, ins, outs, rest)
        barrier = pltpu.get_barrier_semaphore()
        awaited = greet_routes(routes, net.here.me, barrier)
        if near:
            others = net.here.near()
            for other in others:
                pl.semaphore_signal(barrier, inc=1, device_id=mesh_id(other))
            awaited = awaited + len(others)
        for greeting in greetings:
            awaited = awaited + greeting(net.here, barrier)
        pl.semaphore_wait(barrier, awaited)
        waits = [(0.0, number, flow) for number, flow in enumerate(flows)]
        while waits:
            unused, number, flow = waits.pop(0)
            when = next(flow, None)
            if when is not None:
                waits = sorted(waits + [(when, number, flow)], key=lambda wait: wait[:2])
        net.finish()
        assert net.used <= n_sems, net.used

    vmem = pl.BlockSpec(memory_space=pltpu.VMEM)
    anywhere = pl.BlockSpec(memory_space=pl.ANY)
    return pl.pallas_call(
        kernel,
        out_shape=[jax.ShapeDtypeStruct(s, t) for s, t, unused in outputs],
        in_specs=[vmem if k in in_vmem else anywhere for k in range(n_in)],
        out_specs=[vmem if inside else anywhere for unused, unused2, inside in outputs],
        scratch_shapes=list(scratch) + [pltpu.SemaphoreType.DMA((n_sems,))],
        compiler_params=pltpu.CompilerParams(
            collective_id=collective_id, has_side_effects=True, vmem_limit_bytes=VMEM_LIMIT
        ),
    )(*inputs)


def together(flows):
    waits, now = [(next(flow), number, flow) for number, flow in enumerate(flows)], 0.0
    while waits:
        waits = sorted(waits, key=lambda wait: wait[:2])
        now, number, flow = waits.pop(0)
        yield now
        when = next(flow, None)
        if when is not None:
            waits.append((when, number, flow))
    return now


def resumed(when, flow):
    yield when
    yield from flow


def column_gather(net, source, out, half_of, now=0.0):
    here = net.here

    def slot(by, core):
        return out.at[here.member_at(lax.rem(here.z + by, 4), core)]

    core, other = here.core, 1 - here.core
    right, left, sibling = here.step("z", 1), here.step("z", 3), here.sibling()
    keep = net.local(source, slot(0, core))
    a = net.push(source, slot(0, core), right)
    b = net.push(source, slot(0, core), left)
    s = [net.push(source, slot(0, core), sibling)]
    now += time_of(source)
    yield now
    net.got(a, slot(3, core))
    c = net.push(half_of(slot(3, core), 0), half_of(slot(3, core), 0), right)
    s.append(net.push(slot(3, core), slot(3, core), sibling))
    net.got(b, slot(1, core))
    d = net.push(half_of(slot(1, core), 1), half_of(slot(1, core), 1), left)
    s.append(net.push(slot(1, core), slot(1, core), sibling))
    now += time_of(source, 100.0)
    yield now
    net.got(c, half_of(slot(2, core), 0))
    net.got(d, half_of(slot(2, core), 1))
    s.append(net.push(slot(2, core), slot(2, core), sibling))
    yield now + time_of(source, 200.0)
    for number, by in zip(s, (0, 3, 1, 2)):
        net.got(number, slot(by, other))
    keep.wait()


def row_half(size):
    first = (size // 2 + 15) // 16 * 16

    def half(ref, k):
        return ref.at[pl.ds(0, first)] if k == 0 else ref.at[pl.ds(first, size - first)]

    return half


def ring_gather(net, axis, source, slot, half, now, rate):
    right, left = net.here.step(axis, 1), net.here.step(axis, 3)
    a = net.push(source, slot(0), right)
    b = net.push(source, slot(0), left)
    now += time_of(source, rate)
    yield now
    net.got(a, slot(3))
    c = net.push(half(slot(3), 0), half(slot(3), 0), right)
    net.got(b, slot(1))
    d = net.push(half(slot(1), 1), half(slot(1), 1), left)
    now += time_of(source, 2 * rate)
    yield now
    net.got(c, half(slot(2), 0))
    net.got(d, half(slot(2), 1))
    return now


def swap_pair(net, payload, target, begin, now):
    here = net.here
    yield begin
    number = net.push(payload.at[1 - here.z_lo], target, here.partner())
    yield now
    net.got(number, target)


def plane_gather(net, payload, pair, out, rate=50.0, now=0.0):
    here = net.here
    z, x, y = here.z_lo, here.x, here.y
    rows = row_half(48)
    two = lambda ref, k: ref.at[pl.ds(2 * k, 2)]
    swap = []

    def first():
        if pair is None:
            swap.append(net.push(payload.at[1 - z], out.at[z, x, y], here.partner()))
        keep = net.local(payload.at[z], out.at[z, x, y])
        then = yield from ring_gather(
            net, "x", payload.at[z], lambda by: out.at[z, lax.rem(x + by, 4), y], rows, now, rate
        )
        keep.wait()
        bundle = lambda by: out.at[z, :, lax.rem(y + by, 4)]
        yield from ring_gather(net, "y", bundle(0), bundle, two, then, rate)

    def second():
        w = 1 - z
        then, source = now, pair
        if pair is None:
            then, source = now + time_of(payload.at[0], rate), out.at[w, x, y]
            yield then
            net.got(swap[0], source)
        else:
            keep = net.local(pair, out.at[w, x, y])
        then = yield from ring_gather(
            net, "y", source, lambda by: out.at[w, x, lax.rem(y + by, 4)], rows, then, rate
        )
        if pair is not None:
            keep.wait()
        bundle = lambda by: out.at[w, lax.rem(x + by, 4)]
        yield from ring_gather(net, "x", bundle(0), bundle, two, then, rate)

    return [first(), second()]


def add(target, *parts):
    total = parts[0][...].astype(F32)
    for part in parts[1:]:
        total = total + part[...].astype(F32)
    target[...] = total.astype(target.dtype)


def ring_sum(net, axis, block, half, halves, wholes, target, now, rate=50.0):
    right, left = net.here.step(axis, 1), net.here.step(axis, 3)
    lower, upper = halves
    a = net.push(half(block(2), 0), lower, right)
    b = net.push(half(block(2), 1), upper, left)
    now += time_of(lower, rate)
    yield now
    net.got(a, lower)
    add(half(block(1), 0), half(block(1), 0), lower)
    c = net.push(block(1), wholes[0], right)
    net.got(b, upper)
    add(half(block(3), 1), half(block(3), 1), upper)
    d = net.push(block(3), wholes[1], left)
    now += time_of(wholes[0], rate)
    yield now
    net.got(c, wholes[0])
    net.got(d, wholes[1])
    add(target, block(0), wholes[0], wholes[1])
    return now


def column_sum(net, parts, out, sums, sibling_parts, halves, wholes, now=0.0):
    here = net.here
    half = row_half(parts.shape[1])
    at = lambda by: lax.rem(here.z + by, 4)
    numbers = {}
    for by in (2, 1, 3, 0):
        numbers[by] = net.push(
            parts.at[here.member_at(at(by), 1 - here.core)], sibling_parts.at[at(by)], here.sibling()
        )
    now += HOP
    for by in (2, 1, 3):
        now += time_of(sums.at[0], 200.0) - HOP
        yield now
        net.got(numbers[by], sibling_parts.at[at(by)])
        add(sums.at[at(by)], parts.at[here.member_at(at(by), here.core)], sibling_parts.at[at(by)])
        if by == 2:
            ring = ring_sum(
                net, "z", lambda by: sums.at[at(by)], half, (halves.at[0], halves.at[1]),
                (wholes.at[0], wholes.at[1]), out, now,
            )
            when = next(ring)
    net.got(numbers[0], sibling_parts.at[at(0)])
    add(sums.at[at(0)], parts.at[here.member_at(at(0), here.core)], sibling_parts.at[at(0)])
    yield when
    now = yield from ring
    return now


def column_sum_rows(net, parts, out, scratch, k, now):
    sums, sibling_parts, halves, wholes = scratch
    rows, half_rows = pl.ds(k * PART, PART), pl.ds(k * PART // 2, PART // 2)
    now = yield from column_sum(
        net, parts.at[:, rows], out.at[rows], sums.at[:, rows], sibling_parts.at[:, rows], halves.at[:, half_rows],
        wholes.at[:, rows], now=now,
    )
    return now


def column_sum_scratch(rows, columns):
    return [
        pltpu.VMEM((4, rows, columns), BF16),
        pltpu.VMEM((4, rows, columns), BF16),
        pltpu.VMEM((2, rows // 2, columns), BF16),
        pltpu.VMEM((2, rows, columns), BF16),
    ]


def plane_sum(net, parts, out, held, pairs, bundles, rows_a, rows_b, blocks, rate=50.0, now=2.0):
    here = net.here
    at_x = lambda by: lax.rem(here.x + by, 4)
    at_y = lambda by: lax.rem(here.y + by, 4)
    pair = lambda ref, k: ref.at[pl.ds(2 * k, 2)]
    half = row_half(48)

    def first():
        if parts is not None:
            copy = net.local(parts.at[0], held.at[0])
            yield now
            copy.wait()
        mine = held.at[0, :, here.y]
        then = yield from ring_sum(
            net, "y", lambda by: held.at[0, :, at_y(by)], pair, (pairs.at[0], pairs.at[1]),
            (bundles.at[0], bundles.at[1]), mine, now, rate,
        )
        yield from ring_sum(
            net, "x", lambda by: held.at[0, at_x(by), here.y], half, (rows_a.at[0], rows_b.at[0]),
            (blocks.at[0], blocks.at[1]), out.at[0], then, rate,
        )

    def second():
        if parts is not None:
            copy = net.local(parts.at[1], held.at[1])
            yield now
            copy.wait()
        mine = held.at[1, here.x]
        then = yield from ring_sum(
            net, "x", lambda by: held.at[1, at_x(by)], pair, (pairs.at[2], pairs.at[3]),
            (bundles.at[2], bundles.at[3]), mine, now, rate,
        )
        yield from ring_sum(
            net, "y", lambda by: held.at[1, here.x, at_y(by)], half, (rows_a.at[1], rows_b.at[1]),
            (blocks.at[2], blocks.at[3]), out.at[1], then, rate,
        )

    return [first(), second()]


def plane_sum_scratch(columns):
    return [
        pltpu.VMEM((2, 4, 4, 48, columns), BF16),
        pltpu.VMEM((4, 2, 48, columns), BF16),
        pltpu.VMEM((4, 4, 48, columns), BF16),
        pltpu.VMEM((2, 32, columns), BF16),
        pltpu.VMEM((2, 16, columns), BF16),
        pltpu.VMEM((4, 48, columns), BF16),
    ]


def column_deal(net, parts, out, passing, half, now=0.0, begin=0.0):
    here = net.here
    z = here.z_lo
    if begin:
        yield begin
        now = max(now, begin)
    core, other = here.core, 1 - here.core
    lower, upper = passing

    def slot(by, core):
        return out.at[here.member_at(lax.rem(here.z + by, 4), core)]

    right, left, sibling = here.step("z", 1), here.step("z", 3), here.sibling()
    keep = net.local(parts.at[z], slot(0, core))
    e = net.push(half(parts.at[z], 0), lower, right)
    f = net.push(half(parts.at[z], 1), upper, left)
    a = net.push(parts.at[1 - z], slot(0, core), right)
    b = net.push(parts.at[1 - z], slot(0, core), left)
    s = [net.push(parts.at[z], slot(0, core), sibling)]
    now += time_of(parts.at[0])
    yield now
    net.got(e, lower)
    c = net.push(lower, half(slot(3, core), 0), right)
    net.got(f, upper)
    d = net.push(upper, half(slot(1, core), 1), left)
    net.got(a, slot(3, core))
    s.append(net.push(slot(3, core), slot(3, core), sibling))
    net.got(b, slot(1, core))
    s.append(net.push(slot(1, core), slot(1, core), sibling))
    now += time_of(parts.at[0])
    yield now
    net.got(c, half(slot(2, core), 0))
    net.got(d, half(slot(2, core), 1))
    s.append(net.push(slot(2, core), slot(2, core), sibling))
    yield now + HOP
    for number, by in zip(s, (0, 3, 1, 2)):
        net.got(number, slot(by, other))
    keep.wait()


def column_route(me, pieces):
    z, place, unused, unused2 = parts_of(me[0])
    mine = z * 4 + me[1]

    def where(member):
        return (member // 4) * PLANE + place, lax.rem(member, 4)

    def after(i):
        return lax.rem(mine + 1 + i, 8)

    def before(i):
        return lax.rem(mine + 7 - i, 8)

    return Route(
        7,
        lambda i: where(after(i)),
        lambda i: where(before(i)),
        [
            (
                a,
                lambda i, cut=cut: cut(after(i)),
                b,
                lambda i, slot=slot: slot(mine),
                lambda i, slot=slot: slot(before(i)),
            )
            for a, cut, b, slot in pieces
        ],
    )


def plane_route(me, pieces):
    z, place, unused, unused2 = parts_of(me[0])

    def after(i):
        return lax.rem(place + 1 + i, PLANE)

    def before(i):
        return lax.rem(place + 15 - i, PLANE)

    return Route(
        15,
        lambda i: (z * PLANE + after(i), me[1]),
        lambda i: (z * PLANE + before(i), me[1]),
        [
            (
                a,
                lambda i, cut=cut: cut(after(i)),
                b,
                lambda i, slot=slot: slot(place),
                lambda i, slot=slot: slot(before(i)),
            )
            for a, cut, b, slot in pieces
        ],
    )


def own_copies(net, ins, outs, copies):
    started = [net.local(ins[a].at[cut], outs[b].at[slot]) for a, cut, b, slot in copies]
    yield 100.0
    for copy in started:
        copy.wait()


ROW_HALF = row_half(TOK)


def mirrored(z, x):
    return x + z * (3 - 2 * x)


def query_routes(me, q_in, q_out):
    z_me, place, x, y = parts_of(me[0])
    base = z_me * PLANE

    def plain(i):
        return lax.rem(y + 1 + i, 4)

    def plain_before(i):
        return lax.rem(y + 3 - i, 4)

    def other(i):
        return lax.rem(y + i, 4)

    def other_before(i):
        return lax.rem(y + 4 - i, 4)

    first = Route(
        3,
        lambda i: (base + 4 * x + plain(i), me[1]),
        lambda i: (base + 4 * x + plain_before(i), me[1]),
        [
            (
                q_in,
                lambda i: (0, crossed(plain(i))),
                q_out,
                lambda i: (0, crossed(y)),
                lambda i: (0, crossed(plain_before(i))),
            )
        ],
    )
    second = Route(
        4,
        lambda i: (base + 4 * (3 - x) + other(i), me[1]),
        lambda i: (base + 4 * (3 - x) + other_before(i), me[1]),
        [
            (
                q_in,
                lambda i: (1, crossed(other(i))),
                q_out,
                lambda i: (1, crossed(y)),
                lambda i: (1, crossed(other_before(i))),
            )
        ],
    )
    return [first, second], [(q_in, (0, crossed(y)), q_out, (0, crossed(y)))]


def pack_attention(pack, query_weight, keyval_weight, router_lines, first_gain, second_gain, rep):
    blank = jnp.zeros((3, 48), F32)
    lines = router_lines[...].astype(F32)
    small = jnp.concatenate(
        [
            lines[:5], blank, lines[5:], blank, first_gain[...].astype(F32), second_gain[...].astype(F32),
            jnp.zeros((6, 48), F32),
        ],
        0,
    ).T.astype(BF16)
    fill = jnp.zeros((48, PACK - ROUTER_AT - 24), BF16)
    for k in range(4):

        @pl.when(rep == k)
        def fill_in(k=k):
            for z in range(2):
                m = 4 * z + k
                pack[z] = jnp.concatenate(
                    [
                        query_weight[:, m * QROWS : (m + 1) * QROWS],
                        keyval_weight[:, m * HEAD_DIM : (m + 1) * HEAD_DIM],
                        keyval_weight[:, (HEADS + m) * HEAD_DIM : (HEADS + m + 1) * HEAD_DIM],
                        small,
                        fill,
                    ],
                    1,
                )


def pack_experts(net, pack, gate_up_weight, down_weight):
    copies = []
    for z in range(2):
        for expert in range(5):
            for side in range(2):
                source = pl.ds(pl.multiple_of(side * FF + net.here.rep * TOK, TOK), TOK)
                target = pl.ds(expert * 256 + side * TOK, TOK)
                copies.append((gate_up_weight.at[5 * z + expert, :, source], pack.at[z, :, target]))
            source = pl.ds(pl.multiple_of(net.here.rep * TOK, TOK), TOK)
            target = pl.ds(GATE_UP + expert * TOK, TOK)
            copies.append((down_weight.at[5 * z + expert, :, source], pack.at[z, :, target]))
    return [net.local(source, target) for source, target in copies]


def forward(
    x, segments, query_weight, keyval_weight, router_lines, first_gain, out_rows, choices, dy, gate_up_weight,
    down_weight, cosine, sine, second_gain,
):
    def plan(net, ins, outs, scratch):
        here = net.here
        me = here.me
        place, x_at, y_at = here.place, here.x, here.y
        (x_all, attn_all, segment_all, q, kv, ints, normed, linear, out_slice, x_traded, pair, low_rows, parts,
         total) = scratch[:14]
        attending, summing = scratch[14:20], scratch[20:24]
        segment_here, attn, pack, segment_rows, lines, q_here, kv_here, o_here = scratch[24:32]
        (q_kept, kv_kept, starts, o_kept, o_low, lse, lines_kept, turned, residual, own_normed, normed_all, pack_all,
         dy_all, choices_all, dy_traded, choices_traded, out_given) = outs[:17]
        x, segments, out_rows, choices, dy, cosine, sine = ins[0], ins[1], ins[6], ins[7], ins[8], ins[11], ins[12]
        routes, own = query_routes(me, 0, 0)
        routes = [
            plane_route(
                me,
                [
                    (1, lambda p: (0, crossed(lax.rem(p, 4))), 1, lambda p: (0, p)),
                    (1, lambda p: (1, crossed(lax.rem(p, 4))), 1, lambda p: (1, p)),
                    (2, lambda p: crossed(lax.rem(p, 4)), 2, lambda p: p),
                ],
            )
        ] + routes
        own = own + [
            (1, (0, crossed(y_at)), 1, (0, place)),
            (1, (1, crossed(y_at)), 1, (1, place)),
            (2, crossed(y_at), 2, place),
        ]
        segment_routes = [column_route(me, [(0, lambda m: slice(None), 0, lambda m: m)])]
        choice_routes = [column_route(me, [(0, lambda m: slice(None), 0, lambda m: m)])]
        spreading = spread_rows(net, out_rows, out_slice)
        trading = trade(net, [(x, x_traded)], 45.0, 66.0)

        def chain():
            pack_attention(attn, ins[2], ins[3], ins[4], ins[5], ins[13], here.rep)
            segment_rows[...] = jnp.broadcast_to(segments[...], (8, TOK))
            marked = follow_routes(net, segment_routes, [segment_rows], [segment_all])
            next(marked)
            own_mark = net.local(segment_rows, segment_all.at[here.member])
            now = yield from together(plane_gather(net, attn, None, attn_all) + [column_gather(net, x, x_all, ROW_HALF)])
            for unused in marked:
                pass
            own_mark.wait()
            project(x_all, attn_all, cosine, sine, q, kv, turned, normed, linear)
            for sequence in range(4):
                ints[sequence] = jnp.concatenate(
                    [
                        segment_all[sequence, 0:1, :],
                        segment_all[4 + sequence, 0:1, :],
                        jnp.zeros((6, TOK), jnp.int32),
                    ],
                    0,
                )
            targets = [q_here, kv_here, segment_here]
            going = follow_routes(net, routes, [q, kv, ints], targets, now + 22.0)
            copies = own_copies(net, [q, kv, ints], targets, own)
            now = next(going)
            next(copies)
            turn_into(lines, normed)
            kept = [net.local(lines, lines_kept)]
            yield now
            for unused in going:
                pass
            for unused in copies:
                pass
            kept += [net.local(q_here, q_kept), net.local(kv_here, kv_kept)]
            document_starts(segment_here, starts, x_at)
            unpack_queries(q_here, attending[0])
            unpack_keys(kv_here, attending[1], attending[2], x_at)
            for third in range(3):

                def step(k, carry):
                    attend_step(x_at, k, *attending[:3], starts, *attending[3:], o_here, o_low, lse)
                    return carry

                lax.fori_loop(3 * third, 3 * third + 3, step, 0)
                now += 7.0
                yield now
            for unused in spreading:
                pass
            turn_into(low_rows, o_low)
            for block in range(4):
                columns = slice(block * 384, (block + 1) * 384)
                weights = out_slice[:, :, columns].reshape(QROWS, 384)
                product = jnp.dot(low_rows[...], weights, preferred_element_type=F32)
                parts[:, :, columns] = product.astype(BF16).reshape(8, TOK, 384)
            kept += [net.local(out_slice, out_given), net.local(o_here, o_kept)]

            def tail(k, now):
                rows = pl.ds(k * PART, PART)
                now = yield from column_sum_rows(net, parts, total, summing, k, now)
                for unused in trading:
                    pass
                gain = turned[GAIN_TWO_AT : GAIN_TWO_AT + 1, :].astype(F32)
                hidden = x_traded[rows, :].astype(F32) + RESIDUAL_SCALE * total[rows, :]
                scale = lax.rsqrt(jnp.sum(hidden * hidden, -1, keepdims=True) * (1.0 / D) + NORM_EPS)
                residual[rows, :] = hidden
                own_normed[rows, :] = (hidden * scale * gain).astype(BF16)
                yield from column_gather(net, own_normed.at[rows], normed_all.at[:, rows], row_half(PART), now)

            yield from together([tail(k, now + 3.0 + 8.0 / PARTS * k) for k in range(PARTS)])
            for copy in kept:
                copy.wait()

        def gather_dy():
            yield from trade(net, [(choices, choices_traded), (dy, dy_traded)], 0.0, 24.0)
            sent = follow_routes(net, choice_routes, [choices_traded], [choices_all], 50.0)
            when = next(sent)
            own_choices = net.local(choices_traded, choices_all.at[here.member])
            yield from together([resumed(when, sent), column_gather(net, dy_traded, dy_all, ROW_HALF, 27.0)])
            own_choices.wait()

        def gather_experts():
            packing = pack_experts(net, pack, ins[9], ins[10])
            yield 22.0
            for copy in packing:
                copy.wait()
            yield from swap_pair(net, pack, pair, 22.0, 43.0)
            yield 46.0
            yield from together(plane_gather(net, pack, pair, pack_all, rate=30.0, now=46.0))

        flows = [chain(), spreading, gather_dy(), trading, gather_experts()]
        return flows, routes + segment_routes + choice_routes, True, [greet_trader]

    return comm(
        [
            x, segments, query_weight, keyval_weight, router_lines, first_gain, out_rows, choices, dy, gate_up_weight,
            down_weight, cosine, sine, second_gain,
        ],
        (1, 2, 3, 4, 5, 11, 12, 13),
        [
            ((2, 4, QROWS, TOK), BF16, False),
            ((2, PLANE, TOK, TOK), BF16, False),
            ((2, 8, RUN), F32, True),
            ((QROWS, 2 * RUN), F32, False),
            ((QROWS, 2 * RUN), BF16, True),
            ((8, 2 * RUN), F32, True),
            ((D, COLUMN), BF16, False),
            ((PACK, D), BF16, True),
            ((TOK, D), F32, True),
            ((TOK, D), BF16, True),
            ((8, TOK, D), BF16, False),
            ((2, 4, 4, 48, EXPERT_PACK), BF16, False),
            ((8, TOK, D), BF16, False),
            ((8, 8, TOK), jnp.int32, False),
            ((TOK, D), BF16, False),
            ((8, TOK), jnp.int32, False),
            ((4, 48, D), BF16, False),
        ],
        [
            pltpu.VMEM((8, TOK, D), BF16),
            pltpu.VMEM((2, 4, 4, 48, PACK), BF16),
            pltpu.VMEM((8, 8, TOK), jnp.int32),
            pltpu.VMEM((2, 4, QROWS, TOK), BF16),
            pltpu.VMEM((2, 4, TOK, TOK), BF16),
            pltpu.VMEM((4, 8, TOK), jnp.int32),
            pltpu.VMEM((COLUMN, D), BF16),
            pltpu.VMEM((ROUTER_AT, COLUMN), F32),
            pltpu.VMEM((4, 48, D), BF16),
            pltpu.VMEM((TOK, D), BF16),
            pltpu.VMEM((48, EXPERT_PACK), BF16),
            pltpu.VMEM((COLUMN, QROWS), BF16),
            pltpu.VMEM((8, TOK, D), BF16),
            pltpu.VMEM((TOK, D), F32),
        ]
        + attend_scratch()
        + column_sum_scratch(TOK, D)
        + [
            pltpu.VMEM((PLANE, 8, TOK), jnp.int32),
            pltpu.VMEM((2, 48, PACK), BF16),
            pltpu.VMEM((2, 48, EXPERT_PACK), BF16),
            pltpu.VMEM((8, TOK), jnp.int32),
            pltpu.VMEM((D, COLUMN), BF16),
            pltpu.VMEM((2, 4, QROWS, TOK), BF16),
            pltpu.VMEM((2, PLANE, TOK, TOK), BF16),
            pltpu.VMEM((QROWS, 2 * RUN), F32),
        ],
        512,
        0,
        plan,
    )


def experts(hn_all, dy_all, pack_all, choices, residual, dy, turned):
    def plan(net, ins, outs, scratch):
        (hn, dy_here, pack, hn_lines, dy_lines, hidden, joined, shares, share_rows, pull_rows, pulls, back, mixture,
         total, low, pull_parts) = scratch[:16]
        summing, held = scratch[16:20], scratch[20:26]
        gate_up, down = pack.at[:, :GATE_UP], pack.at[:, GATE_UP:]
        routes = column_route(net.here.me, [(0, lambda m: m, 0, lambda m: m)])
        mixture_out, grad_out, logits_out, low_all, pack_sum = outs
        mine = net.here.member

        def z_chain(k, now):
            rows = pl.ds(k * PART, PART)
            if k == 0:
                pulled = follow_routes(net, [routes], [pulls], [pull_parts])
                next(pulled)
                own = net.local(pulls.at[mine], pull_parts.at[mine])
            now = yield from column_sum_rows(net, back, total, summing, k, now)
            if k == 0:
                for unused in pulled:
                    pass
                own.wait()
                logit_grads(pull_parts, shares, logits_out)
            residual_grad(total, ins[4], ins[5], ins[6], grad_out, low, logits_out, k)
            yield from column_gather(net, low.at[rows], low_all.at[:, rows], row_half(PART), now)

        def grads(now):
            sums = []

            def weights(first, size, at):
                part = pl.ds(first, size)
                flow = together(plane_sum(net, None, pack_sum.at[:, :, part], *columns_of(held, part), now=at))
                sums.append(resumed(next(flow), flow))

            turn_into(hn_lines, hn)

            def gate_up_step(j, carry):
                place = pl.ds(pl.multiple_of(j * 256, 256), 256)
                product = jnp.dot(
                    hn_lines[...], joined[:, :, place].reshape(COLUMN, 256), preferred_element_type=F32
                )
                held[0][:, :, :, :, place] = product.astype(BF16).reshape(2, 4, 4, 48, 256)
                return carry

            lax.fori_loop(0, 5, gate_up_step, 0)
            weights(0, GATE_UP, now)

            def back_step(j, carry):
                place = pl.ds(pl.multiple_of(j * 256, 256), 256)
                product = product_nt(joined[...].reshape(COLUMN, GATE_UP), gate_up[place, :])
                back[:, :, place] = product.astype(BF16).reshape(8, TOK, 256)
                return carry

            lax.fori_loop(0, D // 256, back_step, 0)
            chains = [z_chain(k, now + 5.0 + 6.0 / PARTS * k) for k in range(PARTS)]
            sums += [resumed(next(flow), flow) for flow in chains]

            def after():
                turn_into(dy_lines, dy_here)
                yield now + 8.0
                for at, size in ((0, 256), (256, 256), (512, 128)):
                    product = RESIDUAL_SCALE * jnp.dot(
                        dy_lines[...], hidden[:, :, at : at + size].reshape(COLUMN, size), preferred_element_type=F32
                    )
                    held[0][:, :, :, :, GATE_UP + at : GATE_UP + at + size] = product.astype(BF16).reshape(
                        2, 4, 4, 48, size
                    )
                part = pl.ds(GATE_UP, EXPERT_PACK - GATE_UP)
                flow = together(
                    plane_sum(net, None, pack_sum.at[:, :, part], *columns_of(held, part), now=now + 14.0)
                )
                when = next(flow)

                def mixture_step(j, carry):
                    place = pl.ds(pl.multiple_of(j * 256, 256), 256)
                    product = product_nt(hidden[...].reshape(COLUMN, 640), down[place, :])
                    mixture[:, :, place] = product.astype(BF16).reshape(8, TOK, 256)
                    return carry

                def mix():
                    yield now + 20.0
                    lax.fori_loop(0, D // 256, mixture_step, 0)
                    store = net.local(mixture, mixture_out)
                    yield now + 60.0
                    store.wait()

                yield from together([resumed(when, flow), mix()])

            yield from together(sums + [after()])

        def chain():
            loads = [net.local(ins[0], hn), net.local(ins[2], pack), net.local(ins[1], dy_here)]
            loads[0].wait()
            expert_shares(hn, ins[6], ins[3], shares, share_rows, net.here.z_lo)
            for load in loads[1:]:
                load.wait()
            for k in range(2):
                experts_forward(hn, dy_here, gate_up, down, hidden, joined, share_rows, pull_rows, k)
            turn_pull(pull_rows, pulls)
            yield 0.0
            yield from grads(1.0)

        return [chain()], [routes], True, []

    wide = lambda rows, columns: pltpu.VMEM((rows, columns), BF16)
    blocks = lambda columns, dtype=BF16: pltpu.VMEM((8, TOK, columns), dtype)
    return comm(
        [hn_all, dy_all, pack_all, choices, residual, dy, turned],
        (3, 4, 5, 6),
        [
            ((8, TOK, D), BF16, False),
            ((TOK, D), BF16, True),
            ((16, TOK), F32, True),
            ((8, TOK, D), BF16, False),
            ((2, 48, EXPERT_PACK), BF16, True),
        ],
        [
            blocks(D), blocks(D), wide(D, EXPERT_PACK), wide(D, COLUMN), wide(D, COLUMN), blocks(640),
            blocks(GATE_UP), pltpu.VMEM((8, 16, TOK), F32), blocks(8, F32), blocks(8, F32),
            pltpu.VMEM((8, 8, TOK), F32), blocks(D), blocks(D), pltpu.VMEM((TOK, D), F32), wide(TOK, D),
            pltpu.VMEM((8, 8, TOK), F32),
        ]
        + column_sum_scratch(TOK, D)
        + plane_sum_scratch(EXPERT_PACK),
        320,
        3,
        plan,
    )


def columns_of(refs, columns):
    return [ref.at[(slice(None),) * (len(ref.shape) - 1) + (columns,)] for ref in refs]


def backward(
    q_here, kv_here, mixture, residual, lines, turned, hn, logits, cosine, sine, o_low, grad_lin, pack, grad,
    o_here, lse, starts, out_rows,
):
    def plan(net, ins, outs, scratch):
        me = net.here.me
        place, x_at, y_at = net.here.place, net.here.x, net.here.y
        mine = net.here.member
        (dq, dkv, lines_here, grad_lin_here, row_send, row_parts, row_sum, lower, upper, lower_pack, upper_pack,
         attn_sum, grads, rows_of_grads, routed, hn_lines, normed_parts, mixture_sum, low_out) = scratch[:19]
        held = scratch[19:25]
        one_sum, other_sum = scratch[25:29], scratch[29:33]
        queries, do, key_rows, value_rows, key_lines, key_grad, value_grad, query_grad, delta = scratch[33:42]
        dq_send, dkv_send = scratch[42:44]
        routes, own = query_routes(me, 0, 0)
        routes = [plane_route(me, [(1, lambda p: (slice(None), p), 1, lambda p: p)])] + routes
        own = own + [(1, (slice(None), place), 1, place)]
        rows_in = [plane_route(me, [(0, lambda p: p, 0, lambda p: p)])]
        rows_out = [
            Route(
                4,
                lambda i: (4 * mine + place // 4, i),
                lambda i: (
                    (me[0] // 4) // 4 * PLANE + 4 * lax.rem(me[0], 4) + i,
                    lax.rem(me[0] // 4, 4),
                ),
                [(0, lambda i: slice(None), 3, lambda i: lax.rem(place, 4), lambda i: i)],
                index=lambda i: lax.rem(place, 4),
                may_be_self=True,
            ),
        ]
        half = row_half(48)

        def rows():
            keep = net.local(row_send.at[place], row_parts.at[place])
            yield from follow_routes(net, rows_in, [row_send], [row_parts], 20.0)
            keep.wait()
            total = row_parts[0].astype(F32)
            for k in range(1, PLANE):
                total = total + row_parts[k].astype(F32)
            row_sum[...] = total.astype(BF16)
            yield from follow_routes(net, rows_out, [row_sum], outs, 45.0)

        def chain():
            loads = [net.local(ins[4], lines_here), net.local(ins[11], grad_lin_here)]
            unpack_queries(ins[0], queries)
            spread_keys(ins[1], key_rows, value_rows, key_lines, x_at)
            key_grad[...] = jnp.zeros_like(key_grad)
            value_grad[...] = jnp.zeros_like(value_grad)
            loads[1].wait()
            weights = ins[17][...].reshape(QROWS, D)
            do[...] = product_nt(weights, grad_lin_here[...]).astype(BF16)
            total = jnp.dot(ins[10][...], grad_lin_here[...], preferred_element_type=F32)
            for k in range(PLANE):
                row_send[k] = total[12 * k : 12 * k + 12].astype(BF16)
            row_flow = rows()
            row_when = next(row_flow)
            now = 6.0
            for third in range(3):

                def step(k, carry):
                    attend_back_step(
                        x_at, k, queries, do, ins[14], ins[15], ins[16], key_rows, value_rows, key_lines,
                        key_grad, value_grad, query_grad, delta, dq_send,
                    )
                    return carry

                lax.fori_loop(3 * third, 3 * third + 3, step, 0)
                now += 5.0
                yield now
            collect_keys(key_grad, value_grad, dkv_send)
            going = follow_routes(net, routes, [dq_send, dkv_send], [dq, dkv], now + 22.0)
            copies = own_copies(net, [dq_send, dkv_send], [dq, dkv], own)
            when = next(going)
            next(copies)
            turn_into(hn_lines, ins[6])
            yield row_when
            row_when = next(row_flow)
            yield when
            for unused in going:
                pass
            for unused in copies:
                pass
            loads[0].wait()
            weight_grads(dq, dkv, lines_here, hn_lines, ins[7], ins[8], ins[9], held[0], grads, routed)
            now = when + 10.0

            def weights():
                then = yield from together(plane_sum(net, None, attn_sum, *held, now=now))
                yield from column_deal(net, attn_sum, outs[1], (lower, upper), half, then)

            def normed():
                normed_grads(grads, rows_of_grads, ins[5], normed_parts)
                yield from together(
                    [column_sum_rows(net, normed_parts, outs[0], one_sum, k, now + 6.0 + 8.0 / PARTS * k) for k in range(PARTS)]
                )

            yield from together([weights(), normed(), resumed(row_when, row_flow)])

        def layer_output():
            now = yield from column_sum(net, ins[2], mixture_sum, *other_sum)
            low_out[...] = (ins[3][...] + RESIDUAL_SCALE * mixture_sum[...]).astype(BF16)
            yield from trade(net, [(low_out, outs[4])], 48.0, 75.0)

        flows = [
            trade(net, [(ins[13], outs[5])], 0.0, 30.0),
            layer_output(),
            chain(),
            column_deal(net, ins[12], outs[2], (lower_pack, upper_pack), half, begin=24.0),
        ]
        return flows, routes + rows_in + rows_out, True, [greet_trader]

    return comm(
        [
            q_here, kv_here, mixture, residual, lines, turned, hn, logits, cosine, sine, o_low, grad_lin, pack, grad,
            o_here, lse, starts, out_rows,
        ],
        (0, 1, 2, 3, 5, 6, 7, 8, 9, 10, 14, 15, 16, 17),
        [
            ((TOK, D), F32, True),
            ((8, 48, PACK), BF16, False),
            ((8, 48, EXPERT_PACK), BF16, False),
            ((4, 12, D), BF16, False),
            ((TOK, D), BF16, False),
            ((TOK, D), BF16, False),
        ],
        [
            pltpu.VMEM((2, 4, QROWS, TOK), BF16),
            pltpu.VMEM((PLANE, 2, TOK, TOK), BF16),
            pltpu.VMEM((D, COLUMN), BF16),
            pltpu.VMEM((COLUMN, D), BF16),
            pltpu.VMEM((PLANE, 12, D), BF16),
            pltpu.VMEM((PLANE, 12, D), BF16),
            pltpu.VMEM((12, D), BF16),
            pltpu.VMEM((32, PACK), BF16),
            pltpu.VMEM((16, PACK), BF16),
            pltpu.VMEM((32, EXPERT_PACK), BF16),
            pltpu.VMEM((16, EXPERT_PACK), BF16),
            pltpu.VMEM((2, 48, PACK), BF16),
            pltpu.VMEM((PACK, COLUMN), BF16),
            pltpu.VMEM((COLUMN, PACK), BF16),
            pltpu.VMEM((PACK, TOK), BF16),
            pltpu.VMEM((D, TOK), BF16),
            pltpu.VMEM((8, TOK, D), BF16),
            pltpu.VMEM((TOK, D), F32),
            pltpu.VMEM((TOK, D), BF16),
        ]
        + plane_sum_scratch(PACK)
        + column_sum_scratch(TOK, D)
        + column_sum_scratch(TOK, D)
        + attend_back_scratch()
        + [pltpu.VMEM((2, 4, QROWS, TOK), BF16), pltpu.VMEM((2, PLANE, TOK, TOK), BF16)],
        480,
        4,
        plan,
    )


NT = (((1,), (1,)), ((), ()))


def product_nt(one, other):
    return lax.dot_general(one, other, NT, preferred_element_type=F32)


def unit(size):
    rows = lax.broadcasted_iota(jnp.int32, (size, size), 0)
    return (rows == lax.broadcasted_iota(jnp.int32, (size, size), 1)).astype(BF16)


def turn_into(target, source, block=256):
    ones = unit(block)

    def step(k, carry):
        place = pl.ds(pl.multiple_of(k * block, block), block)
        if len(source.shape) == 3:
            part = source[:, :, place].reshape(target.shape[1], block)
        else:
            part = source[:, place]
        target[place, :] = product_nt(ones, part).astype(BF16)
        return carry

    lax.fori_loop(0, source.shape[-1] // block, step, 0)


def project(x_ref, attn_ref, cos_ref, sin_ref, q_ref, kv_ref, turned_ref, normed, linear):
    ones = unit(PACK)
    for z in range(2):
        weights = attn_ref[z].reshape(D // 2, PACK)
        turned_ref[:, z * (D // 2) : (z + 1) * (D // 2)] = product_nt(ones, weights).astype(BF16)
    gain = turned_ref[GAIN_ONE_AT : GAIN_ONE_AT + 1, :].astype(F32)

    def norm(k, carry):
        place = pl.ds(pl.multiple_of(k * TOK, TOK), TOK)
        values = x_ref[k].astype(F32)
        scale = lax.rsqrt(jnp.sum(values * values, -1, keepdims=True) * (1.0 / D) + NORM_EPS)
        normed[place, :] = (values * scale * gain).astype(BF16)
        return carry

    lax.fori_loop(0, 8, norm, 0)
    for part in range(2):
        place = slice(part * 512, (part + 1) * 512)
        linear[:, place] = product_nt(turned_ref[:ROUTER_AT, :], normed[place, :])
    for z in range(2):
        cosine, sine = cos_ref[z], sin_ref[z]
        for sequence in range(4):
            at = (4 * z + sequence) * TOK
            for head in range(GROUP + 1):
                rows = head * HEAD_DIM
                front = linear[rows : rows + HALF, at : at + TOK]
                behind = linear[rows + HALF : rows + HEAD_DIM, at : at + TOK]
                one = (front * cosine - behind * sine).astype(BF16)
                two = (behind * cosine + front * sine).astype(BF16)
                if head < GROUP:
                    q_ref[z, sequence, rows : rows + HALF, :] = one
                    q_ref[z, sequence, rows + HALF : rows + HEAD_DIM, :] = two
                else:
                    kv_ref[z, sequence, :HALF, :] = one
                    kv_ref[z, sequence, HALF:HEAD_DIM, :] = two
            kv_ref[z, sequence, HEAD_DIM:, :] = linear[QROWS + HEAD_DIM : ROUTER_AT, at : at + TOK].astype(BF16)


def local_kernel(kernel, inputs, smem, anywhere_in, outputs, scratch):
    vmem = pl.BlockSpec(memory_space=pltpu.VMEM)
    anywhere = pl.BlockSpec(memory_space=pl.ANY)
    scalars = pl.BlockSpec(memory_space=pltpu.SMEM)
    return pl.pallas_call(
        kernel,
        out_shape=[jax.ShapeDtypeStruct(shape, dtype) for shape, dtype, unused in outputs],
        in_specs=[
            scalars if k in smem else anywhere if k in anywhere_in else vmem for k in range(len(inputs))
        ],
        out_specs=[vmem if inside else anywhere for unused, unused2, inside in outputs],
        scratch_shapes=scratch,
        compiler_params=pltpu.CompilerParams(vmem_limit_bytes=VMEM_LIMIT),
    )(*inputs)


def expert_shares(hn, turned_ref, choices_ref, share_ref, share_rows, z):
    row = lax.broadcasted_iota(jnp.int32, (16, TOK), 0)
    router = turned_ref[ROUTER_AT : ROUTER_AT + 16, :]

    def route(block, carry):
        logits = product_nt(router, hn[block])
        named = choices_ref[block]
        named = named + jnp.where(named >= 5, 3, 0)
        chosen = row == named[0:1]
        for k in range(1, 8):
            chosen = jnp.logical_or(chosen, row == named[k : k + 1])
        logits = jnp.where(chosen, logits, MASK_FILL)
        exponent = jnp.where(chosen, jnp.exp(logits - jnp.max(logits, 0, keepdims=True)), 0.0)
        share_ref[block] = exponent / jnp.sum(exponent, 0, keepdims=True)
        mine = share_ref[block, pl.ds(pl.multiple_of(z * 8, 8), 8), :]
        share_rows[block] = mine.T
        return carry

    lax.fori_loop(0, 8, route, 0)


def experts_forward(hn, dy, gate_up, down, hidden, joined, share_rows, pull_rows, k):
    rows = pl.ds(k * 64, 64)
    for expert in range(5):
        both = jnp.dot(
            hn[:, rows, :].reshape(512, D),
            gate_up[:, expert * 256 : expert * 256 + 256],
            preferred_element_type=F32,
        )
        gate, up = both[:, :TOK], both[:, TOK:]
        pulled = RESIDUAL_SCALE * jnp.dot(
            dy[:, rows, :].reshape(512, D),
            down[:, expert * TOK : (expert + 1) * TOK],
            preferred_element_type=F32,
        )
        share = share_rows[:, rows, expert : expert + 1].reshape(512, 1)
        sigmoid = 1.0 / (1.0 + jnp.exp(-gate))
        silu = gate * sigmoid
        act = (silu * up).astype(BF16).astype(F32)
        hidden[:, rows, expert * TOK : (expert + 1) * TOK] = (share * act).astype(BF16).reshape(8, 64, TOK)
        pull_rows[:, rows, expert : expert + 1] = jnp.sum(act * pulled, 1, keepdims=True).reshape(8, 64, 1)
        grad = share * pulled
        left = (grad * up * (sigmoid + silu * (1.0 - sigmoid))).astype(BF16)
        joined[:, rows, expert * 256 : expert * 256 + TOK] = left.reshape(8, 64, TOK)
        joined[:, rows, expert * 256 + TOK : expert * 256 + 256] = (grad * silu).astype(BF16).reshape(8, 64, TOK)


def turn_pull(pull_rows, pull_ref):
    pull_rows[:, :, 5:8] = jnp.zeros((8, TOK, 3), F32)

    def step(block, carry):
        pull_ref[block] = pull_rows[block].T
        return carry

    lax.fori_loop(0, 8, step, 0)


def logit_grads(pull_ref, share_ref, logit_ref):
    shard, rep = my_place()
    shares = share_ref[(shard // PLANE) * 4 + rep]
    pulls = []
    for z in range(2):
        total = pull_ref[4 * z]
        for quarter in range(1, 4):
            total = total + pull_ref[4 * z + quarter]
        pulls.append(total)
    pull = jnp.concatenate(pulls, 0)
    logit_ref[...] = shares * (pull - jnp.sum(shares * pull, 0, keepdims=True))


def residual_grad(sum_ref, residual_ref, dy_ref, turned_ref, grad_ref, low_ref, logit_ref, k):
    rows = pl.ds(k * PART, PART)
    logits = logit_ref[...].T[k * PART : (k + 1) * PART]
    router = turned_ref[ROUTER_AT : ROUTER_AT + 16, :].astype(F32)
    gain = turned_ref[GAIN_TWO_AT : GAIN_TWO_AT + 1, :].astype(F32)
    grad_normed = sum_ref[rows, :] + jnp.dot(
        logits, router, precision=PRECISE, preferred_element_type=F32
    )
    residual = residual_ref[rows, :]
    scale = lax.rsqrt(jnp.sum(residual * residual, -1, keepdims=True) * (1.0 / D) + NORM_EPS)
    weighted = grad_normed * gain
    mean = jnp.sum(weighted * residual, -1, keepdims=True) * (1.0 / D)
    grad = dy_ref[rows, :].astype(F32) + scale * weighted - residual * (scale * scale * scale * mean)
    grad_ref[rows, :] = grad.astype(BF16)
    low_ref[rows, :] = (RESIDUAL_SCALE * grad).astype(BF16)


def weight_grads(dq_ref, dkv_ref, lines_ref, hn_lines, logit_ref, cos_ref, sin_ref, weight_ref, grads, routed):
    grads[ROUTER_AT:, :] = jnp.zeros((PACK - ROUTER_AT, COLUMN), BF16)
    for z in range(2):
        cosine, sine = cos_ref[z], sin_ref[z]
        for sequence in range(4):
            at = (4 * z + sequence) * TOK
            column = crossed(sequence)
            total = dkv_ref[column, z].astype(F32)
            for quarter in range(1, 4):
                total = total + dkv_ref[4 * quarter + column, z].astype(F32)
            for head in range(GROUP + 1):
                rows = head * HEAD_DIM
                if head < GROUP:
                    front = dq_ref[z, sequence, rows : rows + HALF, :].astype(F32)
                    behind = dq_ref[z, sequence, rows + HALF : rows + HEAD_DIM, :].astype(F32)
                else:
                    front, behind = total[:HALF], total[HALF:HEAD_DIM]
                grads[rows : rows + HALF, at : at + TOK] = (front * cosine + behind * sine).astype(BF16)
                grads[rows + HALF : rows + HEAD_DIM, at : at + TOK] = (behind * cosine - front * sine).astype(BF16)
            grads[QROWS + HEAD_DIM : ROUTER_AT, at : at + TOK] = total[HEAD_DIM:].astype(BF16)
    routed[...] = jnp.zeros_like(routed)
    routed[ROUTER_AT : ROUTER_AT + 16, :] = logit_ref[...].astype(BF16)

    def weight_step(k, carry):
        place = pl.ds(pl.multiple_of(k * 192, 192), 192)
        total = product_nt(lines_ref[place, :], grads[...]) + product_nt(hn_lines[place, :], routed[...])
        weight_ref[k // 4, lax.rem(k, 4)] = total.astype(BF16).reshape(4, 48, PACK)
        return carry

    lax.fori_loop(0, 8, weight_step, 0)


def normed_grads(grads, rows_of_grads, turned_ref, normed_ref):
    turn_into(rows_of_grads, grads)

    def step(k, carry):
        place = pl.ds(pl.multiple_of(k * 256, 256), 256)
        total = jnp.dot(rows_of_grads[...], turned_ref[:, place], preferred_element_type=F32)
        normed_ref[:, :, place] = total.astype(BF16).reshape(8, TOK, 256)
        return carry

    lax.fori_loop(0, D // 256, step, 0)


def assemble_kernel(
    attn, pack, out_rows, query_weight, keyval_weight, router_weight, gate_up_weight, first_gain, second_gain,
    normed_grad, traded_grad, x, turned, traded_out, input_grad, layer_out,
    query_grad, keyval_grad, out_grad, router_grad, gate_up_grad, down_grad, first_grad, second_grad,
):
    layer_out[...] = traded_out[...]
    values = x[...].astype(F32)
    scale = lax.rsqrt(jnp.sum(values * values, -1, keepdims=True) * (1.0 / D) + NORM_EPS)
    weighted = normed_grad[...] * turned[GAIN_ONE_AT : GAIN_ONE_AT + 1, :].astype(F32)
    mean = jnp.sum(weighted * values, -1, keepdims=True) * (1.0 / D)
    input_grad[...] = traded_grad[...].astype(F32) + scale * weighted - values * (scale * scale * scale * mean)
    parts = [attn[m].astype(F32) for m in range(HEADS)]
    query = jnp.concatenate([part[:, :QROWS] for part in parts], 1)
    key = jnp.concatenate([part[:, QROWS : QROWS + HEAD_DIM] for part in parts], 1)
    value = jnp.concatenate([part[:, QROWS + HEAD_DIM : ROUTER_AT] for part in parts], 1)
    query_grad[...] = query
    keyval_grad[:, : HEADS * HEAD_DIM] = key
    keyval_grad[:, HEADS * HEAD_DIM :] = value
    router = parts[0]
    for part in parts[1:]:
        router = router + part
    router = jnp.concatenate([router[:, ROUTER_AT : ROUTER_AT + 5], router[:, ROUTER_AT + 8 : ROUTER_AT + 13]], 1)
    blank = jnp.zeros((48, TOK - EXPERTS - 2), F32)
    for k in range(4):
        out_grad[12 * k : 12 * k + 12, :] = out_rows[k].astype(F32)
    first = jnp.sum(query * query_weight[...].astype(F32), 1, keepdims=True)
    half = HEADS * HEAD_DIM
    first = first + jnp.sum(key * keyval_weight[:, :half].astype(F32), 1, keepdims=True)
    first = first + jnp.sum(value * keyval_weight[:, half:].astype(F32), 1, keepdims=True)
    second = jnp.sum(router * router_weight[...].astype(F32).T, 1, keepdims=True)
    for expert in range(EXPERTS):
        z, local = expert // 5, expert % 5
        rows = []
        for side in range(2):
            at = local * 256 + side * TOK
            rows += [pack[4 * z + q, :, at : at + TOK].astype(F32) for q in range(4)]
        whole = jnp.concatenate(rows, 1)
        gate_up_grad[expert] = whole
        second = second + jnp.sum(whole * gate_up_weight[expert].astype(F32), 1, keepdims=True)
        at = GATE_UP + local * TOK
        down_grad[expert] = jnp.concatenate(
            [pack[4 * z + q, :, at : at + TOK].astype(F32) for q in range(4)], 1
        )
    lines = jnp.concatenate([router, first, second, blank], 1).T
    router_grad[...] = lines[:EXPERTS]
    first_grad[...] = lines[EXPERTS : EXPERTS + 1] / first_gain[...].astype(F32)
    second_grad[...] = lines[EXPERTS + 1 : EXPERTS + 2] / second_gain[...].astype(F32)


def assemble(*inputs):
    shapes = [(48, D), (48, 1024), (48, D), (EXPERTS, 48), (EXPERTS, 48, 2 * FF), (EXPERTS, 48, FF), (1, 48), (1, 48)]
    outputs = [((TOK, D), F32, True), ((TOK, D), BF16, True)] + [(shape, F32, True) for shape in shapes]
    return local_kernel(assemble_kernel, inputs, (), (), outputs, [])


def run_of(x, step):
    run = (step > x).astype(jnp.int32)
    block = step - run * (x + 1)
    return run, block, block == 0, jnp.logical_or(step == x, step == 8)


def run_base(x, run):
    return (x + run * (7 - 2 * x)) * RUN


def unpack_queries(source, target):
    for run in range(2):
        for part in range(4):
            target[run, :, part * TOK : (part + 1) * TOK] = source[run, part]


def document_starts(segment_ref, starts, x):
    segments = [segment_ref[:, z, :].astype(F32) for z in range(2)]
    earlier = []
    for number in range(1, 5):
        count = [
            jnp.sum(
                jnp.sum((part < number).astype(F32), 0, keepdims=True), 1, keepdims=True
            )
            for part in segments
        ]
        earlier.append(count[0] + count[1])
    for run in range(2):
        first = 4 * (x + run * (3 - 2 * x))
        mark = jnp.concatenate([segment_ref[first + crossed(k), run : run + 1, :] for k in range(4)], 1)
        start = jnp.zeros((1, RUN), F32)
        for number in range(1, 5):
            start = jnp.where(mark == number, earlier[number - 1], start)
        starts[run, 0:1, :] = start


def visible_block(starts, x, run, block):
    key = lax.broadcasted_iota(jnp.int32, (RUN, RUN), 0).astype(F32)
    shift = (block * RUN).astype(F32)
    start = starts[run, 0:1, :] - shift
    lane = lax.broadcasted_iota(jnp.int32, (1, RUN), 1)
    query = (TOK * crossed(lane // TOK) + lax.rem(lane, TOK)).astype(F32) + (run_base(x, run).astype(F32) - shift)
    return jnp.logical_and(key >= start, key <= query)


def unpack_keys(kv_ref, key_rows, value_lines, x):
    ones = unit(TOK)

    def step(j, carry):
        place = pl.ds(pl.multiple_of(j * TOK, TOK), TOK)
        block = kv_ref.at[j // PLANE, lax.rem(j, PLANE)]
        key_rows[place, :] = product_nt(ones, block[:HEAD_DIM, :]).astype(BF16)
        value_lines[:, place] = block[HEAD_DIM:, :]
        return carry

    lax.fori_loop(0, (8 - x) * 4, step, 0)


def attend_step(x, step, queries, key_rows, value_lines, starts, peak, total, acc, o_ref, low_ref, lse_ref):
    run, block, first, last = run_of(x, step)

    @pl.when(first)
    def begin():
        peak[...] = jnp.full_like(peak, MASK_FILL)
        total[...] = jnp.zeros_like(total)
        acc[...] = jnp.zeros_like(acc)

    place = pl.ds(pl.multiple_of(block * RUN, RUN), RUN)
    keys, values = key_rows[place, :], value_lines[:, place]
    seen = visible_block(starts, x, run, block)
    for h in range(GROUP):
        rows = slice(h * HEAD_DIM, (h + 1) * HEAD_DIM)
        scores = jnp.dot(
            keys, queries[run, rows, :] * jnp.asarray(SCORE_SCALE, BF16), preferred_element_type=F32
        )
        scores = jnp.where(seen, scores, MASK_FILL)
        before = peak[h : h + 1, :]
        top = jnp.maximum(before, jnp.max(scores, 0, keepdims=True))
        weights = jnp.exp(scores - top)
        fade = jnp.exp(before - top)
        peak[h : h + 1, :] = top
        total[h : h + 1, :] = fade * total[h : h + 1, :] + jnp.sum(weights, 0, keepdims=True)
        acc[rows, :] = fade * acc[rows, :] + jnp.dot(
            values, weights.astype(BF16), preferred_element_type=F32
        )

    @pl.when(last)
    def end():
        cols = pl.ds(pl.multiple_of(run * RUN, RUN), RUN)
        for h in range(GROUP):
            rows = slice(h * HEAD_DIM, (h + 1) * HEAD_DIM)
            attended = acc[rows, :] / total[h : h + 1, :]
            o_ref[rows, cols] = attended
            low_ref[rows, cols] = attended.astype(BF16)
            lse_ref[h : h + 1, cols] = peak[h : h + 1, :] + jnp.log(total[h : h + 1, :])


def attend_scratch():
    return [
        pltpu.VMEM((2, QROWS, RUN), BF16),
        pltpu.VMEM((SEQ, HEAD_DIM), BF16),
        pltpu.VMEM((HEAD_DIM, SEQ), BF16),
        pltpu.VMEM((8, RUN), F32),
        pltpu.VMEM((8, RUN), F32),
        pltpu.VMEM((QROWS, RUN), F32),
    ]


def spread_keys(kv_ref, key_rows, value_rows, key_lines, x):
    ones = unit(TOK)

    def step(j, carry):
        place = pl.ds(pl.multiple_of(j * TOK, TOK), TOK)
        block = kv_ref[j // PLANE, lax.rem(j, PLANE)]
        turned = product_nt(ones, block).astype(BF16)
        key_rows[place, :] = turned[:, :HEAD_DIM]
        value_rows[place, :] = turned[:, HEAD_DIM:]
        key_lines[:, place] = block[:HEAD_DIM]
        return carry

    lax.fori_loop(0, (8 - x) * 4, step, 0)


def attend_back_step(
    x, step, queries, do_ref, o_ref, lse_ref, starts, key_rows, value_rows, key_lines,
    key_grad, value_grad, query_grad, delta, dq_ref,
):
    run, block, first, last = run_of(x, step)
    cols = pl.ds(pl.multiple_of(run * RUN, RUN), RUN)

    @pl.when(first)
    def begin():
        query_grad[...] = jnp.zeros_like(query_grad)
        for h in range(GROUP):
            rows = slice(h * HEAD_DIM, (h + 1) * HEAD_DIM)
            delta[h : h + 1, :] = jnp.sum(
                do_ref[rows, cols].astype(F32) * o_ref[rows, cols], 0, keepdims=True
            )

    place = pl.ds(pl.multiple_of(block * RUN, RUN), RUN)
    keys, values, lines = key_rows[place, :], value_rows[place, :], key_lines[:, place]
    seen = visible_block(starts, x, run, block)
    dk, dv = key_grad[place, :], value_grad[place, :]
    for h in range(GROUP):
        rows = slice(h * HEAD_DIM, (h + 1) * HEAD_DIM)
        q = queries[run, rows, :] * jnp.asarray(SCORE_SCALE, BF16)
        do = do_ref[rows, cols]
        scores = jnp.dot(keys, q, preferred_element_type=F32)
        weights = jnp.exp(jnp.where(seen, scores, MASK_FILL) - lse_ref[h : h + 1, cols])
        pull = jnp.dot(values, do, preferred_element_type=F32)
        ds = (weights * (pull - delta[h : h + 1, :])).astype(BF16)
        dv = dv + product_nt(weights.astype(BF16), do)
        dk = dk + product_nt(ds, q)
        query_grad[rows, :] += jnp.dot(lines, ds, preferred_element_type=F32)
    key_grad[place, :] = dk
    value_grad[place, :] = dv

    @pl.when(last)
    def end():
        scaled = (SCORE_SCALE * query_grad[...]).astype(BF16)
        for part in range(4):
            dq_ref[run, part] = scaled[:, part * TOK : (part + 1) * TOK]


def collect_keys(key_grad, value_grad, dkv_ref):
    ones = unit(HEAD_DIM)

    def step(j, carry):
        place = pl.ds(pl.multiple_of(j * TOK, TOK), TOK)
        dkv_ref[j // PLANE, lax.rem(j, PLANE), :HEAD_DIM, :] = product_nt(
            ones, key_grad[place, :].astype(BF16)
        ).astype(BF16)
        dkv_ref[j // PLANE, lax.rem(j, PLANE), HEAD_DIM:, :] = product_nt(
            ones, value_grad[place, :].astype(BF16)
        ).astype(BF16)
        return carry

    lax.fori_loop(0, SEQ // TOK, step, 0)


def attend_back_scratch():
    return [
        pltpu.VMEM((2, QROWS, RUN), BF16),
        pltpu.VMEM((QROWS, 2 * RUN), BF16),
        pltpu.VMEM((SEQ, HEAD_DIM), BF16),
        pltpu.VMEM((SEQ, HEAD_DIM), BF16),
        pltpu.VMEM((HEAD_DIM, SEQ), BF16),
        pltpu.VMEM((SEQ, HEAD_DIM), F32),
        pltpu.VMEM((SEQ, HEAD_DIM), F32),
        pltpu.VMEM((QROWS, RUN), F32),
        pltpu.VMEM((8, RUN), F32),
    ]


def shards(
    layer_input,
    segments,
    choices,
    first_gain,
    query_weight,
    key_value_matrix,
    output_weight,
    second_gain,
    router_weight,
    gate_up_weight,
    down_weight,
    cotangent,
):
    shard, rep = my_place()
    z, place, x, y = parts_of(shard)

    frequency = ROPE_BASE ** (-jnp.arange(0, HEAD_DIM, 2, dtype=F32) / HEAD_DIM)
    column_place = (
        (jnp.arange(2, dtype=jnp.int32)[:, None] * PLANE + place) * TOK
        + jnp.arange(TOK, dtype=jnp.int32)[None, :]
    )
    angle = column_place.astype(F32)[:, None, :] * frequency[None, :, None]
    cosine, sine = jnp.cos(angle), jnp.sin(angle)
    (
        q_here, kv_here, starts, o_here, o_low, lse, normed_lines, turned, residual, normed_two, normed_two_all,
        expert_pack, dy_all, choices_all, dy_traded, choices_traded, out_slice,
    ) = forward(
        layer_input[0],
        segments,
        query_weight,
        key_value_matrix,
        router_weight.T,
        first_gain[None],
        output_weight,
        choices[0].T,
        cotangent[0],
        jnp.swapaxes(gate_up_weight, 0, 1),
        jnp.swapaxes(down_weight, 0, 1),
        cosine,
        sine,
        second_gain[None],
    )

    mixture_part, grad_residual, grad_logits, grad_lin_all, pack_sum = experts(
        normed_two_all,
        dy_all,
        expert_pack.reshape(D, EXPERT_PACK),
        choices_all,
        residual,
        dy_traded,
        turned,
    )
    grad_normed, attn_own, pack_own, out_own, layer_out, grad_back = backward(
        q_here, kv_here, mixture_part, residual, normed_lines, turned, normed_two, grad_logits,
        cosine, sine, o_low, grad_lin_all.reshape(COLUMN, D), pack_sum, grad_residual, o_here, lse, starts, out_slice,
    )
    (
        input_grad, layer_out, query_grad, keyval_grad, out_grad_rows, router_grad, gate_up_grad, down_grad,
        first_grad, second_grad,
    ) = assemble(
        attn_own,
        pack_own,
        out_own,
        query_weight,
        key_value_matrix,
        router_weight.T,
        jnp.swapaxes(gate_up_weight, 0, 1),
        first_gain[None],
        second_gain[None],
        grad_normed,
        grad_back,
        layer_input[0],
        turned,
        layer_out,
    )
    return (
        layer_out[None],
        input_grad[None],
        first_grad[0],
        query_grad,
        keyval_grad,
        out_grad_rows,
        second_grad[0],
        router_grad.T,
        jnp.swapaxes(gate_up_grad, 0, 1),
        jnp.swapaxes(down_grad, 0, 1),
    )


def solution(mesh):
    row = P("shard", None)
    rows = P("shard", None, None)
    own = P("rep", "shard", None)
    in_specs = (own, P("rep", "shard"), own, P("shard"), row, row, row, P("shard"), row, rows, rows, own)
    out_specs = (own, own, P("shard"), row, row, row, P("shard"), row, rows, rows)
    return jax.shard_map(shards, mesh=mesh, in_specs=in_specs, out_specs=out_specs, check_vma=False)
```

```python
import jax
import jax.numpy as jnp
from jax import lax
from jax.experimental import pallas as pl
from jax.experimental.pallas import tpu as pltpu
from jax.sharding import PartitionSpec as P

D = 1536
HEADS = 8
GROUP = 3
HEAD_DIM = 64
HALF = HEAD_DIM // 2
FF = 512
EXPERTS = 10
TOK = 128
SEQ = 4096
PLANE = 16
RUN = 512
QROWS = GROUP * HEAD_DIM
PACK = 384
ROUTER_AT = 320
GAIN_ONE_AT = 336
GAIN_TWO_AT = 337
COLUMN = 8 * TOK
PARTS = 2
PART = TOK // PARTS
GATE_UP = 1280
EXPERT_PACK = 1920

NORM_EPS = 1e-06
RESIDUAL_SCALE = 0.22
SCORE_SCALE = 0.015625
ROPE_BASE = 10000.0
MASK_FILL = -1e30
PRECISE = lax.Precision.HIGHEST
BF16 = jnp.bfloat16
F32 = jnp.float32
VMEM_LIMIT = 56 * 1024 * 1024


def my_place():
    return lax.axis_index("shard"), lax.axis_index("rep")


def parts_of(shard):
    place = lax.rem(shard, PLANE)
    return shard // PLANE, place, place // 4, lax.rem(place, 4)


def same(one, other):
    return jnp.logical_and(one[0] == other[0], one[1] == other[1])


def crossed(number):
    if isinstance(number, int):
        return (0, 2, 1, 3)[number]
    return number + (number == 1).astype(jnp.int32) - (number == 2).astype(jnp.int32)


class Place:
    def __init__(self, me):
        self.me = me
        self.shard, self.rep = me
        self.z_lo, self.place, self.x, self.y = parts_of(self.shard)
        self.core = lax.rem(self.rep, 2)
        self.z = (self.rep // 2) * 2 + self.z_lo
        self.member = self.z_lo * 4 + self.rep

    def device(self, z, x, y, core):
        return lax.rem(z, 2) * PLANE + 4 * x + y, (z // 2) * 2 + core

    def step(self, axis, by):
        z, x, y = self.z, self.x, self.y
        if axis == "z":
            z = lax.rem(z + by, 4)
        elif axis == "x":
            x = lax.rem(x + by, 4)
        else:
            y = lax.rem(y + by, 4)
        return self.device(z, x, y, self.core)

    def sibling(self):
        return self.shard, self.rep + 1 - 2 * self.core

    def partner(self):
        return self.shard + (1 - 2 * self.z_lo) * PLANE, self.rep

    def trader(self):
        return self.z_lo * PLANE + 4 * mirrored(self.z_lo, self.x) + crossed(self.rep), crossed(self.y)

    def member_at(self, z, core):
        return lax.rem(z, 2) * 4 + (z // 2) * 2 + core

    def near(self):
        result = [self.sibling()]
        for axis in ("z", "x", "y"):
            result += [self.step(axis, 1), self.step(axis, 3)]
        return result


def mesh_id(place):
    return {"shard": place[0], "rep": place[1]}


class Net:
    def __init__(self, here, sems):
        self.here, self.sems, self.used, self.sent = here, sems, 0, []

    def take(self, count=1):
        first = self.used
        self.used += count
        return first

    def push(self, source, target, to):
        number = self.take(2)
        copy = pltpu.make_async_remote_copy(
            src_ref=source,
            dst_ref=target,
            send_sem=self.sems.at[number],
            recv_sem=self.sems.at[number + 1],
            device_id=mesh_id(to),
        )
        copy.start()
        self.sent.append(copy)
        return number + 1

    def got(self, number, region):
        pltpu.make_async_remote_copy(
            src_ref=region,
            dst_ref=region,
            send_sem=self.sems.at[number],
            recv_sem=self.sems.at[number],
            device_id=mesh_id(self.here.sibling()),
        ).wait_recv()

    def local(self, source, target):
        copy = pltpu.make_async_copy(source, target, self.sems.at[self.take()])
        copy.start()
        return copy

    def finish(self):
        for copy in self.sent:
            copy.wait_send()


class Route:
    def __init__(self, n, to, source, pieces, index=None, may_be_self=False):
        self.n, self.to, self.source, self.pieces = n, to, source, pieces
        self.index = index or (lambda i: i)
        self.may_be_self = may_be_self


def each(n, body):
    if n <= 8:
        for i in range(n):
            body(i)
    else:

        def step(i, carry):
            body(i)
            return carry

        lax.fori_loop(0, n, step, 0)


def greet_routes(routes, me, barrier):
    awaited = 0
    for route in routes:

        def greet(i, route=route):
            source = route.source(i)

            def signal():
                pl.semaphore_signal(barrier, inc=1, device_id=mesh_id(source))

            if route.may_be_self:
                pl.when(jnp.logical_not(same(source, me)))(signal)
            else:
                signal()

        each(route.n, greet)
        awaited = awaited + route.n
        if route.may_be_self:
            for i in range(route.n):
                awaited = awaited - same(route.to(i), me).astype(jnp.int32)
    return awaited


HOP = 2.0


def time_of(ref, rate=50.0):
    size = jnp.dtype(ref.dtype).itemsize / 1000.0
    for extent in ref.shape:
        size *= extent
    return HOP + size / rate


def follow_routes(net, routes, ins, outs, guess=15.0):
    me = net.here.me
    held = []
    for route in routes:
        count = route.n * len(route.pieces)
        held.append((net.take(count), net.take(count), net.take(len(route.pieces))))

    def remote(route, base, i, k, piece):
        source_in, cut, target_out, slot, unused = piece
        return pltpu.make_async_remote_copy(
            src_ref=ins[source_in].at[cut(i)],
            dst_ref=outs[target_out].at[slot(i)],
            send_sem=net.sems.at[base[0] + i * len(route.pieces) + k],
            recv_sem=net.sems.at[base[1] + route.index(i) * len(route.pieces) + k],
            device_id=mesh_id(route.to(i)),
        )

    def within(base, i, k, piece):
        source_in, cut, target_out, slot, unused = piece
        return pltpu.make_async_copy(
            ins[source_in].at[cut(i)], outs[target_out].at[slot(i)], net.sems.at[base[2] + k]
        )

    for route, base in zip(routes, held):

        def start(i, route=route, base=base):
            for k, piece in enumerate(route.pieces):
                copy = remote(route, base, i, k, piece)
                if route.may_be_self:
                    here = same(route.to(i), me)
                    pl.when(jnp.logical_not(here))(copy.start)
                    pl.when(here)(within(base, i, k, piece).start)
                else:
                    copy.start()

        each(route.n, start)
    yield guess
    for route, base in zip(routes, held):

        def arrive(i, route=route, base=base):
            for k, piece in enumerate(route.pieces):
                region = outs[piece[2]].at[piece[4](i)]
                place = route.source(i)
                sem = net.sems.at[base[1] + i * len(route.pieces) + k]
                copy = pltpu.make_async_remote_copy(
                    src_ref=region, dst_ref=region, send_sem=sem, recv_sem=sem, device_id=mesh_id(place)
                )
                if route.may_be_self:
                    pl.when(jnp.logical_not(same(place, me)))(copy.wait_recv)
                else:
                    copy.wait_recv()

        each(route.n, arrive)

        def leave(i, route=route, base=base):
            for k, piece in enumerate(route.pieces):
                copy = remote(route, base, i, k, piece)
                if route.may_be_self:
                    here = same(route.to(i), me)
                    pl.when(jnp.logical_not(here))(copy.wait_send)
                    pl.when(here)(within(base, i, k, piece).wait)
                else:
                    copy.wait_send()

        each(route.n, leave)


def trade(net, pieces, begin=0.0, now=30.0):
    other = net.here.trader()
    here = same(other, net.here.me)
    if begin:
        yield begin
    copies = []
    for source, target in pieces:
        number = net.take(2)
        remote = pltpu.make_async_remote_copy(
            src_ref=source,
            dst_ref=target,
            send_sem=net.sems.at[number],
            recv_sem=net.sems.at[number + 1],
            device_id=mesh_id(other),
        )
        within = pltpu.make_async_copy(source, target, net.sems.at[net.take()])
        pl.when(jnp.logical_not(here))(remote.start)
        pl.when(here)(within.start)
        copies.append((remote, within))
    yield now
    for remote, within in copies:
        pl.when(jnp.logical_not(here))(remote.wait)
        pl.when(here)(within.wait)


def greet_trader(here, barrier):
    other = here.trader()
    away = jnp.logical_not(same(other, here.me))

    @pl.when(away)
    def signal():
        pl.semaphore_signal(barrier, inc=1, device_id=mesh_id(other))

    return away.astype(jnp.int32)


def spread_rows(net, rows, out):
    here = net.here
    ahead = lax.rem(here.x - here.rep + 4, 4)
    pair = lambda k: out.at[pl.ds(2 * k, 2)]
    row_halves = row_half(48)

    def at(by):
        return out.at[lax.rem(here.y + by, 4)]

    def copy(number, source, target, to):
        return pltpu.make_async_remote_copy(
            src_ref=source,
            dst_ref=target,
            send_sem=net.sems.at[number],
            recv_sem=net.sems.at[number + 1],
            device_id=mesh_id(to),
        )

    def come(number, region):
        copy(number, region, region, here.sibling()).wait_recv()

    up, down, right, left = here.step("y", 1), here.step("y", 3), here.step("x", 1), here.step("x", 3)
    numbers = [net.take(2) for k in range(8)]
    keep = pltpu.make_async_copy(rows, at(0), net.sems.at[net.take()])
    first = [copy(numbers[0], rows, at(0), up), copy(numbers[1], rows, at(0), down)]
    second = [
        copy(numbers[2], row_halves(at(3), 0), row_halves(at(3), 0), up),
        copy(numbers[3], row_halves(at(1), 1), row_halves(at(1), 1), down),
    ]
    third = [copy(numbers[4], out, out, right), copy(numbers[5], out, out, left)]
    on_right = copy(numbers[6], pair(0), pair(0), right)
    on_left = copy(numbers[7], pair(1), pair(1), left)

    @pl.when(ahead == 0)
    def begin():
        keep.start()
        first[0].start()
        first[1].start()

    now = time_of(rows)
    yield now

    @pl.when(ahead == 0)
    def hand_on():
        come(numbers[0], at(3))
        second[0].start()
        come(numbers[1], at(1))
        second[1].start()

    now += time_of(rows, 100.0)
    yield now

    @pl.when(ahead == 0)
    def go_out():
        come(numbers[2], row_halves(at(2), 0))
        come(numbers[3], row_halves(at(2), 1))
        keep.wait()
        third[0].start()
        third[1].start()

    now += time_of(out, 70.0)
    yield now

    @pl.when(ahead == 1)
    def to_right():
        come(numbers[4], out)
        on_right.start()

    @pl.when(ahead == 3)
    def to_left():
        come(numbers[5], out)
        on_left.start()

    now += time_of(out, 140.0)
    yield now

    @pl.when(ahead == 2)
    def end():
        come(numbers[6], pair(0))
        come(numbers[7], pair(1))

    @pl.when(ahead == 0)
    def sent():
        for each_copy in first + second + third:
            each_copy.wait_send()

    pl.when(ahead == 1)(on_right.wait_send)
    pl.when(ahead == 3)(on_left.wait_send)


def comm(inputs, in_vmem, outputs, scratch, n_sems, collective_id, plan):
    n_in, n_out = len(inputs), len(outputs)

    def kernel(*refs):
        ins, outs = refs[:n_in], refs[n_in : n_in + n_out]
        rest, sems = refs[n_in + n_out : -1], refs[-1]
        net = Net(Place(my_place()), sems)
        flows, routes, near, greetings = plan(net, ins, outs, rest)
        barrier = pltpu.get_barrier_semaphore()
        awaited = greet_routes(routes, net.here.me, barrier)
        if near:
            others = net.here.near()
            for other in others:
                pl.semaphore_signal(barrier, inc=1, device_id=mesh_id(other))
            awaited = awaited + len(others)
        for greeting in greetings:
            awaited = awaited + greeting(net.here, barrier)
        pl.semaphore_wait(barrier, awaited)
        waits = [(0.0, number, flow) for number, flow in enumerate(flows)]
        while waits:
            unused, number, flow = waits.pop(0)
            when = next(flow, None)
            if when is not None:
                waits = sorted(waits + [(when, number, flow)], key=lambda wait: wait[:2])
        net.finish()
        assert net.used <= n_sems, net.used

    vmem = pl.BlockSpec(memory_space=pltpu.VMEM)
    anywhere = pl.BlockSpec(memory_space=pl.ANY)
    return pl.pallas_call(
        kernel,
        out_shape=[jax.ShapeDtypeStruct(s, t) for s, t, unused in outputs],
        in_specs=[vmem if k in in_vmem else anywhere for k in range(n_in)],
        out_specs=[vmem if inside else anywhere for unused, unused2, inside in outputs],
        scratch_shapes=list(scratch) + [pltpu.SemaphoreType.DMA((n_sems,))],
        compiler_params=pltpu.CompilerParams(
            collective_id=collective_id, has_side_effects=True, vmem_limit_bytes=VMEM_LIMIT
        ),
    )(*inputs)


def together(flows):
    waits, now = [(next(flow), number, flow) for number, flow in enumerate(flows)], 0.0
    while waits:
        waits = sorted(waits, key=lambda wait: wait[:2])
        now, number, flow = waits.pop(0)
        yield now
        when = next(flow, None)
        if when is not None:
            waits.append((when, number, flow))
    return now


def resumed(when, flow):
    yield when
    yield from flow


def column_gather(net, source, out, half_of, now=0.0):
    here = net.here

    def slot(by, core):
        return out.at[here.member_at(lax.rem(here.z + by, 4), core)]

    core, other = here.core, 1 - here.core
    right, left, sibling = here.step("z", 1), here.step("z", 3), here.sibling()
    keep = net.local(source, slot(0, core))
    a = net.push(source, slot(0, core), right)
    b = net.push(source, slot(0, core), left)
    s = [net.push(source, slot(0, core), sibling)]
    now += time_of(source)
    yield now
    net.got(a, slot(3, core))
    c = net.push(half_of(slot(3, core), 0), half_of(slot(3, core), 0), right)
    s.append(net.push(slot(3, core), slot(3, core), sibling))
    net.got(b, slot(1, core))
    d = net.push(half_of(slot(1, core), 1), half_of(slot(1, core), 1), left)
    s.append(net.push(slot(1, core), slot(1, core), sibling))
    now += time_of(source, 100.0)
    yield now
    net.got(c, half_of(slot(2, core), 0))
    net.got(d, half_of(slot(2, core), 1))
    s.append(net.push(slot(2, core), slot(2, core), sibling))
    yield now + time_of(source, 200.0)
    for number, by in zip(s, (0, 3, 1, 2)):
        net.got(number, slot(by, other))
    keep.wait()


def row_half(size):
    first = (size // 2 + 15) // 16 * 16

    def half(ref, k):
        return ref.at[pl.ds(0, first)] if k == 0 else ref.at[pl.ds(first, size - first)]

    return half


def ring_gather(net, axis, source, slot, half, now, rate):
    right, left = net.here.step(axis, 1), net.here.step(axis, 3)
    a = net.push(source, slot(0), right)
    b = net.push(source, slot(0), left)
    now += time_of(source, rate)
    yield now
    net.got(a, slot(3))
    c = net.push(half(slot(3), 0), half(slot(3), 0), right)
    net.got(b, slot(1))
    d = net.push(half(slot(1), 1), half(slot(1), 1), left)
    now += time_of(source, 2 * rate)
    yield now
    net.got(c, half(slot(2), 0))
    net.got(d, half(slot(2), 1))
    return now


def swap_pair(net, payload, target, begin, now):
    here = net.here
    yield begin
    number = net.push(payload.at[1 - here.z_lo], target, here.partner())
    yield now
    net.got(number, target)


def plane_gather(net, payload, pair, out, rate=50.0, now=0.0):
    here = net.here
    z, x, y = here.z_lo, here.x, here.y
    rows = row_half(48)
    two = lambda ref, k: ref.at[pl.ds(2 * k, 2)]
    swap = []

    def first():
        if pair is None:
            swap.append(net.push(payload.at[1 - z], out.at[z, x, y], here.partner()))
        keep = net.local(payload.at[z], out.at[z, x, y])
        then = yield from ring_gather(
            net, "x", payload.at[z], lambda by: out.at[z, lax.rem(x + by, 4), y], rows, now, rate
        )
        keep.wait()
        bundle = lambda by: out.at[z, :, lax.rem(y + by, 4)]
        yield from ring_gather(net, "y", bundle(0), bundle, two, then, rate)

    def second():
        w = 1 - z
        then, source = now, pair
        if pair is None:
            then, source = now + time_of(payload.at[0], rate), out.at[w, x, y]
            yield then
            net.got(swap[0], source)
        else:
            keep = net.local(pair, out.at[w, x, y])
        then = yield from ring_gather(
            net, "y", source, lambda by: out.at[w, x, lax.rem(y + by, 4)], rows, then, rate
        )
        if pair is not None:
            keep.wait()
        bundle = lambda by: out.at[w, lax.rem(x + by, 4)]
        yield from ring_gather(net, "x", bundle(0), bundle, two, then, rate)

    return [first(), second()]


def add(target, *parts):
    total = parts[0][...].astype(F32)
    for part in parts[1:]:
        total = total + part[...].astype(F32)
    target[...] = total.astype(target.dtype)


def ring_sum(net, axis, block, half, halves, wholes, target, now, rate=50.0):
    right, left = net.here.step(axis, 1), net.here.step(axis, 3)
    lower, upper = halves
    a = net.push(half(block(2), 0), lower, right)
    b = net.push(half(block(2), 1), upper, left)
    now += time_of(lower, rate)
    yield now
    net.got(a, lower)
    add(half(block(1), 0), half(block(1), 0), lower)
    c = net.push(block(1), wholes[0], right)
    net.got(b, upper)
    add(half(block(3), 1), half(block(3), 1), upper)
    d = net.push(block(3), wholes[1], left)
    now += time_of(wholes[0], rate)
    yield now
    net.got(c, wholes[0])
    net.got(d, wholes[1])
    add(target, block(0), wholes[0], wholes[1])
    return now


def column_sum(net, parts, out, sums, sibling_parts, halves, wholes, now=0.0):
    here = net.here
    half = row_half(parts.shape[1])
    at = lambda by: lax.rem(here.z + by, 4)
    numbers = {}
    for by in (2, 1, 3, 0):
        numbers[by] = net.push(
            parts.at[here.member_at(at(by), 1 - here.core)], sibling_parts.at[at(by)], here.sibling()
        )
    now += HOP
    for by in (2, 1, 3):
        now += time_of(sums.at[0], 200.0) - HOP
        yield now
        net.got(numbers[by], sibling_parts.at[at(by)])
        add(sums.at[at(by)], parts.at[here.member_at(at(by), here.core)], sibling_parts.at[at(by)])
        if by == 2:
            ring = ring_sum(
                net, "z", lambda by: sums.at[at(by)], half, (halves.at[0], halves.at[1]),
                (wholes.at[0], wholes.at[1]), out, now,
            )
            when = next(ring)
    net.got(numbers[0], sibling_parts.at[at(0)])
    add(sums.at[at(0)], parts.at[here.member_at(at(0), here.core)], sibling_parts.at[at(0)])
    yield when
    now = yield from ring
    return now


def column_sum_rows(net, parts, out, scratch, k, now):
    sums, sibling_parts, halves, wholes = scratch
    rows, half_rows = pl.ds(k * PART, PART), pl.ds(k * PART // 2, PART // 2)
    now = yield from column_sum(
        net, parts.at[:, rows], out.at[rows], sums.at[:, rows], sibling_parts.at[:, rows], halves.at[:, half_rows],
        wholes.at[:, rows], now=now,
    )
    return now


def column_sum_scratch(rows, columns):
    return [
        pltpu.VMEM((4, rows, columns), BF16),
        pltpu.VMEM((4, rows, columns), BF16),
        pltpu.VMEM((2, rows // 2, columns), BF16),
        pltpu.VMEM((2, rows, columns), BF16),
    ]


def plane_sum(net, parts, out, held, pairs, bundles, rows_a, rows_b, blocks, rate=50.0, now=2.0):
    here = net.here
    at_x = lambda by: lax.rem(here.x + by, 4)
    at_y = lambda by: lax.rem(here.y + by, 4)
    pair = lambda ref, k: ref.at[pl.ds(2 * k, 2)]
    half = row_half(48)

    def first():
        if parts is not None:
            copy = net.local(parts.at[0], held.at[0])
            yield now
            copy.wait()
        mine = held.at[0, :, here.y]
        then = yield from ring_sum(
            net, "y", lambda by: held.at[0, :, at_y(by)], pair, (pairs.at[0], pairs.at[1]),
            (bundles.at[0], bundles.at[1]), mine, now, rate,
        )
        yield from ring_sum(
            net, "x", lambda by: held.at[0, at_x(by), here.y], half, (rows_a.at[0], rows_b.at[0]),
            (blocks.at[0], blocks.at[1]), out.at[0], then, rate,
        )

    def second():
        if parts is not None:
            copy = net.local(parts.at[1], held.at[1])
            yield now
            copy.wait()
        mine = held.at[1, here.x]
        then = yield from ring_sum(
            net, "x", lambda by: held.at[1, at_x(by)], pair, (pairs.at[2], pairs.at[3]),
            (bundles.at[2], bundles.at[3]), mine, now, rate,
        )
        yield from ring_sum(
            net, "y", lambda by: held.at[1, here.x, at_y(by)], half, (rows_a.at[1], rows_b.at[1]),
            (blocks.at[2], blocks.at[3]), out.at[1], then, rate,
        )

    return [first(), second()]


def plane_sum_scratch(columns):
    return [
        pltpu.VMEM((2, 4, 4, 48, columns), BF16),
        pltpu.VMEM((4, 2, 48, columns), BF16),
        pltpu.VMEM((4, 4, 48, columns), BF16),
        pltpu.VMEM((2, 32, columns), BF16),
        pltpu.VMEM((2, 16, columns), BF16),
        pltpu.VMEM((4, 48, columns), BF16),
    ]


def column_deal(net, parts, out, passing, half, now=0.0, begin=0.0):
    here = net.here
    z = here.z_lo
    if begin:
        yield begin
        now = max(now, begin)
    core, other = here.core, 1 - here.core
    lower, upper = passing

    def slot(by, core):
        return out.at[here.member_at(lax.rem(here.z + by, 4), core)]

    right, left, sibling = here.step("z", 1), here.step("z", 3), here.sibling()
    keep = net.local(parts.at[z], slot(0, core))
    e = net.push(half(parts.at[z], 0), lower, right)
    f = net.push(half(parts.at[z], 1), upper, left)
    a = net.push(parts.at[1 - z], slot(0, core), right)
    b = net.push(parts.at[1 - z], slot(0, core), left)
    s = [net.push(parts.at[z], slot(0, core), sibling)]
    now += time_of(parts.at[0])
    yield now
    net.got(e, lower)
    c = net.push(lower, half(slot(3, core), 0), right)
    net.got(f, upper)
    d = net.push(upper, half(slot(1, core), 1), left)
    net.got(a, slot(3, core))
    s.append(net.push(slot(3, core), slot(3, core), sibling))
    net.got(b, slot(1, core))
    s.append(net.push(slot(1, core), slot(1, core), sibling))
    now += time_of(parts.at[0])
    yield now
    net.got(c, half(slot(2, core), 0))
    net.got(d, half(slot(2, core), 1))
    s.append(net.push(slot(2, core), slot(2, core), sibling))
    yield now + HOP
    for number, by in zip(s, (0, 3, 1, 2)):
        net.got(number, slot(by, other))
    keep.wait()


def column_route(me, pieces):
    z, place, unused, unused2 = parts_of(me[0])
    mine = z * 4 + me[1]

    def where(member):
        return (member // 4) * PLANE + place, lax.rem(member, 4)

    def after(i):
        return lax.rem(mine + 1 + i, 8)

    def before(i):
        return lax.rem(mine + 7 - i, 8)

    return Route(
        7,
        lambda i: where(after(i)),
        lambda i: where(before(i)),
        [
            (
                a,
                lambda i, cut=cut: cut(after(i)),
                b,
                lambda i, slot=slot: slot(mine),
                lambda i, slot=slot: slot(before(i)),
            )
            for a, cut, b, slot in pieces
        ],
    )


def plane_route(me, pieces):
    z, place, unused, unused2 = parts_of(me[0])

    def after(i):
        return lax.rem(place + 1 + i, PLANE)

    def before(i):
        return lax.rem(place + 15 - i, PLANE)

    return Route(
        15,
        lambda i: (z * PLANE + after(i), me[1]),
        lambda i: (z * PLANE + before(i), me[1]),
        [
            (
                a,
                lambda i, cut=cut: cut(after(i)),
                b,
                lambda i, slot=slot: slot(place),
                lambda i, slot=slot: slot(before(i)),
            )
            for a, cut, b, slot in pieces
        ],
    )


def own_copies(net, ins, outs, copies):
    started = [net.local(ins[a].at[cut], outs[b].at[slot]) for a, cut, b, slot in copies]
    yield 100.0
    for copy in started:
        copy.wait()


ROW_HALF = row_half(TOK)


def mirrored(z, x):
    return x + z * (3 - 2 * x)


def query_routes(me, q_in, q_out):
    z_me, place, x, y = parts_of(me[0])
    base = z_me * PLANE

    def plain(i):
        return lax.rem(y + 1 + i, 4)

    def plain_before(i):
        return lax.rem(y + 3 - i, 4)

    def other(i):
        return lax.rem(y + i, 4)

    def other_before(i):
        return lax.rem(y + 4 - i, 4)

    first = Route(
        3,
        lambda i: (base + 4 * x + plain(i), me[1]),
        lambda i: (base + 4 * x + plain_before(i), me[1]),
        [
            (
                q_in,
                lambda i: (0, crossed(plain(i))),
                q_out,
                lambda i: (0, crossed(y)),
                lambda i: (0, crossed(plain_before(i))),
            )
        ],
    )
    second = Route(
        4,
        lambda i: (base + 4 * (3 - x) + other(i), me[1]),
        lambda i: (base + 4 * (3 - x) + other_before(i), me[1]),
        [
            (
                q_in,
                lambda i: (1, crossed(other(i))),
                q_out,
                lambda i: (1, crossed(y)),
                lambda i: (1, crossed(other_before(i))),
            )
        ],
    )
    return [first, second], [(q_in, (0, crossed(y)), q_out, (0, crossed(y)))]


def pack_attention(pack, query_weight, keyval_weight, router_lines, first_gain, second_gain, rep):
    blank = jnp.zeros((3, 48), F32)
    lines = router_lines[...].astype(F32)
    small = jnp.concatenate(
        [
            lines[:5], blank, lines[5:], blank, first_gain[...].astype(F32), second_gain[...].astype(F32),
            jnp.zeros((6, 48), F32),
        ],
        0,
    ).T.astype(BF16)
    fill = jnp.zeros((48, PACK - ROUTER_AT - 24), BF16)
    for k in range(4):

        @pl.when(rep == k)
        def fill_in(k=k):
            for z in range(2):
                m = 4 * z + k
                pack[z] = jnp.concatenate(
                    [
                        query_weight[:, m * QROWS : (m + 1) * QROWS],
                        keyval_weight[:, m * HEAD_DIM : (m + 1) * HEAD_DIM],
                        keyval_weight[:, (HEADS + m) * HEAD_DIM : (HEADS + m + 1) * HEAD_DIM],
                        small,
                        fill,
                    ],
                    1,
                )


def pack_experts(net, pack, gate_up_weight, down_weight):
    copies = []
    for z in range(2):
        for expert in range(5):
            for side in range(2):
                source = pl.ds(pl.multiple_of(side * FF + net.here.rep * TOK, TOK), TOK)
                target = pl.ds(expert * 256 + side * TOK, TOK)
                copies.append((gate_up_weight.at[5 * z + expert, :, source], pack.at[z, :, target]))
            source = pl.ds(pl.multiple_of(net.here.rep * TOK, TOK), TOK)
            target = pl.ds(GATE_UP + expert * TOK, TOK)
            copies.append((down_weight.at[5 * z + expert, :, source], pack.at[z, :, target]))
    return [net.local(source, target) for source, target in copies]


def forward(
    x, segments, query_weight, keyval_weight, router_lines, first_gain, out_rows, choices, dy, gate_up_weight,
    down_weight, cosine, sine, second_gain,
):
    def plan(net, ins, outs, scratch):
        here = net.here
        me = here.me
        place, x_at, y_at = here.place, here.x, here.y
        (x_all, attn_all, segment_all, q, kv, ints, normed, linear, out_slice, x_traded, pair, low_rows, parts,
         total) = scratch[:14]
        attending, summing = scratch[14:20], scratch[20:24]
        segment_here, attn, pack, segment_rows, lines, q_here, kv_here, o_here = scratch[24:32]
        (q_kept, kv_kept, starts, o_kept, o_low, lse, lines_kept, turned, residual, own_normed, normed_all, pack_all,
         dy_all, choices_all, dy_traded, choices_traded, out_given) = outs[:17]
        x, segments, out_rows, choices, dy, cosine, sine = ins[0], ins[1], ins[6], ins[7], ins[8], ins[11], ins[12]
        routes, own = query_routes(me, 0, 0)
        routes = [
            plane_route(
                me,
                [
                    (1, lambda p: (0, crossed(lax.rem(p, 4))), 1, lambda p: (0, p)),
                    (1, lambda p: (1, crossed(lax.rem(p, 4))), 1, lambda p: (1, p)),
                    (2, lambda p: crossed(lax.rem(p, 4)), 2, lambda p: p),
                ],
            )
        ] + routes
        own = own + [
            (1, (0, crossed(y_at)), 1, (0, place)),
            (1, (1, crossed(y_at)), 1, (1, place)),
            (2, crossed(y_at), 2, place),
        ]
        segment_routes = [column_route(me, [(0, lambda m: slice(None), 0, lambda m: m)])]
        choice_routes = [column_route(me, [(0, lambda m: slice(None), 0, lambda m: m)])]
        spreading = spread_rows(net, out_rows, out_slice)
        trading = trade(net, [(x, x_traded)], 45.0, 66.0)

        def chain():
            pack_attention(attn, ins[2], ins[3], ins[4], ins[5], ins[13], here.rep)
            segment_rows[...] = jnp.broadcast_to(segments[...], (8, TOK))
            marked = follow_routes(net, segment_routes, [segment_rows], [segment_all])
            next(marked)
            own_mark = net.local(segment_rows, segment_all.at[here.member])
            now = yield from together(plane_gather(net, attn, None, attn_all) + [column_gather(net, x, x_all, ROW_HALF)])
            for unused in marked:
                pass
            own_mark.wait()
            project(x_all, attn_all, cosine, sine, q, kv, turned, normed, linear)
            for sequence in range(4):
                ints[sequence] = jnp.concatenate(
                    [
                        segment_all[sequence, 0:1, :],
                        segment_all[4 + sequence, 0:1, :],
                        jnp.zeros((6, TOK), jnp.int32),
                    ],
                    0,
                )
            targets = [q_here, kv_here, segment_here]
            going = follow_routes(net, routes, [q, kv, ints], targets, now + 22.0)
            copies = own_copies(net, [q, kv, ints], targets, own)
            now = next(going)
            next(copies)
            turn_into(lines, normed)
            kept = [net.local(lines, lines_kept)]
            yield now
            for unused in going:
                pass
            for unused in copies:
                pass
            kept += [net.local(q_here, q_kept), net.local(kv_here, kv_kept)]
            document_starts(segment_here, starts, x_at)
            unpack_queries(q_here, attending[0])
            unpack_keys(kv_here, attending[1], attending[2], x_at)
            for third in range(3):

                def step(k, carry):
                    attend_step(x_at, k, *attending[:3], starts, *attending[3:], o_here, o_low, lse)
                    return carry

                lax.fori_loop(3 * third, 3 * third + 3, step, 0)
                now += 7.0
                yield now
            for unused in spreading:
                pass
            turn_into(low_rows, o_low)
            for block in range(4):
                columns = slice(block * 384, (block + 1) * 384)
                weights = out_slice[:, :, columns].reshape(QROWS, 384)
                product = jnp.dot(low_rows[...], weights, preferred_element_type=F32)
                parts[:, :, columns] = product.astype(BF16).reshape(8, TOK, 384)
            kept += [net.local(out_slice, out_given), net.local(o_here, o_kept)]

            def tail(k, now):
                rows = pl.ds(k * PART, PART)
                now = yield from column_sum_rows(net, parts, total, summing, k, now)
                for unused in trading:
                    pass
                gain = turned[GAIN_ONE_AT : GAIN_ONE_AT + 16, :].astype(F32)[1:2]
                hidden = x_traded[rows, :].astype(F32) + RESIDUAL_SCALE * total[rows, :]
                scale = lax.rsqrt(jnp.sum(hidden * hidden, -1, keepdims=True) * (1.0 / D) + NORM_EPS)
                residual[rows, :] = hidden
                own_normed[rows, :] = (hidden * scale * gain).astype(BF16)
                yield from column_gather(net, own_normed.at[rows], normed_all.at[:, rows], row_half(PART), now)

            yield from together([tail(k, now + 3.0 + 8.0 / PARTS * k) for k in range(PARTS)])
            for copy in kept:
                copy.wait()

        def gather_dy():
            yield from trade(net, [(choices, choices_traded), (dy, dy_traded)], 0.0, 24.0)
            sent = follow_routes(net, choice_routes, [choices_traded], [choices_all], 50.0)
            when = next(sent)
            own_choices = net.local(choices_traded, choices_all.at[here.member])
            yield from together([resumed(when, sent), column_gather(net, dy_traded, dy_all, ROW_HALF, 27.0)])
            own_choices.wait()

        def gather_experts():
            packing = pack_experts(net, pack, ins[9], ins[10])
            yield 22.0
            for copy in packing:
                copy.wait()
            yield from swap_pair(net, pack, pair, 22.0, 43.0)
            yield 46.0
            yield from together(plane_gather(net, pack, pair, pack_all, rate=30.0, now=46.0))

        flows = [chain(), spreading, gather_dy(), trading, gather_experts()]
        return flows, routes + segment_routes + choice_routes, True, [greet_trader]

    return comm(
        [
            x, segments, query_weight, keyval_weight, router_lines, first_gain, out_rows, choices, dy, gate_up_weight,
            down_weight, cosine, sine, second_gain,
        ],
        (1, 2, 3, 4, 5, 11, 12, 13),
        [
            ((2, 4, QROWS, TOK), BF16, False),
            ((2, PLANE, TOK, TOK), BF16, False),
            ((2, 8, RUN), F32, True),
            ((QROWS, 2 * RUN), F32, False),
            ((QROWS, 2 * RUN), BF16, True),
            ((8, 2 * RUN), F32, True),
            ((D, COLUMN), BF16, False),
            ((PACK, D), BF16, True),
            ((TOK, D), F32, True),
            ((TOK, D), BF16, True),
            ((8, TOK, D), BF16, False),
            ((2, 4, 4, 48, EXPERT_PACK), BF16, False),
            ((8, TOK, D), BF16, False),
            ((8, 8, TOK), jnp.int32, False),
            ((TOK, D), BF16, False),
            ((8, TOK), jnp.int32, False),
            ((4, 48, D), BF16, False),
        ],
        [
            pltpu.VMEM((8, TOK, D), BF16),
            pltpu.VMEM((2, 4, 4, 48, PACK), BF16),
            pltpu.VMEM((8, 8, TOK), jnp.int32),
            pltpu.VMEM((2, 4, QROWS, TOK), BF16),
            pltpu.VMEM((2, 4, TOK, TOK), BF16),
            pltpu.VMEM((4, 8, TOK), jnp.int32),
            pltpu.VMEM((COLUMN, D), BF16),
            pltpu.VMEM((ROUTER_AT, COLUMN), F32),
            pltpu.VMEM((4, 48, D), BF16),
            pltpu.VMEM((TOK, D), BF16),
            pltpu.VMEM((48, EXPERT_PACK), BF16),
            pltpu.VMEM((COLUMN, QROWS), BF16),
            pltpu.VMEM((8, TOK, D), BF16),
            pltpu.VMEM((TOK, D), F32),
        ]
        + attend_scratch()
        + column_sum_scratch(TOK, D)
        + [
            pltpu.VMEM((PLANE, 8, TOK), jnp.int32),
            pltpu.VMEM((2, 48, PACK), BF16),
            pltpu.VMEM((2, 48, EXPERT_PACK), BF16),
            pltpu.VMEM((8, TOK), jnp.int32),
            pltpu.VMEM((D, COLUMN), BF16),
            pltpu.VMEM((2, 4, QROWS, TOK), BF16),
            pltpu.VMEM((2, PLANE, TOK, TOK), BF16),
            pltpu.VMEM((QROWS, 2 * RUN), F32),
        ],
        512,
        0,
        plan,
    )


def experts(hn_all, dy_all, pack_all, choices, residual, dy, turned):
    def plan(net, ins, outs, scratch):
        (hn, dy_here, pack, hn_lines, dy_lines, hidden, joined, shares, share_rows, pull_rows, pulls, back, mixture,
         total, low, pull_parts) = scratch[:16]
        summing, held = scratch[16:20], scratch[20:26]
        gate_up, down = pack.at[:, :GATE_UP], pack.at[:, GATE_UP:]
        routes = column_route(net.here.me, [(0, lambda m: m, 0, lambda m: m)])
        mixture_out, grad_out, logits_out, low_all, pack_sum = outs
        mine = net.here.member

        def z_chain(k, now):
            rows = pl.ds(k * PART, PART)
            if k == 0:
                pulled = follow_routes(net, [routes], [pulls], [pull_parts])
                next(pulled)
                own = net.local(pulls.at[mine], pull_parts.at[mine])
            now = yield from column_sum_rows(net, back, total, summing, k, now)
            if k == 0:
                for unused in pulled:
                    pass
                own.wait()
                logit_grads(pull_parts, shares, logits_out)
            residual_grad(total, ins[4], ins[5], ins[6], grad_out, low, logits_out, k)
            yield from column_gather(net, low.at[rows], low_all.at[:, rows], row_half(PART), now)

        def grads(now):
            sums = []

            def weights(first, size, at):
                part = pl.ds(first, size)
                flow = together(plane_sum(net, None, pack_sum.at[:, :, part], *columns_of(held, part), now=at))
                sums.append(resumed(next(flow), flow))

            turn_into(hn_lines, hn)

            def gate_up_step(j, carry):
                place = pl.ds(pl.multiple_of(j * 256, 256), 256)
                product = jnp.dot(
                    hn_lines[...], joined[:, :, place].reshape(COLUMN, 256), preferred_element_type=F32
                )
                held[0][:, :, :, :, place] = product.astype(BF16).reshape(2, 4, 4, 48, 256)
                return carry

            lax.fori_loop(0, 5, gate_up_step, 0)
            weights(0, GATE_UP, now)

            def back_step(j, carry):
                place = pl.ds(pl.multiple_of(j * 256, 256), 256)
                product = product_nt(joined[...].reshape(COLUMN, GATE_UP), gate_up[place, :])
                back[:, :, place] = product.astype(BF16).reshape(8, TOK, 256)
                return carry

            lax.fori_loop(0, D // 256, back_step, 0)
            chains = [z_chain(k, now + 5.0 + 6.0 / PARTS * k) for k in range(PARTS)]
            sums += [resumed(next(flow), flow) for flow in chains]

            def after():
                turn_into(dy_lines, dy_here)
                yield now + 8.0
                for at, size in ((0, 256), (256, 256), (512, 128)):
                    product = RESIDUAL_SCALE * jnp.dot(
                        dy_lines[...], hidden[:, :, at : at + size].reshape(COLUMN, size), preferred_element_type=F32
                    )
                    held[0][:, :, :, :, GATE_UP + at : GATE_UP + at + size] = product.astype(BF16).reshape(
                        2, 4, 4, 48, size
                    )
                part = pl.ds(GATE_UP, EXPERT_PACK - GATE_UP)
                flow = together(
                    plane_sum(net, None, pack_sum.at[:, :, part], *columns_of(held, part), now=now + 14.0)
                )
                when = next(flow)

                def mixture_step(j, carry):
                    place = pl.ds(pl.multiple_of(j * 256, 256), 256)
                    product = product_nt(hidden[...].reshape(COLUMN, 640), down[place, :])
                    mixture[:, :, place] = product.astype(BF16).reshape(8, TOK, 256)
                    return carry

                def mix():
                    yield now + 20.0
                    lax.fori_loop(0, D // 256, mixture_step, 0)
                    store = net.local(mixture, mixture_out)
                    yield now + 60.0
                    store.wait()

                yield from together([resumed(when, flow), mix()])

            yield from together(sums + [after()])

        def chain():
            loads = [net.local(ins[0], hn), net.local(ins[2], pack), net.local(ins[1], dy_here)]
            loads[0].wait()
            expert_shares(hn, ins[6], ins[3], shares, share_rows, net.here.z_lo)
            for load in loads[1:]:
                load.wait()
            for k in range(2):
                experts_forward(hn, dy_here, gate_up, down, hidden, joined, share_rows, pull_rows, k)
            turn_pull(pull_rows, pulls)
            yield 0.0
            yield from grads(1.0)

        return [chain()], [routes], True, []

    wide = lambda rows, columns: pltpu.VMEM((rows, columns), BF16)
    blocks = lambda columns, dtype=BF16: pltpu.VMEM((8, TOK, columns), dtype)
    return comm(
        [hn_all, dy_all, pack_all, choices, residual, dy, turned],
        (3, 4, 5, 6),
        [
            ((8, TOK, D), BF16, False),
            ((TOK, D), BF16, True),
            ((16, TOK), F32, True),
            ((8, TOK, D), BF16, False),
            ((2, 48, EXPERT_PACK), BF16, True),
        ],
        [
            blocks(D), blocks(D), wide(D, EXPERT_PACK), wide(D, COLUMN), wide(D, COLUMN), blocks(640),
            blocks(GATE_UP), pltpu.VMEM((8, 16, TOK), F32), blocks(8, F32), blocks(8, F32),
            pltpu.VMEM((8, 8, TOK), F32), blocks(D), blocks(D), pltpu.VMEM((TOK, D), F32), wide(TOK, D),
            pltpu.VMEM((8, 8, TOK), F32),
        ]
        + column_sum_scratch(TOK, D)
        + plane_sum_scratch(EXPERT_PACK),
        320,
        3,
        plan,
    )


def columns_of(refs, columns):
    return [ref.at[(slice(None),) * (len(ref.shape) - 1) + (columns,)] for ref in refs]


def backward(
    q_here, kv_here, mixture, residual, lines, turned, hn, logits, cosine, sine, o_low, grad_lin, pack, grad,
    o_here, lse, starts, out_rows,
):
    def plan(net, ins, outs, scratch):
        me = net.here.me
        place, x_at, y_at = net.here.place, net.here.x, net.here.y
        mine = net.here.member
        (dq, dkv, lines_here, grad_lin_here, row_send, row_parts, row_sum, lower, upper, lower_pack, upper_pack,
         attn_sum, grads, rows_of_grads, routed, hn_lines, normed_parts, mixture_sum, low_out) = scratch[:19]
        held = scratch[19:25]
        one_sum, other_sum = scratch[25:29], scratch[29:33]
        queries, do, key_rows, value_rows, key_lines, key_grad, value_grad, query_grad, delta = scratch[33:42]
        dq_send, dkv_send = scratch[42:44]
        routes, own = query_routes(me, 0, 0)
        routes = [plane_route(me, [(1, lambda p: (slice(None), p), 1, lambda p: p)])] + routes
        own = own + [(1, (slice(None), place), 1, place)]
        rows_in = [plane_route(me, [(0, lambda p: p, 0, lambda p: p)])]
        rows_out = [
            Route(
                4,
                lambda i: (4 * mine + place // 4, i),
                lambda i: (
                    (me[0] // 4) // 4 * PLANE + 4 * lax.rem(me[0], 4) + i,
                    lax.rem(me[0] // 4, 4),
                ),
                [(0, lambda i: slice(None), 3, lambda i: lax.rem(place, 4), lambda i: i)],
                index=lambda i: lax.rem(place, 4),
                may_be_self=True,
            ),
        ]
        half = row_half(48)

        def rows():
            keep = net.local(row_send.at[place], row_parts.at[place])
            yield from follow_routes(net, rows_in, [row_send], [row_parts], 20.0)
            keep.wait()
            total = row_parts[0].astype(F32)
            for k in range(1, PLANE):
                total = total + row_parts[k].astype(F32)
            row_sum[...] = total.astype(BF16)
            yield from follow_routes(net, rows_out, [row_sum], outs, 45.0)

        def chain():
            loads = [net.local(ins[4], lines_here), net.local(ins[11], grad_lin_here)]
            unpack_queries(ins[0], queries)
            spread_keys(ins[1], key_rows, value_rows, key_lines, x_at)
            key_grad[...] = jnp.zeros_like(key_grad)
            value_grad[...] = jnp.zeros_like(value_grad)
            loads[1].wait()
            weights = ins[17][...].reshape(QROWS, D)
            do[...] = product_nt(weights, grad_lin_here[...]).astype(BF16)
            total = jnp.dot(ins[10][...], grad_lin_here[...], preferred_element_type=F32)
            blank = jnp.zeros((4, D), F32)
            for k in range(PLANE):
                row_send[k] = jnp.concatenate([total[12 * k : 12 * k + 12], blank], 0).astype(BF16)
            row_flow = rows()
            row_when = next(row_flow)
            now = 6.0
            for third in range(3):

                def step(k, carry):
                    attend_back_step(
                        x_at, k, queries, do, ins[14], ins[15], ins[16], key_rows, value_rows, key_lines,
                        key_grad, value_grad, query_grad, delta, dq_send,
                    )
                    return carry

                lax.fori_loop(3 * third, 3 * third + 3, step, 0)
                now += 5.0
                yield now
            collect_keys(key_grad, value_grad, dkv_send)
            going = follow_routes(net, routes, [dq_send, dkv_send], [dq, dkv], now + 22.0)
            copies = own_copies(net, [dq_send, dkv_send], [dq, dkv], own)
            when = next(going)
            next(copies)
            turn_into(hn_lines, ins[6])
            yield row_when
            row_when = next(row_flow)
            yield when
            for unused in going:
                pass
            for unused in copies:
                pass
            loads[0].wait()
            weight_grads(dq, dkv, lines_here, hn_lines, ins[7], ins[8], ins[9], held[0], grads, routed)
            now = when + 10.0

            def weights():
                then = yield from together(plane_sum(net, None, attn_sum, *held, now=now))
                yield from column_deal(net, attn_sum, outs[1], (lower, upper), half, then)

            def normed():
                normed_grads(grads, rows_of_grads, ins[5], normed_parts)
                yield from together(
                    [column_sum_rows(net, normed_parts, outs[0], one_sum, k, now + 6.0 + 8.0 / PARTS * k) for k in range(PARTS)]
                )

            yield from together([weights(), normed(), resumed(row_when, row_flow)])

        def layer_output():
            now = yield from column_sum(net, ins[2], mixture_sum, *other_sum)
            low_out[...] = (ins[3][...] + RESIDUAL_SCALE * mixture_sum[...]).astype(BF16)
            yield from trade(net, [(low_out, outs[4])], 48.0, 75.0)

        flows = [
            trade(net, [(ins[13], outs[5])], 0.0, 30.0),
            layer_output(),
            chain(),
            column_deal(net, ins[12], outs[2], (lower_pack, upper_pack), half, begin=24.0),
        ]
        return flows, routes + rows_in + rows_out, True, [greet_trader]

    return comm(
        [
            q_here, kv_here, mixture, residual, lines, turned, hn, logits, cosine, sine, o_low, grad_lin, pack, grad,
            o_here, lse, starts, out_rows,
        ],
        (0, 1, 2, 3, 5, 6, 7, 8, 9, 10, 14, 15, 16, 17),
        [
            ((TOK, D), F32, True),
            ((8, 48, PACK), BF16, False),
            ((8, 48, EXPERT_PACK), BF16, False),
            ((4, 16, D), BF16, False),
            ((TOK, D), BF16, False),
            ((TOK, D), BF16, False),
        ],
        [
            pltpu.VMEM((2, 4, QROWS, TOK), BF16),
            pltpu.VMEM((PLANE, 2, TOK, TOK), BF16),
            pltpu.VMEM((D, COLUMN), BF16),
            pltpu.VMEM((COLUMN, D), BF16),
            pltpu.VMEM((PLANE, 16, D), BF16),
            pltpu.VMEM((PLANE, 16, D), BF16),
            pltpu.VMEM((16, D), BF16),
            pltpu.VMEM((32, PACK), BF16),
            pltpu.VMEM((16, PACK), BF16),
            pltpu.VMEM((32, EXPERT_PACK), BF16),
            pltpu.VMEM((16, EXPERT_PACK), BF16),
            pltpu.VMEM((2, 48, PACK), BF16),
            pltpu.VMEM((PACK, COLUMN), BF16),
            pltpu.VMEM((COLUMN, PACK), BF16),
            pltpu.VMEM((PACK, TOK), BF16),
            pltpu.VMEM((D, TOK), BF16),
            pltpu.VMEM((8, TOK, D), BF16),
            pltpu.VMEM((TOK, D), F32),
            pltpu.VMEM((TOK, D), BF16),
        ]
        + plane_sum_scratch(PACK)
        + column_sum_scratch(TOK, D)
        + column_sum_scratch(TOK, D)
        + attend_back_scratch()
        + [pltpu.VMEM((2, 4, QROWS, TOK), BF16), pltpu.VMEM((2, PLANE, TOK, TOK), BF16)],
        480,
        4,
        plan,
    )


NT = (((1,), (1,)), ((), ()))


def product_nt(one, other):
    return lax.dot_general(one, other, NT, preferred_element_type=F32)


def unit(size):
    rows = lax.broadcasted_iota(jnp.int32, (size, size), 0)
    return (rows == lax.broadcasted_iota(jnp.int32, (size, size), 1)).astype(BF16)


def turn_into(target, source, block=256):
    ones = unit(block)

    def step(k, carry):
        place = pl.ds(pl.multiple_of(k * block, block), block)
        if len(source.shape) == 3:
            part = source[:, :, place].reshape(target.shape[1], block)
        else:
            part = source[:, place]
        target[place, :] = product_nt(ones, part).astype(BF16)
        return carry

    lax.fori_loop(0, source.shape[-1] // block, step, 0)


def project(x_ref, attn_ref, cos_ref, sin_ref, q_ref, kv_ref, turned_ref, normed, linear):
    ones = unit(PACK)
    for z in range(2):
        weights = attn_ref[z].reshape(D // 2, PACK)
        turned_ref[:, z * (D // 2) : (z + 1) * (D // 2)] = product_nt(ones, weights).astype(BF16)
    gain = turned_ref[GAIN_ONE_AT : GAIN_ONE_AT + 16, :].astype(F32)[0:1]

    def norm(k, carry):
        place = pl.ds(pl.multiple_of(k * TOK, TOK), TOK)
        values = x_ref[k].astype(F32)
        scale = lax.rsqrt(jnp.sum(values * values, -1, keepdims=True) * (1.0 / D) + NORM_EPS)
        normed[place, :] = (values * scale * gain).astype(BF16)
        return carry

    lax.fori_loop(0, 8, norm, 0)
    for part in range(2):
        place = slice(part * 512, (part + 1) * 512)
        linear[:, place] = product_nt(turned_ref[:ROUTER_AT, :], normed[place, :])
    for z in range(2):
        cosine, sine = cos_ref[z], sin_ref[z]
        for sequence in range(4):
            at = (4 * z + sequence) * TOK
            for head in range(GROUP + 1):
                rows = head * HEAD_DIM
                front = linear[rows : rows + HALF, at : at + TOK]
                behind = linear[rows + HALF : rows + HEAD_DIM, at : at + TOK]
                one = (front * cosine - behind * sine).astype(BF16)
                two = (behind * cosine + front * sine).astype(BF16)
                if head < GROUP:
                    q_ref[z, sequence, rows : rows + HALF, :] = one
                    q_ref[z, sequence, rows + HALF : rows + HEAD_DIM, :] = two
                else:
                    kv_ref[z, sequence, :HALF, :] = one
                    kv_ref[z, sequence, HALF:HEAD_DIM, :] = two
            kv_ref[z, sequence, HEAD_DIM:, :] = linear[QROWS + HEAD_DIM : ROUTER_AT, at : at + TOK].astype(BF16)


def local_kernel(kernel, inputs, smem, anywhere_in, outputs, scratch):
    vmem = pl.BlockSpec(memory_space=pltpu.VMEM)
    anywhere = pl.BlockSpec(memory_space=pl.ANY)
    scalars = pl.BlockSpec(memory_space=pltpu.SMEM)
    return pl.pallas_call(
        kernel,
        out_shape=[jax.ShapeDtypeStruct(shape, dtype) for shape, dtype, unused in outputs],
        in_specs=[
            scalars if k in smem else anywhere if k in anywhere_in else vmem for k in range(len(inputs))
        ],
        out_specs=[vmem if inside else anywhere for unused, unused2, inside in outputs],
        scratch_shapes=scratch,
        compiler_params=pltpu.CompilerParams(vmem_limit_bytes=VMEM_LIMIT),
    )(*inputs)


def expert_shares(hn, turned_ref, choices_ref, share_ref, share_rows, z):
    row = lax.broadcasted_iota(jnp.int32, (16, TOK), 0)
    router = turned_ref[ROUTER_AT : ROUTER_AT + 16, :]

    def route(block, carry):
        logits = product_nt(router, hn[block])
        named = choices_ref[block]
        named = named + jnp.where(named >= 5, 3, 0)
        chosen = row == named[0:1]
        for k in range(1, 8):
            chosen = jnp.logical_or(chosen, row == named[k : k + 1])
        logits = jnp.where(chosen, logits, MASK_FILL)
        exponent = jnp.where(chosen, jnp.exp(logits - jnp.max(logits, 0, keepdims=True)), 0.0)
        share_ref[block] = exponent / jnp.sum(exponent, 0, keepdims=True)
        mine = share_ref[block, pl.ds(pl.multiple_of(z * 8, 8), 8), :]
        share_rows[block] = mine.T
        return carry

    lax.fori_loop(0, 8, route, 0)


def experts_forward(hn, dy, gate_up, down, hidden, joined, share_rows, pull_rows, k):
    rows = pl.ds(k * 64, 64)
    for expert in range(5):
        both = jnp.dot(
            hn[:, rows, :].reshape(512, D),
            gate_up[:, expert * 256 : expert * 256 + 256],
            preferred_element_type=F32,
        )
        gate, up = both[:, :TOK], both[:, TOK:]
        pulled = RESIDUAL_SCALE * jnp.dot(
            dy[:, rows, :].reshape(512, D),
            down[:, expert * TOK : (expert + 1) * TOK],
            preferred_element_type=F32,
        )
        share = share_rows[:, rows, expert : expert + 1].reshape(512, 1)
        sigmoid = 1.0 / (1.0 + jnp.exp(-gate))
        silu = gate * sigmoid
        act = (silu * up).astype(BF16).astype(F32)
        hidden[:, rows, expert * TOK : (expert + 1) * TOK] = (share * act).astype(BF16).reshape(8, 64, TOK)
        pull_rows[:, rows, expert : expert + 1] = jnp.sum(act * pulled, 1, keepdims=True).reshape(8, 64, 1)
        grad = share * pulled
        left = (grad * up * (sigmoid + silu * (1.0 - sigmoid))).astype(BF16)
        joined[:, rows, expert * 256 : expert * 256 + TOK] = left.reshape(8, 64, TOK)
        joined[:, rows, expert * 256 + TOK : expert * 256 + 256] = (grad * silu).astype(BF16).reshape(8, 64, TOK)


def turn_pull(pull_rows, pull_ref):
    pull_rows[:, :, 5:8] = jnp.zeros((8, TOK, 3), F32)

    def step(block, carry):
        pull_ref[block] = pull_rows[block].T
        return carry

    lax.fori_loop(0, 8, step, 0)


def logit_grads(pull_ref, share_ref, logit_ref):
    shard, rep = my_place()
    shares = share_ref[(shard // PLANE) * 4 + rep]
    pulls = []
    for z in range(2):
        total = pull_ref[4 * z]
        for quarter in range(1, 4):
            total = total + pull_ref[4 * z + quarter]
        pulls.append(total)
    pull = jnp.concatenate(pulls, 0)
    logit_ref[...] = shares * (pull - jnp.sum(shares * pull, 0, keepdims=True))


def residual_grad(sum_ref, residual_ref, dy_ref, turned_ref, grad_ref, low_ref, logit_ref, k):
    rows = pl.ds(k * PART, PART)
    logits = logit_ref[...].T[k * PART : (k + 1) * PART]
    router = turned_ref[ROUTER_AT : ROUTER_AT + 16, :].astype(F32)
    gain = turned_ref[GAIN_ONE_AT : GAIN_ONE_AT + 16, :].astype(F32)[1:2]
    grad_normed = sum_ref[rows, :] + jnp.dot(
        logits, router, precision=PRECISE, preferred_element_type=F32
    )
    residual = residual_ref[rows, :]
    scale = lax.rsqrt(jnp.sum(residual * residual, -1, keepdims=True) * (1.0 / D) + NORM_EPS)
    weighted = grad_normed * gain
    mean = jnp.sum(weighted * residual, -1, keepdims=True) * (1.0 / D)
    grad = dy_ref[rows, :].astype(F32) + scale * weighted - residual * (scale * scale * scale * mean)
    grad_ref[rows, :] = grad.astype(BF16)
    low_ref[rows, :] = (RESIDUAL_SCALE * grad).astype(BF16)


def weight_grads(dq_ref, dkv_ref, lines_ref, hn_lines, logit_ref, cos_ref, sin_ref, weight_ref, grads, routed):
    grads[ROUTER_AT:, :] = jnp.zeros((PACK - ROUTER_AT, COLUMN), BF16)
    for z in range(2):
        cosine, sine = cos_ref[z], sin_ref[z]
        for sequence in range(4):
            at = (4 * z + sequence) * TOK
            column = crossed(sequence)
            total = dkv_ref[column, z].astype(F32)
            for quarter in range(1, 4):
                total = total + dkv_ref[4 * quarter + column, z].astype(F32)
            for head in range(GROUP + 1):
                rows = head * HEAD_DIM
                if head < GROUP:
                    front = dq_ref[z, sequence, rows : rows + HALF, :].astype(F32)
                    behind = dq_ref[z, sequence, rows + HALF : rows + HEAD_DIM, :].astype(F32)
                else:
                    front, behind = total[:HALF], total[HALF:HEAD_DIM]
                grads[rows : rows + HALF, at : at + TOK] = (front * cosine + behind * sine).astype(BF16)
                grads[rows + HALF : rows + HEAD_DIM, at : at + TOK] = (behind * cosine - front * sine).astype(BF16)
            grads[QROWS + HEAD_DIM : ROUTER_AT, at : at + TOK] = total[HEAD_DIM:].astype(BF16)
    routed[...] = jnp.zeros_like(routed)
    routed[ROUTER_AT : ROUTER_AT + 16, :] = logit_ref[...].astype(BF16)

    def weight_step(k, carry):
        place = pl.ds(pl.multiple_of(k * 192, 192), 192)
        total = product_nt(lines_ref[place, :], grads[...]) + product_nt(hn_lines[place, :], routed[...])
        weight_ref[k // 4, lax.rem(k, 4)] = total.astype(BF16).reshape(4, 48, PACK)
        return carry

    lax.fori_loop(0, 8, weight_step, 0)


def normed_grads(grads, rows_of_grads, turned_ref, normed_ref):
    turn_into(rows_of_grads, grads)

    def step(k, carry):
        place = pl.ds(pl.multiple_of(k * 256, 256), 256)
        total = jnp.dot(rows_of_grads[...], turned_ref[:, place], preferred_element_type=F32)
        normed_ref[:, :, place] = total.astype(BF16).reshape(8, TOK, 256)
        return carry

    lax.fori_loop(0, D // 256, step, 0)


def assemble_kernel(
    attn, pack, out_rows, query_weight, keyval_weight, router_weight, gate_up_weight, first_gain, second_gain,
    normed_grad, traded_grad, x, turned, traded_out, input_grad, layer_out,
    query_grad, keyval_grad, out_grad, router_grad, gate_up_grad, down_grad, first_grad, second_grad,
):
    layer_out[...] = traded_out[...]
    values = x[...].astype(F32)
    scale = lax.rsqrt(jnp.sum(values * values, -1, keepdims=True) * (1.0 / D) + NORM_EPS)
    weighted = normed_grad[...] * turned[GAIN_ONE_AT : GAIN_ONE_AT + 16, :].astype(F32)[0:1]
    mean = jnp.sum(weighted * values, -1, keepdims=True) * (1.0 / D)
    input_grad[...] = traded_grad[...].astype(F32) + scale * weighted - values * (scale * scale * scale * mean)
    parts = [attn[m].astype(F32) for m in range(HEADS)]
    query = jnp.concatenate([part[:, :QROWS] for part in parts], 1)
    key = jnp.concatenate([part[:, QROWS : QROWS + HEAD_DIM] for part in parts], 1)
    value = jnp.concatenate([part[:, QROWS + HEAD_DIM : ROUTER_AT] for part in parts], 1)
    query_grad[...] = query
    keyval_grad[:, : HEADS * HEAD_DIM] = key
    keyval_grad[:, HEADS * HEAD_DIM :] = value
    router = parts[0]
    for part in parts[1:]:
        router = router + part
    router = jnp.concatenate([router[:, ROUTER_AT : ROUTER_AT + 5], router[:, ROUTER_AT + 8 : ROUTER_AT + 13]], 1)
    blank = jnp.zeros((48, TOK - EXPERTS - 2), F32)
    for k in range(4):
        out_grad[12 * k : 12 * k + 12, :] = out_rows[k].astype(F32)[:12]
    first = jnp.sum(query * query_weight[...].astype(F32), 1, keepdims=True)
    half = HEADS * HEAD_DIM
    first = first + jnp.sum(key * keyval_weight[:, :half].astype(F32), 1, keepdims=True)
    first = first + jnp.sum(value * keyval_weight[:, half:].astype(F32), 1, keepdims=True)
    second = jnp.sum(router * router_weight[...].astype(F32).T, 1, keepdims=True)
    for expert in range(EXPERTS):
        z, local = expert // 5, expert % 5
        rows = []
        for side in range(2):
            at = local * 256 + side * TOK
            rows += [pack[4 * z + q, :, at : at + TOK].astype(F32) for q in range(4)]
        whole = jnp.concatenate(rows, 1)
        gate_up_grad[expert] = whole
        second = second + jnp.sum(whole * gate_up_weight[expert].astype(F32), 1, keepdims=True)
        at = GATE_UP + local * TOK
        down_grad[expert] = jnp.concatenate(
            [pack[4 * z + q, :, at : at + TOK].astype(F32) for q in range(4)], 1
        )
    lines = jnp.concatenate([router, first, second, blank], 1).T
    router_grad[...] = lines[:EXPERTS]
    first_grad[...] = lines[EXPERTS : EXPERTS + 1] / first_gain[...].astype(F32)
    second_grad[...] = lines[EXPERTS + 1 : EXPERTS + 2] / second_gain[...].astype(F32)


def assemble(*inputs):
    shapes = [(48, D), (48, 1024), (48, D), (EXPERTS, 48), (EXPERTS, 48, 2 * FF), (EXPERTS, 48, FF), (1, 48), (1, 48)]
    outputs = [((TOK, D), F32, True), ((TOK, D), BF16, True)] + [(shape, F32, True) for shape in shapes]
    return local_kernel(assemble_kernel, inputs, (), (), outputs, [])


def run_of(x, step):
    run = (step > x).astype(jnp.int32)
    block = step - run * (x + 1)
    return run, block, block == 0, jnp.logical_or(step == x, step == 8)


def run_base(x, run):
    return (x + run * (7 - 2 * x)) * RUN


def unpack_queries(source, target):
    for run in range(2):
        for part in range(4):
            target[run, :, part * TOK : (part + 1) * TOK] = source[run, part]


def document_starts(segment_ref, starts, x):
    segments = [segment_ref[:, z, :].astype(F32) for z in range(2)]
    earlier = []
    for number in range(1, 5):
        count = [
            jnp.sum(
                jnp.sum((part < number).astype(F32), 0, keepdims=True), 1, keepdims=True
            )
            for part in segments
        ]
        earlier.append(count[0] + count[1])
    for run in range(2):
        first = 4 * (x + run * (3 - 2 * x))
        mark = jnp.concatenate([segment_ref[first + crossed(k), run : run + 1, :] for k in range(4)], 1)
        start = jnp.zeros((1, RUN), F32)
        for number in range(1, 5):
            start = jnp.where(mark == number, earlier[number - 1], start)
        starts[run, 0:1, :] = start


def visible_block(starts, x, run, block):
    key = lax.broadcasted_iota(jnp.int32, (RUN, RUN), 0).astype(F32)
    shift = (block * RUN).astype(F32)
    start = starts[run, 0:1, :] - shift
    lane = lax.broadcasted_iota(jnp.int32, (1, RUN), 1)
    query = (TOK * crossed(lane // TOK) + lax.rem(lane, TOK)).astype(F32) + (run_base(x, run).astype(F32) - shift)
    return jnp.logical_and(key >= start, key <= query)


def unpack_keys(kv_ref, key_rows, value_lines, x):
    ones = unit(TOK)

    def step(j, carry):
        place = pl.ds(pl.multiple_of(j * TOK, TOK), TOK)
        block = kv_ref.at[j // PLANE, lax.rem(j, PLANE)]
        key_rows[place, :] = product_nt(ones, block[:HEAD_DIM, :]).astype(BF16)
        value_lines[:, place] = block[HEAD_DIM:, :]
        return carry

    lax.fori_loop(0, (8 - x) * 4, step, 0)


def attend_step(x, step, queries, key_rows, value_lines, starts, peak, total, acc, o_ref, low_ref, lse_ref):
    run, block, first, last = run_of(x, step)

    @pl.when(first)
    def begin():
        peak[...] = jnp.full_like(peak, MASK_FILL)
        total[...] = jnp.zeros_like(total)
        acc[...] = jnp.zeros_like(acc)

    place = pl.ds(pl.multiple_of(block * RUN, RUN), RUN)
    keys, values = key_rows[place, :], value_lines[:, place]
    seen = visible_block(starts, x, run, block)
    for h in range(GROUP):
        rows = slice(h * HEAD_DIM, (h + 1) * HEAD_DIM)
        scores = jnp.dot(
            keys, queries[run, rows, :] * jnp.asarray(SCORE_SCALE, BF16), preferred_element_type=F32
        )
        scores = jnp.where(seen, scores, MASK_FILL)
        before = peak[h : h + 1, :]
        top = jnp.maximum(before, jnp.max(scores, 0, keepdims=True))
        weights = jnp.exp(scores - top)
        fade = jnp.exp(before - top)
        peak[h : h + 1, :] = top
        total[h : h + 1, :] = fade * total[h : h + 1, :] + jnp.sum(weights, 0, keepdims=True)
        acc[rows, :] = fade * acc[rows, :] + jnp.dot(
            values, weights.astype(BF16), preferred_element_type=F32
        )

    @pl.when(last)
    def end():
        cols = pl.ds(pl.multiple_of(run * RUN, RUN), RUN)
        for h in range(GROUP):
            rows = slice(h * HEAD_DIM, (h + 1) * HEAD_DIM)
            attended = acc[rows, :] / total[h : h + 1, :]
            o_ref[rows, cols] = attended
            low_ref[rows, cols] = attended.astype(BF16)
            lse_ref[h : h + 1, cols] = peak[h : h + 1, :] + jnp.log(total[h : h + 1, :])


def attend_scratch():
    return [
        pltpu.VMEM((2, QROWS, RUN), BF16),
        pltpu.VMEM((SEQ, HEAD_DIM), BF16),
        pltpu.VMEM((HEAD_DIM, SEQ), BF16),
        pltpu.VMEM((8, RUN), F32),
        pltpu.VMEM((8, RUN), F32),
        pltpu.VMEM((QROWS, RUN), F32),
    ]


def spread_keys(kv_ref, key_rows, value_rows, key_lines, x):
    ones = unit(TOK)

    def step(j, carry):
        place = pl.ds(pl.multiple_of(j * TOK, TOK), TOK)
        block = kv_ref[j // PLANE, lax.rem(j, PLANE)]
        turned = product_nt(ones, block).astype(BF16)
        key_rows[place, :] = turned[:, :HEAD_DIM]
        value_rows[place, :] = turned[:, HEAD_DIM:]
        key_lines[:, place] = block[:HEAD_DIM]
        return carry

    lax.fori_loop(0, (8 - x) * 4, step, 0)


def attend_back_step(
    x, step, queries, do_ref, o_ref, lse_ref, starts, key_rows, value_rows, key_lines,
    key_grad, value_grad, query_grad, delta, dq_ref,
):
    run, block, first, last = run_of(x, step)
    cols = pl.ds(pl.multiple_of(run * RUN, RUN), RUN)

    @pl.when(first)
    def begin():
        query_grad[...] = jnp.zeros_like(query_grad)
        for h in range(GROUP):
            rows = slice(h * HEAD_DIM, (h + 1) * HEAD_DIM)
            delta[h : h + 1, :] = jnp.sum(
                do_ref[rows, cols].astype(F32) * o_ref[rows, cols], 0, keepdims=True
            )

    place = pl.ds(pl.multiple_of(block * RUN, RUN), RUN)
    keys, values, lines = key_rows[place, :], value_rows[place, :], key_lines[:, place]
    seen = visible_block(starts, x, run, block)
    dk, dv = key_grad[place, :], value_grad[place, :]
    for h in range(GROUP):
        rows = slice(h * HEAD_DIM, (h + 1) * HEAD_DIM)
        q = queries[run, rows, :] * jnp.asarray(SCORE_SCALE, BF16)
        do = do_ref[rows, cols]
        scores = jnp.dot(keys, q, preferred_element_type=F32)
        weights = jnp.exp(jnp.where(seen, scores, MASK_FILL) - lse_ref[h : h + 1, cols])
        pull = jnp.dot(values, do, preferred_element_type=F32)
        ds = (weights * (pull - delta[h : h + 1, :])).astype(BF16)
        dv = dv + product_nt(weights.astype(BF16), do)
        dk = dk + product_nt(ds, q)
        query_grad[rows, :] += jnp.dot(lines, ds, preferred_element_type=F32)
    key_grad[place, :] = dk
    value_grad[place, :] = dv

    @pl.when(last)
    def end():
        scaled = (SCORE_SCALE * query_grad[...]).astype(BF16)
        for part in range(4):
            dq_ref[run, part] = scaled[:, part * TOK : (part + 1) * TOK]


def collect_keys(key_grad, value_grad, dkv_ref):
    ones = unit(HEAD_DIM)

    def step(j, carry):
        place = pl.ds(pl.multiple_of(j * TOK, TOK), TOK)
        dkv_ref[j // PLANE, lax.rem(j, PLANE), :HEAD_DIM, :] = product_nt(
            ones, key_grad[place, :].astype(BF16)
        ).astype(BF16)
        dkv_ref[j // PLANE, lax.rem(j, PLANE), HEAD_DIM:, :] = product_nt(
            ones, value_grad[place, :].astype(BF16)
        ).astype(BF16)
        return carry

    lax.fori_loop(0, SEQ // TOK, step, 0)


def attend_back_scratch():
    return [
        pltpu.VMEM((2, QROWS, RUN), BF16),
        pltpu.VMEM((QROWS, 2 * RUN), BF16),
        pltpu.VMEM((SEQ, HEAD_DIM), BF16),
        pltpu.VMEM((SEQ, HEAD_DIM), BF16),
        pltpu.VMEM((HEAD_DIM, SEQ), BF16),
        pltpu.VMEM((SEQ, HEAD_DIM), F32),
        pltpu.VMEM((SEQ, HEAD_DIM), F32),
        pltpu.VMEM((QROWS, RUN), F32),
        pltpu.VMEM((8, RUN), F32),
    ]


def shards(
    layer_input,
    segments,
    choices,
    first_gain,
    query_weight,
    key_value_matrix,
    output_weight,
    second_gain,
    router_weight,
    gate_up_weight,
    down_weight,
    cotangent,
):
    shard, rep = my_place()
    z, place, x, y = parts_of(shard)

    frequency = ROPE_BASE ** (-jnp.arange(0, HEAD_DIM, 2, dtype=F32) / HEAD_DIM)
    column_place = (
        (jnp.arange(2, dtype=jnp.int32)[:, None] * PLANE + place) * TOK
        + jnp.arange(TOK, dtype=jnp.int32)[None, :]
    )
    angle = column_place.astype(F32)[:, None, :] * frequency[None, :, None]
    cosine, sine = jnp.cos(angle), jnp.sin(angle)
    (
        q_here, kv_here, starts, o_here, o_low, lse, normed_lines, turned, residual, normed_two, normed_two_all,
        expert_pack, dy_all, choices_all, dy_traded, choices_traded, out_slice,
    ) = forward(
        layer_input[0],
        segments,
        query_weight,
        key_value_matrix,
        router_weight.T,
        first_gain[None],
        output_weight,
        choices[0].T,
        cotangent[0],
        jnp.swapaxes(gate_up_weight, 0, 1),
        jnp.swapaxes(down_weight, 0, 1),
        cosine,
        sine,
        second_gain[None],
    )

    mixture_part, grad_residual, grad_logits, grad_lin_all, pack_sum = experts(
        normed_two_all,
        dy_all,
        expert_pack.reshape(D, EXPERT_PACK),
        choices_all,
        residual,
        dy_traded,
        turned,
    )
    grad_normed, attn_own, pack_own, out_own, layer_out, grad_back = backward(
        q_here, kv_here, mixture_part, residual, normed_lines, turned, normed_two, grad_logits,
        cosine, sine, o_low, grad_lin_all.reshape(COLUMN, D), pack_sum, grad_residual, o_here, lse, starts, out_slice,
    )
    (
        input_grad, layer_out, query_grad, keyval_grad, out_grad_rows, router_grad, gate_up_grad, down_grad,
        first_grad, second_grad,
    ) = assemble(
        attn_own,
        pack_own,
        out_own,
        query_weight,
        key_value_matrix,
        router_weight.T,
        jnp.swapaxes(gate_up_weight, 0, 1),
        first_gain[None],
        second_gain[None],
        grad_normed,
        grad_back,
        layer_input[0],
        turned,
        layer_out,
    )
    return (
        layer_out[None],
        input_grad[None],
        first_grad[0],
        query_grad,
        keyval_grad,
        out_grad_rows,
        second_grad[0],
        router_grad.T,
        jnp.swapaxes(gate_up_grad, 0, 1),
        jnp.swapaxes(down_grad, 0, 1),
    )


def solution(mesh):
    row = P("shard", None)
    rows = P("shard", None, None)
    own = P("rep", "shard", None)
    in_specs = (own, P("rep", "shard"), own, P("shard"), row, row, row, P("shard"), row, rows, rows, own)
    out_specs = (own, own, P("shard"), row, row, row, P("shard"), row, rows, rows)
    return jax.shard_map(shards, mesh=mesh, in_specs=in_specs, out_specs=out_specs, check_vma=False)
```
